32 devices in a mesh: seq: 8 (over z, x), section: 2 (over core), dp: 2 (over y).
Axes of the slice: x: 2, y: 2, z: 4, core: 2. Of those that a mesh axis runs over, the one named last changes fastest.
Arguments:
- queries: bfloat16 [2, 1024, 3584], P('section', 'seq', 'dp'), may hold values from -5 to 5
- key_vectors: bfloat16 [2, 1024, 3584], P('section', 'seq', 'dp'), may hold values from -5 to 5
- value_vectors: bfloat16 [2, 1024, 3584], P('section', 'seq', 'dp'), may hold values from -6 to 6
- out_grad: bfloat16 [2, 1024, 3584], P('section', 'seq', 'dp'), may hold values from -6 to 6
- doc_lengths: int32 [8], replicated, may hold values from 1 to 384, 1024 in all
Outputs:
- query_grad: bfloat16 [2, 1024, 3584], P('section', 'seq', 'dp')
- key_grad: bfloat16 [2, 1024, 3584], P('section', 'seq', 'dp')
- value_grad: bfloat16 [2, 1024, 3584], P('section', 'seq', 'dp')
The draws below stay inside these ranges and needn't reach their ends.
Inputs may be any that keep to these rules, and one draw needn't show every extreme that they name: `doc_lengths`: the 8 lengths sum to 1024; the longest is exactly 384.
All inputs are finite; a program needn't handle non-finite values.
Results may differ from the reference program's by a relative error of at most 0.024.
Values may be sent and summed in bfloat16 or wider, within the bound.
No kernel may reach another device: no remote copies, remote signals or barrier semaphores. Data moves between devices by JAX's collectives and lax.ppermute only.
A program may use at most 192 MiB of HBM per device.

```python
import math
import jax
import jax.numpy as jnp
import numpy as np
from jax import lax

HEADS = 16
HEAD = 224
DOCS = 8
INNER = 3584
LENGTH = 1024
SECTIONS = 2
LONGEST = 384


def draw_queries(key, part):
    key = jax.random.fold_in(key, 7)
    values = jnp.clip(jax.random.normal(key, (SECTIONS, LENGTH, INNER), jnp.float32), -5.0, 5.0)
    return values.astype(jnp.bfloat16)


def draw_key_vectors(key, part):
    key = jax.random.fold_in(key, 9)
    values = jnp.clip(jax.random.normal(key, (SECTIONS, LENGTH, INNER), jnp.float32), -5.0, 5.0)
    return values.astype(jnp.bfloat16)


def levels(stream_key, extent, cuts, low, high):
    def one(dim, shards_of):
        draws = jax.random.uniform(jax.random.fold_in(jax.random.fold_in(stream_key, 6), dim), (shards_of,), jnp.float32, low / len(cuts), high / len(cuts))
        return jnp.repeat(jnp.exp(draws), extent[dim] // shards_of).reshape((-1,) + (1,) * (len(extent) - dim - 1))

    level = one(*cuts[0])
    for cut in cuts[1:]:
        level = level * one(*cut)
    return level


def profile(count, total, bound, lean):
    portions = [(1 << 20) // math.isqrt(grade ** lean) + 1 for grade in range(2, count + 1)]
    spare, given = total - bound - (count - 1), [1] * (count - 1)
    while spare > 0:
        movable = [i for i in range(count - 1) if given[i] < bound]
        mass, remaining = sum([portions[i] for i in movable]), spare
        for i in movable:
            addition = min(bound - given[i], max(1, remaining * portions[i] // mass), spare)
            given[i] = given[i] + addition
            spare = spare - addition
    return np.array([bound] + given)


def ragged(key, count, total, limit, skew):
    if count == 2:
        one = jax.random.randint(key, (), max(1, total - limit), min(limit, total - 1) + 1)
        return jnp.stack([one, total - one])
    tallies = jnp.asarray(profile(count, total, limit, skew), jnp.int32)
    twos = (count - 1) // 2
    giver, receiver = tallies[1:1 + 2 * twos:2], tallies[2:2 + 2 * twos:2]
    room = jnp.minimum(giver - 1, limit - receiver)
    moved = jax.random.randint(jax.random.fold_in(key, 1), (twos,), 0, 1 << 20) % (room + 1)
    tallies = tallies.at[1:1 + 2 * twos:2].set(giver - moved).at[2:2 + 2 * twos:2].set(receiver + moved)
    return tallies[jax.random.permutation(jax.random.fold_in(key, 2), count)]


def bell_draw(own_key, shape, deviation, bound, shards=(), kind=jnp.bfloat16):
    values = deviation * jax.random.normal(own_key, shape, jnp.float32)
    if shards:
        values = values * levels(own_key, shape, shards, -0.22, 0.18)
    return jnp.clip(values, -bound, bound).astype(kind)


def setup_inputs(seed: int = 0) -> dict:
    keys = jax.random.split(jax.random.key(seed), 6)
    return {
        "queries": draw_queries(jax.random.fold_in(keys[5], 71), 0),
        "key_vectors": draw_key_vectors(jax.random.fold_in(keys[5], 71), 0),
        "value_vectors": bell_draw(keys[2], (SECTIONS, LENGTH, INNER), 1.0, 6.0, ((0, 2), (1, 8), (2, 2))),
        "out_grad": bell_draw(keys[3], (SECTIONS, LENGTH, INNER), 1.0, 6.0, ((0, 2), (1, 8), (2, 2))),
        "doc_lengths": ragged(keys[4], DOCS, LENGTH, LONGEST, 2).astype(jnp.int32),
    }


def head_grads(query_head, key_head, value_head, cot_head, allowed):
    scaling = HEAD ** -0.5
    scores = jnp.dot(query_head, key_head.T, preferred_element_type=jnp.float32) * scaling
    scores = jnp.where(allowed, scores, -jnp.inf)
    row_max = jnp.max(scores, axis=1, keepdims=True)
    exponent = jnp.exp(scores - row_max)
    weights = exponent / jnp.sum(exponent, axis=1, keepdims=True)
    rounded = weights.astype(jnp.bfloat16)
    attended = jnp.dot(rounded, value_head, preferred_element_type=jnp.float32).astype(jnp.bfloat16)
    row_dot = jnp.sum(cot_head.astype(jnp.float32) * attended.astype(jnp.float32), axis=1, keepdims=True)
    prob_grad = jnp.dot(cot_head, value_head.T, preferred_element_type=jnp.float32)
    score_grad = (weights * (prob_grad - row_dot) * scaling).astype(jnp.bfloat16)
    query_part = jnp.dot(score_grad, key_head, preferred_element_type=jnp.float32).astype(jnp.bfloat16)
    key_part = jnp.dot(score_grad.T, query_head, preferred_element_type=jnp.float32).astype(jnp.bfloat16)
    value_part = jnp.dot(rounded.T, cot_head, preferred_element_type=jnp.float32).astype(jnp.bfloat16)
    return query_part, key_part, value_part


def split_heads(matrix):
    return matrix.reshape(LENGTH, HEADS, HEAD).transpose(1, 0, 2)


def join_heads(stacked):
    return stacked.transpose(1, 0, 2).reshape(LENGTH, INNER)


def reference(queries, key_vectors, value_vectors, out_grad, doc_lengths):
    positions = jnp.arange(LENGTH, dtype=jnp.int32)
    bounds = jnp.cumsum(doc_lengths)
    doc_index = jnp.sum((positions[:, None] >= bounds[None, :]).astype(jnp.int32), axis=1)
    allowed = (doc_index[:, None] == doc_index[None, :]) & (positions[:, None] >= positions[None, :])

    def one_section(carry, members):
        query_rows, key_rows, value_rows, cot_rows = members

        def per_head(parts):
            return head_grads(parts[0], parts[1], parts[2], parts[3], allowed)

        query_part, key_part, value_part = lax.map(
            per_head, (split_heads(query_rows), split_heads(key_rows), split_heads(value_rows), split_heads(cot_rows)))
        return carry, (join_heads(query_part), join_heads(key_part), join_heads(value_part))

    begin = jnp.zeros((), jnp.float32)
    unused, (query_grad, key_grad, value_grad) = lax.scan(
        one_section, begin, (queries, key_vectors, value_vectors, out_grad))
    return (query_grad, key_grad, value_grad)
```

```python
import functools
import jax
import jax.numpy as jnp
from jax import lax
from jax.experimental import pallas as pl
from jax.experimental.pallas import tpu as pltpu
from jax.sharding import PartitionSpec as P

HEAD = 224
LANES = 128
FLOOR = -1e30


def pick_slot(stacked, slot):
    return lax.dynamic_index_in_dim(stacked, slot, 0, keepdims=False)


def put_slot(stacked, update, slot):
    return lax.dynamic_update_index_in_dim(stacked, update, slot, 0)


def spread_shards(queries, key_vectors, value_vectors, out_grad, doc_lengths):
    local_rows = queries.shape[1]
    local_width = queries.shape[2]
    head_count = local_width // HEAD
    seq_size = lax.axis_size("seq")
    group = seq_size // head_count
    scaling = HEAD ** (-0.5)

    def spread(matrix):
        shaped = matrix.reshape(local_rows, head_count, 1, HEAD)
        copies = jnp.broadcast_to(shaped, (local_rows, head_count, group, HEAD))
        return copies.reshape(local_rows, seq_size * HEAD)

    query_head, key_head, value_head, cot_head = (
        lax.all_to_all(spread(queries), "seq", split_axis=1, concat_axis=0, tiled=True),
        lax.all_to_all(spread(key_vectors), "seq", split_axis=1, concat_axis=0, tiled=True),
        lax.all_to_all(spread(value_vectors), "seq", split_axis=1, concat_axis=0, tiled=True),
        lax.all_to_all(spread(out_grad), "seq", split_axis=1, concat_axis=0, tiled=True),
    )
    length = key_head.shape[0]
    member = lax.axis_index("seq") % group
    blocks = 2 * group
    block = length // blocks
    bounds = jnp.cumsum(doc_lengths)
    positions = jnp.arange(length, dtype=jnp.int32)
    doc_index = jnp.sum((positions[:, None] >= bounds[None, :]).astype(jnp.int32), axis=1)
    row_list = [member, blocks - 1 - member]
    query_list = []
    cot_list = []
    pos_list = []
    for which in range(2):
        offset = row_list[which] * block
        query_list.append(lax.dynamic_slice_in_dim(query_head, offset, block, 0))
        cot_list.append(lax.dynamic_slice_in_dim(cot_head, offset, block, 0))
        pos_list.append(offset + jnp.arange(block, dtype=jnp.int32))
    query_stack = jnp.stack(query_list)
    cot_stack = jnp.stack(cot_list)
    pos_stack = jnp.stack(pos_list)
    doc_stack = jnp.take(doc_index, pos_stack)
    plan = []
    for number in range(blocks + 1):
        first = number <= member
        slot = jnp.where(first, 0, 1).astype(jnp.int32)
        col_block = jnp.where(first, number, number - member - 1)
        flag = None
        plan.append((slot, col_block, flag))
    row_max = jnp.full((2, block), -jnp.inf, jnp.float32)
    row_sum = jnp.zeros((2, block), jnp.float32)
    stored = []
    for slot, col_block, flag in plan:

        def score_tile(carry, slot=slot, col_block=col_block):
            maxima, totals = carry
            query_rows = pick_slot(query_stack, slot)
            key_rows = lax.dynamic_slice_in_dim(key_head, col_block * block, block, 0)
            col_docs = lax.dynamic_slice_in_dim(doc_index, col_block * block, block, 0)
            col_positions = col_block * block + jnp.arange(block, dtype=jnp.int32)
            raw = jnp.dot(query_rows, key_rows.T, preferred_element_type=jnp.float32) * scaling
            allowed = (pick_slot(doc_stack, slot)[:, None] == col_docs[None, :]) & (
                pick_slot(pos_stack, slot)[:, None] >= col_positions[None, :]
            )
            scores = jnp.where(allowed, raw, -jnp.inf)
            before = pick_slot(maxima, slot)
            after = jnp.maximum(before, jnp.max(scores, axis=1))
            safe = jnp.where(jnp.isfinite(after), after, 0.0)
            total = pick_slot(totals, slot) * jnp.exp(before - safe) + jnp.sum(
                jnp.exp(scores - safe[:, None]), axis=1
            )
            return (scores, put_slot(maxima, after, slot), put_slot(totals, total, slot))

        scores, row_max, row_sum = score_tile((row_max, row_sum))
        stored.append(scores)

    def tile_weights(scores, slot):
        return (
            jnp.exp(scores - pick_slot(row_max, slot)[:, None]) / pick_slot(row_sum, slot)[:, None]
        )

    summed = jnp.zeros((2, block, HEAD), jnp.float32)
    for (slot, col_block, flag), scores in zip(plan, stored):

        def add_values(carry, slot=slot, col_block=col_block, scores=scores):
            rounded = tile_weights(scores, slot).astype(jnp.bfloat16)
            value_rows = lax.dynamic_slice_in_dim(value_head, col_block * block, block, 0)
            term = jnp.dot(rounded, value_rows, preferred_element_type=jnp.float32)
            return put_slot(carry, pick_slot(carry, slot) + term, slot)

        summed = add_values(summed)
    attended = summed.astype(jnp.bfloat16)
    row_dot = jnp.sum(cot_stack.astype(jnp.float32) * attended.astype(jnp.float32), axis=2)
    query_acc = jnp.zeros((2, block, HEAD), jnp.float32)
    key_acc = jnp.zeros((length, HEAD), jnp.float32)
    value_acc = jnp.zeros((length, HEAD), jnp.float32)
    for (slot, col_block, flag), scores in zip(plan, stored):

        def backward_tile(carry, slot=slot, col_block=col_block, scores=scores):
            query_sum, key_sum, value_sum = carry
            weights = tile_weights(scores, slot)
            rounded = weights.astype(jnp.bfloat16)
            query_rows = pick_slot(query_stack, slot)
            cot_rows = pick_slot(cot_stack, slot)
            start = col_block * block
            key_rows = lax.dynamic_slice_in_dim(key_head, start, block, 0)
            value_rows = lax.dynamic_slice_in_dim(value_head, start, block, 0)
            value_term = jnp.dot(rounded.T, cot_rows, preferred_element_type=jnp.float32)
            prob_grad = jnp.dot(cot_rows, value_rows.T, preferred_element_type=jnp.float32)
            score_grad = (
                weights * (prob_grad - pick_slot(row_dot, slot)[:, None]) * scaling
            ).astype(jnp.bfloat16)
            query_term = jnp.dot(score_grad, key_rows, preferred_element_type=jnp.float32)
            key_term = jnp.dot(score_grad.T, query_rows, preferred_element_type=jnp.float32)
            query_sum = put_slot(query_sum, pick_slot(query_sum, slot) + query_term, slot)
            key_sum = lax.dynamic_update_slice_in_dim(
                key_sum, lax.dynamic_slice_in_dim(key_sum, start, block, 0) + key_term, start, 0
            )
            value_sum = lax.dynamic_update_slice_in_dim(
                value_sum,
                lax.dynamic_slice_in_dim(value_sum, start, block, 0) + value_term,
                start,
                0,
            )
            return (query_sum, key_sum, value_sum)

        query_acc, key_acc, value_acc = backward_tile((query_acc, key_acc, value_acc))
    query_rounded = query_acc.astype(jnp.bfloat16)
    key_back, value_back = (
        lax.all_to_all(key_acc, "seq", split_axis=0, concat_axis=1, tiled=True),
        lax.all_to_all(value_acc, "seq", split_axis=0, concat_axis=1, tiled=True),
    )

    def settle(received):
        shaped = received.astype(jnp.float32).reshape(local_rows, head_count, group, HEAD)
        return jnp.sum(shaped, axis=2).reshape(1, local_rows, local_width).astype(jnp.bfloat16)

    query_full = jnp.zeros((length, HEAD), jnp.bfloat16)
    for which in range(2):
        query_full = lax.dynamic_update_slice_in_dim(
            query_full, query_rounded[which], row_list[which] * block, 0
        )
    query_back = lax.all_to_all(query_full, "seq", split_axis=0, concat_axis=1, tiled=True)
    query_out = settle(query_back)
    return (query_out, settle(key_back), settle(value_back))


def head_span(head):
    low = head * HEAD // LANES * LANES
    high = -(-(head + 1) * HEAD // LANES) * LANES
    return low, high


def head_mask(head):
    low, high = head_span(head)
    lane = lax.broadcasted_iota(jnp.int32, (1, high - low), 1) + low
    inside = (lane >= head * HEAD) & (lane < (head + 1) * HEAD)
    return inside.astype(jnp.float32).astype(jnp.bfloat16)


def matmul(left, right, dims):
    return lax.dot_general(left, right, (dims, ((), ())), preferred_element_type=jnp.float32)


NT = ((1,), (1,))
NN = ((1,), (0,))
TN = ((0,), (0,))


def tile_masks(place_ref, lengths_ref, rows):
    me = place_ref[0]
    odd = lax.rem(me, 2)
    shape = (rows, rows)
    row = lax.broadcasted_iota(jnp.int32, shape, 0)
    col = lax.broadcasted_iota(jnp.int32, shape, 1)

    def first_of(block):
        position = block * rows + row
        start = jnp.zeros_like(position)
        bound = jnp.int32(0)
        for doc in range(lengths_ref.shape[0]):
            bound = bound + lengths_ref[doc]
            start = jnp.where(position >= bound, bound, start)
        return position, start

    def allowed(query, key_block):
        position, start = query
        keys = key_block * rows + col
        return (keys >= start) & (keys <= position)

    own = first_of(me)
    mate = first_of(me + 1 - 2 * odd)
    third = first_of(me + 1)
    return odd, (
        allowed(own, me),
        allowed(own, me - 2),
        allowed(mate, me - 2 * odd),
        allowed(third, me - 2),
    )


def scores_of(head, refs, odd, masks, scaling):
    q_own, q_mate, q_third, o_own, o_mate, o_third, k_own, k_back, v_own, v_back = refs
    low, high = head_span(head)
    keep = head_mask(head)
    is_odd = odd == 1

    def read(ref):
        return ref[0, :, low:high]

    qs, qm = read(q_own), read(q_mate)
    os, om = read(o_own), read(o_mate)
    qt = jnp.where(is_odd, read(q_third), qm)
    ot = jnp.where(is_odd, read(o_third), om)
    ks, kb = read(k_own) * keep, read(k_back) * keep
    vs, vb = read(v_own) * keep, read(v_back) * keep
    km = jnp.where(is_odd, kb, ks)
    vm = jnp.where(is_odd, vb, vs)
    pairs = ((qs, ks, os, vs), (qs, kb, os, vb), (qm, km, om, vm), (qt, kb, ot, vb))
    scores = [
        jnp.where(mask, matmul(q, k, NT) * scaling, FLOOR) for (q, k, _, _), mask in zip(pairs, masks)
    ]
    grads = [matmul(o, v, NT) for _, _, o, v in pairs]
    return scores, grads, (qs, qm, qt, os, om, ot, ks, kb, km), keep


def stats_kernel(heads, scaling, place_ref, lengths_ref, *refs):
    inputs, out_ref = refs[:10], refs[10]
    rows = out_ref.shape[1]
    odd, masks = tile_masks(place_ref, lengths_ref, rows)
    lane = lax.broadcasted_iota(jnp.int32, (rows, LANES), 1)
    result = jnp.zeros((rows, LANES), jnp.float32)
    for head in range(heads):
        scores, grads, _, _ = scores_of(head, inputs, odd, masks, scaling)
        for group, tiles in enumerate(((0, 1), (2,), (3,))):
            top = functools.reduce(
                jnp.maximum, [jnp.max(scores[t], axis=1, keepdims=True) for t in tiles]
            )
            exps = [jnp.exp(scores[t] - top) for t in tiles]
            total = sum(jnp.sum(e, axis=1, keepdims=True) for e in exps)
            dots = sum(jnp.sum(e * grads[t], axis=1, keepdims=True) for e, t in zip(exps, tiles))
            for kind, value in enumerate((top, total, dots)):
                result = jnp.where(lane == (group * 3 + kind) * heads + head, value, result)
    out_ref[0] = result


def merge_stats(heads, odd, mine, mate, up, down, zig):
    width = 3 * heads
    lane = lax.broadcasted_iota(jnp.int32, mine.shape, 1)
    is_odd = odd == 1

    def to(value, source, target):
        shift = (target - source) * width % LANES
        return value if shift == 0 else pltpu.roll(value, shift, 1)

    def by_group(own, partner, third):
        return jnp.where(lane < width, own, jnp.where(lane < 2 * width, partner, third))

    parts = (
        mine,
        by_group(
            to(mate, 1, 0), to(mate, 0, 1), jnp.where(is_odd, to(zig, 0, 2), to(mate, 0, 2))
        ),
        by_group(
            jnp.where(is_odd, to(mate, 2, 0), to(zig, 2, 0)),
            jnp.where(is_odd, to(up, 2, 1), to(mine, 2, 1)),
            jnp.where(is_odd, to(down, 1, 2), to(mine, 1, 2)),
        ),
    )
    split = []
    for part in parts:
        total = pltpu.roll(part, LANES - heads, 1)
        dots = pltpu.roll(part, LANES - 2 * heads, 1)
        split.append((jnp.where(total > 0, part, FLOOR), total, dots))
    top = functools.reduce(jnp.maximum, [s[0] for s in split])
    scales = [jnp.exp(s[0] - top) for s in split]
    total = sum(w * s[1] for w, s in zip(scales, split))
    dots = sum(w * s[2] for w, s in zip(scales, split))
    safe = jnp.where(total > 0, total, 1.0)
    return top + jnp.log(safe), dots / safe


def grads_kernel(heads, scaling, place_ref, lengths_ref, *refs):
    inputs, stats, outs = refs[:10], refs[10:15], refs[15:]
    rows = inputs[0].shape[1]
    odd, masks = tile_masks(place_ref, lengths_ref, rows)
    is_odd = odd == 1
    shift, dots = merge_stats(heads, odd, *[ref[0] for ref in stats])
    carry = [None] * len(outs)

    def emit(head, values):
        low, high = head_span(head)
        last = head == heads - 1
        for number, value in enumerate(values):
            start = low
            if carry[number] is not None:
                outs[number][0, :, low : low + LANES] = (
                    value[:, :LANES] + carry[number]
                ).astype(jnp.bfloat16)
                start = low + LANES
            stop = high if last else high - LANES
            if stop > start:
                outs[number][0, :, start:stop] = value[:, start - low : stop - low].astype(
                    jnp.bfloat16
                )
            carry[number] = None if last else value[:, high - LANES - low :]

    for head in range(heads):
        scores, grads, values, keep = scores_of(head, inputs, odd, masks, scaling)
        qs, qm, qt, os, om, ot, ks, kb, km = values
        groups = (0, 0, 1, 2)
        weights, slopes = [], []
        for tile in range(4):
            at = groups[tile] * 3 * heads + head
            weight = jnp.where(masks[tile], jnp.exp(scores[tile] - shift[:, at : at + 1]), 0.0)
            slope = weight * (grads[tile] - dots[:, at : at + 1]) * scaling
            weights.append(weight.astype(jnp.bfloat16))
            slopes.append(slope.astype(jnp.bfloat16))
        none = jnp.zeros_like(weights[0])

        def to_keys(tiles, own, mate, third):
            first = [tiles[0], jnp.where(is_odd, none, tiles[2])]
            second = [tiles[1], tiles[3], jnp.where(is_odd, tiles[2], none)]
            return (
                matmul(jnp.concatenate(first, 0), jnp.concatenate([own, mate], 0), TN),
                matmul(jnp.concatenate(second, 0), jnp.concatenate([own, third, mate], 0), TN),
            )

        qs, qm, qt = qs * keep, qm * keep, qt * keep
        os, om, ot = os * keep, om * keep, ot * keep
        query_own = matmul(
            jnp.concatenate(slopes[:2], 1), jnp.concatenate([ks, kb], 0), NN
        )
        query_third = matmul(slopes[3], kb, NN)
        query_mate = matmul(slopes[2], km, NN) + jnp.where(is_odd, 0.0, query_third)
        key_own, key_back = to_keys(slopes, qs, qm, qt)
        value_own, value_back = to_keys(weights, os, om, ot)
        emit(
            head,
            (query_own, query_mate, query_third, key_own, key_back, value_own, value_back),
        )


def halo_shards(queries, key_vectors, value_vectors, out_grad, doc_lengths):
    _, rows, width = queries.shape
    seq_size = lax.axis_size("seq")
    me = lax.axis_index("seq").astype(jnp.int32)
    scaling = HEAD ** (-0.5)
    chunks = 2
    part = width // chunks
    heads = part // HEAD
    devices = range(seq_size)
    mates = [(s, s ^ 1) for s in devices]
    ahead = [(s, s + 2) for s in devices if s + 2 < seq_size]
    behind = [(s, s - 2) for s in devices if s >= 2]
    odd_behind = [(s, s - 2) for s in devices if s >= 2 and s % 2 == 1]
    odd_next = [(s, s + 1) for s in devices if s % 2 == 1 and s + 1 < seq_size]
    zigzag = odd_next + [(t, s) for s, t in odd_next]

    def send(value, pairs):
        return lax.ppermute(value, "seq", pairs)

    q_mate = send(queries, mates)
    o_mate = send(out_grad, mates)
    k_back = send(key_vectors, ahead)
    v_back = send(value_vectors, ahead)
    q_third = send(q_mate, odd_behind)
    o_third = send(o_mate, odd_behind)
    tensors = (
        queries, q_mate, q_third, out_grad, o_mate, o_third, key_vectors, k_back, value_vectors, v_back,
    )
    place = me[None]
    smem = pl.BlockSpec(memory_space=pltpu.SMEM)
    wide = pl.BlockSpec((1, rows, part), lambda step: (0, 0, step))
    slim = pl.BlockSpec((1, rows, LANES), lambda step: (step, 0, 0))
    tile_flops = 2 * 4 * rows * rows * chunks * heads * 320
    stats = pl.pallas_call(
        functools.partial(stats_kernel, heads, scaling),
        grid=(chunks,),
        in_specs=[smem, smem] + [wide] * 10,
        out_specs=slim,
        out_shape=jax.ShapeDtypeStruct((chunks, rows, LANES), jnp.float32),
        cost_estimate=pl.CostEstimate(
            flops=2 * tile_flops, bytes_accessed=20 * rows * width, transcendentals=0
        ),
    )(place, doc_lengths, *tensors)
    others = (send(stats, mates), send(stats, ahead), send(stats, behind), send(stats, zigzag))
    query_own, query_mate, query_third, key_own, key_back, value_own, value_back = pl.pallas_call(
        functools.partial(grads_kernel, heads, scaling),
        grid=(chunks,),
        in_specs=[smem, smem] + [wide] * 10 + [slim] * 5,
        out_specs=[wide] * 7,
        out_shape=[jax.ShapeDtypeStruct((1, rows, width), jnp.bfloat16)] * 7,
        cost_estimate=pl.CostEstimate(
            flops=7 * tile_flops, bytes_accessed=34 * rows * width, transcendentals=0
        ),
    )(place, doc_lengths, *tensors, stats, *others)

    def total(first, *rest):
        value = first.astype(jnp.float32)
        for term in rest:
            value = value + term.astype(jnp.float32)
        return value.astype(jnp.bfloat16)

    value_ready = total(value_own, send(value_back, behind))
    key_ready = total(key_own, send(key_back, behind))
    query_ready = total(query_own, send(query_mate, mates), send(query_third, odd_next))
    return query_ready, key_ready, value_ready


def shards(queries, key_vectors, value_vectors, out_grad, doc_lengths):
    _, rows, width = queries.shape
    length = rows * lax.axis_size("seq")
    longest = length * 3 // 8
    fits = longest <= 3 * rows and lax.axis_size("seq") % 2 == 0 and width % (2 * LANES) == 0
    plan = halo_shards if fits and width % (2 * HEAD) == 0 else spread_shards
    return plan(queries, key_vectors, value_vectors, out_grad, doc_lengths)


def solution(mesh):
    return jax.shard_map(
        shards,
        mesh=mesh,
        in_specs=(
            P("section", "seq", "dp"),
            P("section", "seq", "dp"),
            P("section", "seq", "dp"),
            P("section", "seq", "dp"),
            P(),
        ),
        out_specs=(P("section", "seq", "dp"), P("section", "seq", "dp"), P("section", "seq", "dp")),
        check_vma=False,
    )
```

```python
import functools
import jax
import jax.numpy as jnp
from jax import lax
from jax.experimental import pallas as pl
from jax.experimental.pallas import tpu as pltpu
from jax.sharding import PartitionSpec as P

HEAD = 224
LANES = 128
FLOOR = -1e30


def pick_slot(stacked, slot):
    return lax.dynamic_index_in_dim(stacked, slot, 0, keepdims=False)


def put_slot(stacked, update, slot):
    return lax.dynamic_update_index_in_dim(stacked, update, slot, 0)


def spread_shards(queries, key_vectors, value_vectors, out_grad, doc_lengths):
    local_rows = queries.shape[1]
    local_width = queries.shape[2]
    head_count = local_width // HEAD
    seq_size = lax.axis_size("seq")
    group = seq_size // head_count
    scaling = HEAD ** (-0.5)

    def spread(matrix):
        shaped = matrix.reshape(local_rows, head_count, 1, HEAD)
        copies = jnp.broadcast_to(shaped, (local_rows, head_count, group, HEAD))
        return copies.reshape(local_rows, seq_size * HEAD)

    query_head, key_head, value_head, cot_head = (
        lax.all_to_all(spread(queries), "seq", split_axis=1, concat_axis=0, tiled=True),
        lax.all_to_all(spread(key_vectors), "seq", split_axis=1, concat_axis=0, tiled=True),
        lax.all_to_all(spread(value_vectors), "seq", split_axis=1, concat_axis=0, tiled=True),
        lax.all_to_all(spread(out_grad), "seq", split_axis=1, concat_axis=0, tiled=True),
    )
    length = key_head.shape[0]
    member = lax.axis_index("seq") % group
    blocks = 2 * group
    block = length // blocks
    bounds = jnp.cumsum(doc_lengths)
    positions = jnp.arange(length, dtype=jnp.int32)
    doc_index = jnp.sum((positions[:, None] >= bounds[None, :]).astype(jnp.int32), axis=1)
    row_list = [member, blocks - 1 - member]
    query_list = []
    cot_list = []
    pos_list = []
    for which in range(2):
        offset = row_list[which] * block
        query_list.append(lax.dynamic_slice_in_dim(query_head, offset, block, 0))
        cot_list.append(lax.dynamic_slice_in_dim(cot_head, offset, block, 0))
        pos_list.append(offset + jnp.arange(block, dtype=jnp.int32))
    query_stack = jnp.stack(query_list)
    cot_stack = jnp.stack(cot_list)
    pos_stack = jnp.stack(pos_list)
    doc_stack = jnp.take(doc_index, pos_stack)
    plan = []
    for number in range(blocks + 1):
        first = number <= member
        slot = jnp.where(first, 0, 1).astype(jnp.int32)
        col_block = jnp.where(first, number, number - member - 1)
        flag = None
        plan.append((slot, col_block, flag))
    row_max = jnp.full((2, block), -jnp.inf, jnp.float32)
    row_sum = jnp.zeros((2, block), jnp.float32)
    stored = []
    for slot, col_block, flag in plan:

        def score_tile(carry, slot=slot, col_block=col_block):
            maxima, totals = carry
            query_rows = pick_slot(query_stack, slot)
            key_rows = lax.dynamic_slice_in_dim(key_head, col_block * block, block, 0)
            col_docs = lax.dynamic_slice_in_dim(doc_index, col_block * block, block, 0)
            col_positions = col_block * block + jnp.arange(block, dtype=jnp.int32)
            raw = jnp.dot(query_rows, key_rows.T, preferred_element_type=jnp.float32) * scaling
            allowed = (pick_slot(doc_stack, slot)[:, None] == col_docs[None, :]) & (
                pick_slot(pos_stack, slot)[:, None] >= col_positions[None, :]
            )
            scores = jnp.where(allowed, raw, -jnp.inf)
            before = pick_slot(maxima, slot)
            after = jnp.maximum(before, jnp.max(scores, axis=1))
            safe = jnp.where(jnp.isfinite(after), after, 0.0)
            total = pick_slot(totals, slot) * jnp.exp(before - safe) + jnp.sum(
                jnp.exp(scores - safe[:, None]), axis=1
            )
            return (scores, put_slot(maxima, after, slot), put_slot(totals, total, slot))

        scores, row_max, row_sum = score_tile((row_max, row_sum))
        stored.append(scores)

    def tile_weights(scores, slot):
        return (
            jnp.exp(scores - pick_slot(row_max, slot)[:, None]) / pick_slot(row_sum, slot)[:, None]
        )

    summed = jnp.zeros((2, block, HEAD), jnp.float32)
    for (slot, col_block, flag), scores in zip(plan, stored):

        def add_values(carry, slot=slot, col_block=col_block, scores=scores):
            rounded = tile_weights(scores, slot).astype(jnp.bfloat16)
            value_rows = lax.dynamic_slice_in_dim(value_head, col_block * block, block, 0)
            term = jnp.dot(rounded, value_rows, preferred_element_type=jnp.float32)
            return put_slot(carry, pick_slot(carry, slot) + term, slot)

        summed = add_values(summed)
    attended = summed.astype(jnp.bfloat16)
    row_dot = jnp.sum(cot_stack.astype(jnp.float32) * attended.astype(jnp.float32), axis=2)
    query_acc = jnp.zeros((2, block, HEAD), jnp.float32)
    key_acc = jnp.zeros((length, HEAD), jnp.float32)
    value_acc = jnp.zeros((length, HEAD), jnp.float32)
    for (slot, col_block, flag), scores in zip(plan, stored):

        def backward_tile(carry, slot=slot, col_block=col_block, scores=scores):
            query_sum, key_sum, value_sum = carry
            weights = tile_weights(scores, slot)
            rounded = weights.astype(jnp.bfloat16)
            query_rows = pick_slot(query_stack, slot)
            cot_rows = pick_slot(cot_stack, slot)
            start = col_block * block
            key_rows = lax.dynamic_slice_in_dim(key_head, start, block, 0)
            value_rows = lax.dynamic_slice_in_dim(value_head, start, block, 0)
            value_term = jnp.dot(rounded.T, cot_rows, preferred_element_type=jnp.float32)
            prob_grad = jnp.dot(cot_rows, value_rows.T, preferred_element_type=jnp.float32)
            score_grad = (
                weights * (prob_grad - pick_slot(row_dot, slot)[:, None]) * scaling
            ).astype(jnp.bfloat16)
            query_term = jnp.dot(score_grad, key_rows, preferred_element_type=jnp.float32)
            key_term = jnp.dot(score_grad.T, query_rows, preferred_element_type=jnp.float32)
            query_sum = put_slot(query_sum, pick_slot(query_sum, slot) + query_term, slot)
            key_sum = lax.dynamic_update_slice_in_dim(
                key_sum, lax.dynamic_slice_in_dim(key_sum, start, block, 0) + key_term, start, 0
            )
            value_sum = lax.dynamic_update_slice_in_dim(
                value_sum,
                lax.dynamic_slice_in_dim(value_sum, start, block, 0) + value_term,
                start,
                0,
            )
            return (query_sum, key_sum, value_sum)

        query_acc, key_acc, value_acc = backward_tile((query_acc, key_acc, value_acc))
    query_rounded = query_acc.astype(jnp.bfloat16)
    key_back, value_back = (
        lax.all_to_all(key_acc, "seq", split_axis=0, concat_axis=1, tiled=True),
        lax.all_to_all(value_acc, "seq", split_axis=0, concat_axis=1, tiled=True),
    )

    def settle(received):
        shaped = received.astype(jnp.float32).reshape(local_rows, head_count, group, HEAD)
        return jnp.sum(shaped, axis=2).reshape(1, local_rows, local_width).astype(jnp.bfloat16)

    query_full = jnp.zeros((length, HEAD), jnp.bfloat16)
    for which in range(2):
        query_full = lax.dynamic_update_slice_in_dim(
            query_full, query_rounded[which], row_list[which] * block, 0
        )
    query_back = lax.all_to_all(query_full, "seq", split_axis=0, concat_axis=1, tiled=True)
    query_out = settle(query_back)
    return (query_out, settle(key_back), settle(value_back))


NT = ((1,), (1,))
NN = ((1,), (0,))
TN = ((0,), (0,))
KINDS = 3
SLOT = 16


def head_span(head):
    low = head * HEAD // LANES * LANES
    high = -(-(head + 1) * HEAD // LANES) * LANES
    return low, high


def head_mask(head):
    low, high = head_span(head)
    lane = lax.broadcasted_iota(jnp.int32, (1, high - low), 1) + low
    inside = (lane >= head * HEAD) & (lane < (head + 1) * HEAD)
    return inside.astype(jnp.float32).astype(jnp.bfloat16)


def matmul(left, right, dims):
    return lax.dot_general(left, right, (dims, ((), ())), preferred_element_type=jnp.float32)


def stack_rows(*values):
    return jnp.concatenate(values, axis=0)


def allowed(lengths_ref, rows, query_block, key_block):
    shape = (rows, rows)
    position = query_block * rows + lax.broadcasted_iota(jnp.int32, shape, 0)
    keys = key_block * rows + lax.broadcasted_iota(jnp.int32, shape, 1)
    start = jnp.zeros_like(position)
    bound = jnp.int32(0)
    for doc in range(lengths_ref.shape[0]):
        bound = bound + lengths_ref[doc]
        start = jnp.where(position >= bound, bound, start)
    return (keys >= start) & (keys <= position)


def even_plan(lengths_ref, rows, me):
    def pair(query, key):
        return allowed(lengths_ref, rows, query, key)

    mask = stack_rows(
        jnp.concatenate([pair(me, me), pair(me, me - 2)], axis=1),
        jnp.concatenate([pair(me + 1, me), pair(me + 1, me - 2)], axis=1),
    )
    return (((0, 1), (0, 1), mask),)


def odd_plan(lengths_ref, rows, me):
    def pair(query, key):
        return allowed(lengths_ref, rows, query, key)

    mask = stack_rows(pair(me, me - 2), pair(me - 1, me - 2), pair(me + 1, me - 2))
    return (((0,), (0,), pair(me, me)), ((0, 1, 2), (1,), mask))


def gather_head(ref, number, slots, low, high):
    return stack_rows(*[ref[slot][number, :, low:high] for slot in slots])


def tile_values(plan, head, queries, keys, scaling):
    low, high = head_span(head)
    keep = head_mask(head)
    out = []
    for query_slots, key_slots, mask in plan:
        q = gather_head(queries, 0, query_slots, low, high)
        o = gather_head(queries, 1, query_slots, low, high)
        k = gather_head(keys, 0, key_slots, low, high) * keep
        v = gather_head(keys, 1, key_slots, low, high) * keep
        scores = jnp.where(mask, matmul(q, k, NT) * scaling, FLOOR)
        out.append((q, o, k, scores, matmul(o, v, NT)))
    return out, keep


def row_part(value, slot, rows):
    return value[slot * rows : (slot + 1) * rows]


def stats_kernel(heads, scaling, place_ref, lengths_ref, own, mate, third, key_own, key_back, out_ref):
    rows = own.shape[1]
    me = place_ref[0]
    total = out_ref.shape[0]
    lane = lax.broadcasted_iota(jnp.int32, (rows, LANES), 1)
    queries, keys = (own, mate, third), (key_own, key_back)
    out_ref[...] = jnp.zeros_like(out_ref)

    def collect(plan, groups):
        results = [jnp.zeros((rows, LANES), jnp.float32) for _ in range(groups)]
        for head in range(heads):
            tiles, _ = tile_values(plan, head, queries, keys, scaling)
            parts = [[] for _ in range(groups)]
            for (slots, _, _), (_, _, _, scores, grads) in zip(plan, tiles):
                for number, slot in enumerate(slots):
                    parts[slot].append((row_part(scores, number, rows), row_part(grads, number, rows)))
            for group, pieces in enumerate(parts):
                top = functools.reduce(
                    jnp.maximum, [jnp.max(s, axis=1, keepdims=True) for s, _ in pieces]
                )
                exps = [jnp.exp(s - top) for s, _ in pieces]
                sums = sum(jnp.sum(e, axis=1, keepdims=True) for e in exps)
                dots = sum(
                    jnp.sum(e * g, axis=1, keepdims=True) for e, (_, g) in zip(exps, pieces)
                )
                for kind, value in enumerate((top, sums, dots)):
                    results[group] = jnp.where(lane == kind * heads + head, value, results[group])
        return [result.T[:SLOT] for result in results]

    @pl.when(lax.rem(me, 2) == 0)
    def _():
        own_stats, mate_stats = collect(even_plan(lengths_ref, rows, me), 2)
        out_ref[me + 1, :SLOT] = own_stats
        out_ref[me + 1, SLOT:] = mate_stats

        @pl.when(me > 0)
        def _():
            out_ref[me - 1, :SLOT] = own_stats

        out_ref[me, :SLOT] = own_stats
        out_ref[me, SLOT:] = mate_stats

    @pl.when(lax.rem(me, 2) == 1)
    def _():
        own_stats, mate_stats, third_stats = collect(odd_plan(lengths_ref, rows, me), 3)
        out_ref[me - 1, :SLOT] = own_stats
        out_ref[me - 1, SLOT:] = mate_stats

        @pl.when(me >= 2)
        def _():
            out_ref[me - 2, :SLOT] = mate_stats

        @pl.when(me + 1 < total)
        def _():
            out_ref[me + 1, :SLOT] = third_stats
            out_ref[me + 2, :SLOT] = third_stats

        out_ref[me, :SLOT] = own_stats
        out_ref[me, SLOT:] = mate_stats

    return None


def merge_stats(heads, parts):
    split = []
    for part in parts:
        top, total, dots = (part[kind * heads : (kind + 1) * heads] for kind in range(KINDS))
        split.append((jnp.where(total > 0, top, FLOOR), total, dots))
    top = functools.reduce(jnp.maximum, [s[0] for s in split])
    scales = [jnp.exp(s[0] - top) for s in split]
    total = sum(w * s[1] for w, s in zip(scales, split))
    dots = sum(w * s[2] for w, s in zip(scales, split))
    safe = jnp.where(total > 0, total, 1.0)
    return stack_rows(top + jnp.log(safe), dots / safe)


def grads_kernel(
    heads, scaling, place_ref, lengths_ref, own, mate, third, key_own, key_back, mine_ref, stats_ref,
    query_own, query_mate, query_third, key_out, back_out,
):
    rows = own.shape[1]
    me = place_ref[0]
    total = stats_ref.shape[0]
    queries, keys = (own, mate, third), (key_own, key_back)

    def slot(index, second):
        part = stats_ref[jnp.clip(index, 0, total - 1)][SLOT * second : SLOT * (second + 1)]
        return jnp.where((index >= 0) & (index < total), part, 0.0)

    def columns(groups):
        merged = [merge_stats(heads, parts) for parts in groups]
        used = sum(m.shape[0] for m in merged)
        return stack_rows(*merged, jnp.zeros((LANES - used, rows), jnp.float32)).T

    def run(plan, stats, outs):
        carry = {}

        def emit(head, name, value):
            ref, number = outs[name]
            low, high = head_span(head)
            last = head == heads - 1
            start = low
            if name in carry:
                ref[number, :, low : low + LANES] = (
                    value[:, :LANES] + carry.pop(name)
                ).astype(jnp.bfloat16)
                start = low + LANES
            stop = high if last else high - LANES
            if stop > start:
                ref[number, :, start:stop] = value[:, start - low : stop - low].astype(jnp.bfloat16)
            if not last:
                carry[name] = value[:, high - LANES - low :]

        for head in range(heads):
            tiles, keep = tile_values(plan, head, queries, keys, scaling)
            sums = {}

            def add(name, value):
                sums[name] = sums[name] + value if name in sums else value

            for (query_slots, key_slots, mask), (q, o, k, scores, grads) in zip(plan, tiles):
                def column(kind):
                    at = [2 * heads * s + kind * heads + head for s in query_slots]
                    return stack_rows(*[stats[:, c : c + 1] for c in at])

                weight = jnp.where(mask, jnp.exp(scores - column(0)), 0.0)
                slope = (weight * (grads - column(1)) * scaling).astype(jnp.bfloat16)
                weight = weight.astype(jnp.bfloat16)
                from_keys = matmul(slope, k, NN)
                for number, s in enumerate(query_slots):
                    add(("q", s), row_part(from_keys, number, rows))
                to_keys = matmul(slope, q * keep, TN)
                to_values = matmul(weight, o * keep, TN)
                for number, s in enumerate(key_slots):
                    add(("k", s), row_part(to_keys, number, rows))
                    add(("v", s), row_part(to_values, number, rows))
            for name, value in sums.items():
                emit(head, name, value)

    outs = {
        ("q", 0): (query_own, 0),
        ("q", 1): (query_mate, 0),
        ("q", 2): (query_third, 0),
        ("k", 0): (key_out, 0),
        ("v", 0): (key_out, 1),
        ("k", 1): (back_out, 0),
        ("v", 1): (back_out, 1),
    }
    mine_own, mine_mate = mine_ref[me][:SLOT], mine_ref[me][SLOT:]

    @pl.when(lax.rem(me, 2) == 0)
    def _():
        groups = (
            (mine_own, slot(me + 1, 1), slot(me - 1, 0)),
            (mine_mate, slot(me + 1, 0)),
        )
        run(even_plan(lengths_ref, rows, me), columns(groups), outs)

    @pl.when(lax.rem(me, 2) == 1)
    def _():
        mine_third = jnp.where(me + 1 < total, mine_ref[jnp.minimum(me + 1, total - 1)][:SLOT], 0.0)
        groups = (
            (mine_own, slot(me - 1, 1)),
            (mine_mate, slot(me - 1, 0), slot(me - 2, 0)),
            (mine_third, slot(me + 1, 0), slot(me + 2, 0)),
        )
        run(odd_plan(lengths_ref, rows, me), columns(groups), outs)


def halo_shards(queries, key_vectors, value_vectors, out_grad, doc_lengths):
    _, rows, width = queries.shape
    seq_size = lax.axis_size("seq")
    me = lax.axis_index("seq").astype(jnp.int32)
    scaling = HEAD ** (-0.5)
    chunks = 2
    part = width // chunks
    heads = part // HEAD
    devices = range(seq_size)
    mates = [(s, s ^ 1) for s in devices]
    ahead = [(s, s + 2) for s in devices if s + 2 < seq_size]
    behind = [(s, s - 2) for s in devices if s >= 2]
    odd_behind = [(s, s - 2) for s in devices if s >= 2 and s % 2 == 1]
    odd_next = [(s, s + 1) for s in devices if s % 2 == 1 and s + 1 < seq_size]

    def send(value, pairs):
        return lax.ppermute(value, "seq", pairs)

    def pack(first, second, chunk):
        cut = [lax.slice_in_dim(a, chunk * part, (chunk + 1) * part, axis=2) for a in (first, second)]
        return jnp.concatenate(cut, axis=0)

    place = me[None]
    smem = pl.BlockSpec(memory_space=pltpu.SMEM)
    vmem = pl.BlockSpec(memory_space=pltpu.VMEM)
    tile_flops = 2 * 4 * rows * rows * heads * 320
    moved = []
    for chunk in range(chunks):
        query_own = pack(queries, out_grad, chunk)
        key_own = pack(key_vectors, value_vectors, chunk)
        query_mate = send(query_own, mates)
        key_back = send(key_own, ahead)
        query_third = send(query_mate, odd_behind)
        moved.append((query_own, query_mate, query_third, key_own, key_back))
    parts = []
    for tensors in moved:
        stats = pl.pallas_call(
            functools.partial(stats_kernel, heads, scaling),
            in_specs=[smem, smem] + [vmem] * 5,
            out_specs=vmem,
            out_shape=jax.ShapeDtypeStruct((seq_size, 2 * SLOT, rows), jnp.float32),
            cost_estimate=pl.CostEstimate(
                flops=2 * tile_flops, bytes_accessed=20 * rows * part, transcendentals=0
            ),
        )(place, doc_lengths, *tensors)
        others = lax.all_to_all(stats, "seq", split_axis=0, concat_axis=0, tiled=True)
        single = jax.ShapeDtypeStruct((1, rows, part), jnp.bfloat16)
        double = jax.ShapeDtypeStruct((2, rows, part), jnp.bfloat16)
        query_own, query_mate, query_third, key_own, key_back = pl.pallas_call(
            functools.partial(grads_kernel, heads, scaling),
            in_specs=[smem, smem] + [vmem] * 7,
            out_specs=[vmem] * 5,
            out_shape=[single, single, single, double, double],
            cost_estimate=pl.CostEstimate(
                flops=7 * tile_flops, bytes_accessed=34 * rows * part, transcendentals=0
            ),
        )(place, doc_lengths, *tensors, stats, others)
        key_sent = send(key_back, behind)
        query_sent = send(query_mate, mates)
        third_sent = send(query_third, odd_next)

        def total(*terms):
            return sum(term.astype(jnp.float32) for term in terms).astype(jnp.bfloat16)

        key_sum = total(key_own, key_sent)
        parts.append((total(query_own, query_sent, third_sent), key_sum[:1], key_sum[1:]))
    return tuple(jnp.concatenate(pieces, axis=2) for pieces in zip(*parts))


def shards(queries, key_vectors, value_vectors, out_grad, doc_lengths):
    _, rows, width = queries.shape
    seq_size = lax.axis_size("seq")
    longest = rows * seq_size * 3 // 8
    fits = longest <= 3 * rows and seq_size % 2 == 0 and rows == LANES
    aligned = width % (2 * HEAD) == 0 and (width // 2) % LANES == 0
    plan = halo_shards if fits and aligned else spread_shards
    return plan(queries, key_vectors, value_vectors, out_grad, doc_lengths)


def solution(mesh):
    return jax.shard_map(
        shards,
        mesh=mesh,
        in_specs=(
            P("section", "seq", "dp"),
            P("section", "seq", "dp"),
            P("section", "seq", "dp"),
            P("section", "seq", "dp"),
            P(),
        ),
        out_specs=(P("section", "seq", "dp"), P("section", "seq", "dp"), P("section", "seq", "dp")),
        check_vma=False,
    )
```

```python
import functools
import math
import jax
import jax.numpy as jnp
from jax import lax
from jax.experimental import pallas as pl
from jax.experimental.pallas import tpu as pltpu
from jax.sharding import PartitionSpec as P

HEAD = 224
LANES = 128
FLOOR = -1e30


def pick_slot(stacked, slot):
    return lax.dynamic_index_in_dim(stacked, slot, 0, keepdims=False)


def put_slot(stacked, update, slot):
    return lax.dynamic_update_index_in_dim(stacked, update, slot, 0)


def spread_shards(queries, key_vectors, value_vectors, out_grad, doc_lengths):
    local_rows = queries.shape[1]
    local_width = queries.shape[2]
    head_count = local_width // HEAD
    seq_size = lax.axis_size("seq")
    group = seq_size // head_count
    scaling = HEAD ** (-0.5)

    def spread(matrix):
        shaped = matrix.reshape(local_rows, head_count, 1, HEAD)
        copies = jnp.broadcast_to(shaped, (local_rows, head_count, group, HEAD))
        return copies.reshape(local_rows, seq_size * HEAD)

    query_head, key_head, value_head, cot_head = (
        lax.all_to_all(spread(queries), "seq", split_axis=1, concat_axis=0, tiled=True),
        lax.all_to_all(spread(key_vectors), "seq", split_axis=1, concat_axis=0, tiled=True),
        lax.all_to_all(spread(value_vectors), "seq", split_axis=1, concat_axis=0, tiled=True),
        lax.all_to_all(spread(out_grad), "seq", split_axis=1, concat_axis=0, tiled=True),
    )
    length = key_head.shape[0]
    member = lax.axis_index("seq") % group
    blocks = 2 * group
    block = length // blocks
    bounds = jnp.cumsum(doc_lengths)
    positions = jnp.arange(length, dtype=jnp.int32)
    doc_index = jnp.sum((positions[:, None] >= bounds[None, :]).astype(jnp.int32), axis=1)
    row_list = [member, blocks - 1 - member]
    query_list = []
    cot_list = []
    pos_list = []
    for which in range(2):
        offset = row_list[which] * block
        query_list.append(lax.dynamic_slice_in_dim(query_head, offset, block, 0))
        cot_list.append(lax.dynamic_slice_in_dim(cot_head, offset, block, 0))
        pos_list.append(offset + jnp.arange(block, dtype=jnp.int32))
    query_stack = jnp.stack(query_list)
    cot_stack = jnp.stack(cot_list)
    pos_stack = jnp.stack(pos_list)
    doc_stack = jnp.take(doc_index, pos_stack)
    plan = []
    for number in range(blocks + 1):
        first = number <= member
        slot = jnp.where(first, 0, 1).astype(jnp.int32)
        col_block = jnp.where(first, number, number - member - 1)
        flag = None
        plan.append((slot, col_block, flag))
    row_max = jnp.full((2, block), -jnp.inf, jnp.float32)
    row_sum = jnp.zeros((2, block), jnp.float32)
    stored = []
    for slot, col_block, flag in plan:

        def score_tile(carry, slot=slot, col_block=col_block):
            maxima, totals = carry
            query_rows = pick_slot(query_stack, slot)
            key_rows = lax.dynamic_slice_in_dim(key_head, col_block * block, block, 0)
            col_docs = lax.dynamic_slice_in_dim(doc_index, col_block * block, block, 0)
            col_positions = col_block * block + jnp.arange(block, dtype=jnp.int32)
            raw = jnp.dot(query_rows, key_rows.T, preferred_element_type=jnp.float32) * scaling
            allowed = (pick_slot(doc_stack, slot)[:, None] == col_docs[None, :]) & (
                pick_slot(pos_stack, slot)[:, None] >= col_positions[None, :]
            )
            scores = jnp.where(allowed, raw, -jnp.inf)
            before = pick_slot(maxima, slot)
            after = jnp.maximum(before, jnp.max(scores, axis=1))
            safe = jnp.where(jnp.isfinite(after), after, 0.0)
            total = pick_slot(totals, slot) * jnp.exp(before - safe) + jnp.sum(
                jnp.exp(scores - safe[:, None]), axis=1
            )
            return (scores, put_slot(maxima, after, slot), put_slot(totals, total, slot))

        scores, row_max, row_sum = score_tile((row_max, row_sum))
        stored.append(scores)

    def tile_weights(scores, slot):
        return (
            jnp.exp(scores - pick_slot(row_max, slot)[:, None]) / pick_slot(row_sum, slot)[:, None]
        )

    summed = jnp.zeros((2, block, HEAD), jnp.float32)
    for (slot, col_block, flag), scores in zip(plan, stored):

        def add_values(carry, slot=slot, col_block=col_block, scores=scores):
            rounded = tile_weights(scores, slot).astype(jnp.bfloat16)
            value_rows = lax.dynamic_slice_in_dim(value_head, col_block * block, block, 0)
            term = jnp.dot(rounded, value_rows, preferred_element_type=jnp.float32)
            return put_slot(carry, pick_slot(carry, slot) + term, slot)

        summed = add_values(summed)
    attended = summed.astype(jnp.bfloat16)
    row_dot = jnp.sum(cot_stack.astype(jnp.float32) * attended.astype(jnp.float32), axis=2)
    query_acc = jnp.zeros((2, block, HEAD), jnp.float32)
    key_acc = jnp.zeros((length, HEAD), jnp.float32)
    value_acc = jnp.zeros((length, HEAD), jnp.float32)
    for (slot, col_block, flag), scores in zip(plan, stored):

        def backward_tile(carry, slot=slot, col_block=col_block, scores=scores):
            query_sum, key_sum, value_sum = carry
            weights = tile_weights(scores, slot)
            rounded = weights.astype(jnp.bfloat16)
            query_rows = pick_slot(query_stack, slot)
            cot_rows = pick_slot(cot_stack, slot)
            start = col_block * block
            key_rows = lax.dynamic_slice_in_dim(key_head, start, block, 0)
            value_rows = lax.dynamic_slice_in_dim(value_head, start, block, 0)
            value_term = jnp.dot(rounded.T, cot_rows, preferred_element_type=jnp.float32)
            prob_grad = jnp.dot(cot_rows, value_rows.T, preferred_element_type=jnp.float32)
            score_grad = (
                weights * (prob_grad - pick_slot(row_dot, slot)[:, None]) * scaling
            ).astype(jnp.bfloat16)
            query_term = jnp.dot(score_grad, key_rows, preferred_element_type=jnp.float32)
            key_term = jnp.dot(score_grad.T, query_rows, preferred_element_type=jnp.float32)
            query_sum = put_slot(query_sum, pick_slot(query_sum, slot) + query_term, slot)
            key_sum = lax.dynamic_update_slice_in_dim(
                key_sum, lax.dynamic_slice_in_dim(key_sum, start, block, 0) + key_term, start, 0
            )
            value_sum = lax.dynamic_update_slice_in_dim(
                value_sum,
                lax.dynamic_slice_in_dim(value_sum, start, block, 0) + value_term,
                start,
                0,
            )
            return (query_sum, key_sum, value_sum)

        query_acc, key_acc, value_acc = backward_tile((query_acc, key_acc, value_acc))
    query_rounded = query_acc.astype(jnp.bfloat16)
    key_back, value_back = (
        lax.all_to_all(key_acc, "seq", split_axis=0, concat_axis=1, tiled=True),
        lax.all_to_all(value_acc, "seq", split_axis=0, concat_axis=1, tiled=True),
    )

    def settle(received):
        shaped = received.astype(jnp.float32).reshape(local_rows, head_count, group, HEAD)
        return jnp.sum(shaped, axis=2).reshape(1, local_rows, local_width).astype(jnp.bfloat16)

    query_full = jnp.zeros((length, HEAD), jnp.bfloat16)
    for which in range(2):
        query_full = lax.dynamic_update_slice_in_dim(
            query_full, query_rounded[which], row_list[which] * block, 0
        )
    query_back = lax.all_to_all(query_full, "seq", split_axis=0, concat_axis=1, tiled=True)
    query_out = settle(query_back)
    return (query_out, settle(key_back), settle(value_back))


NT = ((1,), (1,))
NN = ((1,), (0,))
TN = ((0,), (0,))
KINDS = 3
GROUP = 8
SLOT = KINDS * GROUP


def head_span(head):
    low = head * HEAD // LANES * LANES
    high = -(-(head + 1) * HEAD // LANES) * LANES
    return low, high


def head_mask(head):
    low, high = head_span(head)
    lane = lax.broadcasted_iota(jnp.int32, (1, high - low), 1) + low
    inside = (lane >= head * HEAD) & (lane < (head + 1) * HEAD)
    return inside.astype(jnp.float32).astype(jnp.bfloat16)


def matmul(left, right, dims):
    return lax.dot_general(left, right, (dims, ((), ())), preferred_element_type=jnp.float32)


def stack(values, axis):
    return values[0] if len(values) == 1 else jnp.concatenate(values, axis=axis)


def allowed(lengths_ref, rows, query_block, key_block):
    shape = (rows, rows)
    position = query_block * rows + lax.broadcasted_iota(jnp.int32, shape, 1)
    keys = key_block * rows + lax.broadcasted_iota(jnp.int32, shape, 0)
    start = jnp.zeros_like(position)
    bound = jnp.int32(0)
    for doc in range(lengths_ref.shape[0]):
        bound = bound + lengths_ref[doc]
        start = jnp.where(position >= bound, bound, start)
    return (keys >= start) & (keys <= position)


def make_tile(lengths_ref, rows, queries, keys):
    mask = stack(
        [stack([allowed(lengths_ref, rows, q, k) for _, q in queries], 1) for _, k in keys], 0
    )
    return [slot for slot, _ in queries], [slot for slot, _ in keys], mask


def tile_values(plan, head, queries, keys):
    low, high = head_span(head)
    keep = head_mask(head)

    def gather(refs, number, slots):
        return stack([refs[slot][number][0, :, low:high] for slot in slots], 0)

    out = []
    for query_slots, key_slots, mask in plan:
        q, o = (gather(queries, number, query_slots) for number in range(2))
        k, v = (gather(keys, number, key_slots) * keep for number in range(2))
        out.append((q, o, k, matmul(k, q, NT), matmul(v, o, NT)))
    return out, keep


def collect_stats(heads, power, step, plan, queries, keys, rows, out_ref, slots):
    for head in range(heads):
        tiles, _ = tile_values(plan, head, queries, keys)
        parts = {}
        for (query_slots, _, mask), (_, _, _, raw, grads) in zip(plan, tiles):
            raw = jnp.where(mask, raw, FLOOR)
            for number, slot in enumerate(query_slots):
                cut = slice(number * rows, (number + 1) * rows)
                parts.setdefault(slot, []).append((raw[:, cut], grads[:, cut]))
        for slot, pieces in parts.items():
            top = functools.reduce(
                jnp.maximum, [jnp.max(s, axis=0, keepdims=True) for s, _ in pieces]
            )
            exps = [jnp.exp2((s - top) * power) for s, _ in pieces]
            sums = sum(jnp.sum(e, axis=0, keepdims=True) for e in exps)
            dots = sum(jnp.sum(e * g, axis=0, keepdims=True) for e, (_, g) in zip(exps, pieces))
            for kind, value in enumerate((top, sums, dots)):
                row = slots[slot] * SLOT + kind * GROUP + step * heads + head
                out_ref[pl.ds(row, 1), :] = value


def merge_stats(scaling, parts):
    split = []
    for part in parts:
        top, total, dots = (part[kind * GROUP : (kind + 1) * GROUP] for kind in range(KINDS))
        split.append((jnp.where(total > 0, top, FLOOR), total, dots))
    top = functools.reduce(jnp.maximum, [s[0] for s in split])
    scales = [jnp.exp((s[0] - top) * scaling) for s in split]
    total = sum(w * s[1] for w, s in zip(scales, split))
    dots = sum(w * s[2] for w, s in zip(scales, split))
    safe = jnp.where(total > 0, total, 1.0)
    return top + jnp.log(safe) / scaling, dots / safe


def collect_grads(heads, scaling, power, step, plan, queries, keys, rows, merged, outs, base):
    carry = {}

    def emit(head, name, value):
        ref, number = outs[name]
        low, high = head_span(head)
        first, last = head * HEAD % LANES == 0, (head + 1) * HEAD % LANES == 0

        def put(start, stop, piece):
            if name in base:
                old, at = base[name]
                piece = piece + old[at, :, start:stop].astype(jnp.float32)
            ref[number, :, start:stop] = piece.astype(jnp.bfloat16)

        start, stop = low, high
        if not first:
            put(low, low + LANES, value[:, :LANES] + carry.pop(name))
            start = low + LANES
        if not last:
            carry[name] = value[:, high - LANES - low :]
            stop = high - LANES
        if stop > start:
            put(start, stop, value[:, start - low : stop - low])

    for head in range(heads):
        tiles, keep = tile_values(plan, head, queries, keys)
        sums = {}

        def add(name, value):
            sums[name] = sums[name] + value if name in sums else value

        for (query_slots, key_slots, mask), (q, o, k, raw, grads) in zip(plan, tiles):
            def row(kind):
                at = step * heads + head + kind * GROUP
                return stack([merged[slot][pl.ds(at, 1), :] for slot in query_slots], 1)

            weight = jnp.where(mask, jnp.exp2((raw - row(0)) * power), 0.0)
            slope = (weight * (grads - row(1)) * scaling).astype(jnp.bfloat16)
            weight = weight.astype(jnp.bfloat16)
            to_queries = matmul(slope, k, TN)
            to_keys = matmul(slope, q * keep, NN)
            to_values = matmul(weight, o * keep, NN)
            for number, slot in enumerate(query_slots):
                add(("q", slot), to_queries[number * rows : (number + 1) * rows])
            for number, slot in enumerate(key_slots):
                cut = slice(number * rows, (number + 1) * rows)
                add(("k", slot), to_keys[cut])
                add(("v", slot), to_values[cut])
        for name, value in sums.items():
            emit(head, name, value)


def by_parity(me, even, odd):
    pl.when(lax.rem(me, 2) == 0)(even)
    pl.when(lax.rem(me, 2) == 1)(odd)


def first_stats(heads, power, place_ref, lengths_ref, qo, oo, qm, om, ko, vo, kb, vb, out_ref):
    rows, me, step = qo.shape[1], place_ref[0], pl.program_id(0)
    queries, keys = ((qo, oo), (qm, om)), ((ko, vo), (kb, vb))

    def even():
        plan = [
            make_tile(lengths_ref, rows, ((0, me), (1, me + 1)), ((0, me), (1, me - 2)))
        ]
        collect_stats(heads, power, step, plan, queries, keys, rows, out_ref, (1, 0))

    def odd():
        plan = [
            make_tile(lengths_ref, rows, ((0, me),), ((0, me),)),
            make_tile(lengths_ref, rows, ((0, me), (1, me - 1)), ((1, me - 2),)),
        ]
        collect_stats(heads, power, step, plan, queries, keys, rows, out_ref, (0, 1))

    by_parity(me, even, odd)


def third_stats(heads, power, place_ref, lengths_ref, qt, ot, kb, vb, first_ref, out_ref):
    rows, me, step = qt.shape[1], place_ref[0], pl.program_id(0)

    def even():
        out_ref[...] = first_ref[SLOT : 2 * SLOT]

    def odd():
        plan = [make_tile(lengths_ref, rows, ((0, me + 1),), ((0, me - 2),))]
        collect_stats(heads, power, step, plan, ((qt, ot),), ((kb, vb),), rows, out_ref, (0,))

    by_parity(me, even, odd)


def odd_block_grads(
    heads, scaling, power, place_ref, lengths_ref, qo, oo, qm, om, ko, vo, kb, vb, mine, mate,
    query_out, own_out, back_out, merged,
):
    rows, me, step = qo.shape[1], place_ref[0], pl.program_id(0)
    keys = ((ko, vo), (kb, vb))
    shift, dots = merge_stats(scaling, (mine[:SLOT], mate[:SLOT]))
    merged[:GROUP], merged[GROUP:] = shift, dots
    outs = {
        ("q", 0): (query_out, 0),
        ("k", 0): (own_out, 0),
        ("v", 0): (own_out, 1),
        ("k", 1): (back_out, 0),
        ("v", 1): (back_out, 1),
    }

    def run(block, queries):
        own = me
        plan = [make_tile(lengths_ref, rows, ((0, block),), ((0, own), (1, own - 2)))]
        collect_grads(
            heads, scaling, power, step, plan, queries, keys, rows, (merged,), outs, {}
        )

    by_parity(me, lambda: run(me + 1, ((qm, om),)), lambda: run(me, ((qo, oo),)))


def even_block_grads(
    heads, scaling, power, place_ref, lengths_ref, qo, oo, qm, om, qt, ot, ko, vo, kb, vb, mine, mate, up,
    third, zig, down, own_part, back_part, query_out, third_out, own_out, back_out, merged, merged_third,
):
    rows, me, step = qo.shape[1], place_ref[0], pl.program_id(0)

    def even():
        shift, dots = merge_stats(scaling, (mine[SLOT:], mate[SLOT:], zig[...]))
        merged[:GROUP], merged[GROUP:] = shift, dots
        plan = [make_tile(lengths_ref, rows, ((0, me),), ((0, me), (1, me - 2)))]
        outs = {
            ("q", 0): (query_out, 0),
            ("k", 0): (own_out, 0),
            ("v", 0): (own_out, 1),
            ("k", 1): (back_out, 0),
            ("v", 1): (back_out, 1),
        }
        base = {
            ("k", 0): (own_part, 0),
            ("v", 0): (own_part, 1),
            ("k", 1): (back_part, 0),
            ("v", 1): (back_part, 1),
        }
        collect_grads(
            heads, scaling, power, step, plan, ((qo, oo),), ((ko, vo), (kb, vb)), rows, (merged,), outs, base
        )
        third_out[...] = jnp.zeros_like(third_out)

    def odd():
        shift, dots = merge_stats(scaling, (mine[SLOT:], mate[SLOT:], up[...]))
        merged[:GROUP], merged[GROUP:] = shift, dots
        shift, dots = merge_stats(scaling, (third[...], zig[...], down[SLOT:]))
        merged_third[:GROUP], merged_third[GROUP:] = shift, dots
        plan = [make_tile(lengths_ref, rows, ((0, me - 1), (1, me + 1)), ((0, me - 2),))]
        outs = {
            ("q", 0): (query_out, 0),
            ("q", 1): (third_out, 0),
            ("k", 0): (back_out, 0),
            ("v", 0): (back_out, 1),
        }
        base = {("k", 0): (back_part, 0), ("v", 0): (back_part, 1)}
        collect_grads(
            heads, scaling, power, step, plan, ((qm, om), (qt, ot)), ((kb, vb),), rows,
            (merged, merged_third), outs, base,
        )
        own_out[...] = own_part[...]

    by_parity(me, even, odd)


def halo_shards(queries, key_vectors, value_vectors, out_grad, doc_lengths):
    _, rows, width = queries.shape
    seq_size = lax.axis_size("seq")
    me = lax.axis_index("seq").astype(jnp.int32)
    scaling = HEAD ** (-0.5)
    power = scaling * math.log2(math.e)
    steps = width // HEAD // 4
    part = width // steps
    heads = part // HEAD
    devices = range(seq_size)
    odds = [s for s in devices if s % 2]
    mates = [(s, s ^ 1) for s in devices]
    ahead = [(s, s + 2) for s in devices if s + 2 < seq_size]
    behind = [(s, s - 2) for s in devices if s >= 2]
    odd_ahead = [(s, s + 2) for s in odds if s + 2 < seq_size]
    odd_behind = [(s, s - 2) for s in odds if s >= 2]
    odd_next = [(s, s + 1) for s in odds if s + 1 < seq_size]
    zigzag = odd_next + [(t, s) for s, t in odd_next]
    even_to_odd = [(s - 1, s) for s in odds]
    odd_to_even = [(s, s - 1) for s in odds]

    def send(value, pairs):
        return lax.ppermute(value, "seq", pairs)

    smem = pl.BlockSpec(memory_space=pltpu.SMEM)
    wide = pl.BlockSpec((1, rows, part), lambda step: (0, 0, step))
    pair = pl.BlockSpec((2, rows, part), lambda step: (0, 0, step))

    def slim(count):
        return pl.BlockSpec((count * SLOT, rows), lambda step: (0, 0))

    def stats_shape(count):
        return jax.ShapeDtypeStruct((count * SLOT, rows), jnp.float32)

    def shape(count):
        return jax.ShapeDtypeStruct((count, rows, width), jnp.bfloat16)

    def call(kernel, tiles, products, arguments, in_specs, out_specs, out_shape, scratch=0):
        flops = 2 * products * tiles * rows * rows * width * 3 // 2
        return pl.pallas_call(
            kernel,
            grid=(steps,),
            in_specs=[smem, smem] + in_specs,
            out_specs=out_specs,
            out_shape=out_shape,
            scratch_shapes=[pltpu.VMEM((2 * GROUP, rows), jnp.float32)] * scratch,
            cost_estimate=pl.CostEstimate(
                flops=flops, bytes_accessed=20 * rows * width, transcendentals=0
            ),
        )(me[None], doc_lengths, *arguments)

    query_mate = send(queries, mates)
    grad_mate = send(out_grad, mates)
    key_back = send(key_vectors, ahead)
    value_back = send(value_vectors, ahead)
    query_third = send(query_mate, odd_behind)
    grad_third = send(grad_mate, odd_behind)
    rows_here = (queries, out_grad, query_mate, grad_mate)
    rows_third = (query_third, grad_third)
    back = (key_back, value_back)
    cols = (key_vectors, value_vectors) + back

    mine = call(
        functools.partial(first_stats, heads, power), 4, 2, (*rows_here, *cols), [wide] * 8, slim(2),
        stats_shape(2),
    )
    mate = send(mine, mates)
    down = send(mine, odd_behind)
    query_a, own_part, back_part = call(
        functools.partial(odd_block_grads, heads, scaling, power), 2, 5, (*rows_here, *cols, mine, mate),
        [wide] * 8 + [slim(2)] * 2, [wide, pair, pair], [shape(1), shape(2), shape(2)], 1,
    )
    from_even = send(query_a, even_to_odd)
    third = call(
        functools.partial(third_stats, heads, power), 1, 2, (*rows_third, *back, mine),
        [wide] * 4 + [slim(2)], slim(1), stats_shape(1),
    )
    zig = send(third, zigzag)
    up = send(third, odd_ahead)
    query_b, query_c, key_own, key_sent = call(
        functools.partial(even_block_grads, heads, scaling, power), 2, 5,
        (*rows_here, *rows_third, *cols, mine, mate, up, third, zig, down, own_part, back_part),
        [wide] * 10 + [slim(2)] * 2 + [slim(1)] * 3 + [slim(2)] + [pair] * 2,
        [wide, wide, pair, pair], [shape(1), shape(1), shape(2), shape(2)], 2,
    )
    key_back_sum = send(key_sent, behind)
    from_odd = send(query_b, odd_to_even)
    from_third = send(query_c, odd_next)

    def total(*terms):
        return sum(term.astype(jnp.float32) for term in terms).astype(jnp.bfloat16)

    query_own = jnp.where(lax.rem(me, 2) == 0, query_b, query_a)
    query_ready = total(query_own, from_even, from_odd, from_third)
    key_ready = total(key_own[:1], key_back_sum[:1])
    value_ready = total(key_own[1:], key_back_sum[1:])
    return query_ready, key_ready, value_ready


def shards(queries, key_vectors, value_vectors, out_grad, doc_lengths):
    _, rows, width = queries.shape
    seq_size = lax.axis_size("seq")
    longest = rows * seq_size * 3 // 8
    fits = longest <= 3 * rows and seq_size % 2 == 0 and rows == LANES
    heads = width // HEAD
    plan = halo_shards if fits and heads % 4 == 0 and heads <= GROUP else spread_shards
    return plan(queries, key_vectors, value_vectors, out_grad, doc_lengths)


def solution(mesh):
    return jax.shard_map(
        shards,
        mesh=mesh,
        in_specs=(
            P("section", "seq", "dp"),
            P("section", "seq", "dp"),
            P("section", "seq", "dp"),
            P("section", "seq", "dp"),
            P(),
        ),
        out_specs=(P("section", "seq", "dp"), P("section", "seq", "dp"), P("section", "seq", "dp")),
        check_vma=False,
    )
```

```python
import functools
import math
import jax
import jax.numpy as jnp
from jax import lax
from jax.experimental import pallas as pl
from jax.experimental.pallas import tpu as pltpu
from jax.sharding import PartitionSpec as P

HEAD = 224
LANES = 128
FLOOR = -1e30


def pick_slot(stacked, slot):
    return lax.dynamic_index_in_dim(stacked, slot, 0, keepdims=False)


def put_slot(stacked, update, slot):
    return lax.dynamic_update_index_in_dim(stacked, update, slot, 0)


def spread_shards(queries, key_vectors, value_vectors, out_grad, doc_lengths):
    local_rows = queries.shape[1]
    local_width = queries.shape[2]
    head_count = local_width // HEAD
    seq_size = lax.axis_size("seq")
    group = seq_size // head_count
    scaling = HEAD ** (-0.5)

    def spread(matrix):
        shaped = matrix.reshape(local_rows, head_count, 1, HEAD)
        copies = jnp.broadcast_to(shaped, (local_rows, head_count, group, HEAD))
        return copies.reshape(local_rows, seq_size * HEAD)

    query_head, key_head, value_head, cot_head = (
        lax.all_to_all(spread(queries), "seq", split_axis=1, concat_axis=0, tiled=True),
        lax.all_to_all(spread(key_vectors), "seq", split_axis=1, concat_axis=0, tiled=True),
        lax.all_to_all(spread(value_vectors), "seq", split_axis=1, concat_axis=0, tiled=True),
        lax.all_to_all(spread(out_grad), "seq", split_axis=1, concat_axis=0, tiled=True),
    )
    length = key_head.shape[0]
    member = lax.axis_index("seq") % group
    blocks = 2 * group
    block = length // blocks
    bounds = jnp.cumsum(doc_lengths)
    positions = jnp.arange(length, dtype=jnp.int32)
    doc_index = jnp.sum((positions[:, None] >= bounds[None, :]).astype(jnp.int32), axis=1)
    row_list = [member, blocks - 1 - member]
    query_list = []
    cot_list = []
    pos_list = []
    for which in range(2):
        offset = row_list[which] * block
        query_list.append(lax.dynamic_slice_in_dim(query_head, offset, block, 0))
        cot_list.append(lax.dynamic_slice_in_dim(cot_head, offset, block, 0))
        pos_list.append(offset + jnp.arange(block, dtype=jnp.int32))
    query_stack = jnp.stack(query_list)
    cot_stack = jnp.stack(cot_list)
    pos_stack = jnp.stack(pos_list)
    doc_stack = jnp.take(doc_index, pos_stack)
    plan = []
    for number in range(blocks + 1):
        first = number <= member
        slot = jnp.where(first, 0, 1).astype(jnp.int32)
        col_block = jnp.where(first, number, number - member - 1)
        flag = None
        plan.append((slot, col_block, flag))
    row_max = jnp.full((2, block), -jnp.inf, jnp.float32)
    row_sum = jnp.zeros((2, block), jnp.float32)
    stored = []
    for slot, col_block, flag in plan:

        def score_tile(carry, slot=slot, col_block=col_block):
            maxima, totals = carry
            query_rows = pick_slot(query_stack, slot)
            key_rows = lax.dynamic_slice_in_dim(key_head, col_block * block, block, 0)
            col_docs = lax.dynamic_slice_in_dim(doc_index, col_block * block, block, 0)
            col_positions = col_block * block + jnp.arange(block, dtype=jnp.int32)
            raw = jnp.dot(query_rows, key_rows.T, preferred_element_type=jnp.float32) * scaling
            allowed = (pick_slot(doc_stack, slot)[:, None] == col_docs[None, :]) & (
                pick_slot(pos_stack, slot)[:, None] >= col_positions[None, :]
            )
            scores = jnp.where(allowed, raw, -jnp.inf)
            before = pick_slot(maxima, slot)
            after = jnp.maximum(before, jnp.max(scores, axis=1))
            safe = jnp.where(jnp.isfinite(after), after, 0.0)
            total = pick_slot(totals, slot) * jnp.exp(before - safe) + jnp.sum(
                jnp.exp(scores - safe[:, None]), axis=1
            )
            return (scores, put_slot(maxima, after, slot), put_slot(totals, total, slot))

        scores, row_max, row_sum = score_tile((row_max, row_sum))
        stored.append(scores)

    def tile_weights(scores, slot):
        return (
            jnp.exp(scores - pick_slot(row_max, slot)[:, None]) / pick_slot(row_sum, slot)[:, None]
        )

    summed = jnp.zeros((2, block, HEAD), jnp.float32)
    for (slot, col_block, flag), scores in zip(plan, stored):

        def add_values(carry, slot=slot, col_block=col_block, scores=scores):
            rounded = tile_weights(scores, slot).astype(jnp.bfloat16)
            value_rows = lax.dynamic_slice_in_dim(value_head, col_block * block, block, 0)
            term = jnp.dot(rounded, value_rows, preferred_element_type=jnp.float32)
            return put_slot(carry, pick_slot(carry, slot) + term, slot)

        summed = add_values(summed)
    attended = summed.astype(jnp.bfloat16)
    row_dot = jnp.sum(cot_stack.astype(jnp.float32) * attended.astype(jnp.float32), axis=2)
    query_acc = jnp.zeros((2, block, HEAD), jnp.float32)
    key_acc = jnp.zeros((length, HEAD), jnp.float32)
    value_acc = jnp.zeros((length, HEAD), jnp.float32)
    for (slot, col_block, flag), scores in zip(plan, stored):

        def backward_tile(carry, slot=slot, col_block=col_block, scores=scores):
            query_sum, key_sum, value_sum = carry
            weights = tile_weights(scores, slot)
            rounded = weights.astype(jnp.bfloat16)
            query_rows = pick_slot(query_stack, slot)
            cot_rows = pick_slot(cot_stack, slot)
            start = col_block * block
            key_rows = lax.dynamic_slice_in_dim(key_head, start, block, 0)
            value_rows = lax.dynamic_slice_in_dim(value_head, start, block, 0)
            value_term = jnp.dot(rounded.T, cot_rows, preferred_element_type=jnp.float32)
            prob_grad = jnp.dot(cot_rows, value_rows.T, preferred_element_type=jnp.float32)
            score_grad = (
                weights * (prob_grad - pick_slot(row_dot, slot)[:, None]) * scaling
            ).astype(jnp.bfloat16)
            query_term = jnp.dot(score_grad, key_rows, preferred_element_type=jnp.float32)
            key_term = jnp.dot(score_grad.T, query_rows, preferred_element_type=jnp.float32)
            query_sum = put_slot(query_sum, pick_slot(query_sum, slot) + query_term, slot)
            key_sum = lax.dynamic_update_slice_in_dim(
                key_sum, lax.dynamic_slice_in_dim(key_sum, start, block, 0) + key_term, start, 0
            )
            value_sum = lax.dynamic_update_slice_in_dim(
                value_sum,
                lax.dynamic_slice_in_dim(value_sum, start, block, 0) + value_term,
                start,
                0,
            )
            return (query_sum, key_sum, value_sum)

        query_acc, key_acc, value_acc = backward_tile((query_acc, key_acc, value_acc))
    query_rounded = query_acc.astype(jnp.bfloat16)
    key_back, value_back = (
        lax.all_to_all(key_acc, "seq", split_axis=0, concat_axis=1, tiled=True),
        lax.all_to_all(value_acc, "seq", split_axis=0, concat_axis=1, tiled=True),
    )

    def settle(received):
        shaped = received.astype(jnp.float32).reshape(local_rows, head_count, group, HEAD)
        return jnp.sum(shaped, axis=2).reshape(1, local_rows, local_width).astype(jnp.bfloat16)

    query_full = jnp.zeros((length, HEAD), jnp.bfloat16)
    for which in range(2):
        query_full = lax.dynamic_update_slice_in_dim(
            query_full, query_rounded[which], row_list[which] * block, 0
        )
    query_back = lax.all_to_all(query_full, "seq", split_axis=0, concat_axis=1, tiled=True)
    query_out = settle(query_back)
    return (query_out, settle(key_back), settle(value_back))


NT = ((1,), (1,))
NN = ((1,), (0,))
TN = ((0,), (0,))
KINDS = 3
GROUP = 8
SLOT = KINDS * GROUP


def head_span(head):
    low = head * HEAD // LANES * LANES
    high = -(-(head + 1) * HEAD // LANES) * LANES
    return low, high


def head_mask(head):
    low, high = head_span(head)
    lane = lax.broadcasted_iota(jnp.int32, (1, high - low), 1) + low
    inside = (lane >= head * HEAD) & (lane < (head + 1) * HEAD)
    return inside.astype(jnp.float32).astype(jnp.bfloat16)


def matmul(left, right, dims):
    return lax.dot_general(left, right, (dims, ((), ())), preferred_element_type=jnp.float32)


def stack(values, axis):
    return values[0] if len(values) == 1 else jnp.concatenate(values, axis=axis)


def allowed(lengths_ref, rows, query_block, key_block):
    shape = (rows, rows)
    position = query_block * rows + lax.broadcasted_iota(jnp.int32, shape, 1)
    keys = key_block * rows + lax.broadcasted_iota(jnp.int32, shape, 0)
    start = jnp.zeros_like(position)
    bound = jnp.int32(0)
    for doc in range(lengths_ref.shape[0]):
        bound = bound + lengths_ref[doc]
        start = jnp.where(position >= bound, bound, start)
    return (keys >= start) & (keys <= position)


def make_tile(lengths_ref, rows, queries, keys):
    mask = stack(
        [stack([allowed(lengths_ref, rows, q, k) for _, q in queries], 1) for _, k in keys], 0
    )
    return [slot for slot, _ in queries], [slot for slot, _ in keys], mask


def tile_values(plan, head, queries, keys):
    low, high = head_span(head)
    keep = head_mask(head)

    def gather(refs, number, slots):
        return stack([refs[slot][number][0, :, low:high] for slot in slots], 0)

    out = []
    for query_slots, key_slots, mask in plan:
        q, o = (gather(queries, number, query_slots) for number in range(2))
        k, v = (gather(keys, number, key_slots) * keep for number in range(2))
        out.append((q, o, k, matmul(k, q, NT), matmul(v, o, NT)))
    return out, keep


def tiles_ahead(heads, plan, queries, keys):
    ready = tile_values(plan, 0, queries, keys)
    for head in range(heads):
        now = ready
        if head + 1 < heads:
            ready = tile_values(plan, head + 1, queries, keys)
        yield head, now


def collect_stats(heads, power, step, plan, queries, keys, rows, out_ref, slots):
    for head, (tiles, _) in tiles_ahead(heads, plan, queries, keys):
        parts = {}
        for (query_slots, _, mask), (_, _, _, raw, grads) in zip(plan, tiles):
            raw = jnp.where(mask, raw, FLOOR)
            for number, slot in enumerate(query_slots):
                cut = slice(number * rows, (number + 1) * rows)
                parts.setdefault(slot, []).append((raw[:, cut], grads[:, cut]))
        for slot, pieces in parts.items():
            top = functools.reduce(
                jnp.maximum, [jnp.max(s, axis=0, keepdims=True) for s, _ in pieces]
            )
            exps = [jnp.exp2((s - top) * power) for s, _ in pieces]
            sums = sum(jnp.sum(e, axis=0, keepdims=True) for e in exps)
            dots = sum(jnp.sum(e * g, axis=0, keepdims=True) for e, (_, g) in zip(exps, pieces))
            for kind, value in enumerate((top, sums, dots)):
                row = slots[slot] * SLOT + kind * GROUP + step * heads + head
                out_ref[pl.ds(row, 1), :] = value


def merge_stats(scaling, parts):
    split = []
    for part in parts:
        top, total, dots = (part[kind * GROUP : (kind + 1) * GROUP] for kind in range(KINDS))
        split.append((jnp.where(total > 0, top, FLOOR), total, dots))
    top = functools.reduce(jnp.maximum, [s[0] for s in split])
    scales = [jnp.exp((s[0] - top) * scaling) for s in split]
    total = sum(w * s[1] for w, s in zip(scales, split))
    dots = sum(w * s[2] for w, s in zip(scales, split))
    safe = jnp.where(total > 0, total, 1.0)
    return top + jnp.log(safe) / scaling, dots / safe


def collect_grads(heads, scaling, power, step, plan, queries, keys, rows, merged, outs, base):
    carry = {}

    def emit(head, name, value):
        ref, number = outs[name]
        low, high = head_span(head)
        first, last = head * HEAD % LANES == 0, (head + 1) * HEAD % LANES == 0

        def put(start, stop, piece):
            if name in base:
                old, at = base[name]
                piece = piece + old[at, :, start:stop].astype(jnp.float32)
            ref[number, :, start:stop] = piece.astype(jnp.bfloat16)

        start, stop = low, high
        if not first:
            put(low, low + LANES, value[:, :LANES] + carry.pop(name))
            start = low + LANES
        if not last:
            carry[name] = value[:, high - LANES - low :]
            stop = high - LANES
        if stop > start:
            put(start, stop, value[:, start - low : stop - low])

    for head, (tiles, keep) in tiles_ahead(heads, plan, queries, keys):
        sums = {}

        def add(name, value):
            sums[name] = sums[name] + value if name in sums else value

        for (query_slots, key_slots, mask), (q, o, k, raw, grads) in zip(plan, tiles):
            def row(kind):
                at = step * heads + head + kind * GROUP
                return stack([merged[slot][pl.ds(at, 1), :] for slot in query_slots], 1)

            weight = jnp.where(mask, jnp.exp2((raw - row(0)) * power), 0.0)
            slope = (weight * (grads - row(1)) * scaling).astype(jnp.bfloat16)
            weight = weight.astype(jnp.bfloat16)
            to_queries = matmul(slope, k, TN)
            to_keys = matmul(slope, q * keep, NN)
            to_values = matmul(weight, o * keep, NN)
            for number, slot in enumerate(query_slots):
                add(("q", slot), to_queries[number * rows : (number + 1) * rows])
            for number, slot in enumerate(key_slots):
                cut = slice(number * rows, (number + 1) * rows)
                add(("k", slot), to_keys[cut])
                add(("v", slot), to_values[cut])
        for name, value in sums.items():
            emit(head, name, value)


def by_parity(me, even, odd):
    pl.when(lax.rem(me, 2) == 0)(even)
    pl.when(lax.rem(me, 2) == 1)(odd)


def first_stats(heads, power, place_ref, lengths_ref, qo, oo, qm, om, ko, vo, kb, vb, out_ref):
    rows, me, step = qo.shape[1], place_ref[0], pl.program_id(0)
    queries, keys = ((qo, oo), (qm, om)), ((ko, vo), (kb, vb))

    def even():
        plan = [
            make_tile(lengths_ref, rows, ((0, me), (1, me + 1)), ((0, me), (1, me - 2)))
        ]
        collect_stats(heads, power, step, plan, queries, keys, rows, out_ref, (1, 0))

    def odd():
        plan = [
            make_tile(lengths_ref, rows, ((0, me),), ((0, me),)),
            make_tile(lengths_ref, rows, ((0, me), (1, me - 1)), ((1, me - 2),)),
        ]
        collect_stats(heads, power, step, plan, queries, keys, rows, out_ref, (0, 1))

    by_parity(me, even, odd)


def third_stats(heads, power, place_ref, lengths_ref, qt, ot, kb, vb, first_ref, after, out_ref):
    rows, me, step = qt.shape[1], place_ref[0], pl.program_id(0)

    def even():
        out_ref[...] = first_ref[SLOT : 2 * SLOT]

    def odd():
        plan = [make_tile(lengths_ref, rows, ((0, me + 1),), ((0, me - 2),))]
        collect_stats(heads, power, step, plan, ((qt, ot),), ((kb, vb),), rows, out_ref, (0,))

    by_parity(me, even, odd)


def odd_block_grads(
    heads, scaling, power, place_ref, lengths_ref, qo, oo, qm, om, ko, vo, kb, vb, mine, mate,
    query_out, own_out, back_out, merged,
):
    rows, me, step = qo.shape[1], place_ref[0], pl.program_id(0)
    keys = ((ko, vo), (kb, vb))
    shift, dots = merge_stats(scaling, (mine[:SLOT], mate[:SLOT]))
    merged[:GROUP], merged[GROUP:] = shift, dots
    outs = {
        ("q", 0): (query_out, 0),
        ("k", 0): (own_out, 0),
        ("v", 0): (own_out, 1),
        ("k", 1): (back_out, 0),
        ("v", 1): (back_out, 1),
    }

    def run(block, queries):
        own = me
        plan = [make_tile(lengths_ref, rows, ((0, block),), ((0, own), (1, own - 2)))]
        collect_grads(
            heads, scaling, power, step, plan, queries, keys, rows, (merged,), outs, {}
        )

    by_parity(me, lambda: run(me + 1, ((qm, om),)), lambda: run(me, ((qo, oo),)))


def even_block_grads(
    heads, scaling, power, place_ref, lengths_ref, qo, oo, qm, om, qt, ot, ko, vo, kb, vb, mine, mate, up,
    third, zig, down, own_part, back_part, query_out, third_out, own_out, back_out, merged, merged_third,
):
    rows, me, step = qo.shape[1], place_ref[0], pl.program_id(0)

    def even():
        shift, dots = merge_stats(scaling, (mine[SLOT:], mate[SLOT:], zig[...]))
        merged[:GROUP], merged[GROUP:] = shift, dots
        plan = [make_tile(lengths_ref, rows, ((0, me),), ((0, me), (1, me - 2)))]
        outs = {
            ("q", 0): (query_out, 0),
            ("k", 0): (own_out, 0),
            ("v", 0): (own_out, 1),
            ("k", 1): (back_out, 0),
            ("v", 1): (back_out, 1),
        }
        base = {
            ("k", 0): (own_part, 0),
            ("v", 0): (own_part, 1),
            ("k", 1): (back_part, 0),
            ("v", 1): (back_part, 1),
        }
        collect_grads(
            heads, scaling, power, step, plan, ((qo, oo),), ((ko, vo), (kb, vb)), rows, (merged,), outs, base
        )
        third_out[...] = jnp.zeros_like(third_out)

    def odd():
        shift, dots = merge_stats(scaling, (mine[SLOT:], mate[SLOT:], up[...]))
        merged[:GROUP], merged[GROUP:] = shift, dots
        shift, dots = merge_stats(scaling, (third[...], zig[...], down[SLOT:]))
        merged_third[:GROUP], merged_third[GROUP:] = shift, dots
        plan = [make_tile(lengths_ref, rows, ((0, me - 1), (1, me + 1)), ((0, me - 2),))]
        outs = {
            ("q", 0): (query_out, 0),
            ("q", 1): (third_out, 0),
            ("k", 0): (back_out, 0),
            ("v", 0): (back_out, 1),
        }
        base = {("k", 0): (back_part, 0), ("v", 0): (back_part, 1)}
        collect_grads(
            heads, scaling, power, step, plan, ((qm, om), (qt, ot)), ((kb, vb),), rows,
            (merged, merged_third), outs, base,
        )
        own_out[...] = own_part[...]

    by_parity(me, even, odd)


def halo_shards(queries, key_vectors, value_vectors, out_grad, doc_lengths):
    _, rows, width = queries.shape
    seq_size = lax.axis_size("seq")
    me = lax.axis_index("seq").astype(jnp.int32)
    scaling = HEAD ** (-0.5)
    power = scaling * math.log2(math.e)
    steps = width // HEAD // 4
    part = width // steps
    heads = part // HEAD
    devices = range(seq_size)
    odds = [s for s in devices if s % 2]
    mates = [(s, s ^ 1) for s in devices]
    ahead = [(s, s + 2) for s in devices if s + 2 < seq_size]
    behind = [(s, s - 2) for s in devices if s >= 2]
    odd_ahead = [(s, s + 2) for s in odds if s + 2 < seq_size]
    odd_behind = [(s, s - 2) for s in odds if s >= 2]
    odd_next = [(s, s + 1) for s in odds if s + 1 < seq_size]
    zigzag = odd_next + [(t, s) for s, t in odd_next]
    even_to_odd = [(s - 1, s) for s in odds]
    odd_to_even = [(s, s - 1) for s in odds]

    def send(value, pairs):
        return lax.ppermute(value, "seq", pairs)

    smem = pl.BlockSpec(memory_space=pltpu.SMEM)
    wide = pl.BlockSpec((1, rows, part), lambda step: (0, 0, step))
    pair = pl.BlockSpec((2, rows, part), lambda step: (0, 0, step))

    def slim(count):
        return pl.BlockSpec((count * SLOT, rows), lambda step: (0, 0))

    def stats_shape(count):
        return jax.ShapeDtypeStruct((count * SLOT, rows), jnp.float32)

    def shape(count):
        return jax.ShapeDtypeStruct((count, rows, width), jnp.bfloat16)

    def call(kernel, tiles, products, arguments, in_specs, out_specs, out_shape, scratch=0):
        flops = 2 * products * tiles * rows * rows * width * 3 // 2
        return pl.pallas_call(
            kernel,
            grid=(steps,),
            in_specs=[smem, smem] + in_specs,
            out_specs=out_specs,
            out_shape=out_shape,
            scratch_shapes=[pltpu.VMEM((2 * GROUP, rows), jnp.float32)] * scratch,
            compiler_params=pltpu.CompilerParams(vmem_limit_bytes=20 * 1024 * 1024),
            cost_estimate=pl.CostEstimate(
                flops=flops, bytes_accessed=20 * rows * width, transcendentals=0
            ),
        )(me[None], doc_lengths, *arguments)

    query_mate = send(queries, mates)
    grad_mate = send(out_grad, mates)
    key_back = send(key_vectors, ahead)
    value_back = send(value_vectors, ahead)
    query_third = send(query_mate, odd_behind)
    grad_third = send(grad_mate, odd_behind)
    rows_here = (queries, out_grad, query_mate, grad_mate)
    rows_third = (query_third, grad_third)
    back = (key_back, value_back)
    cols = (key_vectors, value_vectors) + back

    mine = call(
        functools.partial(first_stats, heads, power), 4, 2, (*rows_here, *cols), [wide] * 8, slim(2),
        stats_shape(2),
    )
    mate = send(mine, mates)
    down = send(mine, odd_behind)
    query_a, own_part, back_part = call(
        functools.partial(odd_block_grads, heads, scaling, power), 2, 5, (*rows_here, *cols, mine, mate),
        [wide] * 8 + [slim(2)] * 2, [wide, pair, pair], [shape(1), shape(2), shape(2)], 1,
    )
    from_even = send(query_a, even_to_odd)
    third = call(
        functools.partial(third_stats, heads, power), 1, 2, (*rows_third, *back, mine, query_a),
        [wide] * 4 + [slim(2), pl.BlockSpec(memory_space=pl.ANY)], slim(1), stats_shape(1),
    )
    zig = send(third, zigzag)
    up = send(third, odd_ahead)
    query_b, query_c, key_own, key_sent = call(
        functools.partial(even_block_grads, heads, scaling, power), 2, 5,
        (*rows_here, *rows_third, *cols, mine, mate, up, third, zig, down, own_part, back_part),
        [wide] * 10 + [slim(2)] * 2 + [slim(1)] * 3 + [slim(2)] + [pair] * 2,
        [wide, wide, pair, pair], [shape(1), shape(1), shape(2), shape(2)], 2,
    )
    key_back_sum = send(key_sent, behind)
    from_odd = send(query_b, odd_to_even)
    from_third = send(query_c, odd_next)

    def total(*terms):
        return sum(term.astype(jnp.float32) for term in terms).astype(jnp.bfloat16)

    key_ready = total(key_own[:1], key_back_sum[:1])
    value_ready = total(key_own[1:], key_back_sum[1:])
    query_own = jnp.where(lax.rem(me, 2) == 0, query_b, query_a)
    query_own, key_ready, value_ready = lax.optimization_barrier((query_own, key_ready, value_ready))
    query_ready = total(query_own, from_even, from_odd, from_third)
    return query_ready, key_ready, value_ready


def shards(queries, key_vectors, value_vectors, out_grad, doc_lengths):
    _, rows, width = queries.shape
    seq_size = lax.axis_size("seq")
    longest = rows * seq_size * 3 // 8
    fits = longest <= 3 * rows and seq_size % 2 == 0 and rows == LANES
    heads = width // HEAD
    plan = halo_shards if fits and heads % 4 == 0 and heads <= GROUP else spread_shards
    return plan(queries, key_vectors, value_vectors, out_grad, doc_lengths)


def solution(mesh):
    return jax.shard_map(
        shards,
        mesh=mesh,
        in_specs=(
            P("section", "seq", "dp"),
            P("section", "seq", "dp"),
            P("section", "seq", "dp"),
            P("section", "seq", "dp"),
            P(),
        ),
        out_specs=(P("section", "seq", "dp"), P("section", "seq", "dp"), P("section", "seq", "dp")),
        check_vma=False,
    )
```

```python
import functools
import math
import jax
import jax.numpy as jnp
from jax import lax
from jax.experimental import pallas as pl
from jax.experimental.pallas import tpu as pltpu
from jax.sharding import PartitionSpec as P

HEAD = 224
LANES = 128
FLOOR = -1e30


def pick_slot(stacked, slot):
    return lax.dynamic_index_in_dim(stacked, slot, 0, keepdims=False)


def put_slot(stacked, update, slot):
    return lax.dynamic_update_index_in_dim(stacked, update, slot, 0)


def spread_shards(queries, key_vectors, value_vectors, out_grad, doc_lengths):
    local_rows = queries.shape[1]
    local_width = queries.shape[2]
    head_count = local_width // HEAD
    seq_size = lax.axis_size("seq")
    group = seq_size // head_count
    scaling = HEAD ** (-0.5)

    def spread(matrix):
        shaped = matrix.reshape(local_rows, head_count, 1, HEAD)
        copies = jnp.broadcast_to(shaped, (local_rows, head_count, group, HEAD))
        return copies.reshape(local_rows, seq_size * HEAD)

    query_head, key_head, value_head, cot_head = (
        lax.all_to_all(spread(queries), "seq", split_axis=1, concat_axis=0, tiled=True),
        lax.all_to_all(spread(key_vectors), "seq", split_axis=1, concat_axis=0, tiled=True),
        lax.all_to_all(spread(value_vectors), "seq", split_axis=1, concat_axis=0, tiled=True),
        lax.all_to_all(spread(out_grad), "seq", split_axis=1, concat_axis=0, tiled=True),
    )
    length = key_head.shape[0]
    member = lax.axis_index("seq") % group
    blocks = 2 * group
    block = length // blocks
    bounds = jnp.cumsum(doc_lengths)
    positions = jnp.arange(length, dtype=jnp.int32)
    doc_index = jnp.sum((positions[:, None] >= bounds[None, :]).astype(jnp.int32), axis=1)
    row_list = [member, blocks - 1 - member]
    query_list = []
    cot_list = []
    pos_list = []
    for which in range(2):
        offset = row_list[which] * block
        query_list.append(lax.dynamic_slice_in_dim(query_head, offset, block, 0))
        cot_list.append(lax.dynamic_slice_in_dim(cot_head, offset, block, 0))
        pos_list.append(offset + jnp.arange(block, dtype=jnp.int32))
    query_stack = jnp.stack(query_list)
    cot_stack = jnp.stack(cot_list)
    pos_stack = jnp.stack(pos_list)
    doc_stack = jnp.take(doc_index, pos_stack)
    plan = []
    for number in range(blocks + 1):
        first = number <= member
        slot = jnp.where(first, 0, 1).astype(jnp.int32)
        col_block = jnp.where(first, number, number - member - 1)
        flag = None
        plan.append((slot, col_block, flag))
    row_max = jnp.full((2, block), -jnp.inf, jnp.float32)
    row_sum = jnp.zeros((2, block), jnp.float32)
    stored = []
    for slot, col_block, flag in plan:

        def score_tile(carry, slot=slot, col_block=col_block):
            maxima, totals = carry
            query_rows = pick_slot(query_stack, slot)
            key_rows = lax.dynamic_slice_in_dim(key_head, col_block * block, block, 0)
            col_docs = lax.dynamic_slice_in_dim(doc_index, col_block * block, block, 0)
            col_positions = col_block * block + jnp.arange(block, dtype=jnp.int32)
            raw = jnp.dot(query_rows, key_rows.T, preferred_element_type=jnp.float32) * scaling
            allowed = (pick_slot(doc_stack, slot)[:, None] == col_docs[None, :]) & (
                pick_slot(pos_stack, slot)[:, None] >= col_positions[None, :]
            )
            scores = jnp.where(allowed, raw, -jnp.inf)
            before = pick_slot(maxima, slot)
            after = jnp.maximum(before, jnp.max(scores, axis=1))
            safe = jnp.where(jnp.isfinite(after), after, 0.0)
            total = pick_slot(totals, slot) * jnp.exp(before - safe) + jnp.sum(
                jnp.exp(scores - safe[:, None]), axis=1
            )
            return (scores, put_slot(maxima, after, slot), put_slot(totals, total, slot))

        scores, row_max, row_sum = score_tile((row_max, row_sum))
        stored.append(scores)

    def tile_weights(scores, slot):
        return (
            jnp.exp(scores - pick_slot(row_max, slot)[:, None]) / pick_slot(row_sum, slot)[:, None]
        )

    summed = jnp.zeros((2, block, HEAD), jnp.float32)
    for (slot, col_block, flag), scores in zip(plan, stored):

        def add_values(carry, slot=slot, col_block=col_block, scores=scores):
            rounded = tile_weights(scores, slot).astype(jnp.bfloat16)
            value_rows = lax.dynamic_slice_in_dim(value_head, col_block * block, block, 0)
            term = jnp.dot(rounded, value_rows, preferred_element_type=jnp.float32)
            return put_slot(carry, pick_slot(carry, slot) + term, slot)

        summed = add_values(summed)
    attended = summed.astype(jnp.bfloat16)
    row_dot = jnp.sum(cot_stack.astype(jnp.float32) * attended.astype(jnp.float32), axis=2)
    query_acc = jnp.zeros((2, block, HEAD), jnp.float32)
    key_acc = jnp.zeros((length, HEAD), jnp.float32)
    value_acc = jnp.zeros((length, HEAD), jnp.float32)
    for (slot, col_block, flag), scores in zip(plan, stored):

        def backward_tile(carry, slot=slot, col_block=col_block, scores=scores):
            query_sum, key_sum, value_sum = carry
            weights = tile_weights(scores, slot)
            rounded = weights.astype(jnp.bfloat16)
            query_rows = pick_slot(query_stack, slot)
            cot_rows = pick_slot(cot_stack, slot)
            start = col_block * block
            key_rows = lax.dynamic_slice_in_dim(key_head, start, block, 0)
            value_rows = lax.dynamic_slice_in_dim(value_head, start, block, 0)
            value_term = jnp.dot(rounded.T, cot_rows, preferred_element_type=jnp.float32)
            prob_grad = jnp.dot(cot_rows, value_rows.T, preferred_element_type=jnp.float32)
            score_grad = (
                weights * (prob_grad - pick_slot(row_dot, slot)[:, None]) * scaling
            ).astype(jnp.bfloat16)
            query_term = jnp.dot(score_grad, key_rows, preferred_element_type=jnp.float32)
            key_term = jnp.dot(score_grad.T, query_rows, preferred_element_type=jnp.float32)
            query_sum = put_slot(query_sum, pick_slot(query_sum, slot) + query_term, slot)
            key_sum = lax.dynamic_update_slice_in_dim(
                key_sum, lax.dynamic_slice_in_dim(key_sum, start, block, 0) + key_term, start, 0
            )
            value_sum = lax.dynamic_update_slice_in_dim(
                value_sum,
                lax.dynamic_slice_in_dim(value_sum, start, block, 0) + value_term,
                start,
                0,
            )
            return (query_sum, key_sum, value_sum)

        query_acc, key_acc, value_acc = backward_tile((query_acc, key_acc, value_acc))
    query_rounded = query_acc.astype(jnp.bfloat16)
    key_back, value_back = (
        lax.all_to_all(key_acc, "seq", split_axis=0, concat_axis=1, tiled=True),
        lax.all_to_all(value_acc, "seq", split_axis=0, concat_axis=1, tiled=True),
    )

    def settle(received):
        shaped = received.astype(jnp.float32).reshape(local_rows, head_count, group, HEAD)
        return jnp.sum(shaped, axis=2).reshape(1, local_rows, local_width).astype(jnp.bfloat16)

    query_full = jnp.zeros((length, HEAD), jnp.bfloat16)
    for which in range(2):
        query_full = lax.dynamic_update_slice_in_dim(
            query_full, query_rounded[which], row_list[which] * block, 0
        )
    query_back = lax.all_to_all(query_full, "seq", split_axis=0, concat_axis=1, tiled=True)
    query_out = settle(query_back)
    return (query_out, settle(key_back), settle(value_back))


NT = ((1,), (1,))
NN = ((1,), (0,))
TN = ((0,), (0,))
GROUP = 8


def head_span(head):
    low = head * HEAD // LANES * LANES
    high = -(-(head + 1) * HEAD // LANES) * LANES
    return low, high


def head_mask(head):
    low, high = head_span(head)
    lane = lax.broadcasted_iota(jnp.int32, (1, high - low), 1) + low
    inside = (lane >= head * HEAD) & (lane < (head + 1) * HEAD)
    return inside.astype(jnp.float32).astype(jnp.bfloat16)


def matmul(left, right, dims):
    return lax.dot_general(left, right, (dims, ((), ())), preferred_element_type=jnp.float32)


def stack(values, axis):
    return values[0] if len(values) == 1 else jnp.concatenate(values, axis=axis)


def allowed(lengths_ref, rows, query_block, key_block):
    shape = (rows, rows)
    position = query_block * rows + lax.broadcasted_iota(jnp.int32, shape, 1)
    keys = key_block * rows + lax.broadcasted_iota(jnp.int32, shape, 0)
    start = jnp.zeros_like(position)
    bound = jnp.int32(0)
    for doc in range(lengths_ref.shape[0]):
        bound = bound + lengths_ref[doc]
        start = jnp.where(position >= bound, bound, start)
    return (keys >= start) & (keys <= position)


def make_tile(lengths_ref, rows, queries, keys):
    mask = stack(
        [stack([allowed(lengths_ref, rows, q, k) for _, q in queries], 1) for _, k in keys], 0
    )
    return [slot for slot, _ in queries], [slot for slot, _ in keys], mask


def tile_values(plan, head, queries, keys, products):
    low, high = head_span(head)
    keep = head_mask(head)

    def gather(refs, number, slots):
        return stack([refs[slot][number][0, :, low:high] for slot in slots], 0)

    out = []
    for query_slots, key_slots, _ in plan:
        q = [gather(queries, number, query_slots) for number in range(products)]
        k = [gather(keys, number, key_slots) * keep for number in range(products)]
        out.append((q, k, [matmul(b, a, NT) for a, b in zip(q, k)]))
    return out, keep


def tiles_ahead(heads, plan, queries, keys, products):
    ready = tile_values(plan, 0, queries, keys, products)
    for head in range(heads):
        now = ready
        if head + 1 < heads:
            ready = tile_values(plan, head + 1, queries, keys, products)
        yield head, now


def plans(third, lengths_ref, rows, me):
    def even():
        return [make_tile(lengths_ref, rows, ((0, me), (1, me + 1)), ((0, me), (1, me - 2)))]

    def odd():
        met = ((0, me), (1, me - 1)) + (((2, me + 1),) if third else ())
        return [
            make_tile(lengths_ref, rows, ((0, me),), ((0, me),)),
            make_tile(lengths_ref, rows, met, ((1, me - 2),)),
        ]

    return even, odd


def by_parity(me, even, odd):
    pl.when(lax.rem(me, 2) == 0)(even)
    pl.when(lax.rem(me, 2) == 1)(odd)


def at_start(step, refs):
    @pl.when(step == 0)
    def _():
        for ref in refs:
            ref[...] = jnp.zeros_like(ref)


def lane_cut(value, number, rows):
    return value[:, number * rows : (number + 1) * rows]


def row_of(group, kinds, kind, head):
    return pl.ds((group * kinds + kind) * GROUP + head, 1)


def per_query(slots, kinds, kind, head, ref):
    return stack([ref[row_of(slot, kinds, kind, head), :] for slot in slots], 1)


def stats_kernel(third, heads, power, place_ref, lengths_ref, *refs):
    count = 3 if third else 2
    query_refs, (k_own, k_back, o_own, v_own) = refs[:count], refs[count : count + 4]
    o_copy, v_copy, out_ref = refs[count + 4 :]
    rows, me, step = k_own.shape[1], place_ref[0], pl.program_id(0)
    at_start(step, [out_ref])
    o_copy[...], v_copy[...] = o_own[...], v_own[...]
    queries, keys = [(ref,) for ref in query_refs], ((k_own,), (k_back,))

    def run(plan):
        for head, (tiles, _) in tiles_ahead(heads, plan, queries, keys, 1):
            parts = {}
            for (query_slots, _, mask), (_, _, (raw,)) in zip(plan, tiles):
                raw = jnp.where(mask, raw, FLOOR)
                for number, slot in enumerate(query_slots):
                    parts.setdefault(slot, []).append(lane_cut(raw, number, rows))
            for slot, pieces in parts.items():
                top = functools.reduce(
                    jnp.maximum, [jnp.max(p, axis=0, keepdims=True) for p in pieces]
                )
                sums = sum(
                    jnp.sum(jnp.exp2((p - top) * power), axis=0, keepdims=True) for p in pieces
                )
                out_ref[row_of(slot, 2, 0, step * heads + head), :] = top
                out_ref[row_of(slot, 2, 1, step * heads + head), :] = sums

    even, odd = plans(third, lengths_ref, rows, me)
    by_parity(me, lambda: run(even()), lambda: run(odd()))


def group_parts(third, odd, kinds, mine, messages):
    size = kinds * GROUP

    def group(ref, number):
        return ref[number * size : (number + 1) * size, :]

    own = [group(mine, 0), group(messages[0], 1)]
    mate = [group(mine, 1), group(messages[0], 0)]
    if not third:
        return [own, mate]
    _, zig, up, down = messages
    if odd:
        return [own, mate + [group(up, 2)], [group(mine, 2), group(zig, 0), group(down, 1)]]
    return [own + [group(zig, 2)], mate]


def merge_stats(scaling, parts):
    split = [(jnp.where(p[GROUP:] > 0, p[:GROUP], FLOOR), p[GROUP:]) for p in parts]
    top = functools.reduce(jnp.maximum, [s[0] for s in split])
    total = sum(jnp.exp((s[0] - top) * scaling) * s[1] for s in split)
    return top + jnp.log(jnp.where(total > 0, total, 1.0)) / scaling


class Emitter:
    def __init__(self, outs):
        self.outs, self.carry = outs, {}

    def emit(self, head, name, value):
        ref = self.outs[name]
        low, high = head_span(head)
        first, last = head * HEAD % LANES == 0, (head + 1) * HEAD % LANES == 0
        start, stop = low, high
        if not first:
            shared = value[:, :LANES] + self.carry.pop(name)
            ref[0, :, low : low + LANES] = shared.astype(jnp.bfloat16)
            start = low + LANES
        if not last:
            self.carry[name] = value[:, high - LANES - low :]
            stop = high - LANES
        if stop > start:
            ref[0, :, start:stop] = value[:, start - low : stop - low].astype(jnp.bfloat16)


def add_rows(sums, kind, slots, value, rows):
    for number, slot in enumerate(slots):
        piece = value[number * rows : (number + 1) * rows]
        name = (kind, slot)
        sums[name] = sums[name] + piece if name in sums else piece


def add_lanes(sums, slots, value, rows):
    for number, slot in enumerate(slots):
        piece = lane_cut(value, number, rows)
        sums[slot] = sums[slot] + piece if slot in sums else piece


def split_refs(third, refs):
    count = 3 if third else 2
    queries = [(refs[2 * n], refs[2 * n + 1]) for n in range(count)]
    keys = [(refs[2 * n], refs[2 * n + 1]) for n in range(count, count + 2)]
    return queries, keys, refs[2 * count + 4 :]


def values_kernel(third, heads, scaling, power, place_ref, lengths_ref, *refs):
    queries, keys, refs = split_refs(third, refs)
    messages = 4 if third else 1
    mine, others = refs[0], refs[1 : 1 + messages]
    value_own, value_back, shift_ref, dots_ref = refs[1 + messages :]
    rows, me, step = keys[0][0].shape[1], place_ref[0], pl.program_id(0)
    at_start(step, [dots_ref])

    def run(odd, plan):
        groups = group_parts(third, odd, 2, mine, others)
        for number, parts in enumerate(groups):
            shift_ref[number * GROUP : (number + 1) * GROUP, :] = merge_stats(scaling, parts)
        out = Emitter({("v", 0): value_own, ("v", 1): value_back})
        for head, (tiles, keep) in tiles_ahead(heads, plan, queries, keys, 2):
            at = step * heads + head
            sums, dots = {}, {}
            for (query_slots, key_slots, mask), ((_, o), _, (raw, grads)) in zip(plan, tiles):
                shift = per_query(query_slots, 1, 0, at, shift_ref)
                weight = jnp.where(mask, jnp.exp2((raw - shift) * power), 0.0)
                add_lanes(dots, query_slots, jnp.sum(weight * grads, axis=0, keepdims=True), rows)
                add_rows(
                    sums, "v", key_slots, matmul(weight.astype(jnp.bfloat16), o * keep, NN), rows
                )
            for slot, value in dots.items():
                dots_ref[row_of(slot, 1, 0, at), :] = value
            for name, value in sums.items():
                out.emit(head, name, value)

    even, odd = plans(third, lengths_ref, rows, me)
    by_parity(me, lambda: run(False, even()), lambda: run(True, odd()))


def keys_kernel(third, heads, scaling, power, place_ref, lengths_ref, *refs):
    queries, keys, refs = split_refs(third, refs)
    messages = 4 if third else 1
    shift_ref, mine, others = refs[0], refs[1], refs[2 : 2 + messages]
    key_own, key_back, *query_refs, total_ref = refs[2 + messages :]
    rows, me, step = keys[0][0].shape[1], place_ref[0], pl.program_id(0)

    def run(odd, plan):
        for number, parts in enumerate(group_parts(third, odd, 1, mine, others)):
            total_ref[number * GROUP : (number + 1) * GROUP, :] = sum(parts)
        outs = {("k", 0): key_own, ("k", 1): key_back}
        outs.update({("q", slot): ref for slot, ref in enumerate(query_refs)})
        out = Emitter(outs)
        if third and not odd:
            query_refs[2][...] = jnp.zeros_like(query_refs[2])
        for head, (tiles, keep) in tiles_ahead(heads, plan, queries, keys, 2):
            at = step * heads + head
            sums = {}
            for (query_slots, key_slots, mask), ((q, _), (k, _), (raw, grads)) in zip(plan, tiles):
                shift = per_query(query_slots, 1, 0, at, shift_ref)
                dots = per_query(query_slots, 1, 0, at, total_ref)
                weight = jnp.where(mask, jnp.exp2((raw - shift) * power), 0.0)
                slope = (weight * (grads - dots) * scaling).astype(jnp.bfloat16)
                add_rows(sums, "k", key_slots, matmul(slope, q * keep, NN), rows)
                add_rows(sums, "q", query_slots, matmul(slope, k, TN), rows)
            for name, value in sums.items():
                out.emit(head, name, value)

    even, odd = plans(third, lengths_ref, rows, me)
    by_parity(me, lambda: run(False, even()), lambda: run(True, odd()))


def halo_program(third, queries, key_vectors, value_vectors, out_grad, doc_lengths):
    _, rows, width = queries.shape
    seq_size = lax.axis_size("seq")
    me = lax.axis_index("seq").astype(jnp.int32)
    scaling = HEAD ** (-0.5)
    power = scaling * math.log2(math.e)
    steps = width // HEAD // 4
    part = width // steps
    heads = part // HEAD
    count = 3 if third else 2
    devices = range(seq_size)
    odds = [s for s in devices if s % 2]
    mates = [(s, s ^ 1) for s in devices]
    ahead = [(s, s + 2) for s in devices if s + 2 < seq_size]
    behind = [(s, s - 2) for s in devices if s >= 2]
    odd_ahead = [(s, s + 2) for s in odds if s + 2 < seq_size]
    odd_behind = [(s, s - 2) for s in odds if s >= 2]
    odd_next = [(s, s + 1) for s in odds if s + 1 < seq_size]
    zigzag = odd_next + [(t, s) for s, t in odd_next]

    def send(value, pairs):
        return lax.ppermute(value, "seq", pairs)

    def exchange(value):
        return [send(value, pairs) for pairs in ((mates, zigzag, odd_ahead, odd_behind) if third else (mates,))]

    smem = pl.BlockSpec(memory_space=pltpu.SMEM)
    wide = pl.BlockSpec((1, rows, part), lambda step: (0, 0, step))
    wide_shape = jax.ShapeDtypeStruct((1, rows, width), jnp.bfloat16)

    def slim(kinds):
        return pl.BlockSpec((count * kinds * GROUP, rows), lambda step: (0, 0))

    def slim_shape(kinds):
        return jax.ShapeDtypeStruct((count * kinds * GROUP, rows), jnp.float32)

    def call(kernel, products, wides, slims, outs, slim_outs, scratch=()):
        flops = 2 * products * 4 * rows * rows * width * 3 // 2
        return pl.pallas_call(
            kernel,
            grid=(steps,),
            in_specs=[smem, smem] + [wide] * len(wides) + [slim(kinds) for kinds, _ in slims],
            out_specs=[wide] * outs + [slim(kinds) for kinds in slim_outs],
            out_shape=[wide_shape] * outs + [slim_shape(kinds) for kinds in slim_outs],
            scratch_shapes=scratch,
            compiler_params=pltpu.CompilerParams(vmem_limit_bytes=20 * 1024 * 1024),
            cost_estimate=pl.CostEstimate(
                flops=flops, bytes_accessed=20 * rows * width, transcendentals=0
            ),
        )(me[None], doc_lengths, *wides, *[value for _, value in slims])

    query_mate = send(queries, mates)
    key_back = send(key_vectors, ahead)
    grad_mate = send(out_grad, mates)
    value_back = send(value_vectors, ahead)
    query_rows = [queries, query_mate] + ([send(query_mate, odd_behind)] if third else [])
    grad_own, value_own, stats = call(
        functools.partial(stats_kernel, third, heads, power), 1,
        [*query_rows, key_vectors, key_back, out_grad, value_vectors], [], 2, [2],
    )
    grad_rows = [grad_own, grad_mate] + ([send(grad_mate, odd_behind)] if third else [])
    tensors = [t for two in zip(query_rows, grad_rows) for t in two]
    tensors += [key_vectors, value_own, key_back, value_back]
    value_part, value_sent, shift, dots = call(
        functools.partial(values_kernel, third, heads, scaling, power), 3, tensors,
        [(2, value) for value in [stats] + exchange(stats)], 2, [1, 1],
    )
    value_received = send(value_sent, behind)
    key_part, key_sent, query_part, *query_sent = call(
        functools.partial(keys_kernel, third, heads, scaling, power), 4, tensors,
        [(1, value) for value in [shift, dots] + exchange(dots)], 2 + count, [],
        [pltpu.VMEM((count * GROUP, rows), jnp.float32)],
    )
    key_received = send(key_sent, behind)
    query_received = [send(value, pairs) for value, pairs in zip(query_sent, (mates, odd_next))]

    def total(*terms):
        return sum(term.astype(jnp.float32) for term in terms).astype(jnp.bfloat16)

    return (
        total(query_part, *query_received),
        total(key_part, key_received),
        total(value_part, value_received),
    )


def needs_third(rows, doc_lengths):
    count = doc_lengths.shape[0]
    index = jnp.arange(count)
    ends = jnp.sum(jnp.where(index[None, :] <= index[:, None], doc_lengths[None, :], 0), axis=1)
    first, last = (ends - doc_lengths) // rows, (ends - 1) // rows
    return jnp.any((last - first >= 3) & (last % 2 == 0))


def halo_shards(*arguments):
    rows, doc_lengths = arguments[0].shape[1], arguments[-1]
    return lax.cond(
        needs_third(rows, doc_lengths),
        functools.partial(halo_program, True),
        functools.partial(halo_program, False),
        *arguments,
    )


def shards(queries, key_vectors, value_vectors, out_grad, doc_lengths):
    _, rows, width = queries.shape
    seq_size = lax.axis_size("seq")
    longest = rows * seq_size * 3 // 8
    fits = longest <= 3 * rows and seq_size % 2 == 0 and rows == LANES
    heads = width // HEAD
    plan = halo_shards if fits and heads % 4 == 0 and heads <= GROUP else spread_shards
    return plan(queries, key_vectors, value_vectors, out_grad, doc_lengths)


def solution(mesh):
    return jax.shard_map(
        shards,
        mesh=mesh,
        in_specs=(
            P("section", "seq", "dp"),
            P("section", "seq", "dp"),
            P("section", "seq", "dp"),
            P("section", "seq", "dp"),
            P(),
        ),
        out_specs=(P("section", "seq", "dp"), P("section", "seq", "dp"), P("section", "seq", "dp")),
        check_vma=False,
    )
```

```python
import functools
import math
import jax
import jax.numpy as jnp
from jax import lax
from jax.experimental import pallas as pl
from jax.experimental.pallas import tpu as pltpu
from jax.sharding import PartitionSpec as P

HEAD = 224
LANES = 128
FLOOR = -1e30


def pick_slot(stacked, slot):
    return lax.dynamic_index_in_dim(stacked, slot, 0, keepdims=False)


def put_slot(stacked, update, slot):
    return lax.dynamic_update_index_in_dim(stacked, update, slot, 0)


def spread_shards(queries, key_vectors, value_vectors, out_grad, doc_lengths):
    local_rows = queries.shape[1]
    local_width = queries.shape[2]
    head_count = local_width // HEAD
    seq_size = lax.axis_size("seq")
    group = seq_size // head_count
    scaling = HEAD ** (-0.5)

    def spread(matrix):
        shaped = matrix.reshape(local_rows, head_count, 1, HEAD)
        copies = jnp.broadcast_to(shaped, (local_rows, head_count, group, HEAD))
        return copies.reshape(local_rows, seq_size * HEAD)

    query_head, key_head, value_head, cot_head = (
        lax.all_to_all(spread(queries), "seq", split_axis=1, concat_axis=0, tiled=True),
        lax.all_to_all(spread(key_vectors), "seq", split_axis=1, concat_axis=0, tiled=True),
        lax.all_to_all(spread(value_vectors), "seq", split_axis=1, concat_axis=0, tiled=True),
        lax.all_to_all(spread(out_grad), "seq", split_axis=1, concat_axis=0, tiled=True),
    )
    length = key_head.shape[0]
    member = lax.axis_index("seq") % group
    blocks = 2 * group
    block = length // blocks
    bounds = jnp.cumsum(doc_lengths)
    positions = jnp.arange(length, dtype=jnp.int32)
    doc_index = jnp.sum((positions[:, None] >= bounds[None, :]).astype(jnp.int32), axis=1)
    row_list = [member, blocks - 1 - member]
    query_list = []
    cot_list = []
    pos_list = []
    for which in range(2):
        offset = row_list[which] * block
        query_list.append(lax.dynamic_slice_in_dim(query_head, offset, block, 0))
        cot_list.append(lax.dynamic_slice_in_dim(cot_head, offset, block, 0))
        pos_list.append(offset + jnp.arange(block, dtype=jnp.int32))
    query_stack = jnp.stack(query_list)
    cot_stack = jnp.stack(cot_list)
    pos_stack = jnp.stack(pos_list)
    doc_stack = jnp.take(doc_index, pos_stack)
    plan = []
    for number in range(blocks + 1):
        first = number <= member
        slot = jnp.where(first, 0, 1).astype(jnp.int32)
        col_block = jnp.where(first, number, number - member - 1)
        flag = None
        plan.append((slot, col_block, flag))
    row_max = jnp.full((2, block), -jnp.inf, jnp.float32)
    row_sum = jnp.zeros((2, block), jnp.float32)
    stored = []
    for slot, col_block, flag in plan:

        def score_tile(carry, slot=slot, col_block=col_block):
            maxima, totals = carry
            query_rows = pick_slot(query_stack, slot)
            key_rows = lax.dynamic_slice_in_dim(key_head, col_block * block, block, 0)
            col_docs = lax.dynamic_slice_in_dim(doc_index, col_block * block, block, 0)
            col_positions = col_block * block + jnp.arange(block, dtype=jnp.int32)
            raw = jnp.dot(query_rows, key_rows.T, preferred_element_type=jnp.float32) * scaling
            allowed = (pick_slot(doc_stack, slot)[:, None] == col_docs[None, :]) & (
                pick_slot(pos_stack, slot)[:, None] >= col_positions[None, :]
            )
            scores = jnp.where(allowed, raw, -jnp.inf)
            before = pick_slot(maxima, slot)
            after = jnp.maximum(before, jnp.max(scores, axis=1))
            safe = jnp.where(jnp.isfinite(after), after, 0.0)
            total = pick_slot(totals, slot) * jnp.exp(before - safe) + jnp.sum(
                jnp.exp(scores - safe[:, None]), axis=1
            )
            return (scores, put_slot(maxima, after, slot), put_slot(totals, total, slot))

        scores, row_max, row_sum = score_tile((row_max, row_sum))
        stored.append(scores)

    def tile_weights(scores, slot):
        return (
            jnp.exp(scores - pick_slot(row_max, slot)[:, None]) / pick_slot(row_sum, slot)[:, None]
        )

    summed = jnp.zeros((2, block, HEAD), jnp.float32)
    for (slot, col_block, flag), scores in zip(plan, stored):

        def add_values(carry, slot=slot, col_block=col_block, scores=scores):
            rounded = tile_weights(scores, slot).astype(jnp.bfloat16)
            value_rows = lax.dynamic_slice_in_dim(value_head, col_block * block, block, 0)
            term = jnp.dot(rounded, value_rows, preferred_element_type=jnp.float32)
            return put_slot(carry, pick_slot(carry, slot) + term, slot)

        summed = add_values(summed)
    attended = summed.astype(jnp.bfloat16)
    row_dot = jnp.sum(cot_stack.astype(jnp.float32) * attended.astype(jnp.float32), axis=2)
    query_acc = jnp.zeros((2, block, HEAD), jnp.float32)
    key_acc = jnp.zeros((length, HEAD), jnp.float32)
    value_acc = jnp.zeros((length, HEAD), jnp.float32)
    for (slot, col_block, flag), scores in zip(plan, stored):

        def backward_tile(carry, slot=slot, col_block=col_block, scores=scores):
            query_sum, key_sum, value_sum = carry
            weights = tile_weights(scores, slot)
            rounded = weights.astype(jnp.bfloat16)
            query_rows = pick_slot(query_stack, slot)
            cot_rows = pick_slot(cot_stack, slot)
            start = col_block * block
            key_rows = lax.dynamic_slice_in_dim(key_head, start, block, 0)
            value_rows = lax.dynamic_slice_in_dim(value_head, start, block, 0)
            value_term = jnp.dot(rounded.T, cot_rows, preferred_element_type=jnp.float32)
            prob_grad = jnp.dot(cot_rows, value_rows.T, preferred_element_type=jnp.float32)
            score_grad = (
                weights * (prob_grad - pick_slot(row_dot, slot)[:, None]) * scaling
            ).astype(jnp.bfloat16)
            query_term = jnp.dot(score_grad, key_rows, preferred_element_type=jnp.float32)
            key_term = jnp.dot(score_grad.T, query_rows, preferred_element_type=jnp.float32)
            query_sum = put_slot(query_sum, pick_slot(query_sum, slot) + query_term, slot)
            key_sum = lax.dynamic_update_slice_in_dim(
                key_sum, lax.dynamic_slice_in_dim(key_sum, start, block, 0) + key_term, start, 0
            )
            value_sum = lax.dynamic_update_slice_in_dim(
                value_sum,
                lax.dynamic_slice_in_dim(value_sum, start, block, 0) + value_term,
                start,
                0,
            )
            return (query_sum, key_sum, value_sum)

        query_acc, key_acc, value_acc = backward_tile((query_acc, key_acc, value_acc))
    query_rounded = query_acc.astype(jnp.bfloat16)
    key_back, value_back = (
        lax.all_to_all(key_acc, "seq", split_axis=0, concat_axis=1, tiled=True),
        lax.all_to_all(value_acc, "seq", split_axis=0, concat_axis=1, tiled=True),
    )

    def settle(received):
        shaped = received.astype(jnp.float32).reshape(local_rows, head_count, group, HEAD)
        return jnp.sum(shaped, axis=2).reshape(1, local_rows, local_width).astype(jnp.bfloat16)

    query_full = jnp.zeros((length, HEAD), jnp.bfloat16)
    for which in range(2):
        query_full = lax.dynamic_update_slice_in_dim(
            query_full, query_rounded[which], row_list[which] * block, 0
        )
    query_back = lax.all_to_all(query_full, "seq", split_axis=0, concat_axis=1, tiled=True)
    query_out = settle(query_back)
    return (query_out, settle(key_back), settle(value_back))


NT = ((1,), (1,))
NN = ((1,), (0,))
TN = ((0,), (0,))
GROUP = 8


def head_span(head):
    low = head * HEAD // LANES * LANES
    high = -(-(head + 1) * HEAD // LANES) * LANES
    return low, high


def head_mask(head):
    low, high = head_span(head)
    lane = lax.broadcasted_iota(jnp.int32, (1, high - low), 1) + low
    inside = (lane >= head * HEAD) & (lane < (head + 1) * HEAD)
    return inside.astype(jnp.float32).astype(jnp.bfloat16)


def matmul(left, right, dims):
    return lax.dot_general(left, right, (dims, ((), ())), preferred_element_type=jnp.float32)


def stack(values, axis):
    return values[0] if len(values) == 1 else jnp.concatenate(values, axis=axis)


def allowed(lengths_ref, rows, query_block, key_block):
    shape = (rows, rows)
    position = query_block * rows + lax.broadcasted_iota(jnp.int32, shape, 1)
    keys = key_block * rows + lax.broadcasted_iota(jnp.int32, shape, 0)
    start = jnp.zeros_like(position)
    bound = jnp.int32(0)
    for doc in range(lengths_ref.shape[0]):
        bound = bound + lengths_ref[doc]
        start = jnp.where(position >= bound, bound, start)
    return (keys >= start) & (keys <= position)


def make_tile(lengths_ref, rows, queries, keys):
    mask = stack(
        [stack([allowed(lengths_ref, rows, q, k) for _, q in queries], 1) for _, k in keys], 0
    )
    return [slot for slot, _ in queries], [slot for slot, _ in keys], mask


def tile_values(plan, head, queries, keys, products):
    low, high = head_span(head)
    keep = head_mask(head)

    def gather(refs, number, slots):
        return stack([refs[slot][number][0, :, low:high] for slot in slots], 0)

    out = []
    for query_slots, key_slots, _ in plan:
        q = [gather(queries, number, query_slots) for number in range(products)]
        k = [gather(keys, number, key_slots) * keep for number in range(products)]
        out.append((q, k, [matmul(b, a, NT) for a, b in zip(q, k)]))
    return out, keep


def tiles_ahead(heads, plan, queries, keys, products):
    ready = tile_values(plan, 0, queries, keys, products)
    for head in range(heads):
        now = ready
        if head + 1 < heads:
            ready = tile_values(plan, head + 1, queries, keys, products)
        yield head, now


def plans(third, lengths_ref, rows, me):
    def even():
        return [make_tile(lengths_ref, rows, ((0, me), (1, me + 1)), ((0, me), (1, me - 2)))]

    def odd():
        met = ((0, me), (1, me - 1)) + (((2, me + 1),) if third else ())
        return [
            make_tile(lengths_ref, rows, ((0, me),), ((0, me),)),
            make_tile(lengths_ref, rows, met, ((1, me - 2),)),
        ]

    return even, odd


def by_parity(me, even, odd):
    pl.when(lax.rem(me, 2) == 0)(even)
    pl.when(lax.rem(me, 2) == 1)(odd)


def at_start(step, refs):
    @pl.when(step == 0)
    def _():
        for ref in refs:
            ref[...] = jnp.zeros_like(ref)


def lane_cut(value, number, rows):
    return value[:, number * rows : (number + 1) * rows]


def row_of(group, kinds, kind, head):
    return pl.ds((group * kinds + kind) * GROUP + head, 1)


def per_query(slots, kinds, kind, head, ref):
    return stack([ref[row_of(slot, kinds, kind, head), :] for slot in slots], 1)


def stats_kernel(third, heads, power, place_ref, lengths_ref, *refs):
    count = 3 if third else 2
    query_refs, (k_own, k_back, o_own, v_own) = refs[:count], refs[count : count + 4]
    o_copy, v_copy, out_ref = refs[count + 4 :]
    rows, me, step = k_own.shape[1], place_ref[0], pl.program_id(0)
    at_start(step, [out_ref])
    o_copy[...], v_copy[...] = o_own[...], v_own[...]
    queries, keys = [(ref,) for ref in query_refs], ((k_own,), (k_back,))

    def run(plan):
        for head, (tiles, _) in tiles_ahead(heads, plan, queries, keys, 1):
            parts = {}
            for (query_slots, _, mask), (_, _, (raw,)) in zip(plan, tiles):
                raw = jnp.where(mask, raw, FLOOR)
                for number, slot in enumerate(query_slots):
                    parts.setdefault(slot, []).append(lane_cut(raw, number, rows))
            for slot, pieces in parts.items():
                top = functools.reduce(
                    jnp.maximum, [jnp.max(p, axis=0, keepdims=True) for p in pieces]
                )
                sums = sum(
                    jnp.sum(jnp.exp2((p - top) * power), axis=0, keepdims=True) for p in pieces
                )
                out_ref[row_of(slot, 2, 0, step * heads + head), :] = top
                out_ref[row_of(slot, 2, 1, step * heads + head), :] = sums

    even, odd = plans(third, lengths_ref, rows, me)
    by_parity(me, lambda: run(even()), lambda: run(odd()))


def group_parts(third, odd, kinds, mine, messages):
    size = kinds * GROUP

    def group(ref, number):
        return ref[number * size : (number + 1) * size, :]

    own = [group(mine, 0), group(messages[0], 1)]
    mate = [group(mine, 1), group(messages[0], 0)]
    if not third:
        return [own, mate]
    _, zig, up, down = messages
    if odd:
        return [own, mate + [group(up, 2)], [group(mine, 2), group(zig, 0), group(down, 1)]]
    return [own + [group(zig, 2)], mate]


def merge_stats(scaling, parts):
    split = [(jnp.where(p[GROUP:] > 0, p[:GROUP], FLOOR), p[GROUP:]) for p in parts]
    top = functools.reduce(jnp.maximum, [s[0] for s in split])
    total = sum(jnp.exp((s[0] - top) * scaling) * s[1] for s in split)
    return top + jnp.log(jnp.where(total > 0, total, 1.0)) / scaling


class Emitter:
    def __init__(self, outs):
        self.outs, self.carry = outs, {}

    def emit(self, head, name, value):
        ref = self.outs[name]
        low, high = head_span(head)
        first, last = head * HEAD % LANES == 0, (head + 1) * HEAD % LANES == 0
        start, stop = low, high
        if not first:
            shared = value[:, :LANES] + self.carry.pop(name)
            ref[0, :, low : low + LANES] = shared.astype(jnp.bfloat16)
            start = low + LANES
        if not last:
            self.carry[name] = value[:, high - LANES - low :]
            stop = high - LANES
        if stop > start:
            ref[0, :, start:stop] = value[:, start - low : stop - low].astype(jnp.bfloat16)


def add_rows(sums, kind, slots, value, rows):
    for number, slot in enumerate(slots):
        piece = value[number * rows : (number + 1) * rows]
        name = (kind, slot)
        sums[name] = sums[name] + piece if name in sums else piece


def add_lanes(sums, slots, value, rows):
    for number, slot in enumerate(slots):
        piece = lane_cut(value, number, rows)
        sums[slot] = sums[slot] + piece if slot in sums else piece


def split_refs(third, refs):
    count = 3 if third else 2
    queries = [(refs[2 * n], refs[2 * n + 1]) for n in range(count)]
    keys = [(refs[2 * n], refs[2 * n + 1]) for n in range(count, count + 2)]
    return queries, keys, refs[2 * count + 4 :]


def values_kernel(third, heads, scaling, power, place_ref, lengths_ref, *refs):
    count, messages = (3, 4) if third else (2, 1)
    queries = [(refs[2 * n], refs[2 * n + 1]) for n in range(count)]
    refs = refs[2 * count :]
    keys, mine, others = [(refs[0],), (refs[1],)], refs[2], refs[3 : 3 + messages]
    value_own, value_back, shift_ref = refs[3 + messages :]
    rows, me, step = keys[0][0].shape[1], place_ref[0], pl.program_id(0)

    def run(odd, plan):
        groups = group_parts(third, odd, 2, mine, others)
        for number, parts in enumerate(groups):
            shift_ref[number * GROUP : (number + 1) * GROUP, :] = merge_stats(scaling, parts)
        out = Emitter({("v", 0): value_own, ("v", 1): value_back})
        for head, (tiles, keep) in tiles_ahead(heads, plan, queries, keys, 1):
            low, high = head_span(head)
            sums = {}
            for (query_slots, key_slots, mask), (_, _, (raw,)) in zip(plan, tiles):
                shift = per_query(query_slots, 1, 0, step * heads + head, shift_ref)
                weight = jnp.where(mask, jnp.exp2((raw - shift) * power), 0.0).astype(jnp.bfloat16)
                o = stack([queries[slot][1][0, :, low:high] for slot in query_slots], 0) * keep
                add_rows(sums, "v", key_slots, matmul(weight, o, NN), rows)
            for name, value in sums.items():
                out.emit(head, name, value)

    even, odd = plans(third, lengths_ref, rows, me)
    by_parity(me, lambda: run(False, even()), lambda: run(True, odd()))


def dots_kernel(third, heads, power, place_ref, lengths_ref, *refs):
    queries, keys, (shift_ref, dots_ref) = split_refs(third, refs)
    rows, me, step = keys[0][0].shape[1], place_ref[0], pl.program_id(0)
    at_start(step, [dots_ref])

    def run(plan):
        for head, (tiles, _) in tiles_ahead(heads, plan, queries, keys, 2):
            at = step * heads + head
            dots = {}
            for (query_slots, _, mask), (_, _, (raw, grads)) in zip(plan, tiles):
                shift = per_query(query_slots, 1, 0, at, shift_ref)
                weight = jnp.where(mask, jnp.exp2((raw - shift) * power), 0.0)
                add_lanes(dots, query_slots, jnp.sum(weight * grads, axis=0, keepdims=True), rows)
            for slot, value in dots.items():
                dots_ref[row_of(slot, 1, 0, at), :] = value

    even, odd = plans(third, lengths_ref, rows, me)
    by_parity(me, lambda: run(even()), lambda: run(odd()))


def keys_kernel(third, heads, scaling, power, place_ref, lengths_ref, *refs):
    queries, keys, refs = split_refs(third, refs)
    messages = 4 if third else 1
    shift_ref, mine, others = refs[0], refs[1], refs[2 : 2 + messages]
    key_own, key_back, *query_refs, total_ref = refs[2 + messages :]
    rows, me, step = keys[0][0].shape[1], place_ref[0], pl.program_id(0)

    def run(odd, plan):
        for number, parts in enumerate(group_parts(third, odd, 1, mine, others)):
            total_ref[number * GROUP : (number + 1) * GROUP, :] = sum(parts)
        outs = {("k", 0): key_own, ("k", 1): key_back}
        outs.update({("q", slot): ref for slot, ref in enumerate(query_refs)})
        out = Emitter(outs)
        if third and not odd:
            query_refs[2][...] = jnp.zeros_like(query_refs[2])
        for head, (tiles, keep) in tiles_ahead(heads, plan, queries, keys, 2):
            at = step * heads + head
            sums = {}
            for (query_slots, key_slots, mask), ((q, _), (k, _), (raw, grads)) in zip(plan, tiles):
                shift = per_query(query_slots, 1, 0, at, shift_ref)
                dots = per_query(query_slots, 1, 0, at, total_ref)
                weight = jnp.where(mask, jnp.exp2((raw - shift) * power), 0.0)
                slope = (weight * (grads - dots) * scaling).astype(jnp.bfloat16)
                add_rows(sums, "k", key_slots, matmul(slope, q * keep, NN), rows)
                add_rows(sums, "q", query_slots, matmul(slope, k, TN), rows)
            for name, value in sums.items():
                out.emit(head, name, value)

    even, odd = plans(third, lengths_ref, rows, me)
    by_parity(me, lambda: run(False, even()), lambda: run(True, odd()))


def halo_program(third, queries, key_vectors, value_vectors, out_grad, doc_lengths):
    _, rows, width = queries.shape
    seq_size = lax.axis_size("seq")
    me = lax.axis_index("seq").astype(jnp.int32)
    scaling = HEAD ** (-0.5)
    power = scaling * math.log2(math.e)
    steps = width // HEAD // 4
    part = width // steps
    heads = part // HEAD
    count = 3 if third else 2
    devices = range(seq_size)
    odds = [s for s in devices if s % 2]
    mates = [(s, s ^ 1) for s in devices]
    ahead = [(s, s + 2) for s in devices if s + 2 < seq_size]
    behind = [(s, s - 2) for s in devices if s >= 2]
    odd_ahead = [(s, s + 2) for s in odds if s + 2 < seq_size]
    odd_behind = [(s, s - 2) for s in odds if s >= 2]
    odd_next = [(s, s + 1) for s in odds if s + 1 < seq_size]
    zigzag = odd_next + [(t, s) for s, t in odd_next]

    def send(value, pairs):
        return lax.ppermute(value, "seq", pairs)

    def exchange(value):
        return [send(value, pairs) for pairs in ((mates, zigzag, odd_ahead, odd_behind) if third else (mates,))]

    smem = pl.BlockSpec(memory_space=pltpu.SMEM)
    wide = pl.BlockSpec((1, rows, part), lambda step: (0, 0, step))
    wide_shape = jax.ShapeDtypeStruct((1, rows, width), jnp.bfloat16)

    def slim(kinds):
        return pl.BlockSpec((count * kinds * GROUP, rows), lambda step: (0, 0))

    def slim_shape(kinds):
        return jax.ShapeDtypeStruct((count * kinds * GROUP, rows), jnp.float32)

    def call(kernel, products, wides, slims, outs, slim_outs, scratch=()):
        flops = 2 * products * 4 * rows * rows * width * 3 // 2
        return pl.pallas_call(
            kernel,
            grid=(steps,),
            in_specs=[smem, smem] + [wide] * len(wides) + [slim(kinds) for kinds, _ in slims],
            out_specs=[wide] * outs + [slim(kinds) for kinds in slim_outs],
            out_shape=[wide_shape] * outs + [slim_shape(kinds) for kinds in slim_outs],
            scratch_shapes=scratch,
            compiler_params=pltpu.CompilerParams(vmem_limit_bytes=20 * 1024 * 1024),
            cost_estimate=pl.CostEstimate(
                flops=flops, bytes_accessed=20 * rows * width, transcendentals=0
            ),
        )(me[None], doc_lengths, *wides, *[value for _, value in slims])

    query_mate = send(queries, mates)
    key_back = send(key_vectors, ahead)
    grad_mate = send(out_grad, mates)
    value_back = send(value_vectors, ahead)
    query_rows = [queries, query_mate] + ([send(query_mate, odd_behind)] if third else [])
    grad_own, value_own, stats = call(
        functools.partial(stats_kernel, third, heads, power), 1,
        [*query_rows, key_vectors, key_back, out_grad, value_vectors], [], 2, [2],
    )
    grad_rows = [grad_own, grad_mate] + ([send(grad_mate, odd_behind)] if third else [])
    tensors = [t for two in zip(query_rows, grad_rows) for t in two]
    tensors += [key_vectors, value_own, key_back, value_back]
    value_part, value_sent, shift = call(
        functools.partial(values_kernel, third, heads, scaling, power), 2,
        tensors[: 2 * count] + [key_vectors, key_back],
        [(2, value) for value in [stats] + exchange(stats)], 2, [1],
    )
    (dots,) = call(
        functools.partial(dots_kernel, third, heads, power), 2, tensors, [(1, shift)], 0, [1]
    )
    value_received = send(value_sent, behind)
    key_part, key_sent, query_part, *query_sent = call(
        functools.partial(keys_kernel, third, heads, scaling, power), 4, tensors,
        [(1, value) for value in [shift, dots] + exchange(dots)], 2 + count, [],
        [pltpu.VMEM((count * GROUP, rows), jnp.float32)],
    )
    key_received = send(key_sent, behind)
    query_received = [send(value, pairs) for value, pairs in zip(query_sent, (mates, odd_next))]

    def total(*terms):
        return sum(term.astype(jnp.float32) for term in terms).astype(jnp.bfloat16)

    return (
        total(query_part, *query_received),
        total(key_part, key_received),
        total(value_part, value_received),
    )


def needs_third(rows, doc_lengths):
    count = doc_lengths.shape[0]
    index = jnp.arange(count)
    ends = jnp.sum(jnp.where(index[None, :] <= index[:, None], doc_lengths[None, :], 0), axis=1)
    first, last = (ends - doc_lengths) // rows, (ends - 1) // rows
    return jnp.any((last - first >= 3) & (last % 2 == 0))


def halo_shards(*arguments):
    rows, doc_lengths = arguments[0].shape[1], arguments[-1]
    return lax.cond(
        needs_third(rows, doc_lengths),
        functools.partial(halo_program, True),
        functools.partial(halo_program, False),
        *arguments,
    )


def shards(queries, key_vectors, value_vectors, out_grad, doc_lengths):
    _, rows, width = queries.shape
    seq_size = lax.axis_size("seq")
    longest = rows * seq_size * 3 // 8
    fits = longest <= 3 * rows and seq_size % 2 == 0 and rows == LANES
    heads = width // HEAD
    plan = halo_shards if fits and heads % 4 == 0 and heads <= GROUP else spread_shards
    return plan(queries, key_vectors, value_vectors, out_grad, doc_lengths)


def solution(mesh):
    return jax.shard_map(
        shards,
        mesh=mesh,
        in_specs=(
            P("section", "seq", "dp"),
            P("section", "seq", "dp"),
            P("section", "seq", "dp"),
            P("section", "seq", "dp"),
            P(),
        ),
        out_specs=(P("section", "seq", "dp"), P("section", "seq", "dp"), P("section", "seq", "dp")),
        check_vma=False,
    )
```

```python
import functools
import math
import jax
import jax.numpy as jnp
from jax import lax
from jax.experimental import pallas as pl
from jax.experimental.pallas import tpu as pltpu
from jax.sharding import PartitionSpec as P

HEAD = 224
LANES = 128
FLOOR = -1e30


def pick_slot(stacked, slot):
    return lax.dynamic_index_in_dim(stacked, slot, 0, keepdims=False)


def put_slot(stacked, update, slot):
    return lax.dynamic_update_index_in_dim(stacked, update, slot, 0)


def spread_shards(queries, key_vectors, value_vectors, out_grad, doc_lengths):
    local_rows = queries.shape[1]
    local_width = queries.shape[2]
    head_count = local_width // HEAD
    seq_size = lax.axis_size("seq")
    group = seq_size // head_count
    scaling = HEAD ** (-0.5)

    def spread(matrix):
        shaped = matrix.reshape(local_rows, head_count, 1, HEAD)
        copies = jnp.broadcast_to(shaped, (local_rows, head_count, group, HEAD))
        return copies.reshape(local_rows, seq_size * HEAD)

    query_head, key_head, value_head, cot_head = (
        lax.all_to_all(spread(queries), "seq", split_axis=1, concat_axis=0, tiled=True),
        lax.all_to_all(spread(key_vectors), "seq", split_axis=1, concat_axis=0, tiled=True),
        lax.all_to_all(spread(value_vectors), "seq", split_axis=1, concat_axis=0, tiled=True),
        lax.all_to_all(spread(out_grad), "seq", split_axis=1, concat_axis=0, tiled=True),
    )
    length = key_head.shape[0]
    member = lax.axis_index("seq") % group
    blocks = 2 * group
    block = length // blocks
    bounds = jnp.cumsum(doc_lengths)
    positions = jnp.arange(length, dtype=jnp.int32)
    doc_index = jnp.sum((positions[:, None] >= bounds[None, :]).astype(jnp.int32), axis=1)
    row_list = [member, blocks - 1 - member]
    query_list = []
    cot_list = []
    pos_list = []
    for which in range(2):
        offset = row_list[which] * block
        query_list.append(lax.dynamic_slice_in_dim(query_head, offset, block, 0))
        cot_list.append(lax.dynamic_slice_in_dim(cot_head, offset, block, 0))
        pos_list.append(offset + jnp.arange(block, dtype=jnp.int32))
    query_stack = jnp.stack(query_list)
    cot_stack = jnp.stack(cot_list)
    pos_stack = jnp.stack(pos_list)
    doc_stack = jnp.take(doc_index, pos_stack)
    plan = []
    for number in range(blocks + 1):
        first = number <= member
        slot = jnp.where(first, 0, 1).astype(jnp.int32)
        col_block = jnp.where(first, number, number - member - 1)
        flag = None
        plan.append((slot, col_block, flag))
    row_max = jnp.full((2, block), -jnp.inf, jnp.float32)
    row_sum = jnp.zeros((2, block), jnp.float32)
    stored = []
    for slot, col_block, flag in plan:

        def score_tile(carry, slot=slot, col_block=col_block):
            maxima, totals = carry
            query_rows = pick_slot(query_stack, slot)
            key_rows = lax.dynamic_slice_in_dim(key_head, col_block * block, block, 0)
            col_docs = lax.dynamic_slice_in_dim(doc_index, col_block * block, block, 0)
            col_positions = col_block * block + jnp.arange(block, dtype=jnp.int32)
            raw = jnp.dot(query_rows, key_rows.T, preferred_element_type=jnp.float32) * scaling
            allowed = (pick_slot(doc_stack, slot)[:, None] == col_docs[None, :]) & (
                pick_slot(pos_stack, slot)[:, None] >= col_positions[None, :]
            )
            scores = jnp.where(allowed, raw, -jnp.inf)
            before = pick_slot(maxima, slot)
            after = jnp.maximum(before, jnp.max(scores, axis=1))
            safe = jnp.where(jnp.isfinite(after), after, 0.0)
            total = pick_slot(totals, slot) * jnp.exp(before - safe) + jnp.sum(
                jnp.exp(scores - safe[:, None]), axis=1
            )
            return (scores, put_slot(maxima, after, slot), put_slot(totals, total, slot))

        scores, row_max, row_sum = score_tile((row_max, row_sum))
        stored.append(scores)

    def tile_weights(scores, slot):
        return (
            jnp.exp(scores - pick_slot(row_max, slot)[:, None]) / pick_slot(row_sum, slot)[:, None]
        )

    summed = jnp.zeros((2, block, HEAD), jnp.float32)
    for (slot, col_block, flag), scores in zip(plan, stored):

        def add_values(carry, slot=slot, col_block=col_block, scores=scores):
            rounded = tile_weights(scores, slot).astype(jnp.bfloat16)
            value_rows = lax.dynamic_slice_in_dim(value_head, col_block * block, block, 0)
            term = jnp.dot(rounded, value_rows, preferred_element_type=jnp.float32)
            return put_slot(carry, pick_slot(carry, slot) + term, slot)

        summed = add_values(summed)
    attended = summed.astype(jnp.bfloat16)
    row_dot = jnp.sum(cot_stack.astype(jnp.float32) * attended.astype(jnp.float32), axis=2)
    query_acc = jnp.zeros((2, block, HEAD), jnp.float32)
    key_acc = jnp.zeros((length, HEAD), jnp.float32)
    value_acc = jnp.zeros((length, HEAD), jnp.float32)
    for (slot, col_block, flag), scores in zip(plan, stored):

        def backward_tile(carry, slot=slot, col_block=col_block, scores=scores):
            query_sum, key_sum, value_sum = carry
            weights = tile_weights(scores, slot)
            rounded = weights.astype(jnp.bfloat16)
            query_rows = pick_slot(query_stack, slot)
            cot_rows = pick_slot(cot_stack, slot)
            start = col_block * block
            key_rows = lax.dynamic_slice_in_dim(key_head, start, block, 0)
            value_rows = lax.dynamic_slice_in_dim(value_head, start, block, 0)
            value_term = jnp.dot(rounded.T, cot_rows, preferred_element_type=jnp.float32)
            prob_grad = jnp.dot(cot_rows, value_rows.T, preferred_element_type=jnp.float32)
            score_grad = (
                weights * (prob_grad - pick_slot(row_dot, slot)[:, None]) * scaling
            ).astype(jnp.bfloat16)
            query_term = jnp.dot(score_grad, key_rows, preferred_element_type=jnp.float32)
            key_term = jnp.dot(score_grad.T, query_rows, preferred_element_type=jnp.float32)
            query_sum = put_slot(query_sum, pick_slot(query_sum, slot) + query_term, slot)
            key_sum = lax.dynamic_update_slice_in_dim(
                key_sum, lax.dynamic_slice_in_dim(key_sum, start, block, 0) + key_term, start, 0
            )
            value_sum = lax.dynamic_update_slice_in_dim(
                value_sum,
                lax.dynamic_slice_in_dim(value_sum, start, block, 0) + value_term,
                start,
                0,
            )
            return (query_sum, key_sum, value_sum)

        query_acc, key_acc, value_acc = backward_tile((query_acc, key_acc, value_acc))
    query_rounded = query_acc.astype(jnp.bfloat16)
    key_back, value_back = (
        lax.all_to_all(key_acc, "seq", split_axis=0, concat_axis=1, tiled=True),
        lax.all_to_all(value_acc, "seq", split_axis=0, concat_axis=1, tiled=True),
    )

    def settle(received):
        shaped = received.astype(jnp.float32).reshape(local_rows, head_count, group, HEAD)
        return jnp.sum(shaped, axis=2).reshape(1, local_rows, local_width).astype(jnp.bfloat16)

    query_full = jnp.zeros((length, HEAD), jnp.bfloat16)
    for which in range(2):
        query_full = lax.dynamic_update_slice_in_dim(
            query_full, query_rounded[which], row_list[which] * block, 0
        )
    query_back = lax.all_to_all(query_full, "seq", split_axis=0, concat_axis=1, tiled=True)
    query_out = settle(query_back)
    return (query_out, settle(key_back), settle(value_back))


NT = ((1,), (1,))
NN = ((1,), (0,))
TN = ((0,), (0,))
GROUP = 8


def head_span(head):
    low = head * HEAD // LANES * LANES
    high = -(-(head + 1) * HEAD // LANES) * LANES
    return low, high


def head_mask(head):
    low, high = head_span(head)
    lane = lax.broadcasted_iota(jnp.int32, (1, high - low), 1) + low
    inside = (lane >= head * HEAD) & (lane < (head + 1) * HEAD)
    return inside.astype(jnp.float32).astype(jnp.bfloat16)


def matmul(left, right, dims):
    return lax.dot_general(left, right, (dims, ((), ())), preferred_element_type=jnp.float32)


def stack(values, axis):
    return values[0] if len(values) == 1 else jnp.concatenate(values, axis=axis)


def allowed(lengths_ref, rows, query_block, key_block):
    shape = (rows, rows)
    position = query_block * rows + lax.broadcasted_iota(jnp.int32, shape, 1)
    keys = key_block * rows + lax.broadcasted_iota(jnp.int32, shape, 0)
    start = jnp.zeros_like(position)
    bound = jnp.int32(0)
    for doc in range(lengths_ref.shape[0]):
        bound = bound + lengths_ref[doc]
        start = jnp.where(position >= bound, bound, start)
    return (keys >= start) & (keys <= position)


def make_tile(lengths_ref, rows, queries, keys):
    mask = stack(
        [stack([allowed(lengths_ref, rows, q, k) for _, q in queries], 1) for _, k in keys], 0
    )
    return [slot for slot, _ in queries], [slot for slot, _ in keys], mask


def tile_values(plan, head, queries, keys, products):
    low, high = head_span(head)
    keep = head_mask(head)

    def gather(refs, number, slots):
        return stack([refs[slot][number][0, :, low:high] for slot in slots], 0)

    out = []
    for query_slots, key_slots, _ in plan:
        q = [gather(queries, number, query_slots) for number in range(products)]
        k = [gather(keys, number, key_slots) * keep for number in range(products)]
        out.append((q, k, [matmul(b, a, NT) for a, b in zip(q, k)]))
    return out, keep


def tiles_ahead(heads, plan, queries, keys, products):
    ready = tile_values(plan, 0, queries, keys, products)
    for head in range(heads):
        now = ready
        if head + 1 < heads:
            ready = tile_values(plan, head + 1, queries, keys, products)
        yield head, now


def plans(third, lengths_ref, rows, me):
    def even():
        return [make_tile(lengths_ref, rows, ((0, me), (1, me + 1)), ((0, me), (1, me - 2)))]

    def odd():
        met = ((0, me), (1, me - 1)) + (((2, me + 1),) if third else ())
        return [
            make_tile(lengths_ref, rows, ((0, me),), ((0, me),)),
            make_tile(lengths_ref, rows, met, ((1, me - 2),)),
        ]

    return even, odd


def by_parity(me, even, odd):
    pl.when(lax.rem(me, 2) == 0)(even)
    pl.when(lax.rem(me, 2) == 1)(odd)


def at_start(step, refs):
    @pl.when(step == 0)
    def _():
        for ref in refs:
            ref[...] = jnp.zeros_like(ref)


def lane_cut(value, number, rows):
    return value[:, number * rows : (number + 1) * rows]


def row_of(group, kinds, kind, head):
    return pl.ds((group * kinds + kind) * GROUP + head, 1)


def per_query(slots, kinds, kind, head, ref):
    return stack([ref[row_of(slot, kinds, kind, head), :] for slot in slots], 1)


def stats_kernel(third, heads, power, place_ref, lengths_ref, *refs):
    count = 3 if third else 2
    query_refs, (k_own, k_back, o_own, v_own) = refs[:count], refs[count : count + 4]
    o_copy, v_copy, out_ref = refs[count + 4 :]
    rows, me, step = k_own.shape[1], place_ref[0], pl.program_id(0)
    at_start(step, [out_ref])
    o_copy[...], v_copy[...] = o_own[...], v_own[...]
    queries, keys = [(ref,) for ref in query_refs], ((k_own,), (k_back,))

    def run(plan):
        for head, (tiles, _) in tiles_ahead(heads, plan, queries, keys, 1):
            parts = {}
            for (query_slots, _, mask), (_, _, (raw,)) in zip(plan, tiles):
                raw = jnp.where(mask, raw, FLOOR)
                for number, slot in enumerate(query_slots):
                    parts.setdefault(slot, []).append(lane_cut(raw, number, rows))
            for slot, pieces in parts.items():
                top = functools.reduce(
                    jnp.maximum, [jnp.max(p, axis=0, keepdims=True) for p in pieces]
                )
                sums = sum(
                    jnp.sum(jnp.exp2((p - top) * power), axis=0, keepdims=True) for p in pieces
                )
                out_ref[row_of(slot, 2, 0, step * heads + head), :] = top
                out_ref[row_of(slot, 2, 1, step * heads + head), :] = sums

    even, odd = plans(third, lengths_ref, rows, me)
    by_parity(me, lambda: run(even()), lambda: run(odd()))


def group_parts(third, odd, kinds, mine, messages):
    size = kinds * GROUP

    def group(ref, number):
        return ref[number * size : (number + 1) * size, :]

    own = [group(mine, 0), group(messages[0], 1)]
    mate = [group(mine, 1), group(messages[0], 0)]
    if not third:
        return [own, mate]
    _, zig, up, down = messages
    if odd:
        return [own, mate + [group(up, 2)], [group(mine, 2), group(zig, 0), group(down, 1)]]
    return [own + [group(zig, 2)], mate]


def merge_stats(scaling, parts):
    split = [(jnp.where(p[GROUP:] > 0, p[:GROUP], FLOOR), p[GROUP:]) for p in parts]
    top = functools.reduce(jnp.maximum, [s[0] for s in split])
    total = sum(jnp.exp((s[0] - top) * scaling) * s[1] for s in split)
    return top + jnp.log(jnp.where(total > 0, total, 1.0)) / scaling


class Emitter:
    def __init__(self, outs):
        self.outs, self.carry = outs, {}

    def emit(self, head, name, value):
        ref = self.outs[name]
        low, high = head_span(head)
        first, last = head * HEAD % LANES == 0, (head + 1) * HEAD % LANES == 0
        start, stop = low, high
        if not first:
            shared = value[:, :LANES] + self.carry.pop(name)
            ref[0, :, low : low + LANES] = shared.astype(jnp.bfloat16)
            start = low + LANES
        if not last:
            self.carry[name] = value[:, high - LANES - low :]
            stop = high - LANES
        if stop > start:
            ref[0, :, start:stop] = value[:, start - low : stop - low].astype(jnp.bfloat16)


def add_rows(sums, kind, slots, value, rows):
    for number, slot in enumerate(slots):
        piece = value[number * rows : (number + 1) * rows]
        name = (kind, slot)
        sums[name] = sums[name] + piece if name in sums else piece


def add_lanes(sums, slots, value, rows):
    for number, slot in enumerate(slots):
        piece = lane_cut(value, number, rows)
        sums[slot] = sums[slot] + piece if slot in sums else piece


def split_refs(third, refs):
    count = 3 if third else 2
    queries = [(refs[2 * n], refs[2 * n + 1]) for n in range(count)]
    keys = [(refs[2 * n], refs[2 * n + 1]) for n in range(count, count + 2)]
    return queries, keys, refs[2 * count + 4 :]


def values_kernel(third, heads, scaling, power, place_ref, lengths_ref, *refs):
    count, messages = (3, 4) if third else (2, 1)
    queries = [(refs[2 * n], refs[2 * n + 1]) for n in range(count)]
    refs = refs[2 * count :]
    keys, mine, others = [(refs[0],), (refs[1],)], refs[2], refs[3 : 3 + messages]
    value_own, value_back, shift_ref = refs[3 + messages :]
    rows, me, step = keys[0][0].shape[1], place_ref[0], pl.program_id(0)

    def run(odd, plan):
        groups = group_parts(third, odd, 2, mine, others)
        for number, parts in enumerate(groups):
            shift_ref[number * GROUP : (number + 1) * GROUP, :] = merge_stats(scaling, parts)
        out = Emitter({("v", 0): value_own, ("v", 1): value_back})
        for head, (tiles, keep) in tiles_ahead(heads, plan, queries, keys, 1):
            low, high = head_span(head)
            sums = {}
            for (query_slots, key_slots, mask), (_, _, (raw,)) in zip(plan, tiles):
                shift = per_query(query_slots, 1, 0, step * heads + head, shift_ref)
                weight = jnp.where(mask, jnp.exp2((raw - shift) * power), 0.0).astype(jnp.bfloat16)
                o = stack([queries[slot][1][0, :, low:high] for slot in query_slots], 0) * keep
                add_rows(sums, "v", key_slots, matmul(weight, o, NN), rows)
            for name, value in sums.items():
                out.emit(head, name, value)

    even, odd = plans(third, lengths_ref, rows, me)
    by_parity(me, lambda: run(False, even()), lambda: run(True, odd()))


def dots_kernel(third, heads, power, place_ref, lengths_ref, *refs):
    queries, keys, (shift_ref, dots_ref) = split_refs(third, refs)
    rows, me, step = keys[0][0].shape[1], place_ref[0], pl.program_id(0)
    at_start(step, [dots_ref])

    def run(plan):
        for head, (tiles, _) in tiles_ahead(heads, plan, queries, keys, 2):
            at = step * heads + head
            dots = {}
            for (query_slots, _, mask), (_, _, (raw, grads)) in zip(plan, tiles):
                shift = per_query(query_slots, 1, 0, at, shift_ref)
                weight = jnp.where(mask, jnp.exp2((raw - shift) * power), 0.0)
                add_lanes(dots, query_slots, jnp.sum(weight * grads, axis=0, keepdims=True), rows)
            for slot, value in dots.items():
                dots_ref[row_of(slot, 1, 0, at), :] = value

    even, odd = plans(third, lengths_ref, rows, me)
    by_parity(me, lambda: run(even()), lambda: run(odd()))


def keys_kernel(third, heads, scaling, power, place_ref, lengths_ref, *refs):
    queries, keys, refs = split_refs(third, refs)
    messages = 4 if third else 1
    shift_ref, mine, others = refs[0], refs[1], refs[2 : 2 + messages]
    key_own, key_back, *query_refs, total_ref = refs[2 + messages :]
    rows, me, step = keys[0][0].shape[1], place_ref[0], pl.program_id(0)

    def run(odd, plan):
        for number, parts in enumerate(group_parts(third, odd, 1, mine, others)):
            total_ref[number * GROUP : (number + 1) * GROUP, :] = sum(parts)
        outs = {("k", 0): key_own, ("k", 1): key_back}
        outs.update({("q", slot): ref for slot, ref in enumerate(query_refs)})
        out = Emitter(outs)
        if third and not odd:
            query_refs[2][...] = jnp.zeros_like(query_refs[2])
        for head, (tiles, keep) in tiles_ahead(heads, plan, queries, keys, 2):
            at = step * heads + head
            sums = {}
            for (query_slots, key_slots, mask), ((q, _), (k, _), (raw, grads)) in zip(plan, tiles):
                shift = per_query(query_slots, 1, 0, at, shift_ref)
                dots = per_query(query_slots, 1, 0, at, total_ref)
                weight = jnp.where(mask, jnp.exp2((raw - shift) * power), 0.0)
                slope = (weight * (grads - dots) * scaling).astype(jnp.bfloat16)
                add_rows(sums, "k", key_slots, matmul(slope, q * keep, NN), rows)
                add_rows(sums, "q", query_slots, matmul(slope, k, TN), rows)
            for name, value in sums.items():
                out.emit(head, name, value)

    even, odd = plans(third, lengths_ref, rows, me)
    by_parity(me, lambda: run(False, even()), lambda: run(True, odd()))


def halo_program(third, queries, key_vectors, value_vectors, out_grad, doc_lengths):
    _, rows, width = queries.shape
    seq_size = lax.axis_size("seq")
    me = lax.axis_index("seq").astype(jnp.int32)
    scaling = HEAD ** (-0.5)
    power = scaling * math.log2(math.e)
    steps = width // HEAD // 4
    part = width // steps
    heads = part // HEAD
    count = 3 if third else 2
    devices = range(seq_size)
    odds = [s for s in devices if s % 2]
    mates = [(s, s ^ 1) for s in devices]
    ahead = [(s, (s + 2) % seq_size) for s in devices]
    behind = [(s, (s - 2) % seq_size) for s in devices]
    odd_ahead = [(s, s + 2) for s in odds if s + 2 < seq_size]
    odd_behind = [(s, s - 2) for s in odds if s >= 2]
    odd_next = [(s, s + 1) for s in odds if s + 1 < seq_size]
    zigzag = odd_next + [(t, s) for s, t in odd_next]

    def send(value, pairs):
        return lax.ppermute(value, "seq", pairs)

    def exchange(value):
        return [send(value, pairs) for pairs in ((mates, zigzag, odd_ahead, odd_behind) if third else (mates,))]

    smem = pl.BlockSpec(memory_space=pltpu.SMEM)
    wide = pl.BlockSpec((1, rows, part), lambda step: (0, 0, step))
    wide_shape = jax.ShapeDtypeStruct((1, rows, width), jnp.bfloat16)

    def slim(kinds):
        return pl.BlockSpec((count * kinds * GROUP, rows), lambda step: (0, 0))

    def slim_shape(kinds):
        return jax.ShapeDtypeStruct((count * kinds * GROUP, rows), jnp.float32)

    def call(kernel, products, wides, slims, outs, slim_outs, scratch=()):
        flops = 2 * products * 4 * rows * rows * width * 3 // 2
        return pl.pallas_call(
            kernel,
            grid=(steps,),
            in_specs=[smem, smem] + [wide] * len(wides) + [slim(kinds) for kinds, _ in slims],
            out_specs=[wide] * outs + [slim(kinds) for kinds in slim_outs],
            out_shape=[wide_shape] * outs + [slim_shape(kinds) for kinds in slim_outs],
            scratch_shapes=scratch,
            compiler_params=pltpu.CompilerParams(vmem_limit_bytes=20 * 1024 * 1024),
            cost_estimate=pl.CostEstimate(
                flops=flops, bytes_accessed=20 * rows * width, transcendentals=0
            ),
        )(me[None], doc_lengths, *wides, *[value for _, value in slims])

    query_mate = send(queries, mates)
    key_back = send(key_vectors, ahead)
    grad_mate = send(out_grad, mates)
    value_back = send(value_vectors, ahead)
    query_rows = [queries, query_mate] + ([send(query_mate, odd_behind)] if third else [])
    grad_own, value_own, stats = call(
        functools.partial(stats_kernel, third, heads, power), 1,
        [*query_rows, key_vectors, key_back, out_grad, value_vectors], [], 2, [2],
    )
    grad_rows = [grad_own, grad_mate] + ([send(grad_mate, odd_behind)] if third else [])
    tensors = [t for two in zip(query_rows, grad_rows) for t in two]
    tensors += [key_vectors, value_own, key_back, value_back]
    value_part, value_sent, shift = call(
        functools.partial(values_kernel, third, heads, scaling, power), 2,
        tensors[: 2 * count] + [key_vectors, key_back],
        [(2, value) for value in [stats] + exchange(stats)], 2, [1],
    )
    (dots,) = call(
        functools.partial(dots_kernel, third, heads, power), 2, tensors, [(1, shift)], 0, [1]
    )
    value_received = send(value_sent, behind)
    key_part, key_sent, query_part, *query_sent = call(
        functools.partial(keys_kernel, third, heads, scaling, power), 4, tensors,
        [(1, value) for value in [shift, dots] + exchange(dots)], 2 + count, [],
        [pltpu.VMEM((count * GROUP, rows), jnp.float32)],
    )
    key_received = send(key_sent, behind)
    query_received = [send(value, pairs) for value, pairs in zip(query_sent, (mates, odd_next))]

    def total(*terms):
        return sum(term.astype(jnp.float32) for term in terms).astype(jnp.bfloat16)

    return (
        total(query_part, *query_received),
        total(key_part, key_received),
        total(value_part, value_received),
    )


def needs_third(rows, doc_lengths):
    shift = rows.bit_length() - 1
    start = jnp.int32(0)
    found = jnp.int32(0)
    for doc in range(doc_lengths.shape[0]):
        end = start + doc_lengths[doc]
        last = (end - 1) >> shift
        found = found | (((last - (start >> shift) >= 3)).astype(jnp.int32) & (last + 1))
        start = end
    return (found & 1) == 1


def halo_shards(*arguments):
    rows, doc_lengths = arguments[0].shape[1], arguments[-1]
    return lax.cond(
        needs_third(rows, doc_lengths),
        functools.partial(halo_program, True),
        functools.partial(halo_program, False),
        *arguments,
    )


def shards(queries, key_vectors, value_vectors, out_grad, doc_lengths):
    _, rows, width = queries.shape
    seq_size = lax.axis_size("seq")
    longest = rows * seq_size * 3 // 8
    fits = longest <= 3 * rows and seq_size % 2 == 0 and rows == LANES
    heads = width // HEAD
    plan = halo_shards if fits and heads % 4 == 0 and heads <= GROUP else spread_shards
    return plan(queries, key_vectors, value_vectors, out_grad, doc_lengths)


def solution(mesh):
    return jax.shard_map(
        shards,
        mesh=mesh,
        in_specs=(
            P("section", "seq", "dp"),
            P("section", "seq", "dp"),
            P("section", "seq", "dp"),
            P("section", "seq", "dp"),
            P(),
        ),
        out_specs=(P("section", "seq", "dp"), P("section", "seq", "dp"), P("section", "seq", "dp")),
        check_vma=False,
    )
```

```python
import functools
import math
import jax
import jax.numpy as jnp
from jax import lax
from jax.experimental import pallas as pl
from jax.experimental.pallas import tpu as pltpu
from jax.sharding import PartitionSpec as P

HEAD = 224
LANES = 128
FLOOR = -1e30


def pick_slot(stacked, slot):
    return lax.dynamic_index_in_dim(stacked, slot, 0, keepdims=False)


def put_slot(stacked, update, slot):
    return lax.dynamic_update_index_in_dim(stacked, update, slot, 0)


def spread_shards(queries, key_vectors, value_vectors, out_grad, doc_lengths):
    local_rows = queries.shape[1]
    local_width = queries.shape[2]
    head_count = local_width // HEAD
    seq_size = lax.axis_size("seq")
    group = seq_size // head_count
    scaling = HEAD ** (-0.5)

    def spread(matrix):
        shaped = matrix.reshape(local_rows, head_count, 1, HEAD)
        copies = jnp.broadcast_to(shaped, (local_rows, head_count, group, HEAD))
        return copies.reshape(local_rows, seq_size * HEAD)

    query_head, key_head, value_head, cot_head = (
        lax.all_to_all(spread(queries), "seq", split_axis=1, concat_axis=0, tiled=True),
        lax.all_to_all(spread(key_vectors), "seq", split_axis=1, concat_axis=0, tiled=True),
        lax.all_to_all(spread(value_vectors), "seq", split_axis=1, concat_axis=0, tiled=True),
        lax.all_to_all(spread(out_grad), "seq", split_axis=1, concat_axis=0, tiled=True),
    )
    length = key_head.shape[0]
    member = lax.axis_index("seq") % group
    blocks = 2 * group
    block = length // blocks
    bounds = jnp.cumsum(doc_lengths)
    positions = jnp.arange(length, dtype=jnp.int32)
    doc_index = jnp.sum((positions[:, None] >= bounds[None, :]).astype(jnp.int32), axis=1)
    row_list = [member, blocks - 1 - member]
    query_list = []
    cot_list = []
    pos_list = []
    for which in range(2):
        offset = row_list[which] * block
        query_list.append(lax.dynamic_slice_in_dim(query_head, offset, block, 0))
        cot_list.append(lax.dynamic_slice_in_dim(cot_head, offset, block, 0))
        pos_list.append(offset + jnp.arange(block, dtype=jnp.int32))
    query_stack = jnp.stack(query_list)
    cot_stack = jnp.stack(cot_list)
    pos_stack = jnp.stack(pos_list)
    doc_stack = jnp.take(doc_index, pos_stack)
    plan = []
    for number in range(blocks + 1):
        first = number <= member
        slot = jnp.where(first, 0, 1).astype(jnp.int32)
        col_block = jnp.where(first, number, number - member - 1)
        flag = None
        plan.append((slot, col_block, flag))
    row_max = jnp.full((2, block), -jnp.inf, jnp.float32)
    row_sum = jnp.zeros((2, block), jnp.float32)
    stored = []
    for slot, col_block, flag in plan:

        def score_tile(carry, slot=slot, col_block=col_block):
            maxima, totals = carry
            query_rows = pick_slot(query_stack, slot)
            key_rows = lax.dynamic_slice_in_dim(key_head, col_block * block, block, 0)
            col_docs = lax.dynamic_slice_in_dim(doc_index, col_block * block, block, 0)
            col_positions = col_block * block + jnp.arange(block, dtype=jnp.int32)
            raw = jnp.dot(query_rows, key_rows.T, preferred_element_type=jnp.float32) * scaling
            allowed = (pick_slot(doc_stack, slot)[:, None] == col_docs[None, :]) & (
                pick_slot(pos_stack, slot)[:, None] >= col_positions[None, :]
            )
            scores = jnp.where(allowed, raw, -jnp.inf)
            before = pick_slot(maxima, slot)
            after = jnp.maximum(before, jnp.max(scores, axis=1))
            safe = jnp.where(jnp.isfinite(after), after, 0.0)
            total = pick_slot(totals, slot) * jnp.exp(before - safe) + jnp.sum(
                jnp.exp(scores - safe[:, None]), axis=1
            )
            return (scores, put_slot(maxima, after, slot), put_slot(totals, total, slot))

        scores, row_max, row_sum = score_tile((row_max, row_sum))
        stored.append(scores)

    def tile_weights(scores, slot):
        return (
            jnp.exp(scores - pick_slot(row_max, slot)[:, None]) / pick_slot(row_sum, slot)[:, None]
        )

    summed = jnp.zeros((2, block, HEAD), jnp.float32)
    for (slot, col_block, flag), scores in zip(plan, stored):

        def add_values(carry, slot=slot, col_block=col_block, scores=scores):
            rounded = tile_weights(scores, slot).astype(jnp.bfloat16)
            value_rows = lax.dynamic_slice_in_dim(value_head, col_block * block, block, 0)
            term = jnp.dot(rounded, value_rows, preferred_element_type=jnp.float32)
            return put_slot(carry, pick_slot(carry, slot) + term, slot)

        summed = add_values(summed)
    attended = summed.astype(jnp.bfloat16)
    row_dot = jnp.sum(cot_stack.astype(jnp.float32) * attended.astype(jnp.float32), axis=2)
    query_acc = jnp.zeros((2, block, HEAD), jnp.float32)
    key_acc = jnp.zeros((length, HEAD), jnp.float32)
    value_acc = jnp.zeros((length, HEAD), jnp.float32)
    for (slot, col_block, flag), scores in zip(plan, stored):

        def backward_tile(carry, slot=slot, col_block=col_block, scores=scores):
            query_sum, key_sum, value_sum = carry
            weights = tile_weights(scores, slot)
            rounded = weights.astype(jnp.bfloat16)
            query_rows = pick_slot(query_stack, slot)
            cot_rows = pick_slot(cot_stack, slot)
            start = col_block * block
            key_rows = lax.dynamic_slice_in_dim(key_head, start, block, 0)
            value_rows = lax.dynamic_slice_in_dim(value_head, start, block, 0)
            value_term = jnp.dot(rounded.T, cot_rows, preferred_element_type=jnp.float32)
            prob_grad = jnp.dot(cot_rows, value_rows.T, preferred_element_type=jnp.float32)
            score_grad = (
                weights * (prob_grad - pick_slot(row_dot, slot)[:, None]) * scaling
            ).astype(jnp.bfloat16)
            query_term = jnp.dot(score_grad, key_rows, preferred_element_type=jnp.float32)
            key_term = jnp.dot(score_grad.T, query_rows, preferred_element_type=jnp.float32)
            query_sum = put_slot(query_sum, pick_slot(query_sum, slot) + query_term, slot)
            key_sum = lax.dynamic_update_slice_in_dim(
                key_sum, lax.dynamic_slice_in_dim(key_sum, start, block, 0) + key_term, start, 0
            )
            value_sum = lax.dynamic_update_slice_in_dim(
                value_sum,
                lax.dynamic_slice_in_dim(value_sum, start, block, 0) + value_term,
                start,
                0,
            )
            return (query_sum, key_sum, value_sum)

        query_acc, key_acc, value_acc = backward_tile((query_acc, key_acc, value_acc))
    query_rounded = query_acc.astype(jnp.bfloat16)
    key_back, value_back = (
        lax.all_to_all(key_acc, "seq", split_axis=0, concat_axis=1, tiled=True),
        lax.all_to_all(value_acc, "seq", split_axis=0, concat_axis=1, tiled=True),
    )

    def settle(received):
        shaped = received.astype(jnp.float32).reshape(local_rows, head_count, group, HEAD)
        return jnp.sum(shaped, axis=2).reshape(1, local_rows, local_width).astype(jnp.bfloat16)

    query_full = jnp.zeros((length, HEAD), jnp.bfloat16)
    for which in range(2):
        query_full = lax.dynamic_update_slice_in_dim(
            query_full, query_rounded[which], row_list[which] * block, 0
        )
    query_back = lax.all_to_all(query_full, "seq", split_axis=0, concat_axis=1, tiled=True)
    query_out = settle(query_back)
    return (query_out, settle(key_back), settle(value_back))


NT = ((1,), (1,))
NN = ((1,), (0,))
TN = ((0,), (0,))
GROUP = 8


def head_span(head):
    low = head * HEAD // LANES * LANES
    high = -(-(head + 1) * HEAD // LANES) * LANES
    return low, high


def head_mask(head):
    low, high = head_span(head)
    lane = lax.broadcasted_iota(jnp.int32, (1, high - low), 1) + low
    inside = (lane >= head * HEAD) & (lane < (head + 1) * HEAD)
    return inside.astype(jnp.float32).astype(jnp.bfloat16)


def matmul(left, right, dims):
    return lax.dot_general(left, right, (dims, ((), ())), preferred_element_type=jnp.float32)


def stack(values, axis):
    return values[0] if len(values) == 1 else jnp.concatenate(values, axis=axis)


def allowed(lengths_ref, rows, query_block, key_block):
    shape = (rows, rows)
    position = query_block * rows + lax.broadcasted_iota(jnp.int32, shape, 1)
    keys = key_block * rows + lax.broadcasted_iota(jnp.int32, shape, 0)
    start = jnp.zeros_like(position)
    bound = jnp.int32(0)
    for doc in range(lengths_ref.shape[0]):
        bound = bound + lengths_ref[doc]
        start = jnp.where(position >= bound, bound, start)
    return (keys >= start) & (keys <= position)


def make_tile(lengths_ref, rows, queries, keys):
    mask = stack(
        [stack([allowed(lengths_ref, rows, q, k) for _, q in queries], 1) for _, k in keys], 0
    )
    return [slot for slot, _ in queries], [slot for slot, _ in keys], mask


def tile_values(plan, head, queries, keys, products):
    low, high = head_span(head)
    keep = head_mask(head)

    def gather(refs, number, slots):
        return stack([refs[slot][number][0, :, low:high] for slot in slots], 0)

    out = []
    for query_slots, key_slots, _ in plan:
        q = [gather(queries, number, query_slots) for number in range(products)]
        k = [gather(keys, number, key_slots) * keep for number in range(products)]
        out.append((q, k, [matmul(b, a, NT) for a, b in zip(q, k)]))
    return out, keep


def tiles_ahead(heads, plan, queries, keys, products):
    ready = tile_values(plan, 0, queries, keys, products)
    for head in range(heads):
        now = ready
        if head + 1 < heads:
            ready = tile_values(plan, head + 1, queries, keys, products)
        yield head, now


def plans(third, lengths_ref, rows, me):
    def even():
        return [make_tile(lengths_ref, rows, ((0, me), (1, me + 1)), ((0, me), (1, me - 2)))]

    def odd(extra=()):
        met = ((0, me), (1, me - 1)) + extra
        return [
            make_tile(lengths_ref, rows, ((0, me),), ((0, me),)),
            make_tile(lengths_ref, rows, met, ((1, me - 2),)),
        ]

    def last():
        return odd(((2, me + 1),))

    return even, odd, last


def by_place(third, me, plan_of, run):
    odd = lax.rem(me, 2) == 1
    even_plan, odd_plan, last_plan = plan_of
    pl.when(lax.rem(me, 2) == 0)(lambda: run("even", even_plan()))
    if third is None:
        pl.when(odd)(lambda: run("odd", odd_plan()))
    else:
        pl.when(odd & (me != third))(lambda: run("odd", odd_plan()))
        pl.when(me == third)(lambda: run("third", last_plan()))


def at_start(step, refs):
    @pl.when(step == 0)
    def _():
        for ref in refs:
            ref[...] = jnp.zeros_like(ref)


def lane_cut(value, number, rows):
    return value[:, number * rows : (number + 1) * rows]


def row_of(group, kinds, kind, head):
    return pl.ds((group * kinds + kind) * GROUP + head, 1)


def per_query(slots, kinds, kind, head, ref):
    return stack([ref[row_of(slot, kinds, kind, head), :] for slot in slots], 1)


def stats_kernel(third, heads, power, place_ref, lengths_ref, *refs):
    count = 2 if third is None else 3
    query_refs, (k_own, k_back, o_own, v_own) = refs[:count], refs[count : count + 4]
    o_copy, v_copy, out_ref = refs[-3:]
    rows, me, step = k_own.shape[1], place_ref[0], pl.program_id(0)
    at_start(step, [out_ref])
    o_copy[...], v_copy[...] = o_own[...], v_own[...]
    queries, keys = [(ref,) for ref in query_refs], ((k_own,), (k_back,))

    def run(_, plan):
        for head, (tiles, _) in tiles_ahead(heads, plan, queries, keys, 1):
            parts = {}
            for (query_slots, _, mask), (_, _, (raw,)) in zip(plan, tiles):
                raw = jnp.where(mask, raw, FLOOR)
                for number, slot in enumerate(query_slots):
                    parts.setdefault(slot, []).append(lane_cut(raw, number, rows))
            for slot, pieces in parts.items():
                top = functools.reduce(
                    jnp.maximum, [jnp.max(p, axis=0, keepdims=True) for p in pieces]
                )
                sums = sum(
                    jnp.sum(jnp.exp2((p - top) * power), axis=0, keepdims=True) for p in pieces
                )
                out_ref[row_of(slot, 2, 0, step * heads + head), :] = top
                out_ref[row_of(slot, 2, 1, step * heads + head), :] = sums

    by_place(third, me, plans(third, lengths_ref, rows, me), run)


def group_parts(third, place, kinds, mine, messages):
    size = kinds * GROUP

    def group(ref, number):
        return ref[number * size : (number + 1) * size, :]

    own = [group(mine, 0), group(messages[0], 1)]
    mate = [group(mine, 1), group(messages[0], 0)]
    if third is None:
        return [own, mate]
    _, near, far = messages
    if place == "even":
        return [own + [group(near, 2)], mate]
    if place == "odd":
        return [own, mate + [group(far, 2)]]
    return [own, mate, [group(mine, 2), group(near, 0), group(far, 1)]]


def merge_stats(scaling, parts):
    split = [(jnp.where(p[GROUP:] > 0, p[:GROUP], FLOOR), p[GROUP:]) for p in parts]
    top = functools.reduce(jnp.maximum, [s[0] for s in split])
    total = sum(jnp.exp((s[0] - top) * scaling) * s[1] for s in split)
    return top + jnp.log(jnp.where(total > 0, total, 1.0)) / scaling


class Emitter:
    def __init__(self, outs):
        self.outs, self.carry = outs, {}

    def emit(self, head, name, value):
        ref = self.outs[name]
        low, high = head_span(head)
        first, last = head * HEAD % LANES == 0, (head + 1) * HEAD % LANES == 0
        start, stop = low, high
        if not first:
            shared = value[:, :LANES] + self.carry.pop(name)
            ref[0, :, low : low + LANES] = shared.astype(jnp.bfloat16)
            start = low + LANES
        if not last:
            self.carry[name] = value[:, high - LANES - low :]
            stop = high - LANES
        if stop > start:
            ref[0, :, start:stop] = value[:, start - low : stop - low].astype(jnp.bfloat16)


def add_rows(sums, kind, slots, value, rows):
    for number, slot in enumerate(slots):
        piece = value[number * rows : (number + 1) * rows]
        name = (kind, slot)
        sums[name] = sums[name] + piece if name in sums else piece


def add_lanes(sums, slots, value, rows):
    for number, slot in enumerate(slots):
        piece = lane_cut(value, number, rows)
        sums[slot] = sums[slot] + piece if slot in sums else piece


def split_refs(third, refs):
    count = 2 if third is None else 3
    queries = [(refs[2 * n], refs[2 * n + 1]) for n in range(count)]
    keys = [(refs[2 * n], refs[2 * n + 1]) for n in range(count, count + 2)]
    return queries, keys, refs[2 * count + 4 :]


def values_kernel(third, heads, scaling, power, place_ref, lengths_ref, *refs):
    count, messages = (2, 1) if third is None else (3, 3)
    queries = [(refs[2 * n], refs[2 * n + 1]) for n in range(count)]
    refs = refs[2 * count :]
    keys, mine, others = [(refs[0],), (refs[1],)], refs[2], refs[3 : 3 + messages]
    value_own, value_back, shift_ref = refs[3 + messages :]
    rows, me, step = keys[0][0].shape[1], place_ref[0], pl.program_id(0)

    def run(place, plan):
        groups = group_parts(third, place, 2, mine, others)
        for number, parts in enumerate(groups):
            shift_ref[number * GROUP : (number + 1) * GROUP, :] = merge_stats(scaling, parts)
        out = Emitter({("v", 0): value_own, ("v", 1): value_back})
        for head, (tiles, keep) in tiles_ahead(heads, plan, queries, keys, 1):
            low, high = head_span(head)
            sums = {}
            for (query_slots, key_slots, mask), (_, _, (raw,)) in zip(plan, tiles):
                shift = per_query(query_slots, 1, 0, step * heads + head, shift_ref)
                weight = jnp.where(mask, jnp.exp2((raw - shift) * power), 0.0).astype(jnp.bfloat16)
                o = stack([queries[slot][1][0, :, low:high] for slot in query_slots], 0) * keep
                add_rows(sums, "v", key_slots, matmul(weight, o, NN), rows)
            for name, value in sums.items():
                out.emit(head, name, value)

    by_place(third, me, plans(third, lengths_ref, rows, me), run)


def dots_kernel(third, heads, power, place_ref, lengths_ref, *refs):
    queries, keys, (shift_ref, dots_ref) = split_refs(third, refs)
    rows, me, step = keys[0][0].shape[1], place_ref[0], pl.program_id(0)
    at_start(step, [dots_ref])

    def run(_, plan):
        for head, (tiles, _) in tiles_ahead(heads, plan, queries, keys, 2):
            at = step * heads + head
            dots = {}
            for (query_slots, _, mask), (_, _, (raw, grads)) in zip(plan, tiles):
                shift = per_query(query_slots, 1, 0, at, shift_ref)
                weight = jnp.where(mask, jnp.exp2((raw - shift) * power), 0.0)
                add_lanes(dots, query_slots, jnp.sum(weight * grads, axis=0, keepdims=True), rows)
            for slot, value in dots.items():
                dots_ref[row_of(slot, 1, 0, at), :] = value

    by_place(third, me, plans(third, lengths_ref, rows, me), run)


def keys_kernel(third, heads, scaling, power, place_ref, lengths_ref, *refs):
    queries, keys, refs = split_refs(third, refs)
    messages = 1 if third is None else 3
    shift_ref, mine, others = refs[0], refs[1], refs[2 : 2 + messages]
    key_own, key_back, *query_refs, total_ref = refs[2 + messages :]
    rows, me, step = keys[0][0].shape[1], place_ref[0], pl.program_id(0)

    def run(place, plan):
        for number, parts in enumerate(group_parts(third, place, 1, mine, others)):
            total_ref[number * GROUP : (number + 1) * GROUP, :] = sum(parts)
        outs = {("k", 0): key_own, ("k", 1): key_back}
        outs.update({("q", slot): ref for slot, ref in enumerate(query_refs)})
        out = Emitter(outs)
        for head, (tiles, keep) in tiles_ahead(heads, plan, queries, keys, 2):
            at = step * heads + head
            sums = {}
            for (query_slots, key_slots, mask), ((q, _), (k, _), (raw, grads)) in zip(plan, tiles):
                shift = per_query(query_slots, 1, 0, at, shift_ref)
                dots = per_query(query_slots, 1, 0, at, total_ref)
                weight = jnp.where(mask, jnp.exp2((raw - shift) * power), 0.0)
                slope = (weight * (grads - dots) * scaling).astype(jnp.bfloat16)
                add_rows(sums, "k", key_slots, matmul(slope, q * keep, NN), rows)
                add_rows(sums, "q", query_slots, matmul(slope, k, TN), rows)
            for name, value in sums.items():
                out.emit(head, name, value)

    by_place(third, me, plans(third, lengths_ref, rows, me), run)


def halo_program(third, queries, key_vectors, value_vectors, out_grad, doc_lengths):
    _, rows, width = queries.shape
    seq_size = lax.axis_size("seq")
    me = lax.axis_index("seq").astype(jnp.int32)
    scaling = HEAD ** (-0.5)
    power = scaling * math.log2(math.e)
    steps = width // HEAD // 4
    part = width // steps
    heads = part // HEAD
    count = 2 if third is None else 3
    devices = range(seq_size)
    mates = [(s, s ^ 1) for s in devices]
    ring = third is None
    ahead = [(s, (s + 2) % seq_size) for s in devices if ring or s + 2 < seq_size]
    behind = [(s, (s - 2) % seq_size) for s in devices if ring or s >= 2]
    if not ring:
        relay, to_even = [(third + 2, third)], [(third, third + 1)]
        near, far = (to_even + [(third + 1, third)], relay + [(third, third + 2)])

    def send(value, pairs):
        return lax.ppermute(value, "seq", pairs)

    def exchange(value):
        return [send(value, pairs) for pairs in ([mates] if ring else [mates, near, far])]

    smem = pl.BlockSpec(memory_space=pltpu.SMEM)
    wide = pl.BlockSpec((1, rows, part), lambda step: (0, 0, step))
    wide_shape = jax.ShapeDtypeStruct((1, rows, width), jnp.bfloat16)

    def slim(kinds):
        return pl.BlockSpec((count * kinds * GROUP, rows), lambda step: (0, 0))

    def slim_shape(kinds):
        return jax.ShapeDtypeStruct((count * kinds * GROUP, rows), jnp.float32)

    def call(kernel, products, wides, slims, outs, slim_outs, scratch=(), after=()):
        flops = 2 * products * 4 * rows * rows * width * 3 // 2
        return pl.pallas_call(
            kernel,
            grid=(steps,),
            in_specs=[smem, smem]
            + [wide] * len(wides)
            + [slim(kinds) for kinds, _ in slims]
            + [pl.BlockSpec(memory_space=pl.ANY)] * len(after),
            out_specs=[wide] * outs + [slim(kinds) for kinds in slim_outs],
            out_shape=[wide_shape] * outs + [slim_shape(kinds) for kinds in slim_outs],
            scratch_shapes=scratch,
            compiler_params=pltpu.CompilerParams(vmem_limit_bytes=20 * 1024 * 1024),
            cost_estimate=pl.CostEstimate(
                flops=flops, bytes_accessed=20 * rows * width, transcendentals=0
            ),
        )(me[None], doc_lengths, *wides, *[value for _, value in slims], *after)

    query_mate = send(queries, mates)
    key_back = send(key_vectors, ahead)
    grad_mate = send(out_grad, mates)
    value_back = send(value_vectors, ahead)
    query_rows = [queries, query_mate] + ([] if ring else [send(query_mate, relay)])
    grad_own, value_own, stats = call(
        functools.partial(stats_kernel, third, heads, power), 1,
        [*query_rows, key_vectors, key_back, out_grad, value_vectors], [], 2, [2],
        after=[] if ring else [value_back],
    )
    grad_rows = [grad_own, grad_mate] + ([] if ring else [send(grad_mate, relay)])
    tensors = [t for two in zip(query_rows, grad_rows) for t in two]
    tensors += [key_vectors, value_own, key_back, value_back]
    value_part, value_sent, shift = call(
        functools.partial(values_kernel, third, heads, scaling, power), 2,
        tensors[: 2 * count] + [key_vectors, key_back],
        [(2, value) for value in [stats] + exchange(stats)], 2, [1],
    )
    (dots,) = call(
        functools.partial(dots_kernel, third, heads, power), 2, tensors, [(1, shift)], 0, [1]
    )
    value_received = send(value_sent, behind)
    key_part, key_sent, query_part, *query_sent = call(
        functools.partial(keys_kernel, third, heads, scaling, power), 4, tensors,
        [(1, value) for value in [shift, dots] + exchange(dots)], 2 + count, [],
        [pltpu.VMEM((count * GROUP, rows), jnp.float32)],
    )
    key_received = send(key_sent, behind)
    query_received = [send(value, pairs) for value, pairs in zip(query_sent, (mates,) if ring else (mates, to_even))]

    def total(*terms):
        return sum(term.astype(jnp.float32) for term in terms).astype(jnp.bfloat16)

    return (
        total(query_part, *query_received),
        total(key_part, key_received),
        total(value_part, value_received),
    )


def program_index(rows, doc_lengths):
    count = doc_lengths.shape[0]
    ends = sum(lax.pad(doc_lengths[: count - n], jnp.int32(0), [(n, 0, 0)]) for n in range(count))
    shift = rows.bit_length() - 1
    first, last = (ends - doc_lengths) >> shift, (ends - 1) >> shift
    spans = (last - first >= 3) & (last & 1 == 0)
    return jnp.sum(jnp.where(spans, (last >> 1) - 1, 0))


def halo_shards(*arguments):
    rows, doc_lengths = arguments[0].shape[1], arguments[-1]
    thirds = range(3, lax.axis_size("seq") - 2, 2)
    programs = [functools.partial(halo_program, third) for third in (None, *thirds)]
    return lax.switch(program_index(rows, doc_lengths), programs, *arguments)


def shards(queries, key_vectors, value_vectors, out_grad, doc_lengths):
    _, rows, width = queries.shape
    seq_size = lax.axis_size("seq")
    longest = rows * seq_size * 3 // 8
    fits = longest <= 3 * rows and seq_size % 2 == 0 and seq_size > 4 and rows == LANES
    heads = width // HEAD
    plan = halo_shards if fits and heads % 4 == 0 and heads <= GROUP else spread_shards
    return plan(queries, key_vectors, value_vectors, out_grad, doc_lengths)


def solution(mesh):
    return jax.shard_map(
        shards,
        mesh=mesh,
        in_specs=(
            P("section", "seq", "dp"),
            P("section", "seq", "dp"),
            P("section", "seq", "dp"),
            P("section", "seq", "dp"),
            P(),
        ),
        out_specs=(P("section", "seq", "dp"), P("section", "seq", "dp"), P("section", "seq", "dp")),
        check_vma=False,
    )
```

```python
import functools
import math
import jax
import jax.numpy as jnp
from jax import lax
from jax.experimental import pallas as pl
from jax.experimental.pallas import tpu as pltpu
from jax.sharding import PartitionSpec as P

HEAD = 224
LANES = 128
FLOOR = -1e30


def pick_slot(stacked, slot):
    return lax.dynamic_index_in_dim(stacked, slot, 0, keepdims=False)


def put_slot(stacked, update, slot):
    return lax.dynamic_update_index_in_dim(stacked, update, slot, 0)


def spread_shards(queries, key_vectors, value_vectors, out_grad, doc_lengths):
    local_rows = queries.shape[1]
    local_width = queries.shape[2]
    head_count = local_width // HEAD
    seq_size = lax.axis_size("seq")
    group = seq_size // head_count
    scaling = HEAD ** (-0.5)

    def spread(matrix):
        shaped = matrix.reshape(local_rows, head_count, 1, HEAD)
        copies = jnp.broadcast_to(shaped, (local_rows, head_count, group, HEAD))
        return copies.reshape(local_rows, seq_size * HEAD)

    query_head, key_head, value_head, cot_head = (
        lax.all_to_all(spread(queries), "seq", split_axis=1, concat_axis=0, tiled=True),
        lax.all_to_all(spread(key_vectors), "seq", split_axis=1, concat_axis=0, tiled=True),
        lax.all_to_all(spread(value_vectors), "seq", split_axis=1, concat_axis=0, tiled=True),
        lax.all_to_all(spread(out_grad), "seq", split_axis=1, concat_axis=0, tiled=True),
    )
    length = key_head.shape[0]
    member = lax.axis_index("seq") % group
    blocks = 2 * group
    block = length // blocks
    bounds = jnp.cumsum(doc_lengths)
    positions = jnp.arange(length, dtype=jnp.int32)
    doc_index = jnp.sum((positions[:, None] >= bounds[None, :]).astype(jnp.int32), axis=1)
    row_list = [member, blocks - 1 - member]
    query_list = []
    cot_list = []
    pos_list = []
    for which in range(2):
        offset = row_list[which] * block
        query_list.append(lax.dynamic_slice_in_dim(query_head, offset, block, 0))
        cot_list.append(lax.dynamic_slice_in_dim(cot_head, offset, block, 0))
        pos_list.append(offset + jnp.arange(block, dtype=jnp.int32))
    query_stack = jnp.stack(query_list)
    cot_stack = jnp.stack(cot_list)
    pos_stack = jnp.stack(pos_list)
    doc_stack = jnp.take(doc_index, pos_stack)
    plan = []
    for number in range(blocks + 1):
        first = number <= member
        slot = jnp.where(first, 0, 1).astype(jnp.int32)
        col_block = jnp.where(first, number, number - member - 1)
        flag = None
        plan.append((slot, col_block, flag))
    row_max = jnp.full((2, block), -jnp.inf, jnp.float32)
    row_sum = jnp.zeros((2, block), jnp.float32)
    stored = []
    for slot, col_block, flag in plan:

        def score_tile(carry, slot=slot, col_block=col_block):
            maxima, totals = carry
            query_rows = pick_slot(query_stack, slot)
            key_rows = lax.dynamic_slice_in_dim(key_head, col_block * block, block, 0)
            col_docs = lax.dynamic_slice_in_dim(doc_index, col_block * block, block, 0)
            col_positions = col_block * block + jnp.arange(block, dtype=jnp.int32)
            raw = jnp.dot(query_rows, key_rows.T, preferred_element_type=jnp.float32) * scaling
            allowed = (pick_slot(doc_stack, slot)[:, None] == col_docs[None, :]) & (
                pick_slot(pos_stack, slot)[:, None] >= col_positions[None, :]
            )
            scores = jnp.where(allowed, raw, -jnp.inf)
            before = pick_slot(maxima, slot)
            after = jnp.maximum(before, jnp.max(scores, axis=1))
            safe = jnp.where(jnp.isfinite(after), after, 0.0)
            total = pick_slot(totals, slot) * jnp.exp(before - safe) + jnp.sum(
                jnp.exp(scores - safe[:, None]), axis=1
            )
            return (scores, put_slot(maxima, after, slot), put_slot(totals, total, slot))

        scores, row_max, row_sum = score_tile((row_max, row_sum))
        stored.append(scores)

    def tile_weights(scores, slot):
        return (
            jnp.exp(scores - pick_slot(row_max, slot)[:, None]) / pick_slot(row_sum, slot)[:, None]
        )

    summed = jnp.zeros((2, block, HEAD), jnp.float32)
    for (slot, col_block, flag), scores in zip(plan, stored):

        def add_values(carry, slot=slot, col_block=col_block, scores=scores):
            rounded = tile_weights(scores, slot).astype(jnp.bfloat16)
            value_rows = lax.dynamic_slice_in_dim(value_head, col_block * block, block, 0)
            term = jnp.dot(rounded, value_rows, preferred_element_type=jnp.float32)
            return put_slot(carry, pick_slot(carry, slot) + term, slot)

        summed = add_values(summed)
    attended = summed.astype(jnp.bfloat16)
    row_dot = jnp.sum(cot_stack.astype(jnp.float32) * attended.astype(jnp.float32), axis=2)
    query_acc = jnp.zeros((2, block, HEAD), jnp.float32)
    key_acc = jnp.zeros((length, HEAD), jnp.float32)
    value_acc = jnp.zeros((length, HEAD), jnp.float32)
    for (slot, col_block, flag), scores in zip(plan, stored):

        def backward_tile(carry, slot=slot, col_block=col_block, scores=scores):
            query_sum, key_sum, value_sum = carry
            weights = tile_weights(scores, slot)
            rounded = weights.astype(jnp.bfloat16)
            query_rows = pick_slot(query_stack, slot)
            cot_rows = pick_slot(cot_stack, slot)
            start = col_block * block
            key_rows = lax.dynamic_slice_in_dim(key_head, start, block, 0)
            value_rows = lax.dynamic_slice_in_dim(value_head, start, block, 0)
            value_term = jnp.dot(rounded.T, cot_rows, preferred_element_type=jnp.float32)
            prob_grad = jnp.dot(cot_rows, value_rows.T, preferred_element_type=jnp.float32)
            score_grad = (
                weights * (prob_grad - pick_slot(row_dot, slot)[:, None]) * scaling
            ).astype(jnp.bfloat16)
            query_term = jnp.dot(score_grad, key_rows, preferred_element_type=jnp.float32)
            key_term = jnp.dot(score_grad.T, query_rows, preferred_element_type=jnp.float32)
            query_sum = put_slot(query_sum, pick_slot(query_sum, slot) + query_term, slot)
            key_sum = lax.dynamic_update_slice_in_dim(
                key_sum, lax.dynamic_slice_in_dim(key_sum, start, block, 0) + key_term, start, 0
            )
            value_sum = lax.dynamic_update_slice_in_dim(
                value_sum,
                lax.dynamic_slice_in_dim(value_sum, start, block, 0) + value_term,
                start,
                0,
            )
            return (query_sum, key_sum, value_sum)

        query_acc, key_acc, value_acc = backward_tile((query_acc, key_acc, value_acc))
    query_rounded = query_acc.astype(jnp.bfloat16)
    key_back, value_back = (
        lax.all_to_all(key_acc, "seq", split_axis=0, concat_axis=1, tiled=True),
        lax.all_to_all(value_acc, "seq", split_axis=0, concat_axis=1, tiled=True),
    )

    def settle(received):
        shaped = received.astype(jnp.float32).reshape(local_rows, head_count, group, HEAD)
        return jnp.sum(shaped, axis=2).reshape(1, local_rows, local_width).astype(jnp.bfloat16)

    query_full = jnp.zeros((length, HEAD), jnp.bfloat16)
    for which in range(2):
        query_full = lax.dynamic_update_slice_in_dim(
            query_full, query_rounded[which], row_list[which] * block, 0
        )
    query_back = lax.all_to_all(query_full, "seq", split_axis=0, concat_axis=1, tiled=True)
    query_out = settle(query_back)
    return (query_out, settle(key_back), settle(value_back))


NT = ((1,), (1,))
NN = ((1,), (0,))
TN = ((0,), (0,))
GROUP = 8


def head_span(head):
    low = head * HEAD // LANES * LANES
    high = -(-(head + 1) * HEAD // LANES) * LANES
    return low, high


def head_mask(head):
    low, high = head_span(head)
    lane = lax.broadcasted_iota(jnp.int32, (1, high - low), 1) + low
    inside = (lane >= head * HEAD) & (lane < (head + 1) * HEAD)
    return inside.astype(jnp.float32).astype(jnp.bfloat16)


def matmul(left, right, dims):
    return lax.dot_general(left, right, (dims, ((), ())), preferred_element_type=jnp.float32)


def stack(values, axis):
    return values[0] if len(values) == 1 else jnp.concatenate(values, axis=axis)


def allowed(lengths_ref, rows, query_block, key_block):
    shape = (rows, rows)
    position = query_block * rows + lax.broadcasted_iota(jnp.int32, shape, 1)
    keys = key_block * rows + lax.broadcasted_iota(jnp.int32, shape, 0)
    start = jnp.zeros_like(position)
    bound = jnp.int32(0)
    for doc in range(lengths_ref.shape[0]):
        bound = bound + lengths_ref[doc]
        start = jnp.where(position >= bound, bound, start)
    return (keys >= start) & (keys <= position)


def make_tile(lengths_ref, rows, queries, keys):
    mask = stack(
        [stack([allowed(lengths_ref, rows, q, k) for _, q in queries], 1) for _, k in keys], 0
    )
    return [slot for slot, _ in queries], [slot for slot, _ in keys], mask


def tile_values(plan, head, queries, keys, products):
    low, high = head_span(head)
    keep = head_mask(head)

    def gather(refs, number, slots):
        return stack([refs[slot][number][0, :, low:high] for slot in slots], 0)

    out = []
    for query_slots, key_slots, _ in plan:
        q = [gather(queries, number, query_slots) for number in range(products)]
        k = [gather(keys, number, key_slots) * keep for number in range(products)]
        out.append((q, k, [matmul(b, a, NT) for a, b in zip(q, k)]))
    return out, keep


def tiles_ahead(heads, plan, queries, keys, products):
    ready = tile_values(plan, 0, queries, keys, products)
    for head in range(heads):
        now = ready
        if head + 1 < heads:
            ready = tile_values(plan, head + 1, queries, keys, products)
        yield head, now


def plans(third, lengths_ref, rows, me):
    def even():
        return [make_tile(lengths_ref, rows, ((0, me), (1, me + 1)), ((0, me), (1, me - 2)))]

    def odd(extra=()):
        met = ((0, me), (1, me - 1)) + extra
        return [
            make_tile(lengths_ref, rows, ((0, me),), ((0, me),)),
            make_tile(lengths_ref, rows, met, ((1, me - 2),)),
        ]

    def last():
        return odd(((2, me + 1),))

    return even, odd, last


def by_place(third, me, plan_of, run):
    odd = lax.rem(me, 2) == 1
    even_plan, odd_plan, last_plan = plan_of
    pl.when(lax.rem(me, 2) == 0)(lambda: run("even", even_plan()))
    if third is None:
        pl.when(odd)(lambda: run("odd", odd_plan()))
    else:
        pl.when(odd & (me != third))(lambda: run("odd", odd_plan()))
        pl.when(me == third)(lambda: run("third", last_plan()))


def at_start(step, refs):
    @pl.when(step == 0)
    def _():
        for ref in refs:
            ref[...] = jnp.zeros_like(ref)


def lane_cut(value, number, rows):
    return value[:, number * rows : (number + 1) * rows]


def row_of(group, kinds, kind, head):
    return pl.ds((group * kinds + kind) * GROUP + head, 1)


def per_query(slots, kinds, kind, head, ref):
    return stack([ref[row_of(slot, kinds, kind, head), :] for slot in slots], 1)


def stats_kernel(third, heads, power, place_ref, lengths_ref, *refs):
    count = 2 if third is None else 3
    query_refs, (k_own, k_back, o_own, v_own) = refs[:count], refs[count : count + 4]
    o_copy, v_copy, out_ref = refs[-3:]
    rows, me, step = k_own.shape[1], place_ref[0], pl.program_id(0)
    at_start(step, [out_ref])
    o_copy[...], v_copy[...] = o_own[...], v_own[...]
    queries, keys = [(ref,) for ref in query_refs], ((k_own,), (k_back,))

    def run(_, plan):
        for head, (tiles, _) in tiles_ahead(heads, plan, queries, keys, 1):
            parts = {}
            for (query_slots, _, mask), (_, _, (raw,)) in zip(plan, tiles):
                raw = jnp.where(mask, raw, FLOOR)
                for number, slot in enumerate(query_slots):
                    parts.setdefault(slot, []).append(lane_cut(raw, number, rows))
            for slot, pieces in parts.items():
                top = functools.reduce(
                    jnp.maximum, [jnp.max(p, axis=0, keepdims=True) for p in pieces]
                )
                sums = sum(
                    jnp.sum(jnp.exp2((p - top) * power), axis=0, keepdims=True) for p in pieces
                )
                out_ref[row_of(slot, 2, 0, step * heads + head), :] = top
                out_ref[row_of(slot, 2, 1, step * heads + head), :] = sums

    by_place(third, me, plans(third, lengths_ref, rows, me), run)


def group_parts(third, place, kinds, mine, messages):
    size = kinds * GROUP

    def group(ref, number):
        return ref[number * size : (number + 1) * size, :]

    own = [group(mine, 0), group(messages[0], 1)]
    mate = [group(mine, 1), group(messages[0], 0)]
    if third is None:
        return [own, mate]
    _, near, far = messages
    if place == "even":
        return [own + [group(near, 2)], mate]
    if place == "odd":
        return [own, mate + [group(far, 2)]]
    return [own, mate, [group(mine, 2), group(near, 0), group(far, 1)]]


def merge_stats(scaling, parts):
    split = [(jnp.where(p[GROUP:] > 0, p[:GROUP], FLOOR), p[GROUP:]) for p in parts]
    top = functools.reduce(jnp.maximum, [s[0] for s in split])
    total = sum(jnp.exp((s[0] - top) * scaling) * s[1] for s in split)
    return top + jnp.log(jnp.where(total > 0, total, 1.0)) / scaling


class Emitter:
    def __init__(self, outs):
        self.outs, self.carry = outs, {}

    def emit(self, head, name, value):
        ref = self.outs[name]
        low, high = head_span(head)
        first, last = head * HEAD % LANES == 0, (head + 1) * HEAD % LANES == 0
        start, stop = low, high
        if not first:
            shared = value[:, :LANES] + self.carry.pop(name)
            ref[0, :, low : low + LANES] = shared.astype(jnp.bfloat16)
            start = low + LANES
        if not last:
            self.carry[name] = value[:, high - LANES - low :]
            stop = high - LANES
        if stop > start:
            ref[0, :, start:stop] = value[:, start - low : stop - low].astype(jnp.bfloat16)


def add_rows(sums, kind, slots, value, rows):
    for number, slot in enumerate(slots):
        piece = value[number * rows : (number + 1) * rows]
        name = (kind, slot)
        sums[name] = sums[name] + piece if name in sums else piece


def add_lanes(sums, slots, value, rows):
    for number, slot in enumerate(slots):
        piece = lane_cut(value, number, rows)
        sums[slot] = sums[slot] + piece if slot in sums else piece


def split_refs(third, refs):
    count = 2 if third is None else 3
    queries = [(refs[2 * n], refs[2 * n + 1]) for n in range(count)]
    keys = [(refs[2 * n], refs[2 * n + 1]) for n in range(count, count + 2)]
    return queries, keys, refs[2 * count + 4 :]


def values_kernel(third, heads, scaling, power, place_ref, lengths_ref, *refs):
    count, messages = (2, 1) if third is None else (3, 3)
    queries = [(refs[2 * n], refs[2 * n + 1]) for n in range(count)]
    refs = refs[2 * count :]
    keys, mine, others = [(refs[0],), (refs[1],)], refs[2], refs[3 : 3 + messages]
    value_own, value_back, shift_ref = refs[3 + messages :]
    rows, me, step = keys[0][0].shape[1], place_ref[0], pl.program_id(0)

    def run(place, plan):
        groups = group_parts(third, place, 2, mine, others)
        for number, parts in enumerate(groups):
            shift_ref[number * GROUP : (number + 1) * GROUP, :] = merge_stats(scaling, parts)
        out = Emitter({("v", 0): value_own, ("v", 1): value_back})
        for head, (tiles, keep) in tiles_ahead(heads, plan, queries, keys, 1):
            low, high = head_span(head)
            sums = {}
            for (query_slots, key_slots, mask), (_, _, (raw,)) in zip(plan, tiles):
                shift = per_query(query_slots, 1, 0, step * heads + head, shift_ref)
                weight = jnp.where(mask, jnp.exp2((raw - shift) * power), 0.0).astype(jnp.bfloat16)
                o = stack([queries[slot][1][0, :, low:high] for slot in query_slots], 0) * keep
                add_rows(sums, "v", key_slots, matmul(weight, o, NN), rows)
            for name, value in sums.items():
                out.emit(head, name, value)

    by_place(third, me, plans(third, lengths_ref, rows, me), run)


def dots_kernel(third, heads, power, place_ref, lengths_ref, *refs):
    queries, keys, (shift_ref, dots_ref) = split_refs(third, refs)
    rows, me, step = keys[0][0].shape[1], place_ref[0], pl.program_id(0)
    at_start(step, [dots_ref])

    def run(_, plan):
        for head, (tiles, _) in tiles_ahead(heads, plan, queries, keys, 2):
            at = step * heads + head
            dots = {}
            for (query_slots, _, mask), (_, _, (raw, grads)) in zip(plan, tiles):
                shift = per_query(query_slots, 1, 0, at, shift_ref)
                weight = jnp.where(mask, jnp.exp2((raw - shift) * power), 0.0)
                add_lanes(dots, query_slots, jnp.sum(weight * grads, axis=0, keepdims=True), rows)
            for slot, value in dots.items():
                dots_ref[row_of(slot, 1, 0, at), :] = value

    by_place(third, me, plans(third, lengths_ref, rows, me), run)


def keys_kernel(third, heads, scaling, power, place_ref, lengths_ref, *refs):
    queries, keys, refs = split_refs(third, refs)
    messages = 1 if third is None else 3
    shift_ref, mine, others = refs[0], refs[1], refs[2 : 2 + messages]
    key_own, key_back, *query_refs, total_ref = refs[2 + messages :]
    rows, me, step = keys[0][0].shape[1], place_ref[0], pl.program_id(0)

    def run(place, plan):
        for number, parts in enumerate(group_parts(third, place, 1, mine, others)):
            total_ref[number * GROUP : (number + 1) * GROUP, :] = sum(parts)
        outs = {("k", 0): key_own, ("k", 1): key_back}
        outs.update({("q", slot): ref for slot, ref in enumerate(query_refs)})
        out = Emitter(outs)
        for head, (tiles, keep) in tiles_ahead(heads, plan, queries, keys, 2):
            at = step * heads + head
            sums = {}
            for (query_slots, key_slots, mask), ((q, _), (k, _), (raw, grads)) in zip(plan, tiles):
                shift = per_query(query_slots, 1, 0, at, shift_ref)
                dots = per_query(query_slots, 1, 0, at, total_ref)
                weight = jnp.where(mask, jnp.exp2((raw - shift) * power), 0.0)
                slope = (weight * (grads - dots) * scaling).astype(jnp.bfloat16)
                add_rows(sums, "k", key_slots, matmul(slope, q * keep, NN), rows)
                add_rows(sums, "q", query_slots, matmul(slope, k, TN), rows)
            for name, value in sums.items():
                out.emit(head, name, value)

    by_place(third, me, plans(third, lengths_ref, rows, me), run)


def sums_kernel(counts, *refs):
    outs = refs[sum(counts) :]
    for count, out in zip(counts, outs):
        terms, refs = refs[:count], refs[count:]
        out[...] = sum(ref[...].astype(jnp.float32) for ref in terms).astype(jnp.bfloat16)


def halo_program(third, queries, key_vectors, value_vectors, out_grad, doc_lengths):
    _, rows, width = queries.shape
    seq_size = lax.axis_size("seq")
    me = lax.axis_index("seq").astype(jnp.int32)
    scaling = HEAD ** (-0.5)
    power = scaling * math.log2(math.e)
    steps = width // HEAD // 4
    part = width // steps
    heads = part // HEAD
    count = 2 if third is None else 3
    devices = range(seq_size)
    mates = [(s, s ^ 1) for s in devices]
    ring = third is None
    chain = [(s, s + 2) for s in devices if s + 2 < seq_size]
    ahead = [(s, (s + 2) % seq_size) for s in devices] if ring else chain
    behind = [(s, (s - 2) % seq_size) for s in devices if ring or s >= 2]
    if not ring:
        relay, to_even = [(third + 2, third)], [(third, third + 1)]
        near, far = (to_even + [(third + 1, third)], relay + [(third, third + 2)])

    def send(value, pairs):
        return lax.ppermute(value, "seq", pairs)

    def exchange(value):
        return [send(value, pairs) for pairs in ([mates] if ring else [mates, near, far])]

    smem = pl.BlockSpec(memory_space=pltpu.SMEM)
    wide = pl.BlockSpec((1, rows, part), lambda step: (0, 0, step))
    wide_shape = jax.ShapeDtypeStruct((1, rows, width), jnp.bfloat16)

    def slim(kinds):
        return pl.BlockSpec((count * kinds * GROUP, rows), lambda step: (0, 0))

    def slim_shape(kinds):
        return jax.ShapeDtypeStruct((count * kinds * GROUP, rows), jnp.float32)

    def call(kernel, products, wides, slims, outs, slim_outs, scratch=(), after=()):
        flops = 2 * products * 4 * rows * rows * width * 3 // 2
        return pl.pallas_call(
            kernel,
            grid=(steps,),
            in_specs=[smem, smem]
            + [wide] * len(wides)
            + [slim(kinds) for kinds, _ in slims]
            + [pl.BlockSpec(memory_space=pl.ANY)] * len(after),
            out_specs=[wide] * outs + [slim(kinds) for kinds in slim_outs],
            out_shape=[wide_shape] * outs + [slim_shape(kinds) for kinds in slim_outs],
            scratch_shapes=scratch,
            compiler_params=pltpu.CompilerParams(vmem_limit_bytes=20 * 1024 * 1024),
            cost_estimate=pl.CostEstimate(
                flops=flops, bytes_accessed=20 * rows * width, transcendentals=0
            ),
        )(me[None], doc_lengths, *wides, *[value for _, value in slims], *after)

    query_mate = send(queries, mates)
    key_back = send(key_vectors, chain)
    grad_mate = send(out_grad, mates)
    value_back = send(value_vectors, ahead)
    query_rows = [queries, query_mate] + ([] if ring else [send(query_mate, relay)])
    grad_own, value_own, stats = call(
        functools.partial(stats_kernel, third, heads, power), 1,
        [*query_rows, key_vectors, key_back, out_grad, value_vectors], [], 2, [2],
        after=[] if ring else [value_back],
    )
    grad_rows = [grad_own, grad_mate] + ([] if ring else [send(grad_mate, relay)])
    tensors = [t for two in zip(query_rows, grad_rows) for t in two]
    tensors += [key_vectors, value_own, key_back, value_back]
    value_part, value_sent, shift = call(
        functools.partial(values_kernel, third, heads, scaling, power), 2,
        tensors[: 2 * count] + [key_vectors, key_back],
        [(2, value) for value in [stats] + exchange(stats)], 2, [1],
    )
    (dots,) = call(
        functools.partial(dots_kernel, third, heads, power), 2, tensors, [(1, shift)], 0, [1]
    )
    value_received = send(value_sent, behind)
    key_part, key_sent, query_part, *query_sent = call(
        functools.partial(keys_kernel, third, heads, scaling, power), 4, tensors,
        [(1, value) for value in [shift, dots] + exchange(dots)], 2 + count, [],
        [pltpu.VMEM((count * GROUP, rows), jnp.float32)],
    )
    key_received = send(key_sent, behind)
    query_received = [send(value, pairs) for value, pairs in zip(query_sent, (mates,) if ring else (mates, to_even))]

    def total(groups):
        flat = [term for terms in groups for term in terms]
        return pl.pallas_call(
            functools.partial(sums_kernel, [len(terms) for terms in groups]),
            grid=(steps,),
            in_specs=[wide] * len(flat),
            out_specs=[wide] * len(groups),
            out_shape=[wide_shape] * len(groups),
            compiler_params=pltpu.CompilerParams(vmem_limit_bytes=20 * 1024 * 1024),
            cost_estimate=pl.CostEstimate(
                flops=rows * width, bytes_accessed=8 * rows * width, transcendentals=0
            ),
        )(*flat)

    (value_ready,) = total([[value_part, value_received]])
    key_ready, query_ready = total([[key_part, key_received], [query_part, *query_received]])
    return query_ready, key_ready, value_ready


def program_index(rows, doc_lengths):
    count = doc_lengths.shape[0]
    ends = sum(lax.pad(doc_lengths[: count - n], jnp.int32(0), [(n, 0, 0)]) for n in range(count))
    shift = rows.bit_length() - 1
    first, last = (ends - doc_lengths) >> shift, (ends - 1) >> shift
    spans = (last - first >= 3) & (last & 1 == 0)
    return jnp.sum(jnp.where(spans, (last >> 1) - 1, 0))


def halo_shards(*arguments):
    rows, doc_lengths = arguments[0].shape[1], arguments[-1]
    thirds = range(3, lax.axis_size("seq") - 2, 2)
    programs = [functools.partial(halo_program, third) for third in (None, *thirds)]
    return lax.switch(program_index(rows, doc_lengths), programs, *arguments)


def shards(queries, key_vectors, value_vectors, out_grad, doc_lengths):
    _, rows, width = queries.shape
    seq_size = lax.axis_size("seq")
    longest = rows * seq_size * 3 // 8
    fits = longest <= 3 * rows and seq_size % 2 == 0 and seq_size > 4 and rows == LANES
    heads = width // HEAD
    plan = halo_shards if fits and heads % 4 == 0 and heads <= GROUP else spread_shards
    return plan(queries, key_vectors, value_vectors, out_grad, doc_lengths)


def solution(mesh):
    return jax.shard_map(
        shards,
        mesh=mesh,
        in_specs=(
            P("section", "seq", "dp"),
            P("section", "seq", "dp"),
            P("section", "seq", "dp"),
            P("section", "seq", "dp"),
            P(),
        ),
        out_specs=(P("section", "seq", "dp"), P("section", "seq", "dp"), P("section", "seq", "dp")),
        check_vma=False,
    )
```

```python
import functools
import math
import jax
import jax.numpy as jnp
from jax import lax
from jax.experimental import pallas as pl
from jax.experimental.pallas import tpu as pltpu
from jax.sharding import PartitionSpec as P

HEAD = 224
LANES = 128
FLOOR = -1e30


def pick_slot(stacked, slot):
    return lax.dynamic_index_in_dim(stacked, slot, 0, keepdims=False)


def put_slot(stacked, update, slot):
    return lax.dynamic_update_index_in_dim(stacked, update, slot, 0)


def spread_shards(queries, key_vectors, value_vectors, out_grad, doc_lengths):
    local_rows = queries.shape[1]
    local_width = queries.shape[2]
    head_count = local_width // HEAD
    seq_size = lax.axis_size("seq")
    group = seq_size // head_count
    scaling = HEAD ** (-0.5)

    def spread(matrix):
        shaped = matrix.reshape(local_rows, head_count, 1, HEAD)
        copies = jnp.broadcast_to(shaped, (local_rows, head_count, group, HEAD))
        return copies.reshape(local_rows, seq_size * HEAD)

    query_head, key_head, value_head, cot_head = (
        lax.all_to_all(spread(queries), "seq", split_axis=1, concat_axis=0, tiled=True),
        lax.all_to_all(spread(key_vectors), "seq", split_axis=1, concat_axis=0, tiled=True),
        lax.all_to_all(spread(value_vectors), "seq", split_axis=1, concat_axis=0, tiled=True),
        lax.all_to_all(spread(out_grad), "seq", split_axis=1, concat_axis=0, tiled=True),
    )
    length = key_head.shape[0]
    member = lax.axis_index("seq") % group
    blocks = 2 * group
    block = length // blocks
    bounds = jnp.cumsum(doc_lengths)
    positions = jnp.arange(length, dtype=jnp.int32)
    doc_index = jnp.sum((positions[:, None] >= bounds[None, :]).astype(jnp.int32), axis=1)
    row_list = [member, blocks - 1 - member]
    query_list = []
    cot_list = []
    pos_list = []
    for which in range(2):
        offset = row_list[which] * block
        query_list.append(lax.dynamic_slice_in_dim(query_head, offset, block, 0))
        cot_list.append(lax.dynamic_slice_in_dim(cot_head, offset, block, 0))
        pos_list.append(offset + jnp.arange(block, dtype=jnp.int32))
    query_stack = jnp.stack(query_list)
    cot_stack = jnp.stack(cot_list)
    pos_stack = jnp.stack(pos_list)
    doc_stack = jnp.take(doc_index, pos_stack)
    plan = []
    for number in range(blocks + 1):
        first = number <= member
        slot = jnp.where(first, 0, 1).astype(jnp.int32)
        col_block = jnp.where(first, number, number - member - 1)
        flag = None
        plan.append((slot, col_block, flag))
    row_max = jnp.full((2, block), -jnp.inf, jnp.float32)
    row_sum = jnp.zeros((2, block), jnp.float32)
    stored = []
    for slot, col_block, flag in plan:

        def score_tile(carry, slot=slot, col_block=col_block):
            maxima, totals = carry
            query_rows = pick_slot(query_stack, slot)
            key_rows = lax.dynamic_slice_in_dim(key_head, col_block * block, block, 0)
            col_docs = lax.dynamic_slice_in_dim(doc_index, col_block * block, block, 0)
            col_positions = col_block * block + jnp.arange(block, dtype=jnp.int32)
            raw = jnp.dot(query_rows, key_rows.T, preferred_element_type=jnp.float32) * scaling
            allowed = (pick_slot(doc_stack, slot)[:, None] == col_docs[None, :]) & (
                pick_slot(pos_stack, slot)[:, None] >= col_positions[None, :]
            )
            scores = jnp.where(allowed, raw, -jnp.inf)
            before = pick_slot(maxima, slot)
            after = jnp.maximum(before, jnp.max(scores, axis=1))
            safe = jnp.where(jnp.isfinite(after), after, 0.0)
            total = pick_slot(totals, slot) * jnp.exp(before - safe) + jnp.sum(
                jnp.exp(scores - safe[:, None]), axis=1
            )
            return (scores, put_slot(maxima, after, slot), put_slot(totals, total, slot))

        scores, row_max, row_sum = score_tile((row_max, row_sum))
        stored.append(scores)

    def tile_weights(scores, slot):
        return (
            jnp.exp(scores - pick_slot(row_max, slot)[:, None]) / pick_slot(row_sum, slot)[:, None]
        )

    summed = jnp.zeros((2, block, HEAD), jnp.float32)
    for (slot, col_block, flag), scores in zip(plan, stored):

        def add_values(carry, slot=slot, col_block=col_block, scores=scores):
            rounded = tile_weights(scores, slot).astype(jnp.bfloat16)
            value_rows = lax.dynamic_slice_in_dim(value_head, col_block * block, block, 0)
            term = jnp.dot(rounded, value_rows, preferred_element_type=jnp.float32)
            return put_slot(carry, pick_slot(carry, slot) + term, slot)

        summed = add_values(summed)
    attended = summed.astype(jnp.bfloat16)
    row_dot = jnp.sum(cot_stack.astype(jnp.float32) * attended.astype(jnp.float32), axis=2)
    query_acc = jnp.zeros((2, block, HEAD), jnp.float32)
    key_acc = jnp.zeros((length, HEAD), jnp.float32)
    value_acc = jnp.zeros((length, HEAD), jnp.float32)
    for (slot, col_block, flag), scores in zip(plan, stored):

        def backward_tile(carry, slot=slot, col_block=col_block, scores=scores):
            query_sum, key_sum, value_sum = carry
            weights = tile_weights(scores, slot)
            rounded = weights.astype(jnp.bfloat16)
            query_rows = pick_slot(query_stack, slot)
            cot_rows = pick_slot(cot_stack, slot)
            start = col_block * block
            key_rows = lax.dynamic_slice_in_dim(key_head, start, block, 0)
            value_rows = lax.dynamic_slice_in_dim(value_head, start, block, 0)
            value_term = jnp.dot(rounded.T, cot_rows, preferred_element_type=jnp.float32)
            prob_grad = jnp.dot(cot_rows, value_rows.T, preferred_element_type=jnp.float32)
            score_grad = (
                weights * (prob_grad - pick_slot(row_dot, slot)[:, None]) * scaling
            ).astype(jnp.bfloat16)
            query_term = jnp.dot(score_grad, key_rows, preferred_element_type=jnp.float32)
            key_term = jnp.dot(score_grad.T, query_rows, preferred_element_type=jnp.float32)
            query_sum = put_slot(query_sum, pick_slot(query_sum, slot) + query_term, slot)
            key_sum = lax.dynamic_update_slice_in_dim(
                key_sum, lax.dynamic_slice_in_dim(key_sum, start, block, 0) + key_term, start, 0
            )
            value_sum = lax.dynamic_update_slice_in_dim(
                value_sum,
                lax.dynamic_slice_in_dim(value_sum, start, block, 0) + value_term,
                start,
                0,
            )
            return (query_sum, key_sum, value_sum)

        query_acc, key_acc, value_acc = backward_tile((query_acc, key_acc, value_acc))
    query_rounded = query_acc.astype(jnp.bfloat16)
    key_back, value_back = (
        lax.all_to_all(key_acc, "seq", split_axis=0, concat_axis=1, tiled=True),
        lax.all_to_all(value_acc, "seq", split_axis=0, concat_axis=1, tiled=True),
    )

    def settle(received):
        shaped = received.astype(jnp.float32).reshape(local_rows, head_count, group, HEAD)
        return jnp.sum(shaped, axis=2).reshape(1, local_rows, local_width).astype(jnp.bfloat16)

    query_full = jnp.zeros((length, HEAD), jnp.bfloat16)
    for which in range(2):
        query_full = lax.dynamic_update_slice_in_dim(
            query_full, query_rounded[which], row_list[which] * block, 0
        )
    query_back = lax.all_to_all(query_full, "seq", split_axis=0, concat_axis=1, tiled=True)
    query_out = settle(query_back)
    return (query_out, settle(key_back), settle(value_back))


NT = ((1,), (1,))
NN = ((1,), (0,))
TN = ((0,), (0,))
GROUP = 8


def head_span(head):
    low = head * HEAD // LANES * LANES
    high = -(-(head + 1) * HEAD // LANES) * LANES
    return low, high


def head_mask(head):
    low, high = head_span(head)
    lane = lax.broadcasted_iota(jnp.int32, (1, high - low), 1) + low
    inside = (lane >= head * HEAD) & (lane < (head + 1) * HEAD)
    return inside.astype(jnp.float32).astype(jnp.bfloat16)


def matmul(left, right, dims):
    return lax.dot_general(left, right, (dims, ((), ())), preferred_element_type=jnp.float32)


def stack(values, axis):
    return values[0] if len(values) == 1 else jnp.concatenate(values, axis=axis)


def allowed(lengths_ref, rows, query_block, key_block):
    shape = (rows, rows)
    position = query_block * rows + lax.broadcasted_iota(jnp.int32, shape, 1)
    keys = key_block * rows + lax.broadcasted_iota(jnp.int32, shape, 0)
    start = jnp.zeros_like(position)
    bound = jnp.int32(0)
    for doc in range(lengths_ref.shape[0]):
        bound = bound + lengths_ref[doc]
        start = jnp.where(position >= bound, bound, start)
    return (keys >= start) & (keys <= position)


def make_tile(lengths_ref, rows, queries, keys):
    mask = stack(
        [stack([allowed(lengths_ref, rows, q, k) for _, q in queries], 1) for _, k in keys], 0
    )
    return [slot for slot, _ in queries], [slot for slot, _ in keys], mask


def tile_values(plan, head, queries, keys, products):
    low, high = head_span(head)
    keep = head_mask(head)

    def gather(refs, number, slots):
        return stack([refs[slot][number][0, :, low:high] for slot in slots], 0)

    out = []
    for query_slots, key_slots, _ in plan:
        q = [gather(queries, number, query_slots) for number in range(products)]
        k = [gather(keys, number, key_slots) * keep for number in range(products)]
        out.append((q, k, [matmul(b, a, NT) for a, b in zip(q, k)]))
    return out, keep


def tiles_ahead(heads, plan, queries, keys, products):
    ready = tile_values(plan, 0, queries, keys, products)
    for head in range(heads):
        now = ready
        if head + 1 < heads:
            ready = tile_values(plan, head + 1, queries, keys, products)
        yield head, now


def plans(third, lengths_ref, rows, me):
    def even():
        return [make_tile(lengths_ref, rows, ((0, me), (1, me + 1)), ((0, me), (1, me - 2)))]

    def odd(extra=()):
        met = ((0, me), (1, me - 1)) + extra
        return [
            make_tile(lengths_ref, rows, ((0, me),), ((0, me),)),
            make_tile(lengths_ref, rows, met, ((1, me - 2),)),
        ]

    def last():
        return odd(((2, me + 1),))

    return even, odd, last


def by_place(third, me, plan_of, run):
    odd = lax.rem(me, 2) == 1
    even_plan, odd_plan, last_plan = plan_of
    pl.when(lax.rem(me, 2) == 0)(lambda: run("even", even_plan()))
    if third is None:
        pl.when(odd)(lambda: run("odd", odd_plan()))
    else:
        pl.when(odd & (me != third))(lambda: run("odd", odd_plan()))
        pl.when(me == third)(lambda: run("third", last_plan()))


def at_start(step, refs):
    @pl.when(step == 0)
    def _():
        for ref in refs:
            ref[...] = jnp.zeros_like(ref)


def lane_cut(value, number, rows):
    return value[:, number * rows : (number + 1) * rows]


def row_of(group, kinds, kind, head):
    return pl.ds((group * kinds + kind) * GROUP + head, 1)


def per_query(slots, kinds, kind, head, ref):
    return stack([ref[row_of(slot, kinds, kind, head), :] for slot in slots], 1)


def stats_kernel(third, heads, power, place_ref, lengths_ref, *refs):
    count = 2 if third is None else 3
    query_refs, (k_own, k_back, o_own, v_own) = refs[:count], refs[count : count + 4]
    o_copy, v_copy, out_ref = refs[-3:]
    rows, me, step = k_own.shape[1], place_ref[0], pl.program_id(0)
    at_start(step, [out_ref])
    o_copy[...], v_copy[...] = o_own[...], v_own[...]
    queries, keys = [(ref,) for ref in query_refs], ((k_own,), (k_back,))

    def run(_, plan):
        for head, (tiles, _) in tiles_ahead(heads, plan, queries, keys, 1):
            parts = {}
            for (query_slots, _, mask), (_, _, (raw,)) in zip(plan, tiles):
                raw = jnp.where(mask, raw, FLOOR)
                for number, slot in enumerate(query_slots):
                    parts.setdefault(slot, []).append(lane_cut(raw, number, rows))
            for slot, pieces in parts.items():
                top = functools.reduce(
                    jnp.maximum, [jnp.max(p, axis=0, keepdims=True) for p in pieces]
                )
                sums = sum(
                    jnp.sum(jnp.exp2((p - top) * power), axis=0, keepdims=True) for p in pieces
                )
                out_ref[row_of(slot, 2, 0, step * heads + head), :] = top
                out_ref[row_of(slot, 2, 1, step * heads + head), :] = sums

    by_place(third, me, plans(third, lengths_ref, rows, me), run)


def group_parts(third, place, kinds, me, mine, message):
    size = kinds * GROUP

    def group(ref, number):
        return ref[number * size : (number + 1) * size, :]

    def sent(device, number):
        return message[device, number * size : (number + 1) * size, :]

    if third is None:
        return [[group(mine, 0), group(message, 1)], [group(mine, 1), group(message, 0)]]
    partner = me + 1 - 2 * lax.rem(me, 2)
    own = [group(mine, 0), sent(partner, 1)]
    mate = [group(mine, 1), sent(partner, 0)]
    if place == "third":
        return [own, mate, [group(mine, 2), sent(third + 1, 0), sent(third + 2, 1)]]
    extra = sent(third, 2)
    if place == "even":
        return [own + [jnp.where(me == third + 1, extra, 0.0)], mate]
    return [own, mate + [jnp.where(me == third + 2, extra, 0.0)]]


def merge_stats(scaling, parts):
    split = [(jnp.where(p[GROUP:] > 0, p[:GROUP], FLOOR), p[GROUP:]) for p in parts]
    top = functools.reduce(jnp.maximum, [s[0] for s in split])
    total = sum(jnp.exp((s[0] - top) * scaling) * s[1] for s in split)
    return top + jnp.log(jnp.where(total > 0, total, 1.0)) / scaling


class Emitter:
    def __init__(self, outs):
        self.outs, self.carry = outs, {}

    def emit(self, head, name, value):
        ref = self.outs[name]
        low, high = head_span(head)
        first, last = head * HEAD % LANES == 0, (head + 1) * HEAD % LANES == 0
        start, stop = low, high
        if not first:
            shared = value[:, :LANES] + self.carry.pop(name)
            ref[0, :, low : low + LANES] = shared.astype(jnp.bfloat16)
            start = low + LANES
        if not last:
            self.carry[name] = value[:, high - LANES - low :]
            stop = high - LANES
        if stop > start:
            ref[0, :, start:stop] = value[:, start - low : stop - low].astype(jnp.bfloat16)


def add_rows(sums, kind, slots, value, rows):
    for number, slot in enumerate(slots):
        piece = value[number * rows : (number + 1) * rows]
        name = (kind, slot)
        sums[name] = sums[name] + piece if name in sums else piece


def add_lanes(sums, slots, value, rows):
    for number, slot in enumerate(slots):
        piece = lane_cut(value, number, rows)
        sums[slot] = sums[slot] + piece if slot in sums else piece


def split_refs(third, refs):
    count = 2 if third is None else 3
    queries = [(refs[2 * n], refs[2 * n + 1]) for n in range(count)]
    keys = [(refs[2 * n], refs[2 * n + 1]) for n in range(count, count + 2)]
    return queries, keys, refs[2 * count + 4 :]


def values_kernel(third, heads, scaling, power, place_ref, lengths_ref, *refs):
    count = 2 if third is None else 3
    queries = [(refs[2 * n], refs[2 * n + 1]) for n in range(count)]
    refs = refs[2 * count :]
    keys, mine, others = [(refs[0],), (refs[1],)], refs[2], refs[3]
    value_own, value_back, shift_ref = refs[4:]
    rows, me, step = keys[0][0].shape[1], place_ref[0], pl.program_id(0)

    def run(place, plan):
        groups = group_parts(third, place, 2, me, mine, others)
        for number, parts in enumerate(groups):
            shift_ref[number * GROUP : (number + 1) * GROUP, :] = merge_stats(scaling, parts)
        out = Emitter({("v", 0): value_own, ("v", 1): value_back})
        for head, (tiles, keep) in tiles_ahead(heads, plan, queries, keys, 1):
            low, high = head_span(head)
            sums = {}
            for (query_slots, key_slots, mask), (_, _, (raw,)) in zip(plan, tiles):
                shift = per_query(query_slots, 1, 0, step * heads + head, shift_ref)
                weight = jnp.where(mask, jnp.exp2((raw - shift) * power), 0.0).astype(jnp.bfloat16)
                o = stack([queries[slot][1][0, :, low:high] for slot in query_slots], 0) * keep
                add_rows(sums, "v", key_slots, matmul(weight, o, NN), rows)
            for name, value in sums.items():
                out.emit(head, name, value)

    by_place(third, me, plans(third, lengths_ref, rows, me), run)


def dots_kernel(third, heads, power, place_ref, lengths_ref, *refs):
    queries, keys, (shift_ref, dots_ref) = split_refs(third, refs)
    rows, me, step = keys[0][0].shape[1], place_ref[0], pl.program_id(0)
    at_start(step, [dots_ref])

    def run(_, plan):
        for head, (tiles, _) in tiles_ahead(heads, plan, queries, keys, 2):
            at = step * heads + head
            dots = {}
            for (query_slots, _, mask), (_, _, (raw, grads)) in zip(plan, tiles):
                shift = per_query(query_slots, 1, 0, at, shift_ref)
                weight = jnp.where(mask, jnp.exp2((raw - shift) * power), 0.0)
                add_lanes(dots, query_slots, jnp.sum(weight * grads, axis=0, keepdims=True), rows)
            for slot, value in dots.items():
                dots_ref[row_of(slot, 1, 0, at), :] = value

    by_place(third, me, plans(third, lengths_ref, rows, me), run)


def keys_kernel(third, heads, scaling, power, place_ref, lengths_ref, *refs):
    queries, keys, refs = split_refs(third, refs)
    shift_ref, mine, others = refs[:3]
    key_own, key_back, *query_refs, total_ref = refs[3:]
    rows, me, step = keys[0][0].shape[1], place_ref[0], pl.program_id(0)

    def run(place, plan):
        for number, parts in enumerate(group_parts(third, place, 1, me, mine, others)):
            total_ref[number * GROUP : (number + 1) * GROUP, :] = sum(parts)
        outs = {("k", 0): key_own, ("k", 1): key_back}
        outs.update({("q", slot): ref for slot, ref in enumerate(query_refs)})
        out = Emitter(outs)
        for head, (tiles, keep) in tiles_ahead(heads, plan, queries, keys, 2):
            at = step * heads + head
            sums = {}
            for (query_slots, key_slots, mask), ((q, _), (k, _), (raw, grads)) in zip(plan, tiles):
                shift = per_query(query_slots, 1, 0, at, shift_ref)
                dots = per_query(query_slots, 1, 0, at, total_ref)
                weight = jnp.where(mask, jnp.exp2((raw - shift) * power), 0.0)
                slope = (weight * (grads - dots) * scaling).astype(jnp.bfloat16)
                add_rows(sums, "k", key_slots, matmul(slope, q * keep, NN), rows)
                add_rows(sums, "q", query_slots, matmul(slope, k, TN), rows)
            for name, value in sums.items():
                out.emit(head, name, value)

    by_place(third, me, plans(third, lengths_ref, rows, me), run)


def sums_kernel(counts, *refs):
    outs = refs[sum(counts) :]
    for count, out in zip(counts, outs):
        terms, refs = refs[:count], refs[count:]
        out[...] = sum(ref[...].astype(jnp.float32) for ref in terms).astype(jnp.bfloat16)


def halo_program(third, queries, key_vectors, value_vectors, out_grad, doc_lengths):
    _, rows, width = queries.shape
    seq_size = lax.axis_size("seq")
    me = lax.axis_index("seq").astype(jnp.int32)
    scaling = HEAD ** (-0.5)
    power = scaling * math.log2(math.e)
    steps = width // HEAD // 4
    part = width // steps
    heads = part // HEAD
    count = 2 if third is None else 3
    devices = range(seq_size)
    mates = [(s, s ^ 1) for s in devices]
    ring = third is None
    chain = [(s, s + 2) for s in devices if s + 2 < seq_size]
    ahead = [(s, (s + 2) % seq_size) for s in devices] if ring else chain
    behind = [(s, s - 2) for s in devices if s >= 2]
    if not ring:
        relay, to_even = [(third + 2, third)], [(third, third + 1)]

    def send(value, pairs):
        return lax.ppermute(value, "seq", pairs)

    def exchange(value):
        if ring:
            return send(value, mates)
        copies = jnp.broadcast_to(value[None], (seq_size, *value.shape))
        return lax.all_to_all(copies, "seq", split_axis=0, concat_axis=0, tiled=True)

    smem = pl.BlockSpec(memory_space=pltpu.SMEM)
    wide = pl.BlockSpec((1, rows, part), lambda step: (0, 0, step))
    wide_shape = jax.ShapeDtypeStruct((1, rows, width), jnp.bfloat16)

    def slim(kinds, value=None):
        if value is not None and value.ndim == 3:
            return pl.BlockSpec((seq_size, count * kinds * GROUP, rows), lambda step: (0, 0, 0))
        return pl.BlockSpec((count * kinds * GROUP, rows), lambda step: (0, 0))

    def slim_shape(kinds):
        return jax.ShapeDtypeStruct((count * kinds * GROUP, rows), jnp.float32)

    def call(kernel, products, wides, slims, outs, slim_outs, scratch=(), after=()):
        flops = 2 * products * 4 * rows * rows * width * 3 // 2
        return pl.pallas_call(
            kernel,
            grid=(steps,),
            in_specs=[smem, smem]
            + [wide] * len(wides)
            + [slim(kinds, value) for kinds, value in slims]
            + [pl.BlockSpec(memory_space=pl.ANY)] * len(after),
            out_specs=[wide] * outs + [slim(kinds) for kinds in slim_outs],
            out_shape=[wide_shape] * outs + [slim_shape(kinds) for kinds in slim_outs],
            scratch_shapes=scratch,
            compiler_params=pltpu.CompilerParams(vmem_limit_bytes=20 * 1024 * 1024),
            cost_estimate=pl.CostEstimate(
                flops=flops, bytes_accessed=20 * rows * width, transcendentals=0
            ),
        )(me[None], doc_lengths, *wides, *[value for _, value in slims], *after)

    query_mate = send(queries, mates)
    key_back = send(key_vectors, chain)
    grad_mate = send(out_grad, mates)
    value_back = send(value_vectors, ahead)
    query_rows = [queries, query_mate] + ([] if ring else [send(query_mate, relay)])
    grad_own, value_own, stats = call(
        functools.partial(stats_kernel, third, heads, power), 1,
        [*query_rows, key_vectors, key_back, out_grad, value_vectors], [], 2, [2],
        after=[] if ring else [value_back],
    )
    grad_rows = [grad_own, grad_mate] + ([] if ring else [send(grad_mate, relay)])
    tensors = [t for two in zip(query_rows, grad_rows) for t in two]
    tensors += [key_vectors, value_own, key_back, value_back]
    value_part, value_sent, shift = call(
        functools.partial(values_kernel, third, heads, scaling, power), 2,
        tensors[: 2 * count] + [key_vectors, key_back],
        [(2, stats), (2, exchange(stats))], 2, [1],
    )
    (dots,) = call(
        functools.partial(dots_kernel, third, heads, power), 2, tensors, [(1, shift)], 0, [1]
    )
    value_received = send(value_sent, behind)
    key_part, key_sent, query_part, *query_sent = call(
        functools.partial(keys_kernel, third, heads, scaling, power), 4, tensors,
        [(1, shift), (1, dots), (1, exchange(dots))], 2 + count, [],
        [pltpu.VMEM((count * GROUP, rows), jnp.float32)],
    )
    key_received = send(key_sent, behind)
    query_received = [send(value, pairs) for value, pairs in zip(query_sent, (mates,) if ring else (mates, to_even))]

    def total(groups):
        flat = [term for terms in groups for term in terms]
        return pl.pallas_call(
            functools.partial(sums_kernel, [len(terms) for terms in groups]),
            grid=(steps,),
            in_specs=[wide] * len(flat),
            out_specs=[wide] * len(groups),
            out_shape=[wide_shape] * len(groups),
            compiler_params=pltpu.CompilerParams(vmem_limit_bytes=20 * 1024 * 1024),
            cost_estimate=pl.CostEstimate(
                flops=rows * width, bytes_accessed=8 * rows * width, transcendentals=0
            ),
        )(*flat)

    value_ready = (value_part.astype(jnp.float32) + value_received.astype(jnp.float32)).astype(jnp.bfloat16)
    key_ready, query_ready = total([[key_part, key_received], [query_part, *query_received]])
    return query_ready, key_ready, value_ready


def program_index(rows, doc_lengths):
    count = doc_lengths.shape[0]
    ends = sum(lax.pad(doc_lengths[: count - n], jnp.int32(0), [(n, 0, 0)]) for n in range(count))
    shift = rows.bit_length() - 1
    first, last = (ends - doc_lengths) >> shift, (ends - 1) >> shift
    spans = (last - first >= 3) & (last & 1 == 0)
    return jnp.sum(jnp.where(spans, (last >> 1) - 1, 0))


def halo_shards(*arguments):
    rows, doc_lengths = arguments[0].shape[1], arguments[-1]
    thirds = range(3, lax.axis_size("seq") - 2, 2)
    programs = [functools.partial(halo_program, third) for third in (None, *thirds)]
    return lax.switch(program_index(rows, doc_lengths), programs, *arguments)


def shards(queries, key_vectors, value_vectors, out_grad, doc_lengths):
    _, rows, width = queries.shape
    seq_size = lax.axis_size("seq")
    longest = rows * seq_size * 3 // 8
    fits = longest <= 3 * rows and seq_size % 2 == 0 and seq_size > 4 and rows == LANES
    heads = width // HEAD
    plan = halo_shards if fits and heads % 4 == 0 and heads <= GROUP else spread_shards
    return plan(queries, key_vectors, value_vectors, out_grad, doc_lengths)


def solution(mesh):
    return jax.shard_map(
        shards,
        mesh=mesh,
        in_specs=(
            P("section", "seq", "dp"),
            P("section", "seq", "dp"),
            P("section", "seq", "dp"),
            P("section", "seq", "dp"),
            P(),
        ),
        out_specs=(P("section", "seq", "dp"), P("section", "seq", "dp"), P("section", "seq", "dp")),
        check_vma=False,
    )
```

```python
import functools
import math
import jax
import jax.numpy as jnp
from jax import lax
from jax.experimental import pallas as pl
from jax.experimental.pallas import tpu as pltpu
from jax.sharding import PartitionSpec as P

HEAD = 224
LANES = 128
FLOOR = -1e30


def pick_slot(stacked, slot):
    return lax.dynamic_index_in_dim(stacked, slot, 0, keepdims=False)


def put_slot(stacked, update, slot):
    return lax.dynamic_update_index_in_dim(stacked, update, slot, 0)


def spread_shards(queries, key_vectors, value_vectors, out_grad, doc_lengths):
    local_rows = queries.shape[1]
    local_width = queries.shape[2]
    head_count = local_width // HEAD
    seq_size = lax.axis_size("seq")
    group = seq_size // head_count
    scaling = HEAD ** (-0.5)

    def spread(matrix):
        shaped = matrix.reshape(local_rows, head_count, 1, HEAD)
        copies = jnp.broadcast_to(shaped, (local_rows, head_count, group, HEAD))
        return copies.reshape(local_rows, seq_size * HEAD)

    query_head, key_head, value_head, cot_head = (
        lax.all_to_all(spread(queries), "seq", split_axis=1, concat_axis=0, tiled=True),
        lax.all_to_all(spread(key_vectors), "seq", split_axis=1, concat_axis=0, tiled=True),
        lax.all_to_all(spread(value_vectors), "seq", split_axis=1, concat_axis=0, tiled=True),
        lax.all_to_all(spread(out_grad), "seq", split_axis=1, concat_axis=0, tiled=True),
    )
    length = key_head.shape[0]
    member = lax.axis_index("seq") % group
    blocks = 2 * group
    block = length // blocks
    bounds = jnp.cumsum(doc_lengths)
    positions = jnp.arange(length, dtype=jnp.int32)
    doc_index = jnp.sum((positions[:, None] >= bounds[None, :]).astype(jnp.int32), axis=1)
    row_list = [member, blocks - 1 - member]
    query_list = []
    cot_list = []
    pos_list = []
    for which in range(2):
        offset = row_list[which] * block
        query_list.append(lax.dynamic_slice_in_dim(query_head, offset, block, 0))
        cot_list.append(lax.dynamic_slice_in_dim(cot_head, offset, block, 0))
        pos_list.append(offset + jnp.arange(block, dtype=jnp.int32))
    query_stack = jnp.stack(query_list)
    cot_stack = jnp.stack(cot_list)
    pos_stack = jnp.stack(pos_list)
    doc_stack = jnp.take(doc_index, pos_stack)
    plan = []
    for number in range(blocks + 1):
        first = number <= member
        slot = jnp.where(first, 0, 1).astype(jnp.int32)
        col_block = jnp.where(first, number, number - member - 1)
        flag = None
        plan.append((slot, col_block, flag))
    row_max = jnp.full((2, block), -jnp.inf, jnp.float32)
    row_sum = jnp.zeros((2, block), jnp.float32)
    stored = []
    for slot, col_block, flag in plan:

        def score_tile(carry, slot=slot, col_block=col_block):
            maxima, totals = carry
            query_rows = pick_slot(query_stack, slot)
            key_rows = lax.dynamic_slice_in_dim(key_head, col_block * block, block, 0)
            col_docs = lax.dynamic_slice_in_dim(doc_index, col_block * block, block, 0)
            col_positions = col_block * block + jnp.arange(block, dtype=jnp.int32)
            raw = jnp.dot(query_rows, key_rows.T, preferred_element_type=jnp.float32) * scaling
            allowed = (pick_slot(doc_stack, slot)[:, None] == col_docs[None, :]) & (
                pick_slot(pos_stack, slot)[:, None] >= col_positions[None, :]
            )
            scores = jnp.where(allowed, raw, -jnp.inf)
            before = pick_slot(maxima, slot)
            after = jnp.maximum(before, jnp.max(scores, axis=1))
            safe = jnp.where(jnp.isfinite(after), after, 0.0)
            total = pick_slot(totals, slot) * jnp.exp(before - safe) + jnp.sum(
                jnp.exp(scores - safe[:, None]), axis=1
            )
            return (scores, put_slot(maxima, after, slot), put_slot(totals, total, slot))

        scores, row_max, row_sum = score_tile((row_max, row_sum))
        stored.append(scores)

    def tile_weights(scores, slot):
        return (
            jnp.exp(scores - pick_slot(row_max, slot)[:, None]) / pick_slot(row_sum, slot)[:, None]
        )

    summed = jnp.zeros((2, block, HEAD), jnp.float32)
    for (slot, col_block, flag), scores in zip(plan, stored):

        def add_values(carry, slot=slot, col_block=col_block, scores=scores):
            rounded = tile_weights(scores, slot).astype(jnp.bfloat16)
            value_rows = lax.dynamic_slice_in_dim(value_head, col_block * block, block, 0)
            term = jnp.dot(rounded, value_rows, preferred_element_type=jnp.float32)
            return put_slot(carry, pick_slot(carry, slot) + term, slot)

        summed = add_values(summed)
    attended = summed.astype(jnp.bfloat16)
    row_dot = jnp.sum(cot_stack.astype(jnp.float32) * attended.astype(jnp.float32), axis=2)
    query_acc = jnp.zeros((2, block, HEAD), jnp.float32)
    key_acc = jnp.zeros((length, HEAD), jnp.float32)
    value_acc = jnp.zeros((length, HEAD), jnp.float32)
    for (slot, col_block, flag), scores in zip(plan, stored):

        def backward_tile(carry, slot=slot, col_block=col_block, scores=scores):
            query_sum, key_sum, value_sum = carry
            weights = tile_weights(scores, slot)
            rounded = weights.astype(jnp.bfloat16)
            query_rows = pick_slot(query_stack, slot)
            cot_rows = pick_slot(cot_stack, slot)
            start = col_block * block
            key_rows = lax.dynamic_slice_in_dim(key_head, start, block, 0)
            value_rows = lax.dynamic_slice_in_dim(value_head, start, block, 0)
            value_term = jnp.dot(rounded.T, cot_rows, preferred_element_type=jnp.float32)
            prob_grad = jnp.dot(cot_rows, value_rows.T, preferred_element_type=jnp.float32)
            score_grad = (
                weights * (prob_grad - pick_slot(row_dot, slot)[:, None]) * scaling
            ).astype(jnp.bfloat16)
            query_term = jnp.dot(score_grad, key_rows, preferred_element_type=jnp.float32)
            key_term = jnp.dot(score_grad.T, query_rows, preferred_element_type=jnp.float32)
            query_sum = put_slot(query_sum, pick_slot(query_sum, slot) + query_term, slot)
            key_sum = lax.dynamic_update_slice_in_dim(
                key_sum, lax.dynamic_slice_in_dim(key_sum, start, block, 0) + key_term, start, 0
            )
            value_sum = lax.dynamic_update_slice_in_dim(
                value_sum,
                lax.dynamic_slice_in_dim(value_sum, start, block, 0) + value_term,
                start,
                0,
            )
            return (query_sum, key_sum, value_sum)

        query_acc, key_acc, value_acc = backward_tile((query_acc, key_acc, value_acc))
    query_rounded = query_acc.astype(jnp.bfloat16)
    key_back, value_back = (
        lax.all_to_all(key_acc, "seq", split_axis=0, concat_axis=1, tiled=True),
        lax.all_to_all(value_acc, "seq", split_axis=0, concat_axis=1, tiled=True),
    )

    def settle(received):
        shaped = received.astype(jnp.float32).reshape(local_rows, head_count, group, HEAD)
        return jnp.sum(shaped, axis=2).reshape(1, local_rows, local_width).astype(jnp.bfloat16)

    query_full = jnp.zeros((length, HEAD), jnp.bfloat16)
    for which in range(2):
        query_full = lax.dynamic_update_slice_in_dim(
            query_full, query_rounded[which], row_list[which] * block, 0
        )
    query_back = lax.all_to_all(query_full, "seq", split_axis=0, concat_axis=1, tiled=True)
    query_out = settle(query_back)
    return (query_out, settle(key_back), settle(value_back))


NT = ((1,), (1,))
NN = ((1,), (0,))
TN = ((0,), (0,))
GROUP = 8


def head_span(head):
    low = head * HEAD // LANES * LANES
    high = -(-(head + 1) * HEAD // LANES) * LANES
    return low, high


def head_mask(head):
    low, high = head_span(head)
    lane = lax.broadcasted_iota(jnp.int32, (1, high - low), 1) + low
    inside = (lane >= head * HEAD) & (lane < (head + 1) * HEAD)
    return inside.astype(jnp.float32).astype(jnp.bfloat16)


def matmul(left, right, dims):
    return lax.dot_general(left, right, (dims, ((), ())), preferred_element_type=jnp.float32)


def stack(values, axis):
    return values[0] if len(values) == 1 else jnp.concatenate(values, axis=axis)


def allowed(lengths_ref, rows, query_block, key_block):
    shape = (rows, rows)
    position = query_block * rows + lax.broadcasted_iota(jnp.int32, shape, 1)
    keys = key_block * rows + lax.broadcasted_iota(jnp.int32, shape, 0)
    start = jnp.zeros_like(position)
    bound = jnp.int32(0)
    for doc in range(lengths_ref.shape[0]):
        bound = bound + lengths_ref[doc]
        start = jnp.where(position >= bound, bound, start)
    return (keys >= start) & (keys <= position)


def make_tile(lengths_ref, rows, queries, keys):
    mask = stack(
        [stack([allowed(lengths_ref, rows, q, k) for _, q in queries], 1) for _, k in keys], 0
    )
    return [slot for slot, _ in queries], [slot for slot, _ in keys], mask


def tile_values(plan, head, queries, keys, products):
    low, high = head_span(head)
    keep = head_mask(head)

    def gather(refs, number, slots):
        return stack([refs[slot][number][0, :, low:high] for slot in slots], 0)

    out = []
    for query_slots, key_slots, _ in plan:
        q = [gather(queries, number, query_slots) for number in range(products)]
        k = [gather(keys, number, key_slots) * keep for number in range(products)]
        out.append((q, k, [matmul(b, a, NT) for a, b in zip(q, k)]))
    return out, keep


def tiles_ahead(heads, plan, queries, keys, products):
    ready = tile_values(plan, 0, queries, keys, products)
    for head in range(heads):
        now = ready
        if head + 1 < heads:
            ready = tile_values(plan, head + 1, queries, keys, products)
        yield head, now


def tile_plan(third, lengths_ref, rows, me):
    mate = me + 1 - 2 * lax.rem(me, 2)
    plan = [make_tile(lengths_ref, rows, ((0, me), (1, mate)), ((0, me), (1, me - 2)))]
    if third is not None:
        slots, keys, mask = make_tile(lengths_ref, rows, ((2, me + 1),), ((1, me - 2),))
        plan.append((slots, keys, mask & (me == third)))
    return plan


def at_start(step, refs):
    @pl.when(step == 0)
    def _():
        for ref in refs:
            ref[...] = jnp.zeros_like(ref)


def lane_cut(value, number, rows):
    return value[:, number * rows : (number + 1) * rows]


def row_of(group, kinds, kind, head):
    return pl.ds((group * kinds + kind) * GROUP + head, 1)


def per_query(slots, kinds, kind, head, ref):
    return stack([ref[row_of(slot, kinds, kind, head), :] for slot in slots], 1)


def stats_kernel(third, heads, power, place_ref, lengths_ref, *refs):
    count = 2 if third is None else 3
    query_refs, (k_own, k_back, o_own, v_own) = refs[:count], refs[count : count + 4]
    o_copy, v_copy, out_ref = refs[-3:]
    rows, me, step = k_own.shape[1], place_ref[0], pl.program_id(0)
    at_start(step, [out_ref])
    o_copy[...], v_copy[...] = o_own[...], v_own[...]
    queries, keys = [(ref,) for ref in query_refs], ((k_own,), (k_back,))

    plan = tile_plan(third, lengths_ref, rows, me)
    for head, (tiles, _) in tiles_ahead(heads, plan, queries, keys, 1):
        parts = {}
        for (query_slots, _, mask), (_, _, (raw,)) in zip(plan, tiles):
            raw = jnp.where(mask, raw, FLOOR)
            for number, slot in enumerate(query_slots):
                parts.setdefault(slot, []).append(lane_cut(raw, number, rows))
        for slot, pieces in parts.items():
            top = functools.reduce(
                jnp.maximum, [jnp.max(p, axis=0, keepdims=True) for p in pieces]
            )
            sums = sum(
                jnp.sum(jnp.exp2((p - top) * power), axis=0, keepdims=True) for p in pieces
            )
            out_ref[row_of(slot, 2, 0, step * heads + head), :] = top
            out_ref[row_of(slot, 2, 1, step * heads + head), :] = sums


def group_parts(third, kinds, mine, messages):
    size = kinds * GROUP

    def group(ref, number):
        return ref[number * size : (number + 1) * size, :]

    own = [group(mine, 0), group(messages[0], 1)]
    mate = [group(mine, 1), group(messages[0], 0)]
    if third is None:
        return [own, mate]
    _, near, far = messages
    return [
        own + [group(near, 2)],
        mate + [group(far, 2)],
        [group(mine, 2), group(near, 0), group(far, 1)],
    ]


def merge_stats(scaling, parts):
    split = [(jnp.where(p[GROUP:] > 0, p[:GROUP], FLOOR), p[GROUP:]) for p in parts]
    top = functools.reduce(jnp.maximum, [s[0] for s in split])
    total = sum(jnp.exp((s[0] - top) * scaling) * s[1] for s in split)
    return top + jnp.log(jnp.where(total > 0, total, 1.0)) / scaling


class Emitter:
    def __init__(self, outs):
        self.outs, self.carry = outs, {}

    def emit(self, head, name, value):
        ref = self.outs[name]
        low, high = head_span(head)
        first, last = head * HEAD % LANES == 0, (head + 1) * HEAD % LANES == 0
        start, stop = low, high
        if not first:
            shared = value[:, :LANES] + self.carry.pop(name)
            ref[0, :, low : low + LANES] = shared.astype(jnp.bfloat16)
            start = low + LANES
        if not last:
            self.carry[name] = value[:, high - LANES - low :]
            stop = high - LANES
        if stop > start:
            ref[0, :, start:stop] = value[:, start - low : stop - low].astype(jnp.bfloat16)


def add_rows(sums, kind, slots, value, rows):
    for number, slot in enumerate(slots):
        piece = value[number * rows : (number + 1) * rows]
        name = (kind, slot)
        sums[name] = sums[name] + piece if name in sums else piece


def add_lanes(sums, slots, value, rows):
    for number, slot in enumerate(slots):
        piece = lane_cut(value, number, rows)
        sums[slot] = sums[slot] + piece if slot in sums else piece


def split_refs(third, refs):
    count = 2 if third is None else 3
    queries = [(refs[2 * n], refs[2 * n + 1]) for n in range(count)]
    keys = [(refs[2 * n], refs[2 * n + 1]) for n in range(count, count + 2)]
    return queries, keys, refs[2 * count + 4 :]


def values_kernel(third, heads, scaling, power, place_ref, lengths_ref, *refs):
    count = 2 if third is None else 3
    queries = [(refs[2 * n], refs[2 * n + 1]) for n in range(count)]
    refs = refs[2 * count :]
    keys, mine, others = [(refs[0],), (refs[1],)], refs[2], refs[3:-3]
    value_own, value_back, shift_ref = refs[-3:]
    rows, me, step = keys[0][0].shape[1], place_ref[0], pl.program_id(0)

    plan = tile_plan(third, lengths_ref, rows, me)
    groups = group_parts(third, 2, mine, others)
    for number, parts in enumerate(groups):
        shift_ref[number * GROUP : (number + 1) * GROUP, :] = merge_stats(scaling, parts)
    out = Emitter({("v", 0): value_own, ("v", 1): value_back})
    for head, (tiles, keep) in tiles_ahead(heads, plan, queries, keys, 1):
        low, high = head_span(head)
        sums = {}
        for (query_slots, key_slots, mask), (_, _, (raw,)) in zip(plan, tiles):
            shift = per_query(query_slots, 1, 0, step * heads + head, shift_ref)
            weight = jnp.where(mask, jnp.exp2((raw - shift) * power), 0.0).astype(jnp.bfloat16)
            o = stack([queries[slot][1][0, :, low:high] for slot in query_slots], 0) * keep
            add_rows(sums, "v", key_slots, matmul(weight, o, NN), rows)
        for name, value in sums.items():
            out.emit(head, name, value)


def dots_kernel(third, heads, power, place_ref, lengths_ref, *refs):
    queries, keys, (shift_ref, dots_ref) = split_refs(third, refs)
    rows, me, step = keys[0][0].shape[1], place_ref[0], pl.program_id(0)
    at_start(step, [dots_ref])

    plan = tile_plan(third, lengths_ref, rows, me)
    for head, (tiles, _) in tiles_ahead(heads, plan, queries, keys, 2):
        at = step * heads + head
        dots = {}
        for (query_slots, _, mask), (_, _, (raw, grads)) in zip(plan, tiles):
            shift = per_query(query_slots, 1, 0, at, shift_ref)
            weight = jnp.where(mask, jnp.exp2((raw - shift) * power), 0.0)
            add_lanes(dots, query_slots, jnp.sum(weight * grads, axis=0, keepdims=True), rows)
        for slot, value in dots.items():
            dots_ref[row_of(slot, 1, 0, at), :] = value


def keys_kernel(third, heads, scaling, power, place_ref, lengths_ref, *refs):
    queries, keys, refs = split_refs(third, refs)
    messages = 1 if third is None else 3
    shift_ref, mine, others = refs[0], refs[1], refs[2 : 2 + messages]
    key_own, key_back, *query_refs, total_ref = refs[2 + messages :]
    rows, me, step = keys[0][0].shape[1], place_ref[0], pl.program_id(0)

    plan = tile_plan(third, lengths_ref, rows, me)
    for number, parts in enumerate(group_parts(third, 1, mine, others)):
        total_ref[number * GROUP : (number + 1) * GROUP, :] = sum(parts)
    outs = {("k", 0): key_own, ("k", 1): key_back}
    outs.update({("q", slot): ref for slot, ref in enumerate(query_refs)})
    out = Emitter(outs)
    for head, (tiles, keep) in tiles_ahead(heads, plan, queries, keys, 2):
        at = step * heads + head
        sums = {}
        for (query_slots, key_slots, mask), ((q, _), (k, _), (raw, grads)) in zip(plan, tiles):
            shift = per_query(query_slots, 1, 0, at, shift_ref)
            dots = per_query(query_slots, 1, 0, at, total_ref)
            weight = jnp.where(mask, jnp.exp2((raw - shift) * power), 0.0)
            slope = (weight * (grads - dots) * scaling).astype(jnp.bfloat16)
            add_rows(sums, "k", key_slots, matmul(slope, q * keep, NN), rows)
            add_rows(sums, "q", query_slots, matmul(slope, k, TN), rows)
        for name, value in sums.items():
            out.emit(head, name, value)


def sums_kernel(counts, *refs):
    outs = refs[sum(counts) :]
    for count, out in zip(counts, outs):
        terms, refs = refs[:count], refs[count:]
        out[...] = sum(ref[...].astype(jnp.float32) for ref in terms).astype(jnp.bfloat16)


def halo_program(third, queries, key_vectors, value_vectors, out_grad, doc_lengths):
    _, rows, width = queries.shape
    seq_size = lax.axis_size("seq")
    me = lax.axis_index("seq").astype(jnp.int32)
    scaling = HEAD ** (-0.5)
    power = scaling * math.log2(math.e)
    steps = width // HEAD // 4
    part = width // steps
    heads = part // HEAD
    count = 2 if third is None else 3
    devices = range(seq_size)
    mates = [(s, s ^ 1) for s in devices]
    ring = third is None
    chain = [(s, s + 2) for s in devices if s + 2 < seq_size]
    ahead = [(s, (s + 2) % seq_size) for s in devices] if ring else chain
    behind = [(s, s - 2) for s in devices if s >= 2]
    if not ring:
        relay, to_even = [(third + 2, third)], [(third, third + 1)]
        near, far = to_even + [(third + 1, third)], relay + [(third, third + 2)]

    def send(value, pairs):
        return lax.ppermute(value, "seq", pairs)

    def exchange(value):
        return [send(value, pairs) for pairs in ([mates] if ring else [mates, near, far])]

    smem = pl.BlockSpec(memory_space=pltpu.SMEM)
    wide = pl.BlockSpec((1, rows, part), lambda step: (0, 0, step))
    wide_shape = jax.ShapeDtypeStruct((1, rows, width), jnp.bfloat16)

    def slim(kinds):
        return pl.BlockSpec((count * kinds * GROUP, rows), lambda step: (0, 0))

    def slim_shape(kinds):
        return jax.ShapeDtypeStruct((count * kinds * GROUP, rows), jnp.float32)

    def call(kernel, products, wides, slims, outs, slim_outs, scratch=(), after=()):
        flops = 2 * products * 4 * rows * rows * width * 3 // 2
        return pl.pallas_call(
            kernel,
            grid=(steps,),
            in_specs=[smem, smem]
            + [wide] * len(wides)
            + [slim(kinds) for kinds, _ in slims]
            + [pl.BlockSpec(memory_space=pl.ANY)] * len(after),
            out_specs=[wide] * outs + [slim(kinds) for kinds in slim_outs],
            out_shape=[wide_shape] * outs + [slim_shape(kinds) for kinds in slim_outs],
            scratch_shapes=scratch,
            compiler_params=pltpu.CompilerParams(vmem_limit_bytes=20 * 1024 * 1024),
            cost_estimate=pl.CostEstimate(
                flops=flops, bytes_accessed=20 * rows * width, transcendentals=0
            ),
        )(me[None], doc_lengths, *wides, *[value for _, value in slims], *after)

    query_mate = send(queries, mates)
    key_back = send(key_vectors, chain)
    grad_mate = send(out_grad, mates)
    value_back = send(value_vectors, ahead)
    query_rows = [queries, query_mate] + ([] if ring else [send(query_mate, relay)])
    grad_own, value_own, stats = call(
        functools.partial(stats_kernel, third, heads, power), 1,
        [*query_rows, key_vectors, key_back, out_grad, value_vectors], [], 2, [2],
        after=[] if ring else [value_back],
    )
    grad_rows = [grad_own, grad_mate] + ([] if ring else [send(grad_mate, relay)])
    tensors = [t for two in zip(query_rows, grad_rows) for t in two]
    tensors += [key_vectors, value_own, key_back, value_back]
    value_part, value_sent, shift = call(
        functools.partial(values_kernel, third, heads, scaling, power), 2,
        tensors[: 2 * count] + [key_vectors, key_back],
        [(2, value) for value in [stats] + exchange(stats)], 2, [1],
    )
    (dots,) = call(
        functools.partial(dots_kernel, third, heads, power), 2, tensors, [(1, shift)], 0, [1]
    )
    value_received = send(value_sent, behind)
    key_part, key_sent, query_part, *query_sent = call(
        functools.partial(keys_kernel, third, heads, scaling, power), 4, tensors,
        [(1, value) for value in [shift, dots] + exchange(dots)], 2 + count, [],
        [pltpu.VMEM((count * GROUP, rows), jnp.float32)],
    )
    key_received = send(key_sent, behind)
    query_received = [send(value, pairs) for value, pairs in zip(query_sent, (mates,) if ring else (mates, to_even))]

    def total(groups):
        flat = [term for terms in groups for term in terms]
        return pl.pallas_call(
            functools.partial(sums_kernel, [len(terms) for terms in groups]),
            grid=(steps,),
            in_specs=[wide] * len(flat),
            out_specs=[wide] * len(groups),
            out_shape=[wide_shape] * len(groups),
            compiler_params=pltpu.CompilerParams(vmem_limit_bytes=20 * 1024 * 1024),
            cost_estimate=pl.CostEstimate(
                flops=rows * width, bytes_accessed=8 * rows * width, transcendentals=0
            ),
        )(*flat)

    value_ready = (value_part.astype(jnp.float32) + value_received.astype(jnp.float32)).astype(jnp.bfloat16)
    key_ready, query_ready = total([[key_part, key_received], [query_part, *query_received]])
    return query_ready, key_ready, value_ready


def program_index(rows, doc_lengths):
    count = doc_lengths.shape[0]
    ends = sum(lax.pad(doc_lengths[: count - n], jnp.int32(0), [(n, 0, 0)]) for n in range(count))
    shift = rows.bit_length() - 1
    first, last = (ends - doc_lengths) >> shift, (ends - 1) >> shift
    spans = (last - first >= 3) & (last & 1 == 0)
    return jnp.sum(jnp.where(spans, (last >> 1) - 1, 0))


def halo_shards(*arguments):
    rows, doc_lengths = arguments[0].shape[1], arguments[-1]
    thirds = range(3, lax.axis_size("seq") - 2, 2)
    programs = [functools.partial(halo_program, third) for third in (None, *thirds)]
    return lax.switch(program_index(rows, doc_lengths), programs, *arguments)


def shards(queries, key_vectors, value_vectors, out_grad, doc_lengths):
    _, rows, width = queries.shape
    seq_size = lax.axis_size("seq")
    longest = rows * seq_size * 3 // 8
    fits = longest <= 3 * rows and seq_size % 2 == 0 and seq_size > 4 and rows == LANES
    heads = width // HEAD
    plan = halo_shards if fits and heads % 4 == 0 and heads <= GROUP else spread_shards
    return plan(queries, key_vectors, value_vectors, out_grad, doc_lengths)


def solution(mesh):
    return jax.shard_map(
        shards,
        mesh=mesh,
        in_specs=(
            P("section", "seq", "dp"),
            P("section", "seq", "dp"),
            P("section", "seq", "dp"),
            P("section", "seq", "dp"),
            P(),
        ),
        out_specs=(P("section", "seq", "dp"), P("section", "seq", "dp"), P("section", "seq", "dp")),
        check_vma=False,
    )
```

```python
import functools
import math
import jax
import jax.numpy as jnp
from jax import lax
from jax.experimental import pallas as pl
from jax.experimental.pallas import tpu as pltpu
from jax.sharding import PartitionSpec as P

HEAD = 224
LANES = 128
FLOOR = -1e30


def pick_slot(stacked, slot):
    return lax.dynamic_index_in_dim(stacked, slot, 0, keepdims=False)


def put_slot(stacked, update, slot):
    return lax.dynamic_update_index_in_dim(stacked, update, slot, 0)


def spread_shards(queries, key_vectors, value_vectors, out_grad, doc_lengths):
    local_rows = queries.shape[1]
    local_width = queries.shape[2]
    head_count = local_width // HEAD
    seq_size = lax.axis_size("seq")
    group = seq_size // head_count
    scaling = HEAD ** (-0.5)

    def spread(matrix):
        shaped = matrix.reshape(local_rows, head_count, 1, HEAD)
        copies = jnp.broadcast_to(shaped, (local_rows, head_count, group, HEAD))
        return copies.reshape(local_rows, seq_size * HEAD)

    query_head, key_head, value_head, cot_head = (
        lax.all_to_all(spread(queries), "seq", split_axis=1, concat_axis=0, tiled=True),
        lax.all_to_all(spread(key_vectors), "seq", split_axis=1, concat_axis=0, tiled=True),
        lax.all_to_all(spread(value_vectors), "seq", split_axis=1, concat_axis=0, tiled=True),
        lax.all_to_all(spread(out_grad), "seq", split_axis=1, concat_axis=0, tiled=True),
    )
    length = key_head.shape[0]
    member = lax.axis_index("seq") % group
    blocks = 2 * group
    block = length // blocks
    bounds = jnp.cumsum(doc_lengths)
    positions = jnp.arange(length, dtype=jnp.int32)
    doc_index = jnp.sum((positions[:, None] >= bounds[None, :]).astype(jnp.int32), axis=1)
    row_list = [member, blocks - 1 - member]
    query_list = []
    cot_list = []
    pos_list = []
    for which in range(2):
        offset = row_list[which] * block
        query_list.append(lax.dynamic_slice_in_dim(query_head, offset, block, 0))
        cot_list.append(lax.dynamic_slice_in_dim(cot_head, offset, block, 0))
        pos_list.append(offset + jnp.arange(block, dtype=jnp.int32))
    query_stack = jnp.stack(query_list)
    cot_stack = jnp.stack(cot_list)
    pos_stack = jnp.stack(pos_list)
    doc_stack = jnp.take(doc_index, pos_stack)
    plan = []
    for number in range(blocks + 1):
        first = number <= member
        slot = jnp.where(first, 0, 1).astype(jnp.int32)
        col_block = jnp.where(first, number, number - member - 1)
        flag = None
        plan.append((slot, col_block, flag))
    row_max = jnp.full((2, block), -jnp.inf, jnp.float32)
    row_sum = jnp.zeros((2, block), jnp.float32)
    stored = []
    for slot, col_block, flag in plan:

        def score_tile(carry, slot=slot, col_block=col_block):
            maxima, totals = carry
            query_rows = pick_slot(query_stack, slot)
            key_rows = lax.dynamic_slice_in_dim(key_head, col_block * block, block, 0)
            col_docs = lax.dynamic_slice_in_dim(doc_index, col_block * block, block, 0)
            col_positions = col_block * block + jnp.arange(block, dtype=jnp.int32)
            raw = jnp.dot(query_rows, key_rows.T, preferred_element_type=jnp.float32) * scaling
            allowed = (pick_slot(doc_stack, slot)[:, None] == col_docs[None, :]) & (
                pick_slot(pos_stack, slot)[:, None] >= col_positions[None, :]
            )
            scores = jnp.where(allowed, raw, -jnp.inf)
            before = pick_slot(maxima, slot)
            after = jnp.maximum(before, jnp.max(scores, axis=1))
            safe = jnp.where(jnp.isfinite(after), after, 0.0)
            total = pick_slot(totals, slot) * jnp.exp(before - safe) + jnp.sum(
                jnp.exp(scores - safe[:, None]), axis=1
            )
            return (scores, put_slot(maxima, after, slot), put_slot(totals, total, slot))

        scores, row_max, row_sum = score_tile((row_max, row_sum))
        stored.append(scores)

    def tile_weights(scores, slot):
        return (
            jnp.exp(scores - pick_slot(row_max, slot)[:, None]) / pick_slot(row_sum, slot)[:, None]
        )

    summed = jnp.zeros((2, block, HEAD), jnp.float32)
    for (slot, col_block, flag), scores in zip(plan, stored):

        def add_values(carry, slot=slot, col_block=col_block, scores=scores):
            rounded = tile_weights(scores, slot).astype(jnp.bfloat16)
            value_rows = lax.dynamic_slice_in_dim(value_head, col_block * block, block, 0)
            term = jnp.dot(rounded, value_rows, preferred_element_type=jnp.float32)
            return put_slot(carry, pick_slot(carry, slot) + term, slot)

        summed = add_values(summed)
    attended = summed.astype(jnp.bfloat16)
    row_dot = jnp.sum(cot_stack.astype(jnp.float32) * attended.astype(jnp.float32), axis=2)
    query_acc = jnp.zeros((2, block, HEAD), jnp.float32)
    key_acc = jnp.zeros((length, HEAD), jnp.float32)
    value_acc = jnp.zeros((length, HEAD), jnp.float32)
    for (slot, col_block, flag), scores in zip(plan, stored):

        def backward_tile(carry, slot=slot, col_block=col_block, scores=scores):
            query_sum, key_sum, value_sum = carry
            weights = tile_weights(scores, slot)
            rounded = weights.astype(jnp.bfloat16)
            query_rows = pick_slot(query_stack, slot)
            cot_rows = pick_slot(cot_stack, slot)
            start = col_block * block
            key_rows = lax.dynamic_slice_in_dim(key_head, start, block, 0)
            value_rows = lax.dynamic_slice_in_dim(value_head, start, block, 0)
            value_term = jnp.dot(rounded.T, cot_rows, preferred_element_type=jnp.float32)
            prob_grad = jnp.dot(cot_rows, value_rows.T, preferred_element_type=jnp.float32)
            score_grad = (
                weights * (prob_grad - pick_slot(row_dot, slot)[:, None]) * scaling
            ).astype(jnp.bfloat16)
            query_term = jnp.dot(score_grad, key_rows, preferred_element_type=jnp.float32)
            key_term = jnp.dot(score_grad.T, query_rows, preferred_element_type=jnp.float32)
            query_sum = put_slot(query_sum, pick_slot(query_sum, slot) + query_term, slot)
            key_sum = lax.dynamic_update_slice_in_dim(
                key_sum, lax.dynamic_slice_in_dim(key_sum, start, block, 0) + key_term, start, 0
            )
            value_sum = lax.dynamic_update_slice_in_dim(
                value_sum,
                lax.dynamic_slice_in_dim(value_sum, start, block, 0) + value_term,
                start,
                0,
            )
            return (query_sum, key_sum, value_sum)

        query_acc, key_acc, value_acc = backward_tile((query_acc, key_acc, value_acc))
    query_rounded = query_acc.astype(jnp.bfloat16)
    key_back, value_back = (
        lax.all_to_all(key_acc, "seq", split_axis=0, concat_axis=1, tiled=True),
        lax.all_to_all(value_acc, "seq", split_axis=0, concat_axis=1, tiled=True),
    )

    def settle(received):
        shaped = received.astype(jnp.float32).reshape(local_rows, head_count, group, HEAD)
        return jnp.sum(shaped, axis=2).reshape(1, local_rows, local_width).astype(jnp.bfloat16)

    query_full = jnp.zeros((length, HEAD), jnp.bfloat16)
    for which in range(2):
        query_full = lax.dynamic_update_slice_in_dim(
            query_full, query_rounded[which], row_list[which] * block, 0
        )
    query_back = lax.all_to_all(query_full, "seq", split_axis=0, concat_axis=1, tiled=True)
    query_out = settle(query_back)
    return (query_out, settle(key_back), settle(value_back))


NT = ((1,), (1,))
NN = ((1,), (0,))
TN = ((0,), (0,))
GROUP = 8


def head_span(head):
    low = head * HEAD // LANES * LANES
    high = -(-(head + 1) * HEAD // LANES) * LANES
    return low, high


def head_mask(head):
    low, high = head_span(head)
    lane = lax.broadcasted_iota(jnp.int32, (1, high - low), 1) + low
    inside = (lane >= head * HEAD) & (lane < (head + 1) * HEAD)
    return inside.astype(jnp.float32).astype(jnp.bfloat16)


def matmul(left, right, dims):
    return lax.dot_general(left, right, (dims, ((), ())), preferred_element_type=jnp.float32)


def stack(values, axis):
    return values[0] if len(values) == 1 else jnp.concatenate(values, axis=axis)


def allowed(lengths_ref, rows, query_block, key_block):
    shape = (rows, rows)
    position = query_block * rows + lax.broadcasted_iota(jnp.int32, shape, 1)
    keys = key_block * rows + lax.broadcasted_iota(jnp.int32, shape, 0)
    start = jnp.zeros_like(position)
    bound = jnp.int32(0)
    for doc in range(lengths_ref.shape[0]):
        bound = bound + lengths_ref[doc]
        start = jnp.where(position >= bound, bound, start)
    return (keys >= start) & (keys <= position)


def make_tile(lengths_ref, rows, queries, keys):
    mask = stack(
        [stack([allowed(lengths_ref, rows, q, k) for _, q in queries], 1) for _, k in keys], 0
    )
    return [slot for slot, _ in queries], [slot for slot, _ in keys], mask


def tile_values(plan, head, queries, keys, products):
    low, high = head_span(head)
    keep = head_mask(head)

    def gather(refs, number, slots):
        return stack([refs[slot][number][0, :, low:high] for slot in slots], 0)

    out = []
    for query_slots, key_slots, _ in plan:
        q = [gather(queries, number, query_slots) for number in range(products)]
        k = [gather(keys, number, key_slots) * keep for number in range(products)]
        out.append((q, k, [matmul(b, a, NT) for a, b in zip(q, k)]))
    return out, keep


def tiles_ahead(heads, plan, queries, keys, products):
    ready = tile_values(plan, 0, queries, keys, products)
    for head in range(heads):
        now = ready
        if head + 1 < heads:
            ready = tile_values(plan, head + 1, queries, keys, products)
        yield head, now


def pair_tile(lengths_ref, rows, me):
    mate = me + 1 - 2 * lax.rem(me, 2)
    return make_tile(lengths_ref, rows, ((0, me), (1, mate)), ((0, me), (1, me - 2)))


def third_tile(third, lengths_ref, rows, me):
    slots, keys, mask = make_tile(lengths_ref, rows, ((2, me + 1),), ((1, me - 2),))
    return slots, keys, mask & (me == third)


def tile_plan(third, lengths_ref, rows, me):
    plan = [pair_tile(lengths_ref, rows, me)]
    return plan if third is None else plan + [third_tile(third, lengths_ref, rows, me)]


def lane_cut(value, number, rows):
    return value[:, number * rows : (number + 1) * rows]


def row_of(group, kinds, kind, head):
    return pl.ds((group * kinds + kind) * GROUP + head, 1)


def per_query(slots, kinds, kind, head, ref):
    return stack([ref[row_of(slot, kinds, kind, head), :] for slot in slots], 1)


def collect_stats(heads, power, step, plan, queries, keys, rows, out_ref, groups):
    for head, (tiles, _) in tiles_ahead(heads, plan, queries, keys, 1):
        for (query_slots, _, mask), (_, _, (raw,)) in zip(plan, tiles):
            raw = jnp.where(mask, raw, FLOOR)
            top = jnp.max(raw, axis=0, keepdims=True)
            sums = jnp.sum(jnp.exp2((raw - top) * power), axis=0, keepdims=True)
            for number, slot in enumerate(query_slots):
                at = step * heads + head
                out_ref[row_of(groups[slot], 2, 0, at), :] = lane_cut(top, number, rows)
                out_ref[row_of(groups[slot], 2, 1, at), :] = lane_cut(sums, number, rows)


def stats_kernel(
    heads, power, place_ref, lengths_ref, q_own, q_mate, k_own, k_back, o_own, v_own, o_copy, v_copy, out_ref
):
    rows, me, step = k_own.shape[1], place_ref[0], pl.program_id(0)
    o_copy[...], v_copy[...] = o_own[...], v_own[...]
    plan = [pair_tile(lengths_ref, rows, me)]
    queries, keys = ((q_own,), (q_mate,)), ((k_own,), (k_back,))
    collect_stats(heads, power, step, plan, queries, keys, rows, out_ref, (0, 1))


def third_stats_kernel(third, heads, power, place_ref, lengths_ref, q_third, k_back, out_ref):
    rows, me, step = k_back.shape[1], place_ref[0], pl.program_id(0)
    plan = [third_tile(third, lengths_ref, rows, me)]
    queries, keys = (None, None, (q_third,)), (None, (k_back,))
    collect_stats(heads, power, step, plan, queries, keys, rows, out_ref, (None, None, 0))


def part_of(ref, kinds, number):
    size = kinds * GROUP
    return ref[number * size : (number + 1) * size, :]


def stats_parts(mine, sent, extra):
    own = [part_of(mine, 2, 0), part_of(sent, 2, 1)]
    mate = [part_of(mine, 2, 1), part_of(sent, 2, 0)]
    if not extra:
        return [own, mate]
    third, near, far, even, odd = extra
    return [own + [near[...]], mate + [far[...]], [third[...], part_of(even, 2, 0), part_of(odd, 2, 1)]]


def dots_parts(mine, sent, extra):
    own = [part_of(mine, 1, 0), part_of(sent, 1, 1)]
    mate = [part_of(mine, 1, 1), part_of(sent, 1, 0)]
    if not extra:
        return [own, mate]
    near, far = extra
    return [
        own + [part_of(near, 1, 2)],
        mate + [part_of(far, 1, 2)],
        [part_of(mine, 1, 2), part_of(near, 1, 0), part_of(far, 1, 1)],
    ]


def merge_stats(scaling, parts):
    split = [(jnp.where(p[GROUP:] > 0, p[:GROUP], FLOOR), p[GROUP:]) for p in parts]
    top = functools.reduce(jnp.maximum, [s[0] for s in split])
    total = sum(jnp.exp((s[0] - top) * scaling) * s[1] for s in split)
    return top + jnp.log(jnp.where(total > 0, total, 1.0)) / scaling


class Emitter:
    def __init__(self, outs):
        self.outs, self.carry = outs, {}

    def emit(self, head, name, value):
        ref = self.outs[name]
        low, high = head_span(head)
        first, last = head * HEAD % LANES == 0, (head + 1) * HEAD % LANES == 0
        start, stop = low, high
        if not first:
            shared = value[:, :LANES] + self.carry.pop(name)
            ref[0, :, low : low + LANES] = shared.astype(jnp.bfloat16)
            start = low + LANES
        if not last:
            self.carry[name] = value[:, high - LANES - low :]
            stop = high - LANES
        if stop > start:
            ref[0, :, start:stop] = value[:, start - low : stop - low].astype(jnp.bfloat16)


def add_rows(sums, kind, slots, value, rows):
    for number, slot in enumerate(slots):
        piece = value[number * rows : (number + 1) * rows]
        name = (kind, slot)
        sums[name] = sums[name] + piece if name in sums else piece


def split_refs(third, refs):
    count = 2 if third is None else 3
    queries = [(refs[2 * n], refs[2 * n + 1]) for n in range(count)]
    keys = [(refs[2 * n], refs[2 * n + 1]) for n in range(count, count + 2)]
    return queries, keys, refs[2 * count + 4 :]


def values_kernel(third, heads, scaling, power, place_ref, lengths_ref, *refs):
    count, last = (2, -3) if third is None else (3, -4)
    queries = [(refs[2 * n], refs[2 * n + 1]) for n in range(count)]
    refs, outs = refs[2 * count : last], refs[last:]
    keys, shift_ref = [(refs[0],), (refs[1],)], outs[-1]
    rows, me, step = keys[0][0].shape[1], place_ref[0], pl.program_id(0)
    plan = tile_plan(third, lengths_ref, rows, me)
    for number, parts in enumerate(stats_parts(refs[2], refs[3], refs[4:])):
        shift_ref[number * GROUP : (number + 1) * GROUP, :] = merge_stats(scaling, parts)
    out = Emitter(dict(zip((("v", 0), ("v", 1), ("b", 2)), outs[:-1])))
    for head, (tiles, keep) in tiles_ahead(heads, plan, queries, keys, 1):
        low, high = head_span(head)
        sums = {}
        for (query_slots, key_slots, mask), (_, (k,), (raw,)) in zip(plan, tiles):
            shift = per_query(query_slots, 1, 0, step * heads + head, shift_ref)
            weight = jnp.where(mask, jnp.exp2((raw - shift) * power), 0.0).astype(jnp.bfloat16)
            o = stack([queries[slot][1][0, :, low:high] for slot in query_slots], 0) * keep
            add_rows(sums, "v", key_slots, matmul(weight, o, NN), rows)
            if query_slots == [2]:
                add_rows(sums, "b", query_slots, matmul(weight, k, TN), rows)
        for name, value in sums.items():
            out.emit(head, name, value)


def dots_kernel(third, heads, power, place_ref, lengths_ref, *refs):
    queries, keys, (shift_ref, *outs) = split_refs(third, refs)
    dots_ref = outs[-1]
    rows, me, step = keys[0][0].shape[1], place_ref[0], pl.program_id(0)
    plan = tile_plan(third, lengths_ref, rows, me)
    out = Emitter(dict(zip((("a", 2),), outs[:-1])))
    for head, (tiles, _) in tiles_ahead(heads, plan, queries, keys, 2):
        at = step * heads + head
        for (query_slots, _, mask), (_, (k, _), (raw, grads)) in zip(plan, tiles):
            shift = per_query(query_slots, 1, 0, at, shift_ref)
            product = jnp.where(mask, jnp.exp2((raw - shift) * power), 0.0) * grads
            dots = jnp.sum(product, axis=0, keepdims=True)
            for number, slot in enumerate(query_slots):
                dots_ref[row_of(slot, 1, 0, at), :] = lane_cut(dots, number, rows)
            if query_slots == [2]:
                out.emit(head, ("a", 2), matmul(product.astype(jnp.bfloat16), k, TN))


def keys_kernel(third, heads, scaling, power, place_ref, lengths_ref, *refs):
    queries, keys, refs = split_refs(third, refs)
    (shift_ref, mine, sent, *extra), outs = refs[:-5], refs[-5:]
    total_ref = outs[-1]
    rows, me, step = keys[0][0].shape[1], place_ref[0], pl.program_id(0)
    plan = tile_plan(third, lengths_ref, rows, me)
    for number, parts in enumerate(dots_parts(mine, sent, extra)):
        total_ref[number * GROUP : (number + 1) * GROUP, :] = sum(parts)
    out = Emitter(dict(zip((("k", 0), ("k", 1), ("q", 0), ("q", 1)), outs[:-1])))
    for head, (tiles, keep) in tiles_ahead(heads, plan, queries, keys, 2):
        at = step * heads + head
        sums = {}
        for (query_slots, key_slots, mask), ((q, _), (k, _), (raw, grads)) in zip(plan, tiles):
            shift = per_query(query_slots, 1, 0, at, shift_ref)
            dots = per_query(query_slots, 1, 0, at, total_ref)
            weight = jnp.where(mask, jnp.exp2((raw - shift) * power), 0.0)
            slope = (weight * (grads - dots) * scaling).astype(jnp.bfloat16)
            add_rows(sums, "k", key_slots, matmul(slope, q * keep, NN), rows)
            if query_slots != [2]:
                add_rows(sums, "q", query_slots, matmul(slope, k, TN), rows)
        for name, value in sums.items():
            out.emit(head, name, value)


def add_refs(*refs):
    return sum(ref[...].astype(jnp.float32) for ref in refs)


def sums_kernel(key_part, key_sent, query_part, query_sent, key_out, query_out):
    key_out[...] = add_refs(key_part, key_sent).astype(jnp.bfloat16)
    query_out[...] = add_refs(query_part, query_sent).astype(jnp.bfloat16)


def third_sums_kernel(
    heads, scaling, key_part, key_sent, query_part, query_sent, a_sent, b_sent, total_ref, key_out, query_out
):
    key_out[...] = add_refs(key_part, key_sent).astype(jnp.bfloat16)
    step = pl.program_id(0)
    rows, part = query_out.shape[1:]
    spread = total_ref[pl.ds(pl.multiple_of(step * GROUP, GROUP), GROUP), :]
    columns = jnp.concatenate([spread, jnp.zeros((LANES - GROUP, rows), jnp.float32)], 0).T
    lane = lax.broadcasted_iota(jnp.int32, (rows, part), 1)
    dots = jnp.zeros((rows, part), jnp.float32)
    for head in range(heads):
        inside = (lane >= head * HEAD) & (lane < (head + 1) * HEAD)
        dots = jnp.where(inside, columns[:, head : head + 1], dots)
    extra = (a_sent[0].astype(jnp.float32) - dots * b_sent[0].astype(jnp.float32)) * scaling
    query_out[0] = (add_refs(query_part, query_sent)[0] + extra).astype(jnp.bfloat16)


def halo_program(third, queries, key_vectors, value_vectors, out_grad, doc_lengths):
    _, rows, width = queries.shape
    seq_size = lax.axis_size("seq")
    me = lax.axis_index("seq").astype(jnp.int32)
    scaling = HEAD ** (-0.5)
    power = scaling * math.log2(math.e)
    steps = width // HEAD // 4
    part = width // steps
    heads = part // HEAD
    count = 2 if third is None else 3
    devices = range(seq_size)
    mates = [(s, s ^ 1) for s in devices]
    ring = third is None
    chain = [(s, s + 2) for s in devices if s + 2 < seq_size]
    ahead = [(s, (s + 2) % seq_size) for s in devices] if ring else chain
    behind = [(s, s - 2) for s in devices if s >= 2]
    if not ring:
        relay, to_odd = [(third + 2, third)], [(third, third + 2)]
        from_even, to_even = [(third + 1, third)], [(third, third + 1)]
        near, far = from_even + to_even, relay + to_odd

    def send(value, pairs):
        return lax.ppermute(value, "seq", pairs)

    smem = pl.BlockSpec(memory_space=pltpu.SMEM)
    wide = pl.BlockSpec((1, rows, part), lambda step: (0, 0, step))
    wide_shape = jax.ShapeDtypeStruct((1, rows, width), jnp.bfloat16)

    def slim(groups, kinds):
        return pl.BlockSpec((groups * kinds * GROUP, rows), lambda step: (0, 0))

    def slim_shape(groups, kinds):
        return jax.ShapeDtypeStruct((groups * kinds * GROUP, rows), jnp.float32)

    def call(kernel, products, wides, slims, outs, slim_outs, plain=False):
        flops = 2 * products * 4 * rows * rows * width * 3 // 2
        lead = [] if plain else [me[None], doc_lengths]
        return pl.pallas_call(
            kernel,
            grid=(steps,),
            in_specs=[smem] * len(lead)
            + [wide] * len(wides)
            + [slim(groups, kinds) for groups, kinds, _ in slims],
            out_specs=[wide] * outs + [slim(*sizes) for sizes in slim_outs],
            out_shape=[wide_shape] * outs + [slim_shape(*sizes) for sizes in slim_outs],
            compiler_params=pltpu.CompilerParams(vmem_limit_bytes=20 * 1024 * 1024),
            cost_estimate=pl.CostEstimate(
                flops=flops, bytes_accessed=20 * rows * width, transcendentals=0
            ),
        )(*lead, *wides, *[value for _, _, value in slims])

    query_mate = send(queries, mates)
    key_back = send(key_vectors, chain)
    grad_mate = send(out_grad, mates)
    value_back = send(value_vectors, ahead)
    query_rows, grad_rows = [queries, query_mate], [out_grad, grad_mate]
    grad_own, value_own, stats = call(
        functools.partial(stats_kernel, heads, power), 1,
        [*query_rows, key_vectors, key_back, out_grad, value_vectors], [], 2, [(2, 2)],
    )
    stats_in = [(2, 2, stats), (2, 2, send(stats, mates))]
    grad_rows[0] = grad_own
    if not ring:
        query_rows.append(send(query_mate, relay))
        held, _ = lax.optimization_barrier((grad_mate, stats))
        grad_rows.append(send(held, relay))
        query_third, _ = lax.optimization_barrier((query_rows[2], value_back))
        (third_stats,) = call(
            functools.partial(third_stats_kernel, third, heads, power), 1,
            [query_third, key_back], [], 0, [(1, 2)],
        )
        stats_in += [(1, 2, third_stats), (1, 2, send(third_stats, to_even)), (1, 2, send(third_stats, to_odd))]
        stats_in += [(2, 2, send(stats, from_even)), (2, 2, send(stats, relay))]
    tensors = [t for two in zip(query_rows, grad_rows) for t in two]
    value_part, value_sent, *weighted, shift = call(
        functools.partial(values_kernel, third, heads, scaling, power), 2,
        tensors + [key_vectors, key_back], stats_in, count, [(count, 1)],
    )
    tensors += [key_vectors, value_own, key_back, value_back]
    *graded, dots = call(
        functools.partial(dots_kernel, third, heads, power), 2, tensors, [(count, 1, shift)],
        count - 2, [(count, 1)],
    )
    value_received = send(value_sent, behind)
    dots_in = [(count, 1, shift), (count, 1, dots), (count, 1, send(dots, mates))]
    if not ring:
        dots_in += [(count, 1, send(dots, pairs)) for pairs in (near, far)]
    key_part, key_sent, query_part, query_sent, totals = call(
        functools.partial(keys_kernel, third, heads, scaling, power), 4, tensors, dots_in,
        4, [(count, 1)],
    )
    key_received = send(key_sent, behind)
    query_received = send(query_sent, mates)
    value_ready = (value_part.astype(jnp.float32) + value_received.astype(jnp.float32)).astype(jnp.bfloat16)
    sums = [key_part, key_received, query_part, query_received]
    if ring:
        key_ready, query_ready = call(sums_kernel, 0, sums, [], 2, [], plain=True)
    else:
        sums += [send(graded[0], to_even), send(weighted[0], to_even)]
        by_step = totals[:GROUP].reshape(steps, heads, rows)
        by_step = jnp.pad(by_step, ((0, 0), (0, GROUP - heads), (0, 0))).reshape(steps * GROUP, rows)
        key_ready, query_ready = call(
            functools.partial(third_sums_kernel, heads, scaling), 0, sums, [(steps, 1, by_step)], 2, [],
            plain=True,
        )
    return query_ready, key_ready, value_ready


def program_index(rows, doc_lengths):
    count = doc_lengths.shape[0]
    ends = sum(lax.pad(doc_lengths[: count - n], jnp.int32(0), [(n, 0, 0)]) for n in range(count))
    shift = rows.bit_length() - 1
    first, last = (ends - doc_lengths) >> shift, (ends - 1) >> shift
    spans = (last - first >= 3) & (last & 1 == 0)
    return jnp.sum(jnp.where(spans, (last >> 1) - 1, 0))


def halo_shards(*arguments):
    rows, doc_lengths = arguments[0].shape[1], arguments[-1]
    thirds = range(3, lax.axis_size("seq") - 2, 2)
    programs = [functools.partial(halo_program, third) for third in (None, *thirds)]
    return lax.switch(program_index(rows, doc_lengths), programs, *arguments)


def shards(queries, key_vectors, value_vectors, out_grad, doc_lengths):
    _, rows, width = queries.shape
    seq_size = lax.axis_size("seq")
    longest = rows * seq_size * 3 // 8
    fits = longest <= 3 * rows and seq_size % 2 == 0 and seq_size > 4 and rows == LANES
    heads = width // HEAD
    plan = halo_shards if fits and heads % 4 == 0 and heads <= GROUP else spread_shards
    return plan(queries, key_vectors, value_vectors, out_grad, doc_lengths)


def solution(mesh):
    return jax.shard_map(
        shards,
        mesh=mesh,
        in_specs=(
            P("section", "seq", "dp"),
            P("section", "seq", "dp"),
            P("section", "seq", "dp"),
            P("section", "seq", "dp"),
            P(),
        ),
        out_specs=(P("section", "seq", "dp"), P("section", "seq", "dp"), P("section", "seq", "dp")),
        check_vma=False,
    )
```

```python
import functools
import math
import jax
import jax.numpy as jnp
from jax import lax
from jax.experimental import pallas as pl
from jax.experimental.pallas import tpu as pltpu
from jax.sharding import PartitionSpec as P

HEAD = 224
LANES = 128
FLOOR = -1e30


def pick_slot(stacked, slot):
    return lax.dynamic_index_in_dim(stacked, slot, 0, keepdims=False)


def put_slot(stacked, update, slot):
    return lax.dynamic_update_index_in_dim(stacked, update, slot, 0)


def spread_shards(queries, key_vectors, value_vectors, out_grad, doc_lengths):
    local_rows = queries.shape[1]
    local_width = queries.shape[2]
    head_count = local_width // HEAD
    seq_size = lax.axis_size("seq")
    group = seq_size // head_count
    scaling = HEAD ** (-0.5)

    def spread(matrix):
        shaped = matrix.reshape(local_rows, head_count, 1, HEAD)
        copies = jnp.broadcast_to(shaped, (local_rows, head_count, group, HEAD))
        return copies.reshape(local_rows, seq_size * HEAD)

    query_head, key_head, value_head, cot_head = (
        lax.all_to_all(spread(queries), "seq", split_axis=1, concat_axis=0, tiled=True),
        lax.all_to_all(spread(key_vectors), "seq", split_axis=1, concat_axis=0, tiled=True),
        lax.all_to_all(spread(value_vectors), "seq", split_axis=1, concat_axis=0, tiled=True),
        lax.all_to_all(spread(out_grad), "seq", split_axis=1, concat_axis=0, tiled=True),
    )
    length = key_head.shape[0]
    member = lax.axis_index("seq") % group
    blocks = 2 * group
    block = length // blocks
    bounds = jnp.cumsum(doc_lengths)
    positions = jnp.arange(length, dtype=jnp.int32)
    doc_index = jnp.sum((positions[:, None] >= bounds[None, :]).astype(jnp.int32), axis=1)
    row_list = [member, blocks - 1 - member]
    query_list = []
    cot_list = []
    pos_list = []
    for which in range(2):
        offset = row_list[which] * block
        query_list.append(lax.dynamic_slice_in_dim(query_head, offset, block, 0))
        cot_list.append(lax.dynamic_slice_in_dim(cot_head, offset, block, 0))
        pos_list.append(offset + jnp.arange(block, dtype=jnp.int32))
    query_stack = jnp.stack(query_list)
    cot_stack = jnp.stack(cot_list)
    pos_stack = jnp.stack(pos_list)
    doc_stack = jnp.take(doc_index, pos_stack)
    plan = []
    for number in range(blocks + 1):
        first = number <= member
        slot = jnp.where(first, 0, 1).astype(jnp.int32)
        col_block = jnp.where(first, number, number - member - 1)
        flag = None
        plan.append((slot, col_block, flag))
    row_max = jnp.full((2, block), -jnp.inf, jnp.float32)
    row_sum = jnp.zeros((2, block), jnp.float32)
    stored = []
    for slot, col_block, flag in plan:

        def score_tile(carry, slot=slot, col_block=col_block):
            maxima, totals = carry
            query_rows = pick_slot(query_stack, slot)
            key_rows = lax.dynamic_slice_in_dim(key_head, col_block * block, block, 0)
            col_docs = lax.dynamic_slice_in_dim(doc_index, col_block * block, block, 0)
            col_positions = col_block * block + jnp.arange(block, dtype=jnp.int32)
            raw = jnp.dot(query_rows, key_rows.T, preferred_element_type=jnp.float32) * scaling
            allowed = (pick_slot(doc_stack, slot)[:, None] == col_docs[None, :]) & (
                pick_slot(pos_stack, slot)[:, None] >= col_positions[None, :]
            )
            scores = jnp.where(allowed, raw, -jnp.inf)
            before = pick_slot(maxima, slot)
            after = jnp.maximum(before, jnp.max(scores, axis=1))
            safe = jnp.where(jnp.isfinite(after), after, 0.0)
            total = pick_slot(totals, slot) * jnp.exp(before - safe) + jnp.sum(
                jnp.exp(scores - safe[:, None]), axis=1
            )
            return (scores, put_slot(maxima, after, slot), put_slot(totals, total, slot))

        scores, row_max, row_sum = score_tile((row_max, row_sum))
        stored.append(scores)

    def tile_weights(scores, slot):
        return (
            jnp.exp(scores - pick_slot(row_max, slot)[:, None]) / pick_slot(row_sum, slot)[:, None]
        )

    summed = jnp.zeros((2, block, HEAD), jnp.float32)
    for (slot, col_block, flag), scores in zip(plan, stored):

        def add_values(carry, slot=slot, col_block=col_block, scores=scores):
            rounded = tile_weights(scores, slot).astype(jnp.bfloat16)
            value_rows = lax.dynamic_slice_in_dim(value_head, col_block * block, block, 0)
            term = jnp.dot(rounded, value_rows, preferred_element_type=jnp.float32)
            return put_slot(carry, pick_slot(carry, slot) + term, slot)

        summed = add_values(summed)
    attended = summed.astype(jnp.bfloat16)
    row_dot = jnp.sum(cot_stack.astype(jnp.float32) * attended.astype(jnp.float32), axis=2)
    query_acc = jnp.zeros((2, block, HEAD), jnp.float32)
    key_acc = jnp.zeros((length, HEAD), jnp.float32)
    value_acc = jnp.zeros((length, HEAD), jnp.float32)
    for (slot, col_block, flag), scores in zip(plan, stored):

        def backward_tile(carry, slot=slot, col_block=col_block, scores=scores):
            query_sum, key_sum, value_sum = carry
            weights = tile_weights(scores, slot)
            rounded = weights.astype(jnp.bfloat16)
            query_rows = pick_slot(query_stack, slot)
            cot_rows = pick_slot(cot_stack, slot)
            start = col_block * block
            key_rows = lax.dynamic_slice_in_dim(key_head, start, block, 0)
            value_rows = lax.dynamic_slice_in_dim(value_head, start, block, 0)
            value_term = jnp.dot(rounded.T, cot_rows, preferred_element_type=jnp.float32)
            prob_grad = jnp.dot(cot_rows, value_rows.T, preferred_element_type=jnp.float32)
            score_grad = (
                weights * (prob_grad - pick_slot(row_dot, slot)[:, None]) * scaling
            ).astype(jnp.bfloat16)
            query_term = jnp.dot(score_grad, key_rows, preferred_element_type=jnp.float32)
            key_term = jnp.dot(score_grad.T, query_rows, preferred_element_type=jnp.float32)
            query_sum = put_slot(query_sum, pick_slot(query_sum, slot) + query_term, slot)
            key_sum = lax.dynamic_update_slice_in_dim(
                key_sum, lax.dynamic_slice_in_dim(key_sum, start, block, 0) + key_term, start, 0
            )
            value_sum = lax.dynamic_update_slice_in_dim(
                value_sum,
                lax.dynamic_slice_in_dim(value_sum, start, block, 0) + value_term,
                start,
                0,
            )
            return (query_sum, key_sum, value_sum)

        query_acc, key_acc, value_acc = backward_tile((query_acc, key_acc, value_acc))
    query_rounded = query_acc.astype(jnp.bfloat16)
    key_back, value_back = (
        lax.all_to_all(key_acc, "seq", split_axis=0, concat_axis=1, tiled=True),
        lax.all_to_all(value_acc, "seq", split_axis=0, concat_axis=1, tiled=True),
    )

    def settle(received):
        shaped = received.astype(jnp.float32).reshape(local_rows, head_count, group, HEAD)
        return jnp.sum(shaped, axis=2).reshape(1, local_rows, local_width).astype(jnp.bfloat16)

    query_full = jnp.zeros((length, HEAD), jnp.bfloat16)
    for which in range(2):
        query_full = lax.dynamic_update_slice_in_dim(
            query_full, query_rounded[which], row_list[which] * block, 0
        )
    query_back = lax.all_to_all(query_full, "seq", split_axis=0, concat_axis=1, tiled=True)
    query_out = settle(query_back)
    return (query_out, settle(key_back), settle(value_back))


NT = ((1,), (1,))
NN = ((1,), (0,))
TN = ((0,), (0,))
GROUP = 8


def head_span(head):
    low = head * HEAD // LANES * LANES
    high = -(-(head + 1) * HEAD // LANES) * LANES
    return low, high


def head_mask(head):
    low, high = head_span(head)
    lane = lax.broadcasted_iota(jnp.int32, (1, high - low), 1) + low
    inside = (lane >= head * HEAD) & (lane < (head + 1) * HEAD)
    return inside.astype(jnp.float32).astype(jnp.bfloat16)


def matmul(left, right, dims):
    return lax.dot_general(left, right, (dims, ((), ())), preferred_element_type=jnp.float32)


def stack(values, axis):
    return values[0] if len(values) == 1 else jnp.concatenate(values, axis=axis)


def allowed(lengths_ref, rows, query_block, key_block):
    shape = (rows, rows)
    position = query_block * rows + lax.broadcasted_iota(jnp.int32, shape, 1)
    keys = key_block * rows + lax.broadcasted_iota(jnp.int32, shape, 0)
    start = jnp.zeros_like(position)
    bound = jnp.int32(0)
    for doc in range(lengths_ref.shape[0]):
        bound = bound + lengths_ref[doc]
        start = jnp.where(position >= bound, bound, start)
    return (keys >= start) & (keys <= position)


def make_tile(lengths_ref, rows, queries, keys):
    mask = stack(
        [stack([allowed(lengths_ref, rows, q, k) for _, q in queries], 1) for _, k in keys], 0
    )
    return [slot for slot, _ in queries], [slot for slot, _ in keys], mask


def tile_values(plan, head, queries, keys, products):
    low, high = head_span(head)
    keep = head_mask(head)

    def gather(refs, number, slots):
        return stack([refs[slot][number][0, :, low:high] for slot in slots], 0)

    out = []
    for query_slots, key_slots, _ in plan:
        q = [gather(queries, number, query_slots) for number in range(products)]
        k = [gather(keys, number, key_slots) * keep for number in range(products)]
        out.append((q, k, [matmul(b, a, NT) for a, b in zip(q, k)]))
    return out, keep


def tiles_ahead(heads, plan, queries, keys, products):
    ready = tile_values(plan, 0, queries, keys, products)
    for head in range(heads):
        now = ready
        if head + 1 < heads:
            ready = tile_values(plan, head + 1, queries, keys, products)
        yield head, now


def pair_tile(lengths_ref, rows, me):
    mate = me + 1 - 2 * lax.rem(me, 2)
    return make_tile(lengths_ref, rows, ((0, me), (1, mate)), ((0, me), (1, me - 2)))


def third_tile(third, lengths_ref, rows, me):
    slots, keys, mask = make_tile(lengths_ref, rows, ((2, me + 1),), ((1, me - 2),))
    return slots, keys, mask & (me == third)


def tile_plan(third, lengths_ref, rows, me):
    plan = [pair_tile(lengths_ref, rows, me)]
    return plan if third is None else plan + [third_tile(third, lengths_ref, rows, me)]


def lane_cut(value, number, rows):
    return value[:, number * rows : (number + 1) * rows]


def row_of(group, kinds, kind, head):
    return pl.ds((group * kinds + kind) * GROUP + head, 1)


def per_query(slots, kinds, kind, head, ref):
    return stack([ref[row_of(slot, kinds, kind, head), :] for slot in slots], 1)


def collect_stats(heads, power, step, plan, queries, keys, rows, out_ref, groups):
    for head, (tiles, _) in tiles_ahead(heads, plan, queries, keys, 1):
        for (query_slots, _, mask), (_, _, (raw,)) in zip(plan, tiles):
            raw = jnp.where(mask, raw, FLOOR)
            top = jnp.max(raw, axis=0, keepdims=True)
            sums = jnp.sum(jnp.exp2((raw - top) * power), axis=0, keepdims=True)
            for number, slot in enumerate(query_slots):
                at = step * heads + head
                out_ref[row_of(groups[slot], 2, 0, at), :] = lane_cut(top, number, rows)
                out_ref[row_of(groups[slot], 2, 1, at), :] = lane_cut(sums, number, rows)


def stats_kernel(
    heads, power, place_ref, lengths_ref, q_own, q_mate, k_own, k_back, o_own, v_own, o_copy, v_copy, out_ref
):
    rows, me, step = k_own.shape[1], place_ref[0], pl.program_id(0)
    o_copy[...], v_copy[...] = o_own[...], v_own[...]
    plan = [pair_tile(lengths_ref, rows, me)]
    queries, keys = ((q_own,), (q_mate,)), ((k_own,), (k_back,))
    collect_stats(heads, power, step, plan, queries, keys, rows, out_ref, (0, 1))


def third_stats_kernel(third, heads, power, place_ref, lengths_ref, q_third, k_back, out_ref):
    rows, me, step = k_back.shape[1], place_ref[0], pl.program_id(0)
    plan = [third_tile(third, lengths_ref, rows, me)]
    queries, keys = (None, None, (q_third,)), (None, (k_back,))
    collect_stats(heads, power, step, plan, queries, keys, rows, out_ref, (None, None, 0))


def part_of(ref, kinds, number):
    size = kinds * GROUP
    return ref[number * size : (number + 1) * size, :]


def stats_parts(mine, sent, extra):
    own = [part_of(mine, 2, 0), part_of(sent, 2, 1)]
    mate = [part_of(mine, 2, 1), part_of(sent, 2, 0)]
    if not extra:
        return [own, mate]
    third, near, far, even, odd = extra
    return [own + [near[...]], mate + [far[...]], [third[...], part_of(even, 2, 0), part_of(odd, 2, 1)]]


def dots_parts(mine, sent, extra):
    own = [part_of(mine, 1, 0), part_of(sent, 1, 1)]
    mate = [part_of(mine, 1, 1), part_of(sent, 1, 0)]
    if not extra:
        return [own, mate]
    near, far = extra
    return [
        own + [part_of(near, 1, 2)],
        mate + [part_of(far, 1, 2)],
        [part_of(mine, 1, 2), part_of(near, 1, 0), part_of(far, 1, 1)],
    ]


def merge_stats(scaling, parts):
    split = [(jnp.where(p[GROUP:] > 0, p[:GROUP], FLOOR), p[GROUP:]) for p in parts]
    top = functools.reduce(jnp.maximum, [s[0] for s in split])
    total = sum(jnp.exp((s[0] - top) * scaling) * s[1] for s in split)
    return top + jnp.log(jnp.where(total > 0, total, 1.0)) / scaling


class Emitter:
    def __init__(self, outs):
        self.outs, self.carry = outs, {}

    def emit(self, head, name, value):
        ref = self.outs[name]
        low, high = head_span(head)
        first, last = head * HEAD % LANES == 0, (head + 1) * HEAD % LANES == 0
        start, stop = low, high
        if not first:
            shared = value[:, :LANES] + self.carry.pop(name)
            ref[0, :, low : low + LANES] = shared.astype(jnp.bfloat16)
            start = low + LANES
        if not last:
            self.carry[name] = value[:, high - LANES - low :]
            stop = high - LANES
        if stop > start:
            ref[0, :, start:stop] = value[:, start - low : stop - low].astype(jnp.bfloat16)


def add_rows(sums, kind, slots, value, rows):
    for number, slot in enumerate(slots):
        piece = value[number * rows : (number + 1) * rows]
        name = (kind, slot)
        sums[name] = sums[name] + piece if name in sums else piece


def split_refs(third, refs):
    count = 2 if third is None else 3
    queries = [(refs[2 * n], refs[2 * n + 1]) for n in range(count)]
    keys = [(refs[2 * n], refs[2 * n + 1]) for n in range(count, count + 2)]
    return queries, keys, refs[2 * count + 4 :]


def values_kernel(third, heads, scaling, power, place_ref, lengths_ref, *refs):
    count, last = (2, -3) if third is None else (3, -4)
    queries = [(refs[2 * n], refs[2 * n + 1]) for n in range(count)]
    refs, outs = refs[2 * count : last], refs[last:]
    keys, shift_ref = [(refs[0],), (refs[1],)], outs[-1]
    rows, me, step = keys[0][0].shape[1], place_ref[0], pl.program_id(0)
    plan = tile_plan(third, lengths_ref, rows, me)
    for number, parts in enumerate(stats_parts(refs[2], refs[3], refs[4:])):
        shift_ref[number * GROUP : (number + 1) * GROUP, :] = merge_stats(scaling, parts)
    out = Emitter(dict(zip((("v", 0), ("v", 1), ("b", 2)), outs[:-1])))
    for head, (tiles, keep) in tiles_ahead(heads, plan, queries, keys, 1):
        low, high = head_span(head)
        sums = {}
        for (query_slots, key_slots, mask), (_, (k,), (raw,)) in zip(plan, tiles):
            shift = per_query(query_slots, 1, 0, step * heads + head, shift_ref)
            weight = jnp.where(mask, jnp.exp2((raw - shift) * power), 0.0).astype(jnp.bfloat16)
            o = stack([queries[slot][1][0, :, low:high] for slot in query_slots], 0) * keep
            add_rows(sums, "v", key_slots, matmul(weight, o, NN), rows)
            if query_slots == [2]:
                add_rows(sums, "b", query_slots, matmul(weight, k, TN), rows)
        for name, value in sums.items():
            out.emit(head, name, value)


def dots_kernel(third, heads, power, place_ref, lengths_ref, *refs):
    queries, keys, (shift_ref, *outs) = split_refs(third, refs)
    dots_ref = outs[-1]
    rows, me, step = keys[0][0].shape[1], place_ref[0], pl.program_id(0)
    plan = tile_plan(third, lengths_ref, rows, me)
    out = Emitter(dict(zip((("a", 2),), outs[:-1])))
    for head, (tiles, _) in tiles_ahead(heads, plan, queries, keys, 2):
        at = step * heads + head
        for (query_slots, _, mask), (_, (k, _), (raw, grads)) in zip(plan, tiles):
            shift = per_query(query_slots, 1, 0, at, shift_ref)
            product = jnp.where(mask, jnp.exp2((raw - shift) * power), 0.0) * grads
            dots = jnp.sum(product, axis=0, keepdims=True)
            for number, slot in enumerate(query_slots):
                dots_ref[row_of(slot, 1, 0, at), :] = lane_cut(dots, number, rows)
            if query_slots == [2]:
                out.emit(head, ("a", 2), matmul(product.astype(jnp.bfloat16), k, TN))


def keys_kernel(third, heads, scaling, power, place_ref, lengths_ref, *refs):
    queries, keys, refs = split_refs(third, refs)
    (shift_ref, mine, sent, *extra), outs = refs[:-5], refs[-5:]
    total_ref = outs[-1]
    rows, me, step = keys[0][0].shape[1], place_ref[0], pl.program_id(0)
    plan = tile_plan(third, lengths_ref, rows, me)
    for number, parts in enumerate(dots_parts(mine, sent, extra)):
        total_ref[number * GROUP : (number + 1) * GROUP, :] = sum(parts)
    out = Emitter(dict(zip((("k", 0), ("k", 1), ("q", 0), ("q", 1)), outs[:-1])))
    for head, (tiles, keep) in tiles_ahead(heads, plan, queries, keys, 2):
        at = step * heads + head
        sums = {}
        for (query_slots, key_slots, mask), ((q, _), (k, _), (raw, grads)) in zip(plan, tiles):
            shift = per_query(query_slots, 1, 0, at, shift_ref)
            dots = per_query(query_slots, 1, 0, at, total_ref)
            weight = jnp.where(mask, jnp.exp2((raw - shift) * power), 0.0)
            slope = (weight * (grads - dots) * scaling).astype(jnp.bfloat16)
            add_rows(sums, "k", key_slots, matmul(slope, q * keep, NN), rows)
            if query_slots != [2]:
                add_rows(sums, "q", query_slots, matmul(slope, k, TN), rows)
        for name, value in sums.items():
            out.emit(head, name, value)


def add_refs(*refs):
    return sum(ref[...].astype(jnp.float32) for ref in refs)


def sums_kernel(key_part, key_sent, query_part, query_sent, key_out, query_out):
    key_out[...] = add_refs(key_part, key_sent).astype(jnp.bfloat16)
    query_out[...] = add_refs(query_part, query_sent).astype(jnp.bfloat16)


def third_sums_kernel(
    heads, scaling, key_part, key_sent, query_part, query_sent, a_sent, b_sent, total_ref, key_out, query_out
):
    key_out[...] = add_refs(key_part, key_sent).astype(jnp.bfloat16)
    step = pl.program_id(0)
    rows, part = query_out.shape[1:]
    spread = total_ref[pl.ds(pl.multiple_of(step * GROUP, GROUP), GROUP), :]
    columns = jnp.concatenate([spread, jnp.zeros((LANES - GROUP, rows), jnp.float32)], 0).T
    lane = lax.broadcasted_iota(jnp.int32, (rows, part), 1)
    dots = jnp.zeros((rows, part), jnp.float32)
    for head in range(heads):
        inside = (lane >= head * HEAD) & (lane < (head + 1) * HEAD)
        dots = jnp.where(inside, columns[:, head : head + 1], dots)
    extra = (a_sent[0].astype(jnp.float32) - dots * b_sent[0].astype(jnp.float32)) * scaling
    query_out[0] = (add_refs(query_part, query_sent)[0] + extra).astype(jnp.bfloat16)


def halo_program(third, queries, key_vectors, value_vectors, out_grad, doc_lengths):
    _, rows, width = queries.shape
    seq_size = lax.axis_size("seq")
    me = lax.axis_index("seq").astype(jnp.int32)
    scaling = HEAD ** (-0.5)
    power = scaling * math.log2(math.e)
    steps = width // HEAD // 4
    part = width // steps
    heads = part // HEAD
    count = 2 if third is None else 3
    devices = range(seq_size)
    mates = [(s, s ^ 1) for s in devices]
    ring = third is None
    chain = [(s, s + 2) for s in devices if s + 2 < seq_size]
    ahead = [(s, (s + 2) % seq_size) for s in devices] if ring else chain
    behind = [(s, s - 2) for s in devices if s >= 2]
    if not ring:
        relay, to_odd = [(third + 2, third)], [(third, third + 2)]
        from_even, to_even = [(third + 1, third)], [(third, third + 1)]
        near, far = from_even + to_even, relay + to_odd

    def send(value, pairs):
        return lax.ppermute(value, "seq", pairs)

    smem = pl.BlockSpec(memory_space=pltpu.SMEM)
    wide = pl.BlockSpec((1, rows, part), lambda step: (0, 0, step))
    wide_shape = jax.ShapeDtypeStruct((1, rows, width), jnp.bfloat16)

    def slim(groups, kinds):
        return pl.BlockSpec((groups * kinds * GROUP, rows), lambda step: (0, 0))

    def slim_shape(groups, kinds):
        return jax.ShapeDtypeStruct((groups * kinds * GROUP, rows), jnp.float32)

    def call(kernel, products, wides, slims, outs, slim_outs, plain=False, scratch=()):
        flops = 2 * products * 4 * rows * rows * width * 3 // 2
        lead = [] if plain else [me[None], doc_lengths]
        return pl.pallas_call(
            kernel,
            grid=(steps,),
            in_specs=[smem] * len(lead)
            + [wide] * len(wides)
            + [slim(groups, kinds) for groups, kinds, _ in slims],
            out_specs=[wide] * outs + [slim(*sizes) for sizes in slim_outs],
            out_shape=[wide_shape] * outs + [slim_shape(*sizes) for sizes in slim_outs],
            scratch_shapes=[pltpu.VMEM((groups * GROUP, rows), jnp.float32) for groups in scratch],
            compiler_params=pltpu.CompilerParams(vmem_limit_bytes=20 * 1024 * 1024),
            cost_estimate=pl.CostEstimate(
                flops=flops, bytes_accessed=20 * rows * width, transcendentals=0
            ),
        )(*lead, *wides, *[value for _, _, value in slims])

    query_mate = send(queries, mates)
    key_back = send(key_vectors, chain)
    grad_mate = send(out_grad, mates)
    value_back = send(value_vectors, ahead)
    query_rows, grad_rows = [queries, query_mate], [out_grad, grad_mate]
    grad_own, value_own, stats = call(
        functools.partial(stats_kernel, heads, power), 1,
        [*query_rows, key_vectors, key_back, out_grad, value_vectors], [], 2, [(2, 2)],
    )
    stats_in = [(2, 2, stats), (2, 2, send(stats, mates))]
    grad_rows[0] = grad_own
    if not ring:
        query_rows.append(send(query_mate, relay))
        held, _ = lax.optimization_barrier((grad_mate, stats))
        grad_rows.append(send(held, relay))
        query_third, _ = lax.optimization_barrier((query_rows[2], value_back))
        (third_stats,) = call(
            functools.partial(third_stats_kernel, third, heads, power), 1,
            [query_third, key_back], [], 0, [(1, 2)],
        )
        stats_in += [(1, 2, third_stats), (1, 2, send(third_stats, to_even)), (1, 2, send(third_stats, to_odd))]
        stats_in += [(2, 2, send(stats, from_even)), (2, 2, send(stats, relay))]
    tensors = [t for two in zip(query_rows, grad_rows) for t in two]
    value_part, value_sent, *weighted, shift = call(
        functools.partial(values_kernel, third, heads, scaling, power), 2,
        tensors + [key_vectors, key_back], stats_in, count, [(count, 1)],
    )
    tensors += [key_vectors, value_own, key_back, value_back]
    *graded, dots = call(
        functools.partial(dots_kernel, third, heads, power), 2, tensors, [(count, 1, shift)],
        count - 2, [(count, 1)],
    )
    value_received = send(value_sent, behind)
    dots_in = [(count, 1, shift), (count, 1, dots), (count, 1, send(dots, mates))]
    if not ring:
        dots_in += [(count, 1, send(dots, pairs)) for pairs in (near, far)]
    key_part, key_sent, query_part, query_sent, *totals = call(
        functools.partial(keys_kernel, third, heads, scaling, power), 4, tensors, dots_in,
        4, [] if ring else [(count, 1)], scratch=[count] if ring else [],
    )
    key_received = send(key_sent, behind)
    query_received = send(query_sent, mates)
    value_ready = (value_part.astype(jnp.float32) + value_received.astype(jnp.float32)).astype(jnp.bfloat16)
    sums = [key_part, key_received, query_part, query_received]
    if ring:
        key_ready, query_ready = call(sums_kernel, 0, sums, [], 2, [], plain=True)
    else:
        sums += [send(graded[0], to_even), send(weighted[0], to_even)]
        by_step = totals[0][:GROUP].reshape(steps, heads, rows)
        by_step = jnp.pad(by_step, ((0, 0), (0, GROUP - heads), (0, 0))).reshape(steps * GROUP, rows)
        key_ready, query_ready = call(
            functools.partial(third_sums_kernel, heads, scaling), 0, sums, [(steps, 1, by_step)], 2, [],
            plain=True,
        )
    return query_ready, key_ready, value_ready


def program_index(rows, doc_lengths):
    count = doc_lengths.shape[0]
    ends = sum(lax.pad(doc_lengths[: count - n], jnp.int32(0), [(n, 0, 0)]) for n in range(count))
    shift = rows.bit_length() - 1
    first, last = (ends - doc_lengths) >> shift, (ends - 1) >> shift
    spans = (last - first >= 3) & (last & 1 == 0)
    return jnp.sum(jnp.where(spans, (last >> 1) - 1, 0))


def halo_shards(*arguments):
    rows, doc_lengths = arguments[0].shape[1], arguments[-1]
    thirds = range(3, lax.axis_size("seq") - 2, 2)
    programs = [functools.partial(halo_program, third) for third in (None, *thirds)]
    return lax.switch(program_index(rows, doc_lengths), programs, *arguments)


def shards(queries, key_vectors, value_vectors, out_grad, doc_lengths):
    _, rows, width = queries.shape
    seq_size = lax.axis_size("seq")
    longest = rows * seq_size * 3 // 8
    fits = longest <= 3 * rows and seq_size % 2 == 0 and seq_size > 4 and rows == LANES
    heads = width // HEAD
    plan = halo_shards if fits and heads % 4 == 0 and heads <= GROUP else spread_shards
    return plan(queries, key_vectors, value_vectors, out_grad, doc_lengths)


def solution(mesh):
    return jax.shard_map(
        shards,
        mesh=mesh,
        in_specs=(
            P("section", "seq", "dp"),
            P("section", "seq", "dp"),
            P("section", "seq", "dp"),
            P("section", "seq", "dp"),
            P(),
        ),
        out_specs=(P("section", "seq", "dp"), P("section", "seq", "dp"), P("section", "seq", "dp")),
        check_vma=False,
    )
```

```python
import functools
import math
import jax
import jax.numpy as jnp
from jax import lax
from jax.experimental import pallas as pl
from jax.experimental.pallas import tpu as pltpu
from jax.sharding import PartitionSpec as P

HEAD = 224
LANES = 128
FLOOR = -1e30


def pick_slot(stacked, slot):
    return lax.dynamic_index_in_dim(stacked, slot, 0, keepdims=False)


def put_slot(stacked, update, slot):
    return lax.dynamic_update_index_in_dim(stacked, update, slot, 0)


def spread_shards(queries, key_vectors, value_vectors, out_grad, doc_lengths):
    local_rows = queries.shape[1]
    local_width = queries.shape[2]
    head_count = local_width // HEAD
    seq_size = lax.axis_size("seq")
    group = seq_size // head_count
    scaling = HEAD ** (-0.5)

    def spread(matrix):
        shaped = matrix.reshape(local_rows, head_count, 1, HEAD)
        copies = jnp.broadcast_to(shaped, (local_rows, head_count, group, HEAD))
        return copies.reshape(local_rows, seq_size * HEAD)

    query_head, key_head, value_head, cot_head = (
        lax.all_to_all(spread(queries), "seq", split_axis=1, concat_axis=0, tiled=True),
        lax.all_to_all(spread(key_vectors), "seq", split_axis=1, concat_axis=0, tiled=True),
        lax.all_to_all(spread(value_vectors), "seq", split_axis=1, concat_axis=0, tiled=True),
        lax.all_to_all(spread(out_grad), "seq", split_axis=1, concat_axis=0, tiled=True),
    )
    length = key_head.shape[0]
    member = lax.axis_index("seq") % group
    blocks = 2 * group
    block = length // blocks
    bounds = jnp.cumsum(doc_lengths)
    positions = jnp.arange(length, dtype=jnp.int32)
    doc_index = jnp.sum((positions[:, None] >= bounds[None, :]).astype(jnp.int32), axis=1)
    row_list = [member, blocks - 1 - member]
    query_list = []
    cot_list = []
    pos_list = []
    for which in range(2):
        offset = row_list[which] * block
        query_list.append(lax.dynamic_slice_in_dim(query_head, offset, block, 0))
        cot_list.append(lax.dynamic_slice_in_dim(cot_head, offset, block, 0))
        pos_list.append(offset + jnp.arange(block, dtype=jnp.int32))
    query_stack = jnp.stack(query_list)
    cot_stack = jnp.stack(cot_list)
    pos_stack = jnp.stack(pos_list)
    doc_stack = jnp.take(doc_index, pos_stack)
    plan = []
    for number in range(blocks + 1):
        first = number <= member
        slot = jnp.where(first, 0, 1).astype(jnp.int32)
        col_block = jnp.where(first, number, number - member - 1)
        flag = None
        plan.append((slot, col_block, flag))
    row_max = jnp.full((2, block), -jnp.inf, jnp.float32)
    row_sum = jnp.zeros((2, block), jnp.float32)
    stored = []
    for slot, col_block, flag in plan:

        def score_tile(carry, slot=slot, col_block=col_block):
            maxima, totals = carry
            query_rows = pick_slot(query_stack, slot)
            key_rows = lax.dynamic_slice_in_dim(key_head, col_block * block, block, 0)
            col_docs = lax.dynamic_slice_in_dim(doc_index, col_block * block, block, 0)
            col_positions = col_block * block + jnp.arange(block, dtype=jnp.int32)
            raw = jnp.dot(query_rows, key_rows.T, preferred_element_type=jnp.float32) * scaling
            allowed = (pick_slot(doc_stack, slot)[:, None] == col_docs[None, :]) & (
                pick_slot(pos_stack, slot)[:, None] >= col_positions[None, :]
            )
            scores = jnp.where(allowed, raw, -jnp.inf)
            before = pick_slot(maxima, slot)
            after = jnp.maximum(before, jnp.max(scores, axis=1))
            safe = jnp.where(jnp.isfinite(after), after, 0.0)
            total = pick_slot(totals, slot) * jnp.exp(before - safe) + jnp.sum(
                jnp.exp(scores - safe[:, None]), axis=1
            )
            return (scores, put_slot(maxima, after, slot), put_slot(totals, total, slot))

        scores, row_max, row_sum = score_tile((row_max, row_sum))
        stored.append(scores)

    def tile_weights(scores, slot):
        return (
            jnp.exp(scores - pick_slot(row_max, slot)[:, None]) / pick_slot(row_sum, slot)[:, None]
        )

    summed = jnp.zeros((2, block, HEAD), jnp.float32)
    for (slot, col_block, flag), scores in zip(plan, stored):

        def add_values(carry, slot=slot, col_block=col_block, scores=scores):
            rounded = tile_weights(scores, slot).astype(jnp.bfloat16)
            value_rows = lax.dynamic_slice_in_dim(value_head, col_block * block, block, 0)
            term = jnp.dot(rounded, value_rows, preferred_element_type=jnp.float32)
            return put_slot(carry, pick_slot(carry, slot) + term, slot)

        summed = add_values(summed)
    attended = summed.astype(jnp.bfloat16)
    row_dot = jnp.sum(cot_stack.astype(jnp.float32) * attended.astype(jnp.float32), axis=2)
    query_acc = jnp.zeros((2, block, HEAD), jnp.float32)
    key_acc = jnp.zeros((length, HEAD), jnp.float32)
    value_acc = jnp.zeros((length, HEAD), jnp.float32)
    for (slot, col_block, flag), scores in zip(plan, stored):

        def backward_tile(carry, slot=slot, col_block=col_block, scores=scores):
            query_sum, key_sum, value_sum = carry
            weights = tile_weights(scores, slot)
            rounded = weights.astype(jnp.bfloat16)
            query_rows = pick_slot(query_stack, slot)
            cot_rows = pick_slot(cot_stack, slot)
            start = col_block * block
            key_rows = lax.dynamic_slice_in_dim(key_head, start, block, 0)
            value_rows = lax.dynamic_slice_in_dim(value_head, start, block, 0)
            value_term = jnp.dot(rounded.T, cot_rows, preferred_element_type=jnp.float32)
            prob_grad = jnp.dot(cot_rows, value_rows.T, preferred_element_type=jnp.float32)
            score_grad = (
                weights * (prob_grad - pick_slot(row_dot, slot)[:, None]) * scaling
            ).astype(jnp.bfloat16)
            query_term = jnp.dot(score_grad, key_rows, preferred_element_type=jnp.float32)
            key_term = jnp.dot(score_grad.T, query_rows, preferred_element_type=jnp.float32)
            query_sum = put_slot(query_sum, pick_slot(query_sum, slot) + query_term, slot)
            key_sum = lax.dynamic_update_slice_in_dim(
                key_sum, lax.dynamic_slice_in_dim(key_sum, start, block, 0) + key_term, start, 0
            )
            value_sum = lax.dynamic_update_slice_in_dim(
                value_sum,
                lax.dynamic_slice_in_dim(value_sum, start, block, 0) + value_term,
                start,
                0,
            )
            return (query_sum, key_sum, value_sum)

        query_acc, key_acc, value_acc = backward_tile((query_acc, key_acc, value_acc))
    query_rounded = query_acc.astype(jnp.bfloat16)
    key_back, value_back = (
        lax.all_to_all(key_acc, "seq", split_axis=0, concat_axis=1, tiled=True),
        lax.all_to_all(value_acc, "seq", split_axis=0, concat_axis=1, tiled=True),
    )

    def settle(received):
        shaped = received.astype(jnp.float32).reshape(local_rows, head_count, group, HEAD)
        return jnp.sum(shaped, axis=2).reshape(1, local_rows, local_width).astype(jnp.bfloat16)

    query_full = jnp.zeros((length, HEAD), jnp.bfloat16)
    for which in range(2):
        query_full = lax.dynamic_update_slice_in_dim(
            query_full, query_rounded[which], row_list[which] * block, 0
        )
    query_back = lax.all_to_all(query_full, "seq", split_axis=0, concat_axis=1, tiled=True)
    query_out = settle(query_back)
    return (query_out, settle(key_back), settle(value_back))


NT = ((1,), (1,))
NN = ((1,), (0,))
TN = ((0,), (0,))
GROUP = 8


def head_span(head):
    low = head * HEAD // LANES * LANES
    high = -(-(head + 1) * HEAD // LANES) * LANES
    return low, high


def head_mask(head):
    low, high = head_span(head)
    lane = lax.broadcasted_iota(jnp.int32, (1, high - low), 1) + low
    inside = (lane >= head * HEAD) & (lane < (head + 1) * HEAD)
    return inside.astype(jnp.float32).astype(jnp.bfloat16)


def matmul(left, right, dims):
    return lax.dot_general(left, right, (dims, ((), ())), preferred_element_type=jnp.float32)


def stack(values, axis):
    return values[0] if len(values) == 1 else jnp.concatenate(values, axis=axis)


def allowed(lengths_ref, rows, query_block, key_block):
    shape = (rows, rows)
    position = query_block * rows + lax.broadcasted_iota(jnp.int32, shape, 1)
    keys = key_block * rows + lax.broadcasted_iota(jnp.int32, shape, 0)
    start = jnp.zeros_like(position)
    bound = jnp.int32(0)
    for doc in range(1, lengths_ref.shape[0]):
        bound = bound + lengths_ref[doc]
        start = jnp.where(position >= bound, bound, start)
    return (keys >= start) & (keys <= position)


def make_tile(lengths_ref, rows, queries, keys):
    mask = stack(
        [stack([allowed(lengths_ref, rows, q, k) for _, q in queries], 1) for _, k in keys], 0
    )
    return [slot for slot, _ in queries], [slot for slot, _ in keys], mask


def tile_values(plan, head, queries, keys, products):
    low, high = head_span(head)
    keep = head_mask(head)

    def gather(refs, number, slots):
        return stack([refs[slot][number][0, :, low:high] for slot in slots], 0)

    out = []
    for query_slots, key_slots, _ in plan:
        q = [gather(queries, number, query_slots) for number in range(products)]
        k = [gather(keys, number, key_slots) * keep for number in range(products)]
        out.append((q, k, [matmul(b, a, NT) for a, b in zip(q, k)]))
    return out, keep


def tiles_ahead(heads, plan, queries, keys, products):
    ready = tile_values(plan, 0, queries, keys, products)
    for head in range(heads):
        now = ready
        if head + 1 < heads:
            ready = tile_values(plan, head + 1, queries, keys, products)
        yield head, now


def pair_tile(lengths_ref, rows, me):
    mate = me + 1 - 2 * lax.rem(me, 2)
    return make_tile(lengths_ref, rows, ((0, me), (1, mate)), ((0, me), (1, me - 2)))


def third_tile(third, lengths_ref, rows, me):
    slots, keys, mask = make_tile(lengths_ref, rows, ((2, me + 1),), ((1, me - 2),))
    return slots, keys, mask & (me == third)


def tile_plan(third, lengths_ref, rows, me):
    plan = [pair_tile(lengths_ref, rows, me)]
    return plan if third is None else plan + [third_tile(third, lengths_ref, rows, me)]


def lane_cut(value, number, rows):
    return value[:, number * rows : (number + 1) * rows]


def row_of(group, kinds, kind, head):
    return pl.ds((group * kinds + kind) * GROUP + head, 1)


def per_query(slots, kinds, kind, head, ref):
    return stack([ref[row_of(slot, kinds, kind, head), :] for slot in slots], 1)


def collect_stats(heads, power, step, plan, queries, keys, rows, out_ref, groups):
    for head, (tiles, _) in tiles_ahead(heads, plan, queries, keys, 1):
        for (query_slots, _, mask), (_, _, (raw,)) in zip(plan, tiles):
            raw = jnp.where(mask, raw, FLOOR)
            top = jnp.max(raw, axis=0, keepdims=True)
            sums = jnp.sum(jnp.exp2((raw - top) * power), axis=0, keepdims=True)
            for number, slot in enumerate(query_slots):
                at = step * heads + head
                out_ref[row_of(groups[slot], 2, 0, at), :] = lane_cut(top, number, rows)
                out_ref[row_of(groups[slot], 2, 1, at), :] = lane_cut(sums, number, rows)


def stats_kernel(
    heads, power, place_ref, lengths_ref, q_own, q_mate, k_own, k_back, o_own, v_own, o_copy, v_copy, out_ref
):
    rows, me, step = k_own.shape[1], place_ref[0], pl.program_id(0)
    o_copy[...], v_copy[...] = o_own[...], v_own[...]
    plan = [pair_tile(lengths_ref, rows, me)]
    queries, keys = ((q_own,), (q_mate,)), ((k_own,), (k_back,))
    collect_stats(heads, power, step, plan, queries, keys, rows, out_ref, (0, 1))


def third_stats_kernel(third, heads, power, place_ref, lengths_ref, q_third, k_back, out_ref):
    rows, me, step = k_back.shape[1], place_ref[0], pl.program_id(0)
    plan = [third_tile(third, lengths_ref, rows, me)]
    queries, keys = (None, None, (q_third,)), (None, (k_back,))
    collect_stats(heads, power, step, plan, queries, keys, rows, out_ref, (None, None, 0))


def part_of(ref, kinds, number):
    size = kinds * GROUP
    return ref[number * size : (number + 1) * size, :]


def stats_parts(mine, sent, extra):
    own = [part_of(mine, 2, 0), part_of(sent, 2, 1)]
    mate = [part_of(mine, 2, 1), part_of(sent, 2, 0)]
    if not extra:
        return [own, mate]
    third, near, far, even, odd = extra
    return [own + [near[...]], mate + [far[...]], [third[...], part_of(even, 2, 0), part_of(odd, 2, 1)]]


def dots_parts(mine, sent, extra):
    own = [part_of(mine, 1, 0), part_of(sent, 1, 1)]
    mate = [part_of(mine, 1, 1), part_of(sent, 1, 0)]
    if not extra:
        return [own, mate]
    near, far = extra
    return [
        own + [part_of(near, 1, 2)],
        mate + [part_of(far, 1, 2)],
        [part_of(mine, 1, 2), part_of(near, 1, 0), part_of(far, 1, 1)],
    ]


def merge_stats(scaling, parts):
    split = [(jnp.where(p[GROUP:] > 0, p[:GROUP], FLOOR), p[GROUP:]) for p in parts]
    top = functools.reduce(jnp.maximum, [s[0] for s in split])
    total = sum(jnp.exp((s[0] - top) * scaling) * s[1] for s in split)
    return top + jnp.log(jnp.where(total > 0, total, 1.0)) / scaling


class Emitter:
    def __init__(self, outs):
        self.outs, self.carry = outs, {}

    def emit(self, head, name, value):
        ref = self.outs[name]
        low, high = head_span(head)
        first, last = head * HEAD % LANES == 0, (head + 1) * HEAD % LANES == 0
        start, stop = low, high
        if not first:
            shared = value[:, :LANES] + self.carry.pop(name)
            ref[0, :, low : low + LANES] = shared.astype(jnp.bfloat16)
            start = low + LANES
        if not last:
            self.carry[name] = value[:, high - LANES - low :]
            stop = high - LANES
        if stop > start:
            ref[0, :, start:stop] = value[:, start - low : stop - low].astype(jnp.bfloat16)


def add_rows(sums, kind, slots, value, rows):
    for number, slot in enumerate(slots):
        piece = value[number * rows : (number + 1) * rows]
        name = (kind, slot)
        sums[name] = sums[name] + piece if name in sums else piece


def split_refs(third, refs):
    count = 2 if third is None else 3
    queries = [(refs[2 * n], refs[2 * n + 1]) for n in range(count)]
    keys = [(refs[2 * n], refs[2 * n + 1]) for n in range(count, count + 2)]
    return queries, keys, refs[2 * count + 4 :]


def values_kernel(third, heads, scaling, power, place_ref, lengths_ref, *refs):
    count, last = (2, -3) if third is None else (3, -4)
    queries = [(refs[2 * n], refs[2 * n + 1]) for n in range(count)]
    refs, outs = refs[2 * count : last], refs[last:]
    keys, shift_ref = [(refs[0],), (refs[1],)], outs[-1]
    rows, me, step = keys[0][0].shape[1], place_ref[0], pl.program_id(0)
    plan = tile_plan(third, lengths_ref, rows, me)
    for number, parts in enumerate(stats_parts(refs[2], refs[3], refs[4:])):
        shift_ref[number * GROUP : (number + 1) * GROUP, :] = merge_stats(scaling, parts)
    out = Emitter(dict(zip((("v", 0), ("v", 1), ("b", 2)), outs[:-1])))
    for head, (tiles, keep) in tiles_ahead(heads, plan, queries, keys, 1):
        low, high = head_span(head)
        sums = {}
        for (query_slots, key_slots, mask), (_, (k,), (raw,)) in zip(plan, tiles):
            shift = per_query(query_slots, 1, 0, step * heads + head, shift_ref)
            weight = jnp.where(mask, jnp.exp2((raw - shift) * power), 0.0).astype(jnp.bfloat16)
            o = stack([queries[slot][1][0, :, low:high] for slot in query_slots], 0) * keep
            add_rows(sums, "v", key_slots, matmul(weight, o, NN), rows)
            if query_slots == [2]:
                add_rows(sums, "b", query_slots, matmul(weight, k, TN), rows)
        for name, value in sums.items():
            out.emit(head, name, value)


def dots_kernel(third, heads, power, place_ref, lengths_ref, *refs):
    queries, keys, (shift_ref, *outs) = split_refs(third, refs)
    dots_ref = outs[-1]
    rows, me, step = keys[0][0].shape[1], place_ref[0], pl.program_id(0)
    plan = tile_plan(third, lengths_ref, rows, me)
    out = Emitter(dict(zip((("a", 2),), outs[:-1])))
    for head, (tiles, _) in tiles_ahead(heads, plan, queries, keys, 2):
        at = step * heads + head
        for (query_slots, _, mask), (_, (k, _), (raw, grads)) in zip(plan, tiles):
            shift = per_query(query_slots, 1, 0, at, shift_ref)
            product = jnp.where(mask, jnp.exp2((raw - shift) * power), 0.0) * grads
            dots = jnp.sum(product, axis=0, keepdims=True)
            for number, slot in enumerate(query_slots):
                dots_ref[row_of(slot, 1, 0, at), :] = lane_cut(dots, number, rows)
            if query_slots == [2]:
                out.emit(head, ("a", 2), matmul(product.astype(jnp.bfloat16), k, TN))


def keys_kernel(third, heads, scaling, power, place_ref, lengths_ref, *refs):
    queries, keys, refs = split_refs(third, refs)
    (shift_ref, mine, sent, *extra), outs = refs[:-5], refs[-5:]
    total_ref = outs[-1]
    rows, me, step = keys[0][0].shape[1], place_ref[0], pl.program_id(0)
    plan = tile_plan(third, lengths_ref, rows, me)
    for number, parts in enumerate(dots_parts(mine, sent, extra)):
        total_ref[number * GROUP : (number + 1) * GROUP, :] = sum(parts)
    out = Emitter(dict(zip((("k", 0), ("k", 1), ("q", 0), ("q", 1)), outs[:-1])))
    for head, (tiles, keep) in tiles_ahead(heads, plan, queries, keys, 2):
        at = step * heads + head
        sums = {}
        for (query_slots, key_slots, mask), ((q, _), (k, _), (raw, grads)) in zip(plan, tiles):
            shift = per_query(query_slots, 1, 0, at, shift_ref)
            dots = per_query(query_slots, 1, 0, at, total_ref)
            weight = jnp.where(mask, jnp.exp2((raw - shift) * power), 0.0)
            slope = (weight * (grads - dots) * scaling).astype(jnp.bfloat16)
            add_rows(sums, "k", key_slots, matmul(slope, q * keep, NN), rows)
            if query_slots != [2]:
                add_rows(sums, "q", query_slots, matmul(slope, k, TN), rows)
        for name, value in sums.items():
            out.emit(head, name, value)


def add_refs(*refs):
    return sum(ref[...].astype(jnp.float32) for ref in refs)


def sums_kernel(key_part, key_sent, query_part, query_sent, key_out, query_out):
    key_out[...] = add_refs(key_part, key_sent).astype(jnp.bfloat16)
    query_out[...] = add_refs(query_part, query_sent).astype(jnp.bfloat16)


def third_sums_kernel(
    heads, scaling, key_part, key_sent, query_part, query_sent, a_sent, b_sent, total_ref, key_out, query_out
):
    key_out[...] = add_refs(key_part, key_sent).astype(jnp.bfloat16)
    step = pl.program_id(0)
    rows, part = query_out.shape[1:]
    spread = total_ref[pl.ds(pl.multiple_of(step * GROUP, GROUP), GROUP), :]
    columns = jnp.concatenate([spread, jnp.zeros((LANES - GROUP, rows), jnp.float32)], 0).T
    lane = lax.broadcasted_iota(jnp.int32, (rows, part), 1)
    dots = jnp.zeros((rows, part), jnp.float32)
    for head in range(heads):
        inside = (lane >= head * HEAD) & (lane < (head + 1) * HEAD)
        dots = jnp.where(inside, columns[:, head : head + 1], dots)
    extra = (a_sent[0].astype(jnp.float32) - dots * b_sent[0].astype(jnp.float32)) * scaling
    query_out[0] = (add_refs(query_part, query_sent)[0] + extra).astype(jnp.bfloat16)


def halo_program(third, queries, key_vectors, value_vectors, out_grad, facts):
    _, rows, width = queries.shape
    seq_size = lax.axis_size("seq")
    me = lax.axis_index("seq").astype(jnp.int32)
    scaling = HEAD ** (-0.5)
    power = scaling * math.log2(math.e)
    steps = width // HEAD // 4
    part = width // steps
    heads = part // HEAD
    count = 2 if third is None else 3
    devices = range(seq_size)
    mates = [(s, s ^ 1) for s in devices]
    ring = third is None
    chain = [(s, s + 2) for s in devices if s + 2 < seq_size]
    ahead = [(s, (s + 2) % seq_size) for s in devices] if ring else chain
    behind = [(s, s - 2) for s in devices if s >= 2]
    if not ring:
        relay, to_odd = [(third + 2, third)], [(third, third + 2)]
        from_even, to_even = [(third + 1, third)], [(third, third + 1)]
        near, far = from_even + to_even, relay + to_odd

    def send(value, pairs):
        return lax.ppermute(value, "seq", pairs)

    smem = pl.BlockSpec(memory_space=pltpu.SMEM)
    wide = pl.BlockSpec((1, rows, part), lambda step: (0, 0, step))
    wide_shape = jax.ShapeDtypeStruct((1, rows, width), jnp.bfloat16)

    def slim(groups, kinds):
        return pl.BlockSpec((groups * kinds * GROUP, rows), lambda step: (0, 0))

    def slim_shape(groups, kinds):
        return jax.ShapeDtypeStruct((groups * kinds * GROUP, rows), jnp.float32)

    def call(kernel, products, wides, slims, outs, slim_outs, plain=False, scratch=()):
        flops = 2 * products * 4 * rows * rows * width * 3 // 2
        lead = [] if plain else [me[None], facts]
        return pl.pallas_call(
            kernel,
            grid=(steps,),
            in_specs=[smem] * len(lead)
            + [wide] * len(wides)
            + [slim(groups, kinds) for groups, kinds, _ in slims],
            out_specs=[wide] * outs + [slim(*sizes) for sizes in slim_outs],
            out_shape=[wide_shape] * outs + [slim_shape(*sizes) for sizes in slim_outs],
            scratch_shapes=[pltpu.VMEM((groups * GROUP, rows), jnp.float32) for groups in scratch],
            compiler_params=pltpu.CompilerParams(vmem_limit_bytes=20 * 1024 * 1024),
            cost_estimate=pl.CostEstimate(
                flops=flops, bytes_accessed=20 * rows * width, transcendentals=0
            ),
        )(*lead, *wides, *[value for _, _, value in slims])

    query_mate = send(queries, mates)
    key_back = send(key_vectors, chain)
    grad_mate = send(out_grad, mates)
    value_back = send(value_vectors, ahead)
    query_rows, grad_rows = [queries, query_mate], [out_grad, grad_mate]
    grad_own, value_own, stats = call(
        functools.partial(stats_kernel, heads, power), 1,
        [*query_rows, key_vectors, key_back, out_grad, value_vectors], [], 2, [(2, 2)],
    )
    stats_in = [(2, 2, stats), (2, 2, send(stats, mates))]
    grad_rows[0] = grad_own
    if not ring:
        query_rows.append(send(query_mate, relay))
        held, _ = lax.optimization_barrier((grad_mate, stats))
        grad_rows.append(send(held, relay))
        query_third, _ = lax.optimization_barrier((query_rows[2], value_back))
        (third_stats,) = call(
            functools.partial(third_stats_kernel, third, heads, power), 1,
            [query_third, key_back], [], 0, [(1, 2)],
        )
        stats_in += [(1, 2, third_stats), (1, 2, send(third_stats, to_even)), (1, 2, send(third_stats, to_odd))]
        stats_in += [(2, 2, send(stats, from_even)), (2, 2, send(stats, relay))]
    tensors = [t for two in zip(query_rows, grad_rows) for t in two]
    value_part, value_sent, *weighted, shift = call(
        functools.partial(values_kernel, third, heads, scaling, power), 2,
        tensors + [key_vectors, key_back], stats_in, count, [(count, 1)],
    )
    tensors += [key_vectors, value_own, key_back, value_back]
    *graded, dots = call(
        functools.partial(dots_kernel, third, heads, power), 2, tensors, [(count, 1, shift)],
        count - 2, [(count, 1)],
    )
    value_received = send(value_sent, behind)
    dots_in = [(count, 1, shift), (count, 1, dots), (count, 1, send(dots, mates))]
    if not ring:
        dots_in += [(count, 1, send(dots, pairs)) for pairs in (near, far)]
    key_part, key_sent, query_part, query_sent, *totals = call(
        functools.partial(keys_kernel, third, heads, scaling, power), 4, tensors, dots_in,
        4, [] if ring else [(count, 1)], scratch=[count] if ring else [],
    )
    key_received = send(key_sent, behind)
    query_received = send(query_sent, mates)
    value_ready = (value_part.astype(jnp.float32) + value_received.astype(jnp.float32)).astype(jnp.bfloat16)
    sums = [key_part, key_received, query_part, query_received]
    if ring:
        key_ready, query_ready = call(sums_kernel, 0, sums, [], 2, [], plain=True)
    else:
        sums += [send(graded[0], to_even), send(weighted[0], to_even)]
        by_step = totals[0][:GROUP].reshape(steps, heads, rows)
        by_step = jnp.pad(by_step, ((0, 0), (0, GROUP - heads), (0, 0))).reshape(steps * GROUP, rows)
        key_ready, query_ready = call(
            functools.partial(third_sums_kernel, heads, scaling), 0, sums, [(steps, 1, by_step)], 2, [],
            plain=True,
        )
    return query_ready, key_ready, value_ready


def program_kernel(shift, lengths_ref, out_ref):
    start, found = jnp.int32(0), jnp.int32(0)
    for doc in range(lengths_ref.shape[0]):
        end = start + lengths_ref[doc]
        last = (end - 1) >> shift
        spans = (last - (start >> shift) >= 3) & (last & 1 == 0)
        found = jnp.where(spans, (last >> 1) - 1, found)
        out_ref[doc + 1] = lengths_ref[doc]
        start = end
    out_ref[0] = found


def program_facts(rows, doc_lengths):
    smem = pl.BlockSpec(memory_space=pltpu.SMEM)
    return pl.pallas_call(
        functools.partial(program_kernel, rows.bit_length() - 1),
        in_specs=[smem],
        out_specs=smem,
        out_shape=jax.ShapeDtypeStruct((doc_lengths.shape[0] + 1,), jnp.int32),
    )(doc_lengths)


def halo_shards(*arguments):
    *tensors, doc_lengths = arguments
    facts = program_facts(tensors[0].shape[1], doc_lengths)
    thirds = range(3, lax.axis_size("seq") - 2, 2)
    programs = [functools.partial(halo_program, third) for third in (None, *thirds)]
    return lax.switch(facts[0], programs, *tensors, facts)


def shards(queries, key_vectors, value_vectors, out_grad, doc_lengths):
    _, rows, width = queries.shape
    seq_size = lax.axis_size("seq")
    longest = rows * seq_size * 3 // 8
    fits = longest <= 3 * rows and seq_size % 2 == 0 and seq_size > 4 and rows == LANES
    heads = width // HEAD
    plan = halo_shards if fits and heads % 4 == 0 and heads <= GROUP else spread_shards
    return plan(queries, key_vectors, value_vectors, out_grad, doc_lengths)


def solution(mesh):
    return jax.shard_map(
        shards,
        mesh=mesh,
        in_specs=(
            P("section", "seq", "dp"),
            P("section", "seq", "dp"),
            P("section", "seq", "dp"),
            P("section", "seq", "dp"),
            P(),
        ),
        out_specs=(P("section", "seq", "dp"), P("section", "seq", "dp"), P("section", "seq", "dp")),
        check_vma=False,
    )
```

```python
import functools
import math
import jax
import jax.numpy as jnp
from jax import lax
from jax.experimental import pallas as pl
from jax.experimental.pallas import tpu as pltpu
from jax.sharding import PartitionSpec as P

HEAD = 224
LANES = 128
FLOOR = -1e30


def pick_slot(stacked, slot):
    return lax.dynamic_index_in_dim(stacked, slot, 0, keepdims=False)


def put_slot(stacked, update, slot):
    return lax.dynamic_update_index_in_dim(stacked, update, slot, 0)


def spread_shards(queries, key_vectors, value_vectors, out_grad, doc_lengths):
    local_rows = queries.shape[1]
    local_width = queries.shape[2]
    head_count = local_width // HEAD
    seq_size = lax.axis_size("seq")
    group = seq_size // head_count
    scaling = HEAD ** (-0.5)

    def spread(matrix):
        shaped = matrix.reshape(local_rows, head_count, 1, HEAD)
        copies = jnp.broadcast_to(shaped, (local_rows, head_count, group, HEAD))
        return copies.reshape(local_rows, seq_size * HEAD)

    query_head, key_head, value_head, cot_head = (
        lax.all_to_all(spread(queries), "seq", split_axis=1, concat_axis=0, tiled=True),
        lax.all_to_all(spread(key_vectors), "seq", split_axis=1, concat_axis=0, tiled=True),
        lax.all_to_all(spread(value_vectors), "seq", split_axis=1, concat_axis=0, tiled=True),
        lax.all_to_all(spread(out_grad), "seq", split_axis=1, concat_axis=0, tiled=True),
    )
    length = key_head.shape[0]
    member = lax.axis_index("seq") % group
    blocks = 2 * group
    block = length // blocks
    bounds = jnp.cumsum(doc_lengths)
    positions = jnp.arange(length, dtype=jnp.int32)
    doc_index = jnp.sum((positions[:, None] >= bounds[None, :]).astype(jnp.int32), axis=1)
    row_list = [member, blocks - 1 - member]
    query_list = []
    cot_list = []
    pos_list = []
    for which in range(2):
        offset = row_list[which] * block
        query_list.append(lax.dynamic_slice_in_dim(query_head, offset, block, 0))
        cot_list.append(lax.dynamic_slice_in_dim(cot_head, offset, block, 0))
        pos_list.append(offset + jnp.arange(block, dtype=jnp.int32))
    query_stack = jnp.stack(query_list)
    cot_stack = jnp.stack(cot_list)
    pos_stack = jnp.stack(pos_list)
    doc_stack = jnp.take(doc_index, pos_stack)
    plan = []
    for number in range(blocks + 1):
        first = number <= member
        slot = jnp.where(first, 0, 1).astype(jnp.int32)
        col_block = jnp.where(first, number, number - member - 1)
        flag = None
        plan.append((slot, col_block, flag))
    row_max = jnp.full((2, block), -jnp.inf, jnp.float32)
    row_sum = jnp.zeros((2, block), jnp.float32)
    stored = []
    for slot, col_block, flag in plan:

        def score_tile(carry, slot=slot, col_block=col_block):
            maxima, totals = carry
            query_rows = pick_slot(query_stack, slot)
            key_rows = lax.dynamic_slice_in_dim(key_head, col_block * block, block, 0)
            col_docs = lax.dynamic_slice_in_dim(doc_index, col_block * block, block, 0)
            col_positions = col_block * block + jnp.arange(block, dtype=jnp.int32)
            raw = jnp.dot(query_rows, key_rows.T, preferred_element_type=jnp.float32) * scaling
            allowed = (pick_slot(doc_stack, slot)[:, None] == col_docs[None, :]) & (
                pick_slot(pos_stack, slot)[:, None] >= col_positions[None, :]
            )
            scores = jnp.where(allowed, raw, -jnp.inf)
            before = pick_slot(maxima, slot)
            after = jnp.maximum(before, jnp.max(scores, axis=1))
            safe = jnp.where(jnp.isfinite(after), after, 0.0)
            total = pick_slot(totals, slot) * jnp.exp(before - safe) + jnp.sum(
                jnp.exp(scores - safe[:, None]), axis=1
            )
            return (scores, put_slot(maxima, after, slot), put_slot(totals, total, slot))

        scores, row_max, row_sum = score_tile((row_max, row_sum))
        stored.append(scores)

    def tile_weights(scores, slot):
        return (
            jnp.exp(scores - pick_slot(row_max, slot)[:, None]) / pick_slot(row_sum, slot)[:, None]
        )

    summed = jnp.zeros((2, block, HEAD), jnp.float32)
    for (slot, col_block, flag), scores in zip(plan, stored):

        def add_values(carry, slot=slot, col_block=col_block, scores=scores):
            rounded = tile_weights(scores, slot).astype(jnp.bfloat16)
            value_rows = lax.dynamic_slice_in_dim(value_head, col_block * block, block, 0)
            term = jnp.dot(rounded, value_rows, preferred_element_type=jnp.float32)
            return put_slot(carry, pick_slot(carry, slot) + term, slot)

        summed = add_values(summed)
    attended = summed.astype(jnp.bfloat16)
    row_dot = jnp.sum(cot_stack.astype(jnp.float32) * attended.astype(jnp.float32), axis=2)
    query_acc = jnp.zeros((2, block, HEAD), jnp.float32)
    key_acc = jnp.zeros((length, HEAD), jnp.float32)
    value_acc = jnp.zeros((length, HEAD), jnp.float32)
    for (slot, col_block, flag), scores in zip(plan, stored):

        def backward_tile(carry, slot=slot, col_block=col_block, scores=scores):
            query_sum, key_sum, value_sum = carry
            weights = tile_weights(scores, slot)
            rounded = weights.astype(jnp.bfloat16)
            query_rows = pick_slot(query_stack, slot)
            cot_rows = pick_slot(cot_stack, slot)
            start = col_block * block
            key_rows = lax.dynamic_slice_in_dim(key_head, start, block, 0)
            value_rows = lax.dynamic_slice_in_dim(value_head, start, block, 0)
            value_term = jnp.dot(rounded.T, cot_rows, preferred_element_type=jnp.float32)
            prob_grad = jnp.dot(cot_rows, value_rows.T, preferred_element_type=jnp.float32)
            score_grad = (
                weights * (prob_grad - pick_slot(row_dot, slot)[:, None]) * scaling
            ).astype(jnp.bfloat16)
            query_term = jnp.dot(score_grad, key_rows, preferred_element_type=jnp.float32)
            key_term = jnp.dot(score_grad.T, query_rows, preferred_element_type=jnp.float32)
            query_sum = put_slot(query_sum, pick_slot(query_sum, slot) + query_term, slot)
            key_sum = lax.dynamic_update_slice_in_dim(
                key_sum, lax.dynamic_slice_in_dim(key_sum, start, block, 0) + key_term, start, 0
            )
            value_sum = lax.dynamic_update_slice_in_dim(
                value_sum,
                lax.dynamic_slice_in_dim(value_sum, start, block, 0) + value_term,
                start,
                0,
            )
            return (query_sum, key_sum, value_sum)

        query_acc, key_acc, value_acc = backward_tile((query_acc, key_acc, value_acc))
    query_rounded = query_acc.astype(jnp.bfloat16)
    key_back, value_back = (
        lax.all_to_all(key_acc, "seq", split_axis=0, concat_axis=1, tiled=True),
        lax.all_to_all(value_acc, "seq", split_axis=0, concat_axis=1, tiled=True),
    )

    def settle(received):
        shaped = received.astype(jnp.float32).reshape(local_rows, head_count, group, HEAD)
        return jnp.sum(shaped, axis=2).reshape(1, local_rows, local_width).astype(jnp.bfloat16)

    query_full = jnp.zeros((length, HEAD), jnp.bfloat16)
    for which in range(2):
        query_full = lax.dynamic_update_slice_in_dim(
            query_full, query_rounded[which], row_list[which] * block, 0
        )
    query_back = lax.all_to_all(query_full, "seq", split_axis=0, concat_axis=1, tiled=True)
    query_out = settle(query_back)
    return (query_out, settle(key_back), settle(value_back))


NT = ((1,), (1,))
NN = ((1,), (0,))
TN = ((0,), (0,))
GROUP = 8


def head_span(head):
    low = head * HEAD // LANES * LANES
    high = -(-(head + 1) * HEAD // LANES) * LANES
    return low, high


def head_mask(head):
    low, high = head_span(head)
    lane = lax.broadcasted_iota(jnp.int32, (1, high - low), 1) + low
    inside = (lane >= head * HEAD) & (lane < (head + 1) * HEAD)
    return inside.astype(jnp.float32).astype(jnp.bfloat16)


def matmul(left, right, dims):
    return lax.dot_general(left, right, (dims, ((), ())), preferred_element_type=jnp.float32)


def stack(values, axis):
    return values[0] if len(values) == 1 else jnp.concatenate(values, axis=axis)


def allowed(lengths_ref, rows, query_block, key_block):
    shape = (rows, rows)
    position = query_block * rows + lax.broadcasted_iota(jnp.int32, shape, 1)
    keys = key_block * rows + lax.broadcasted_iota(jnp.int32, shape, 0)
    start = jnp.zeros_like(position)
    bound = jnp.int32(0)
    for doc in range(1, lengths_ref.shape[0]):
        bound = bound + lengths_ref[doc]
        start = jnp.where(position >= bound, bound, start)
    return (keys >= start) & (keys <= position)


def make_tile(lengths_ref, rows, queries, keys):
    mask = stack(
        [stack([allowed(lengths_ref, rows, q, k) for _, q in queries], 1) for _, k in keys], 0
    )
    return [slot for slot, _ in queries], [slot for slot, _ in keys], mask


def tile_values(plan, head, queries, keys, products):
    low, high = head_span(head)
    keep = head_mask(head)

    def gather(refs, number, slots):
        return stack([refs[slot][number][0, :, low:high] for slot in slots], 0)

    out = []
    for query_slots, key_slots, _ in plan:
        q = [gather(queries, number, query_slots) for number in range(products)]
        k = [gather(keys, number, key_slots) * keep for number in range(products)]
        out.append((q, k, [matmul(b, a, NT) for a, b in zip(q, k)]))
    return out, keep


def tiles_ahead(heads, plan, queries, keys, products):
    ready = tile_values(plan, 0, queries, keys, products)
    for head in range(heads):
        now = ready
        if head + 1 < heads:
            ready = tile_values(plan, head + 1, queries, keys, products)
        yield head, now


def pair_tile(lengths_ref, rows, me):
    mate = me + 1 - 2 * lax.rem(me, 2)
    return make_tile(lengths_ref, rows, ((0, me), (1, mate)), ((0, me), (1, me - 2)))


def third_tile(third, lengths_ref, rows, me):
    slots, keys, mask = make_tile(lengths_ref, rows, ((2, me + 1),), ((1, me - 2),))
    return slots, keys, mask & (me == third)


def lane_cut(value, number, rows):
    return value[:, number * rows : (number + 1) * rows]


def row_of(group, kinds, kind, head):
    return pl.ds((group * kinds + kind) * GROUP + head, 1)


def per_query(slots, kinds, kind, head, ref):
    return stack([ref[row_of(slot, kinds, kind, head), :] for slot in slots], 1)


def collect_stats(heads, power, step, plan, queries, keys, rows, out_ref, groups):
    for head, (tiles, _) in tiles_ahead(heads, plan, queries, keys, 1):
        for (query_slots, _, mask), (_, _, (raw,)) in zip(plan, tiles):
            raw = jnp.where(mask, raw, FLOOR)
            top = jnp.max(raw, axis=0, keepdims=True)
            sums = jnp.sum(jnp.exp2((raw - top) * power), axis=0, keepdims=True)
            for number, slot in enumerate(query_slots):
                at = step * heads + head
                out_ref[row_of(groups[slot], 2, 0, at), :] = lane_cut(top, number, rows)
                out_ref[row_of(groups[slot], 2, 1, at), :] = lane_cut(sums, number, rows)


def stats_kernel(
    heads, power, place_ref, lengths_ref, q_own, q_mate, k_own, k_back, o_own, v_own, o_copy, v_copy, out_ref
):
    rows, me, step = k_own.shape[1], place_ref[0], pl.program_id(0)
    o_copy[...], v_copy[...] = o_own[...], v_own[...]
    plan = [pair_tile(lengths_ref, rows, me)]
    queries, keys = ((q_own,), (q_mate,)), ((k_own,), (k_back,))
    collect_stats(heads, power, step, plan, queries, keys, rows, out_ref, (0, 1))


def third_stats_kernel(third, heads, power, place_ref, lengths_ref, q_third, k_back, out_ref):
    rows, me, step = k_back.shape[1], place_ref[0], pl.program_id(0)
    plan = [third_tile(third, lengths_ref, rows, me)]
    queries, keys = (None, None, (q_third,)), (None, (k_back,))
    collect_stats(heads, power, step, plan, queries, keys, rows, out_ref, (None, None, 0))


def part_of(ref, kinds, number):
    size = kinds * GROUP
    return ref[number * size : (number + 1) * size, :]


def group_parts(kinds, mine, sent, extra):
    own = [part_of(mine, kinds, 0), part_of(sent, kinds, 1)]
    mate = [part_of(mine, kinds, 1), part_of(sent, kinds, 0)]
    if extra:
        near, far = extra
        own, mate = own + [near[...]], mate + [far[...]]
    return [own, mate]


def merge_groups(scaling, shift_ref, refs):
    mine, sent, *extra = refs
    for number, parts in enumerate(group_parts(2, mine, sent, extra)):
        shift_ref[number * GROUP : (number + 1) * GROUP, :] = merge_stats(scaling, parts)


def merge_stats(scaling, parts):
    split = [(jnp.where(p[GROUP:] > 0, p[:GROUP], FLOOR), p[GROUP:]) for p in parts]
    top = functools.reduce(jnp.maximum, [s[0] for s in split])
    total = sum(jnp.exp((s[0] - top) * scaling) * s[1] for s in split)
    return top + jnp.log(jnp.where(total > 0, total, 1.0)) / scaling


class Emitter:
    def __init__(self, outs, base={}):
        self.outs, self.base, self.carry = outs, base, {}

    def put(self, name, start, stop, value):
        if name in self.base:
            value = value + self.base[name][0, :, start:stop].astype(jnp.float32)
        self.outs[name][0, :, start:stop] = value.astype(jnp.bfloat16)

    def emit(self, head, name, value):
        low, high = head_span(head)
        first, last = head * HEAD % LANES == 0, (head + 1) * HEAD % LANES == 0
        start, stop = low, high
        if not first:
            self.put(name, low, low + LANES, value[:, :LANES] + self.carry.pop(name))
            start = low + LANES
        if not last:
            self.carry[name] = value[:, high - LANES - low :]
            stop = high - LANES
        if stop > start:
            self.put(name, start, stop, value[:, start - low : stop - low])


def add_rows(sums, kind, slots, value, rows):
    for number, slot in enumerate(slots):
        piece = value[number * rows : (number + 1) * rows]
        name = (kind, slot)
        sums[name] = sums[name] + piece if name in sums else piece


def split_refs(refs):
    return ((refs[0:2], refs[2:4]), (refs[4:6], refs[6:8]), refs[8:])


def values_kernel(merge, heads, scaling, power, place_ref, lengths_ref, q0, o0, q1, o1, k0, k1, *refs):
    queries, keys = ((q0, o0), (q1, o1)), ((k0,), (k1,))
    if merge:
        *stats, value_own, value_back, shift_ref = refs
        merge_groups(scaling, shift_ref, stats)
    else:
        shift_ref, value_own, value_back = refs
    rows, me, step = k0.shape[1], place_ref[0], pl.program_id(0)
    plan = [pair_tile(lengths_ref, rows, me)]
    out = Emitter({("v", 0): value_own, ("v", 1): value_back})
    for head, (tiles, keep) in tiles_ahead(heads, plan, queries, keys, 1):
        low, high = head_span(head)
        sums = {}
        for (query_slots, key_slots, mask), (_, _, (raw,)) in zip(plan, tiles):
            shift = per_query(query_slots, 1, 0, step * heads + head, shift_ref)
            weight = jnp.where(mask, jnp.exp2((raw - shift) * power), 0.0).astype(jnp.bfloat16)
            o = stack([queries[slot][1][0, :, low:high] for slot in query_slots], 0) * keep
            add_rows(sums, "v", key_slots, matmul(weight, o, NN), rows)
        for name, value in sums.items():
            out.emit(head, name, value)


def dots_kernel(merge, heads, scaling, power, place_ref, lengths_ref, *refs):
    queries, keys, refs = split_refs(refs)
    if merge:
        *stats, dots_ref, shift_ref = refs
        merge_groups(scaling, shift_ref, stats)
    else:
        shift_ref, dots_ref = refs
    rows, me, step = keys[0][0].shape[1], place_ref[0], pl.program_id(0)
    plan = [pair_tile(lengths_ref, rows, me)]
    for head, (tiles, _) in tiles_ahead(heads, plan, queries, keys, 2):
        at = step * heads + head
        for (query_slots, _, mask), (_, _, (raw, grads)) in zip(plan, tiles):
            shift = per_query(query_slots, 1, 0, at, shift_ref)
            weight = jnp.where(mask, jnp.exp2((raw - shift) * power), 0.0)
            dots = jnp.sum(weight * grads, axis=0, keepdims=True)
            for number, slot in enumerate(query_slots):
                dots_ref[row_of(slot, 1, 0, at), :] = lane_cut(dots, number, rows)


def keys_kernel(third, heads, scaling, power, place_ref, lengths_ref, *refs):
    queries, keys, refs = split_refs(refs)
    (*base, shift_ref, mine, sent), refs = (refs[:3], refs[3:]) if third is None else (refs[:4], refs[4:])
    *extra, key_own, key_back, query_own, query_mate, total_ref = refs
    rows, me, step = keys[0][0].shape[1], place_ref[0], pl.program_id(0)
    plan = [pair_tile(lengths_ref, rows, me)]
    for number, parts in enumerate(group_parts(1, mine, sent, extra)):
        total_ref[number * GROUP : (number + 1) * GROUP, :] = sum(parts)
    outs = {("k", 0): key_own, ("k", 1): key_back, ("q", 0): query_own, ("q", 1): query_mate}
    out = Emitter(outs, {("k", 1): ref for ref in base})
    for head, (tiles, keep) in tiles_ahead(heads, plan, queries, keys, 2):
        at = step * heads + head
        sums = {}
        for (query_slots, key_slots, mask), ((q, _), (k, _), (raw, grads)) in zip(plan, tiles):
            shift = per_query(query_slots, 1, 0, at, shift_ref)
            dots = per_query(query_slots, 1, 0, at, total_ref)
            weight = jnp.where(mask, jnp.exp2((raw - shift) * power), 0.0)
            slope = (weight * (grads - dots) * scaling).astype(jnp.bfloat16)
            add_rows(sums, "k", key_slots, matmul(slope, q * keep, NN), rows)
            add_rows(sums, "q", query_slots, matmul(slope, k, TN), rows)
        for name, value in sums.items():
            out.emit(head, name, value)


def third_kernel(
    third, heads, scaling, power, place_ref, lengths_ref, q_third, o_third, k_back, v_back, value_part,
    stats, even_stats, odd_stats, even_dots, odd_dots, value_out, key_out, query_out, dots_ref, shift_ref,
):
    rows, me, step = k_back.shape[1], place_ref[0], pl.program_id(0)
    parts = [stats[...], part_of(even_stats, 2, 0), part_of(odd_stats, 2, 1)]
    shift_ref[...] = merge_stats(scaling, parts)
    slots, keys, mask = third_tile(third, lengths_ref, rows, me)
    queries, keys = (None, None, (q_third, o_third)), (None, (k_back, v_back))
    plan = [(slots, [1], mask)]
    out = Emitter({"v": value_out, "k": key_out, "q": query_out}, {"v": value_part})
    for head, (tiles, keep) in tiles_ahead(heads, plan, queries, keys, 2):
        (q, o), (k, _), (raw, grads) = tiles[0]
        at = step * heads + head
        weight = jnp.where(mask, jnp.exp2((raw - shift_ref[pl.ds(at, 1), :]) * power), 0.0)
        dots = jnp.sum(weight * grads, axis=0, keepdims=True)
        dots_ref[pl.ds(at, 1), :] = dots
        total = dots + even_dots[row_of(0, 1, 0, at), :] + odd_dots[row_of(1, 1, 0, at), :]
        slope = (weight * (grads - total) * scaling).astype(jnp.bfloat16)
        out.emit(head, "v", matmul(weight.astype(jnp.bfloat16), o * keep, NN))
        out.emit(head, "k", matmul(slope, q * keep, NN))
        out.emit(head, "q", matmul(slope, k, TN))


def add_refs(*refs):
    return sum(ref[...].astype(jnp.float32) for ref in refs)


def sums_kernel(key_part, key_sent, *refs):
    *query_parts, key_out, query_out = refs
    key_out[...] = add_refs(key_part, key_sent).astype(jnp.bfloat16)
    query_out[...] = add_refs(*query_parts).astype(jnp.bfloat16)


def halo_program(third, queries, key_vectors, value_vectors, out_grad, facts):
    _, rows, width = queries.shape
    seq_size = lax.axis_size("seq")
    me = lax.axis_index("seq").astype(jnp.int32)
    scaling = HEAD ** (-0.5)
    power = scaling * math.log2(math.e)
    steps = width // HEAD // 4
    part = width // steps
    heads = part // HEAD
    devices = range(seq_size)
    mates = [(s, s ^ 1) for s in devices]
    ring = third is None
    chain = [(s, s + 2) for s in devices if s + 2 < seq_size]
    ahead = [(s, (s + 2) % seq_size) for s in devices] if ring else chain
    behind = [(s, s - 2) for s in devices if s >= 2]
    if not ring:
        relay, to_odd = [(third + 2, third)], [(third, third + 2)]
        from_even, to_even = [(third + 1, third)], [(third, third + 1)]

    def send(value, pairs):
        return lax.ppermute(value, "seq", pairs)

    smem = pl.BlockSpec(memory_space=pltpu.SMEM)
    wide = pl.BlockSpec((1, rows, part), lambda step: (0, 0, step))
    wide_shape = jax.ShapeDtypeStruct((1, rows, width), jnp.bfloat16)

    def slim(groups, kinds):
        return pl.BlockSpec((groups * kinds * GROUP, rows), lambda step: (0, 0))

    def slim_shape(groups, kinds):
        return jax.ShapeDtypeStruct((groups * kinds * GROUP, rows), jnp.float32)

    def call(kernel, products, wides, slims, outs, slim_outs, plain=False, scratch=()):
        flops = 2 * products * 4 * rows * rows * width * 3 // 2
        lead = [] if plain else [me[None], facts]
        return pl.pallas_call(
            kernel,
            grid=(steps,),
            in_specs=[smem] * len(lead)
            + [wide] * len(wides)
            + [slim(groups, kinds) for groups, kinds, _ in slims],
            out_specs=[wide] * outs + [slim(*sizes) for sizes in slim_outs],
            out_shape=[wide_shape] * outs + [slim_shape(*sizes) for sizes in slim_outs],
            scratch_shapes=[pltpu.VMEM((groups * GROUP, rows), jnp.float32) for groups in scratch],
            compiler_params=pltpu.CompilerParams(vmem_limit_bytes=20 * 1024 * 1024),
            cost_estimate=pl.CostEstimate(
                flops=flops, bytes_accessed=20 * rows * width, transcendentals=0
            ),
        )(*lead, *wides, *[value for _, _, value in slims])

    query_mate = send(queries, mates)
    key_back = send(key_vectors, chain)
    grad_mate = send(out_grad, mates)
    value_back = send(value_vectors, ahead)
    grad_own, value_own, stats = call(
        functools.partial(stats_kernel, heads, power), 1,
        [queries, query_mate, key_vectors, key_back, out_grad, value_vectors], [], 2, [(2, 2)],
    )
    stats_in = [(2, 2, stats), (2, 2, send(stats, mates))]
    rows_in = [queries, grad_own, query_mate, grad_mate]
    tensors = rows_in + [key_vectors, value_own, key_back, value_back]
    constants = (heads, scaling, power)
    if ring:
        value_part, value_sent, shift = call(
            functools.partial(values_kernel, True, *constants), 2, rows_in + [key_vectors, key_back],
            stats_in, 2, [(2, 1)],
        )
        (dots,) = call(
            functools.partial(dots_kernel, False, *constants), 2, tensors, [(2, 1, shift)], 0, [(2, 1)]
        )
        dots_in = [(2, 1, shift), (2, 1, dots), (2, 1, send(dots, mates))]
        base = []
    else:
        query_third = send(query_mate, relay)
        even_stats, odd_stats = send(stats, from_even), send(stats, relay)
        held, even_stats, odd_stats = lax.optimization_barrier((grad_mate, even_stats, odd_stats))
        grad_third = send(held, relay)
        query_third, _ = lax.optimization_barrier((query_third, value_back))
        (third_stats,) = call(
            functools.partial(third_stats_kernel, third, heads, power), 1, [query_third, key_back], [],
            0, [(1, 2)],
        )
        stats_in += [(1, 2, send(third_stats, to_even)), (1, 2, send(third_stats, to_odd))]
        dots, shift = call(
            functools.partial(dots_kernel, True, *constants), 2, tensors, stats_in, 0, [(2, 1), (2, 1)]
        )
        even_dots, odd_dots = send(dots, from_even), send(dots, relay)
        value_part, value_back_part = call(
            functools.partial(values_kernel, False, *constants), 2, rows_in + [key_vectors, key_back],
            [(2, 1, shift)], 2, [],
        )
        value_sent, key_third, query_extra, third_dots = call(
            functools.partial(third_kernel, third, *constants), 2,
            [query_third, grad_third, key_back, value_back, value_back_part],
            [(1, 2, third_stats), (2, 2, even_stats), (2, 2, odd_stats), (2, 1, even_dots), (2, 1, odd_dots)],
            3, [(1, 1)], scratch=[1],
        )
        dots_in = [(2, 1, shift), (2, 1, dots), (2, 1, send(dots, mates))]
        dots_in += [(1, 1, send(third_dots, to_even)), (1, 1, send(third_dots, to_odd))]
        base = [key_third]
    value_received = send(value_sent, behind)
    key_part, key_sent, query_part, query_sent = call(
        functools.partial(keys_kernel, third, *constants), 4, tensors + base, dots_in, 4, [], scratch=[2],
    )
    key_received = send(key_sent, behind)
    query_received = [send(query_sent, mates)] + ([] if ring else [send(query_extra, to_even)])
    value_ready = (value_part.astype(jnp.float32) + value_received.astype(jnp.float32)).astype(jnp.bfloat16)
    key_ready, query_ready = call(
        sums_kernel, 0, [key_part, key_received, query_part, *query_received], [], 2, [], plain=True
    )
    return query_ready, key_ready, value_ready


def program_kernel(shift, lengths_ref, out_ref):
    start, found = jnp.int32(0), jnp.int32(0)
    for doc in range(lengths_ref.shape[0]):
        end = start + lengths_ref[doc]
        last = (end - 1) >> shift
        spans = (last - (start >> shift) >= 3) & (last & 1 == 0)
        found = jnp.where(spans, (last >> 1) - 1, found)
        out_ref[doc + 1] = lengths_ref[doc]
        start = end
    out_ref[0] = found


def program_facts(rows, doc_lengths):
    smem = pl.BlockSpec(memory_space=pltpu.SMEM)
    return pl.pallas_call(
        functools.partial(program_kernel, rows.bit_length() - 1),
        in_specs=[smem],
        out_specs=smem,
        out_shape=jax.ShapeDtypeStruct((doc_lengths.shape[0] + 1,), jnp.int32),
    )(doc_lengths)


def halo_shards(*arguments):
    *tensors, doc_lengths = arguments
    facts = program_facts(tensors[0].shape[1], doc_lengths)
    thirds = range(3, lax.axis_size("seq") - 2, 2)
    programs = [functools.partial(halo_program, third) for third in (None, *thirds)]
    return lax.switch(facts[0], programs, *tensors, facts)


def shards(queries, key_vectors, value_vectors, out_grad, doc_lengths):
    _, rows, width = queries.shape
    seq_size = lax.axis_size("seq")
    longest = rows * seq_size * 3 // 8
    fits = longest <= 3 * rows and seq_size % 2 == 0 and seq_size > 4 and rows == LANES
    heads = width // HEAD
    plan = halo_shards if fits and heads % 4 == 0 and heads <= GROUP else spread_shards
    return plan(queries, key_vectors, value_vectors, out_grad, doc_lengths)


def solution(mesh):
    return jax.shard_map(
        shards,
        mesh=mesh,
        in_specs=(
            P("section", "seq", "dp"),
            P("section", "seq", "dp"),
            P("section", "seq", "dp"),
            P("section", "seq", "dp"),
            P(),
        ),
        out_specs=(P("section", "seq", "dp"), P("section", "seq", "dp"), P("section", "seq", "dp")),
        check_vma=False,
    )
```

```python
import functools
import math
import jax
import jax.numpy as jnp
from jax import lax
from jax.experimental import pallas as pl
from jax.experimental.pallas import tpu as pltpu
from jax.sharding import PartitionSpec as P

HEAD = 224
LANES = 128
FLOOR = -1e30


def pick_slot(stacked, slot):
    return lax.dynamic_index_in_dim(stacked, slot, 0, keepdims=False)


def put_slot(stacked, update, slot):
    return lax.dynamic_update_index_in_dim(stacked, update, slot, 0)


def spread_shards(queries, key_vectors, value_vectors, out_grad, doc_lengths):
    local_rows = queries.shape[1]
    local_width = queries.shape[2]
    head_count = local_width // HEAD
    seq_size = lax.axis_size("seq")
    group = seq_size // head_count
    scaling = HEAD ** (-0.5)

    def spread(matrix):
        shaped = matrix.reshape(local_rows, head_count, 1, HEAD)
        copies = jnp.broadcast_to(shaped, (local_rows, head_count, group, HEAD))
        return copies.reshape(local_rows, seq_size * HEAD)

    query_head, key_head, value_head, cot_head = (
        lax.all_to_all(spread(queries), "seq", split_axis=1, concat_axis=0, tiled=True),
        lax.all_to_all(spread(key_vectors), "seq", split_axis=1, concat_axis=0, tiled=True),
        lax.all_to_all(spread(value_vectors), "seq", split_axis=1, concat_axis=0, tiled=True),
        lax.all_to_all(spread(out_grad), "seq", split_axis=1, concat_axis=0, tiled=True),
    )
    length = key_head.shape[0]
    member = lax.axis_index("seq") % group
    blocks = 2 * group
    block = length // blocks
    bounds = jnp.cumsum(doc_lengths)
    positions = jnp.arange(length, dtype=jnp.int32)
    doc_index = jnp.sum((positions[:, None] >= bounds[None, :]).astype(jnp.int32), axis=1)
    row_list = [member, blocks - 1 - member]
    query_list = []
    cot_list = []
    pos_list = []
    for which in range(2):
        offset = row_list[which] * block
        query_list.append(lax.dynamic_slice_in_dim(query_head, offset, block, 0))
        cot_list.append(lax.dynamic_slice_in_dim(cot_head, offset, block, 0))
        pos_list.append(offset + jnp.arange(block, dtype=jnp.int32))
    query_stack = jnp.stack(query_list)
    cot_stack = jnp.stack(cot_list)
    pos_stack = jnp.stack(pos_list)
    doc_stack = jnp.take(doc_index, pos_stack)
    plan = []
    for number in range(blocks + 1):
        first = number <= member
        slot = jnp.where(first, 0, 1).astype(jnp.int32)
        col_block = jnp.where(first, number, number - member - 1)
        flag = None
        plan.append((slot, col_block, flag))
    row_max = jnp.full((2, block), -jnp.inf, jnp.float32)
    row_sum = jnp.zeros((2, block), jnp.float32)
    stored = []
    for slot, col_block, flag in plan:

        def score_tile(carry, slot=slot, col_block=col_block):
            maxima, totals = carry
            query_rows = pick_slot(query_stack, slot)
            key_rows = lax.dynamic_slice_in_dim(key_head, col_block * block, block, 0)
            col_docs = lax.dynamic_slice_in_dim(doc_index, col_block * block, block, 0)
            col_positions = col_block * block + jnp.arange(block, dtype=jnp.int32)
            raw = jnp.dot(query_rows, key_rows.T, preferred_element_type=jnp.float32) * scaling
            allowed = (pick_slot(doc_stack, slot)[:, None] == col_docs[None, :]) & (
                pick_slot(pos_stack, slot)[:, None] >= col_positions[None, :]
            )
            scores = jnp.where(allowed, raw, -jnp.inf)
            before = pick_slot(maxima, slot)
            after = jnp.maximum(before, jnp.max(scores, axis=1))
            safe = jnp.where(jnp.isfinite(after), after, 0.0)
            total = pick_slot(totals, slot) * jnp.exp(before - safe) + jnp.sum(
                jnp.exp(scores - safe[:, None]), axis=1
            )
            return (scores, put_slot(maxima, after, slot), put_slot(totals, total, slot))

        scores, row_max, row_sum = score_tile((row_max, row_sum))
        stored.append(scores)

    def tile_weights(scores, slot):
        return (
            jnp.exp(scores - pick_slot(row_max, slot)[:, None]) / pick_slot(row_sum, slot)[:, None]
        )

    summed = jnp.zeros((2, block, HEAD), jnp.float32)
    for (slot, col_block, flag), scores in zip(plan, stored):

        def add_values(carry, slot=slot, col_block=col_block, scores=scores):
            rounded = tile_weights(scores, slot).astype(jnp.bfloat16)
            value_rows = lax.dynamic_slice_in_dim(value_head, col_block * block, block, 0)
            term = jnp.dot(rounded, value_rows, preferred_element_type=jnp.float32)
            return put_slot(carry, pick_slot(carry, slot) + term, slot)

        summed = add_values(summed)
    attended = summed.astype(jnp.bfloat16)
    row_dot = jnp.sum(cot_stack.astype(jnp.float32) * attended.astype(jnp.float32), axis=2)
    query_acc = jnp.zeros((2, block, HEAD), jnp.float32)
    key_acc = jnp.zeros((length, HEAD), jnp.float32)
    value_acc = jnp.zeros((length, HEAD), jnp.float32)
    for (slot, col_block, flag), scores in zip(plan, stored):

        def backward_tile(carry, slot=slot, col_block=col_block, scores=scores):
            query_sum, key_sum, value_sum = carry
            weights = tile_weights(scores, slot)
            rounded = weights.astype(jnp.bfloat16)
            query_rows = pick_slot(query_stack, slot)
            cot_rows = pick_slot(cot_stack, slot)
            start = col_block * block
            key_rows = lax.dynamic_slice_in_dim(key_head, start, block, 0)
            value_rows = lax.dynamic_slice_in_dim(value_head, start, block, 0)
            value_term = jnp.dot(rounded.T, cot_rows, preferred_element_type=jnp.float32)
            prob_grad = jnp.dot(cot_rows, value_rows.T, preferred_element_type=jnp.float32)
            score_grad = (
                weights * (prob_grad - pick_slot(row_dot, slot)[:, None]) * scaling
            ).astype(jnp.bfloat16)
            query_term = jnp.dot(score_grad, key_rows, preferred_element_type=jnp.float32)
            key_term = jnp.dot(score_grad.T, query_rows, preferred_element_type=jnp.float32)
            query_sum = put_slot(query_sum, pick_slot(query_sum, slot) + query_term, slot)
            key_sum = lax.dynamic_update_slice_in_dim(
                key_sum, lax.dynamic_slice_in_dim(key_sum, start, block, 0) + key_term, start, 0
            )
            value_sum = lax.dynamic_update_slice_in_dim(
                value_sum,
                lax.dynamic_slice_in_dim(value_sum, start, block, 0) + value_term,
                start,
                0,
            )
            return (query_sum, key_sum, value_sum)

        query_acc, key_acc, value_acc = backward_tile((query_acc, key_acc, value_acc))
    query_rounded = query_acc.astype(jnp.bfloat16)
    key_back, value_back = (
        lax.all_to_all(key_acc, "seq", split_axis=0, concat_axis=1, tiled=True),
        lax.all_to_all(value_acc, "seq", split_axis=0, concat_axis=1, tiled=True),
    )

    def settle(received):
        shaped = received.astype(jnp.float32).reshape(local_rows, head_count, group, HEAD)
        return jnp.sum(shaped, axis=2).reshape(1, local_rows, local_width).astype(jnp.bfloat16)

    query_full = jnp.zeros((length, HEAD), jnp.bfloat16)
    for which in range(2):
        query_full = lax.dynamic_update_slice_in_dim(
            query_full, query_rounded[which], row_list[which] * block, 0
        )
    query_back = lax.all_to_all(query_full, "seq", split_axis=0, concat_axis=1, tiled=True)
    query_out = settle(query_back)
    return (query_out, settle(key_back), settle(value_back))


NT = ((1,), (1,))
NN = ((1,), (0,))
TN = ((0,), (0,))
GROUP = 8


def head_span(head):
    low = head * HEAD // LANES * LANES
    high = -(-(head + 1) * HEAD // LANES) * LANES
    return low, high


def head_mask(head):
    low, high = head_span(head)
    lane = lax.broadcasted_iota(jnp.int32, (1, high - low), 1) + low
    inside = (lane >= head * HEAD) & (lane < (head + 1) * HEAD)
    return inside.astype(jnp.float32).astype(jnp.bfloat16)


def matmul(left, right, dims):
    return lax.dot_general(left, right, (dims, ((), ())), preferred_element_type=jnp.float32)


def stack(values, axis):
    return values[0] if len(values) == 1 else jnp.concatenate(values, axis=axis)


def allowed(lengths_ref, rows, query_block, key_block):
    shape = (rows, rows)
    position = query_block * rows + lax.broadcasted_iota(jnp.int32, shape, 1)
    keys = key_block * rows + lax.broadcasted_iota(jnp.int32, shape, 0)
    start = jnp.zeros_like(position)
    bound = jnp.int32(0)
    for doc in range(1, lengths_ref.shape[0]):
        bound = bound + lengths_ref[doc]
        start = jnp.where(position >= bound, bound, start)
    return (keys >= start) & (keys <= position)


def make_tile(lengths_ref, rows, queries, keys):
    mask = stack(
        [stack([allowed(lengths_ref, rows, q, k) for _, q in queries], 1) for _, k in keys], 0
    )
    return [slot for slot, _ in queries], [slot for slot, _ in keys], mask


def tile_values(plan, head, queries, keys, products):
    low, high = head_span(head)
    keep = head_mask(head)

    def gather(refs, number, slots):
        return stack([refs[slot][number][0, :, low:high] for slot in slots], 0)

    out = []
    for query_slots, key_slots, _ in plan:
        q = [gather(queries, number, query_slots) for number in range(products)]
        k = [gather(keys, number, key_slots) * keep for number in range(products)]
        out.append((q, k, [matmul(b, a, NT) for a, b in zip(q, k)]))
    return out, keep


def tiles_ahead(heads, plan, queries, keys, products):
    ready = tile_values(plan, 0, queries, keys, products)
    for head in range(heads):
        now = ready
        if head + 1 < heads:
            ready = tile_values(plan, head + 1, queries, keys, products)
        yield head, now


def pair_tile(lengths_ref, rows, me):
    mate = me + 1 - 2 * lax.rem(me, 2)
    return make_tile(lengths_ref, rows, ((0, me), (1, mate)), ((0, me), (1, me - 2)))


def third_tile(third, lengths_ref, rows, me):
    slots, keys, mask = make_tile(lengths_ref, rows, ((2, me + 1),), ((1, me - 2),))
    return slots, keys, mask & (me == third)


def lane_cut(value, number, rows):
    return value[:, number * rows : (number + 1) * rows]


def row_of(group, kinds, kind, head):
    return pl.ds((group * kinds + kind) * GROUP + head, 1)


def per_query(slots, kinds, kind, head, ref):
    return stack([ref[row_of(slot, kinds, kind, head), :] for slot in slots], 1)


def collect_stats(heads, power, step, plan, queries, keys, rows, out_ref, groups):
    for head, (tiles, _) in tiles_ahead(heads, plan, queries, keys, 1):
        for (query_slots, _, mask), (_, _, (raw,)) in zip(plan, tiles):
            raw = jnp.where(mask, raw, FLOOR)
            top = jnp.max(raw, axis=0, keepdims=True)
            sums = jnp.sum(jnp.exp2((raw - top) * power), axis=0, keepdims=True)
            for number, slot in enumerate(query_slots):
                at = step * heads + head
                out_ref[row_of(groups[slot], 2, 0, at), :] = lane_cut(top, number, rows)
                out_ref[row_of(groups[slot], 2, 1, at), :] = lane_cut(sums, number, rows)


def stats_kernel(
    heads, power, place_ref, lengths_ref, q_own, q_mate, k_own, k_back, o_own, v_own, o_copy, v_copy, out_ref
):
    rows, me, step = k_own.shape[1], place_ref[0], pl.program_id(0)
    o_copy[...], v_copy[...] = o_own[...], v_own[...]
    plan = [pair_tile(lengths_ref, rows, me)]
    queries, keys = ((q_own,), (q_mate,)), ((k_own,), (k_back,))
    collect_stats(heads, power, step, plan, queries, keys, rows, out_ref, (0, 1))


def third_stats_kernel(third, heads, power, place_ref, lengths_ref, q_third, k_back, out_ref):
    rows, me, step = k_back.shape[1], place_ref[0], pl.program_id(0)
    plan = [third_tile(third, lengths_ref, rows, me)]
    queries, keys = (None, None, (q_third,)), (None, (k_back,))
    collect_stats(heads, power, step, plan, queries, keys, rows, out_ref, (None, None, 0))


def part_of(ref, kinds, number):
    size = kinds * GROUP
    return ref[number * size : (number + 1) * size, :]


def group_parts(kinds, mine, sent, extra):
    own = [part_of(mine, kinds, 0), part_of(sent, kinds, 1)]
    mate = [part_of(mine, kinds, 1), part_of(sent, kinds, 0)]
    if extra:
        near, far = extra
        own, mate = own + [near[...]], mate + [far[...]]
    return [own, mate]


def merge_groups(scaling, shift_ref, refs):
    mine, sent, *extra = refs
    for number, parts in enumerate(group_parts(2, mine, sent, extra)):
        shift_ref[number * GROUP : (number + 1) * GROUP, :] = merge_stats(scaling, parts)


def merge_stats(scaling, parts):
    split = [(jnp.where(p[GROUP:] > 0, p[:GROUP], FLOOR), p[GROUP:]) for p in parts]
    top = functools.reduce(jnp.maximum, [s[0] for s in split])
    total = sum(jnp.exp((s[0] - top) * scaling) * s[1] for s in split)
    return top + jnp.log(jnp.where(total > 0, total, 1.0)) / scaling


class Emitter:
    def __init__(self, outs, base={}):
        self.outs, self.base, self.carry = outs, base, {}

    def put(self, name, start, stop, value):
        if name in self.base:
            value = value + self.base[name][0, :, start:stop].astype(jnp.float32)
        self.outs[name][0, :, start:stop] = value.astype(jnp.bfloat16)

    def emit(self, head, name, value):
        low, high = head_span(head)
        first, last = head * HEAD % LANES == 0, (head + 1) * HEAD % LANES == 0
        start, stop = low, high
        if not first:
            self.put(name, low, low + LANES, value[:, :LANES] + self.carry.pop(name))
            start = low + LANES
        if not last:
            self.carry[name] = value[:, high - LANES - low :]
            stop = high - LANES
        if stop > start:
            self.put(name, start, stop, value[:, start - low : stop - low])


def add_rows(sums, kind, slots, value, rows):
    for number, slot in enumerate(slots):
        piece = value[number * rows : (number + 1) * rows]
        name = (kind, slot)
        sums[name] = sums[name] + piece if name in sums else piece


def split_refs(refs):
    return ((refs[0:2], refs[2:4]), (refs[4:6], refs[6:8]), refs[8:])


def values_kernel(merge, heads, scaling, power, place_ref, lengths_ref, q0, o0, q1, o1, k0, k1, *refs):
    queries, keys = ((q0, o0), (q1, o1)), ((k0,), (k1,))
    if merge:
        *stats, value_own, value_back, shift_ref = refs
        merge_groups(scaling, shift_ref, stats)
    else:
        shift_ref, value_own, value_back = refs
    rows, me, step = k0.shape[1], place_ref[0], pl.program_id(0)
    plan = [pair_tile(lengths_ref, rows, me)]
    out = Emitter({("v", 0): value_own, ("v", 1): value_back})
    for head, (tiles, keep) in tiles_ahead(heads, plan, queries, keys, 1):
        low, high = head_span(head)
        sums = {}
        for (query_slots, key_slots, mask), (_, _, (raw,)) in zip(plan, tiles):
            shift = per_query(query_slots, 1, 0, step * heads + head, shift_ref)
            weight = jnp.where(mask, jnp.exp2((raw - shift) * power), 0.0).astype(jnp.bfloat16)
            o = stack([queries[slot][1][0, :, low:high] for slot in query_slots], 0) * keep
            add_rows(sums, "v", key_slots, matmul(weight, o, NN), rows)
        for name, value in sums.items():
            out.emit(head, name, value)


def dots_kernel(merge, heads, scaling, power, place_ref, lengths_ref, *refs):
    queries, keys, refs = split_refs(refs)
    if merge:
        *stats, dots_ref, shift_ref = refs
        merge_groups(scaling, shift_ref, stats)
    else:
        shift_ref, dots_ref = refs
    rows, me, step = keys[0][0].shape[1], place_ref[0], pl.program_id(0)
    plan = [pair_tile(lengths_ref, rows, me)]
    for head, (tiles, _) in tiles_ahead(heads, plan, queries, keys, 2):
        at = step * heads + head
        for (query_slots, _, mask), (_, _, (raw, grads)) in zip(plan, tiles):
            shift = per_query(query_slots, 1, 0, at, shift_ref)
            weight = jnp.where(mask, jnp.exp2((raw - shift) * power), 0.0)
            dots = jnp.sum(weight * grads, axis=0, keepdims=True)
            for number, slot in enumerate(query_slots):
                dots_ref[row_of(slot, 1, 0, at), :] = lane_cut(dots, number, rows)


def keys_kernel(third, heads, scaling, power, place_ref, lengths_ref, *refs):
    queries, keys, refs = split_refs(refs)
    (*base, shift_ref, mine, sent), refs = (refs[:3], refs[3:]) if third is None else (refs[:4], refs[4:])
    *extra, key_own, key_back, query_own, query_mate, total_ref = refs
    rows, me, step = keys[0][0].shape[1], place_ref[0], pl.program_id(0)
    plan = [pair_tile(lengths_ref, rows, me)]
    for number, parts in enumerate(group_parts(1, mine, sent, extra)):
        total_ref[number * GROUP : (number + 1) * GROUP, :] = sum(parts)
    outs = {("k", 0): key_own, ("k", 1): key_back, ("q", 0): query_own, ("q", 1): query_mate}
    out = Emitter(outs, {("k", 1): ref for ref in base})
    for head, (tiles, keep) in tiles_ahead(heads, plan, queries, keys, 2):
        at = step * heads + head
        sums = {}
        for (query_slots, key_slots, mask), ((q, _), (k, _), (raw, grads)) in zip(plan, tiles):
            shift = per_query(query_slots, 1, 0, at, shift_ref)
            dots = per_query(query_slots, 1, 0, at, total_ref)
            weight = jnp.where(mask, jnp.exp2((raw - shift) * power), 0.0)
            slope = (weight * (grads - dots) * scaling).astype(jnp.bfloat16)
            add_rows(sums, "k", key_slots, matmul(slope, q * keep, NN), rows)
            add_rows(sums, "q", query_slots, matmul(slope, k, TN), rows)
        for name, value in sums.items():
            out.emit(head, name, value)


def third_kernel(
    third, heads, scaling, power, place_ref, lengths_ref, q_third, o_third, k_back, v_back, value_part,
    stats, even_stats, odd_stats, even_dots, odd_dots, value_out, key_out, query_out, dots_ref, shift_ref,
):
    rows, me, step = k_back.shape[1], place_ref[0], pl.program_id(0)
    parts = [stats[...], part_of(even_stats, 2, 0), part_of(odd_stats, 2, 1)]
    shift_ref[...] = merge_stats(scaling, parts)
    slots, keys, mask = third_tile(third, lengths_ref, rows, me)
    queries, keys = (None, None, (q_third, o_third)), (None, (k_back, v_back))
    plan = [(slots, [1], mask)]
    out = Emitter({"v": value_out, "k": key_out, "q": query_out}, {"v": value_part})
    for head, (tiles, keep) in tiles_ahead(heads, plan, queries, keys, 2):
        (q, o), (k, _), (raw, grads) = tiles[0]
        at = step * heads + head
        weight = jnp.where(mask, jnp.exp2((raw - shift_ref[pl.ds(at, 1), :]) * power), 0.0)
        dots = jnp.sum(weight * grads, axis=0, keepdims=True)
        dots_ref[pl.ds(at, 1), :] = dots
        total = dots + even_dots[row_of(0, 1, 0, at), :] + odd_dots[row_of(1, 1, 0, at), :]
        slope = (weight * (grads - total) * scaling).astype(jnp.bfloat16)
        out.emit(head, "v", matmul(weight.astype(jnp.bfloat16), o * keep, NN))
        out.emit(head, "k", matmul(slope, q * keep, NN))
        out.emit(head, "q", matmul(slope, k, TN))


def add_refs(*refs):
    return sum(ref[...].astype(jnp.float32) for ref in refs)


def sums_kernel(key_part, key_sent, *refs):
    *query_parts, key_out, query_out = refs
    key_out[...] = add_refs(key_part, key_sent).astype(jnp.bfloat16)
    query_out[...] = add_refs(*query_parts).astype(jnp.bfloat16)


def halo_program(third, queries, key_vectors, value_vectors, out_grad, facts):
    _, rows, width = queries.shape
    seq_size = lax.axis_size("seq")
    me = lax.axis_index("seq").astype(jnp.int32)
    scaling = HEAD ** (-0.5)
    power = scaling * math.log2(math.e)
    steps = width // HEAD // 4
    part = width // steps
    heads = part // HEAD
    devices = range(seq_size)
    mates = [(s, s ^ 1) for s in devices]
    ring = third is None
    chain = [(s, s + 2) for s in devices if s + 2 < seq_size]
    ahead = [(s, (s + 2) % seq_size) for s in devices] if ring else chain
    behind = [(s, s - 2) for s in devices if s >= 2]
    if not ring:
        relay, to_odd = [(third + 2, third)], [(third, third + 2)]
        from_even, to_even = [(third + 1, third)], [(third, third + 1)]

    def send(value, pairs):
        return lax.ppermute(value, "seq", pairs)

    smem = pl.BlockSpec(memory_space=pltpu.SMEM)
    wide = pl.BlockSpec((1, rows, part), lambda step: (0, 0, step))
    wide_shape = jax.ShapeDtypeStruct((1, rows, width), jnp.bfloat16)

    def slim(groups, kinds):
        return pl.BlockSpec((groups * kinds * GROUP, rows), lambda step: (0, 0))

    def slim_shape(groups, kinds):
        return jax.ShapeDtypeStruct((groups * kinds * GROUP, rows), jnp.float32)

    def call(kernel, products, wides, slims, outs, slim_outs, plain=False, scratch=()):
        flops = 2 * products * 4 * rows * rows * width * 3 // 2
        lead = [] if plain else [me[None], facts]
        return pl.pallas_call(
            kernel,
            grid=(steps,),
            in_specs=[smem] * len(lead)
            + [wide] * len(wides)
            + [slim(groups, kinds) for groups, kinds, _ in slims],
            out_specs=[wide] * outs + [slim(*sizes) for sizes in slim_outs],
            out_shape=[wide_shape] * outs + [slim_shape(*sizes) for sizes in slim_outs],
            scratch_shapes=[pltpu.VMEM((groups * GROUP, rows), jnp.float32) for groups in scratch],
            compiler_params=pltpu.CompilerParams(vmem_limit_bytes=20 * 1024 * 1024),
            cost_estimate=pl.CostEstimate(
                flops=flops, bytes_accessed=20 * rows * width, transcendentals=0
            ),
        )(*lead, *wides, *[value for _, _, value in slims])

    query_mate = send(queries, mates)
    key_back = send(key_vectors, chain)
    grad_mate = send(out_grad, mates)
    value_back = send(value_vectors, ahead)
    grad_own, value_own, stats = call(
        functools.partial(stats_kernel, heads, power), 1,
        [queries, query_mate, key_vectors, key_back, out_grad, value_vectors], [], 2, [(2, 2)],
    )
    stats_mate = send(stats, mates)
    rows_in = [queries, grad_own, query_mate, grad_mate]
    tensors = rows_in + [key_vectors, value_own, key_back, value_back]
    constants = (heads, scaling, power)
    if ring:
        value_part, value_sent, shift = call(
            functools.partial(values_kernel, True, *constants), 2, rows_in + [key_vectors, key_back],
            [(2, 2, stats), (2, 2, stats_mate)], 2, [(2, 1)],
        )
        (dots,) = call(
            functools.partial(dots_kernel, False, *constants), 2, tensors, [(2, 1, shift)], 0, [(2, 1)]
        )
        dots_in = [(2, 1, shift), (2, 1, dots), (2, 1, send(dots, mates))]
        base = []
    else:
        query_third = send(query_mate, relay)
        even_stats, odd_stats = send(stats, from_even), send(stats, relay)
        held, odd_stats, stats_mate = lax.optimization_barrier((grad_mate, odd_stats, stats_mate))
        grad_third = send(held, relay)
        query_third, even_stats, _ = lax.optimization_barrier((query_third, even_stats, value_back))
        (third_stats,) = call(
            functools.partial(third_stats_kernel, third, heads, power), 1, [query_third, key_back], [],
            0, [(1, 2)],
        )
        stats_in = [(2, 2, stats), (2, 2, stats_mate)]
        stats_in += [(1, 2, send(third_stats, to_even)), (1, 2, send(third_stats, to_odd))]
        dots, shift = call(
            functools.partial(dots_kernel, True, *constants), 2, tensors, stats_in, 0, [(2, 1), (2, 1)]
        )
        even_dots, odd_dots, dots_mate = (send(dots, pairs) for pairs in (from_even, relay, mates))
        value_part, value_back_part = call(
            functools.partial(values_kernel, False, *constants), 2, rows_in + [key_vectors, key_back],
            [(2, 1, shift)], 2, [],
        )
        value_back_part, dots_mate = lax.optimization_barrier((value_back_part, dots_mate))
        value_sent, key_third, query_extra, third_dots = call(
            functools.partial(third_kernel, third, *constants), 2,
            [query_third, grad_third, key_back, value_back, value_back_part],
            [(1, 2, third_stats), (2, 2, even_stats), (2, 2, odd_stats), (2, 1, even_dots), (2, 1, odd_dots)],
            3, [(1, 1)], scratch=[1],
        )
        dots_in = [(2, 1, shift), (2, 1, dots), (2, 1, dots_mate)]
        dots_in += [(1, 1, send(third_dots, to_even)), (1, 1, send(third_dots, to_odd))]
        base = [key_third]
    value_received = send(value_sent, behind)
    key_part, key_sent, query_part, query_sent = call(
        functools.partial(keys_kernel, third, *constants), 4, tensors + base, dots_in, 4, [], scratch=[2],
    )
    key_received = send(key_sent, behind)
    query_received = [send(query_sent, mates)] + ([] if ring else [send(query_extra, to_even)])
    value_ready = (value_part.astype(jnp.float32) + value_received.astype(jnp.float32)).astype(jnp.bfloat16)
    key_ready, query_ready = call(
        sums_kernel, 0, [key_part, key_received, query_part, *query_received], [], 2, [], plain=True
    )
    return query_ready, key_ready, value_ready


def program_kernel(shift, lengths_ref, out_ref):
    start, found = jnp.int32(0), jnp.int32(0)
    for doc in range(lengths_ref.shape[0]):
        end = start + lengths_ref[doc]
        last = (end - 1) >> shift
        spans = (last - (start >> shift) >= 3) & (last & 1 == 0)
        found = jnp.where(spans, (last >> 1) - 1, found)
        out_ref[doc + 1] = lengths_ref[doc]
        start = end
    out_ref[0] = found


def program_facts(rows, doc_lengths):
    smem = pl.BlockSpec(memory_space=pltpu.SMEM)
    return pl.pallas_call(
        functools.partial(program_kernel, rows.bit_length() - 1),
        in_specs=[smem],
        out_specs=smem,
        out_shape=jax.ShapeDtypeStruct((doc_lengths.shape[0] + 1,), jnp.int32),
    )(doc_lengths)


def halo_shards(*arguments):
    *tensors, doc_lengths = arguments
    facts = program_facts(tensors[0].shape[1], doc_lengths)
    thirds = range(3, lax.axis_size("seq") - 2, 2)
    programs = [functools.partial(halo_program, third) for third in (None, *thirds)]
    return lax.switch(facts[0], programs, *tensors, facts)


def shards(queries, key_vectors, value_vectors, out_grad, doc_lengths):
    _, rows, width = queries.shape
    seq_size = lax.axis_size("seq")
    longest = rows * seq_size * 3 // 8
    fits = longest <= 3 * rows and seq_size % 2 == 0 and seq_size > 4 and rows == LANES
    heads = width // HEAD
    plan = halo_shards if fits and heads % 4 == 0 and heads <= GROUP else spread_shards
    return plan(queries, key_vectors, value_vectors, out_grad, doc_lengths)


def solution(mesh):
    return jax.shard_map(
        shards,
        mesh=mesh,
        in_specs=(
            P("section", "seq", "dp"),
            P("section", "seq", "dp"),
            P("section", "seq", "dp"),
            P("section", "seq", "dp"),
            P(),
        ),
        out_specs=(P("section", "seq", "dp"), P("section", "seq", "dp"), P("section", "seq", "dp")),
        check_vma=False,
    )
```

```python
import functools
import math
import jax
import jax.numpy as jnp
from jax import lax
from jax.experimental import pallas as pl
from jax.experimental.pallas import tpu as pltpu
from jax.sharding import PartitionSpec as P

HEAD = 224
LANES = 128
FLOOR = -1e30


def pick_slot(stacked, slot):
    return lax.dynamic_index_in_dim(stacked, slot, 0, keepdims=False)


def put_slot(stacked, update, slot):
    return lax.dynamic_update_index_in_dim(stacked, update, slot, 0)


def spread_shards(queries, key_vectors, value_vectors, out_grad, doc_lengths):
    local_rows = queries.shape[1]
    local_width = queries.shape[2]
    head_count = local_width // HEAD
    seq_size = lax.axis_size("seq")
    group = seq_size // head_count
    scaling = HEAD ** (-0.5)

    def spread(matrix):
        shaped = matrix.reshape(local_rows, head_count, 1, HEAD)
        copies = jnp.broadcast_to(shaped, (local_rows, head_count, group, HEAD))
        return copies.reshape(local_rows, seq_size * HEAD)

    query_head, key_head, value_head, cot_head = (
        lax.all_to_all(spread(queries), "seq", split_axis=1, concat_axis=0, tiled=True),
        lax.all_to_all(spread(key_vectors), "seq", split_axis=1, concat_axis=0, tiled=True),
        lax.all_to_all(spread(value_vectors), "seq", split_axis=1, concat_axis=0, tiled=True),
        lax.all_to_all(spread(out_grad), "seq", split_axis=1, concat_axis=0, tiled=True),
    )
    length = key_head.shape[0]
    member = lax.axis_index("seq") % group
    blocks = 2 * group
    block = length // blocks
    bounds = jnp.cumsum(doc_lengths)
    positions = jnp.arange(length, dtype=jnp.int32)
    doc_index = jnp.sum((positions[:, None] >= bounds[None, :]).astype(jnp.int32), axis=1)
    row_list = [member, blocks - 1 - member]
    query_list = []
    cot_list = []
    pos_list = []
    for which in range(2):
        offset = row_list[which] * block
        query_list.append(lax.dynamic_slice_in_dim(query_head, offset, block, 0))
        cot_list.append(lax.dynamic_slice_in_dim(cot_head, offset, block, 0))
        pos_list.append(offset + jnp.arange(block, dtype=jnp.int32))
    query_stack = jnp.stack(query_list)
    cot_stack = jnp.stack(cot_list)
    pos_stack = jnp.stack(pos_list)
    doc_stack = jnp.take(doc_index, pos_stack)
    plan = []
    for number in range(blocks + 1):
        first = number <= member
        slot = jnp.where(first, 0, 1).astype(jnp.int32)
        col_block = jnp.where(first, number, number - member - 1)
        flag = None
        plan.append((slot, col_block, flag))
    row_max = jnp.full((2, block), -jnp.inf, jnp.float32)
    row_sum = jnp.zeros((2, block), jnp.float32)
    stored = []
    for slot, col_block, flag in plan:

        def score_tile(carry, slot=slot, col_block=col_block):
            maxima, totals = carry
            query_rows = pick_slot(query_stack, slot)
            key_rows = lax.dynamic_slice_in_dim(key_head, col_block * block, block, 0)
            col_docs = lax.dynamic_slice_in_dim(doc_index, col_block * block, block, 0)
            col_positions = col_block * block + jnp.arange(block, dtype=jnp.int32)
            raw = jnp.dot(query_rows, key_rows.T, preferred_element_type=jnp.float32) * scaling
            allowed = (pick_slot(doc_stack, slot)[:, None] == col_docs[None, :]) & (
                pick_slot(pos_stack, slot)[:, None] >= col_positions[None, :]
            )
            scores = jnp.where(allowed, raw, -jnp.inf)
            before = pick_slot(maxima, slot)
            after = jnp.maximum(before, jnp.max(scores, axis=1))
            safe = jnp.where(jnp.isfinite(after), after, 0.0)
            total = pick_slot(totals, slot) * jnp.exp(before - safe) + jnp.sum(
                jnp.exp(scores - safe[:, None]), axis=1
            )
            return (scores, put_slot(maxima, after, slot), put_slot(totals, total, slot))

        scores, row_max, row_sum = score_tile((row_max, row_sum))
        stored.append(scores)

    def tile_weights(scores, slot):
        return (
            jnp.exp(scores - pick_slot(row_max, slot)[:, None]) / pick_slot(row_sum, slot)[:, None]
        )

    summed = jnp.zeros((2, block, HEAD), jnp.float32)
    for (slot, col_block, flag), scores in zip(plan, stored):

        def add_values(carry, slot=slot, col_block=col_block, scores=scores):
            rounded = tile_weights(scores, slot).astype(jnp.bfloat16)
            value_rows = lax.dynamic_slice_in_dim(value_head, col_block * block, block, 0)
            term = jnp.dot(rounded, value_rows, preferred_element_type=jnp.float32)
            return put_slot(carry, pick_slot(carry, slot) + term, slot)

        summed = add_values(summed)
    attended = summed.astype(jnp.bfloat16)
    row_dot = jnp.sum(cot_stack.astype(jnp.float32) * attended.astype(jnp.float32), axis=2)
    query_acc = jnp.zeros((2, block, HEAD), jnp.float32)
    key_acc = jnp.zeros((length, HEAD), jnp.float32)
    value_acc = jnp.zeros((length, HEAD), jnp.float32)
    for (slot, col_block, flag), scores in zip(plan, stored):

        def backward_tile(carry, slot=slot, col_block=col_block, scores=scores):
            query_sum, key_sum, value_sum = carry
            weights = tile_weights(scores, slot)
            rounded = weights.astype(jnp.bfloat16)
            query_rows = pick_slot(query_stack, slot)
            cot_rows = pick_slot(cot_stack, slot)
            start = col_block * block
            key_rows = lax.dynamic_slice_in_dim(key_head, start, block, 0)
            value_rows = lax.dynamic_slice_in_dim(value_head, start, block, 0)
            value_term = jnp.dot(rounded.T, cot_rows, preferred_element_type=jnp.float32)
            prob_grad = jnp.dot(cot_rows, value_rows.T, preferred_element_type=jnp.float32)
            score_grad = (
                weights * (prob_grad - pick_slot(row_dot, slot)[:, None]) * scaling
            ).astype(jnp.bfloat16)
            query_term = jnp.dot(score_grad, key_rows, preferred_element_type=jnp.float32)
            key_term = jnp.dot(score_grad.T, query_rows, preferred_element_type=jnp.float32)
            query_sum = put_slot(query_sum, pick_slot(query_sum, slot) + query_term, slot)
            key_sum = lax.dynamic_update_slice_in_dim(
                key_sum, lax.dynamic_slice_in_dim(key_sum, start, block, 0) + key_term, start, 0
            )
            value_sum = lax.dynamic_update_slice_in_dim(
                value_sum,
                lax.dynamic_slice_in_dim(value_sum, start, block, 0) + value_term,
                start,
                0,
            )
            return (query_sum, key_sum, value_sum)

        query_acc, key_acc, value_acc = backward_tile((query_acc, key_acc, value_acc))
    query_rounded = query_acc.astype(jnp.bfloat16)
    key_back, value_back = (
        lax.all_to_all(key_acc, "seq", split_axis=0, concat_axis=1, tiled=True),
        lax.all_to_all(value_acc, "seq", split_axis=0, concat_axis=1, tiled=True),
    )

    def settle(received):
        shaped = received.astype(jnp.float32).reshape(local_rows, head_count, group, HEAD)
        return jnp.sum(shaped, axis=2).reshape(1, local_rows, local_width).astype(jnp.bfloat16)

    query_full = jnp.zeros((length, HEAD), jnp.bfloat16)
    for which in range(2):
        query_full = lax.dynamic_update_slice_in_dim(
            query_full, query_rounded[which], row_list[which] * block, 0
        )
    query_back = lax.all_to_all(query_full, "seq", split_axis=0, concat_axis=1, tiled=True)
    query_out = settle(query_back)
    return (query_out, settle(key_back), settle(value_back))


NT = ((1,), (1,))
NN = ((1,), (0,))
TN = ((0,), (0,))
GROUP = 8


def head_span(head):
    low = head * HEAD // LANES * LANES
    high = -(-(head + 1) * HEAD // LANES) * LANES
    return low, high


def head_mask(head):
    low, high = head_span(head)
    lane = lax.broadcasted_iota(jnp.int32, (1, high - low), 1) + low
    inside = (lane >= head * HEAD) & (lane < (head + 1) * HEAD)
    return inside.astype(jnp.float32).astype(jnp.bfloat16)


def matmul(left, right, dims):
    return lax.dot_general(left, right, (dims, ((), ())), preferred_element_type=jnp.float32)


def stack(values, axis):
    return values[0] if len(values) == 1 else jnp.concatenate(values, axis=axis)


def allowed(lengths_ref, rows, query_block, key_block):
    shape = (rows, rows)
    position = query_block * rows + lax.broadcasted_iota(jnp.int32, shape, 1)
    keys = key_block * rows + lax.broadcasted_iota(jnp.int32, shape, 0)
    start = jnp.zeros_like(position)
    bound = jnp.int32(0)
    for doc in range(1, lengths_ref.shape[0]):
        bound = bound + lengths_ref[doc]
        start = jnp.where(position >= bound, bound, start)
    return (keys >= start) & (keys <= position)


def make_tile(lengths_ref, rows, queries, keys):
    mask = stack(
        [stack([allowed(lengths_ref, rows, q, k) for _, q in queries], 1) for _, k in keys], 0
    )
    return [slot for slot, _ in queries], [slot for slot, _ in keys], mask


def tile_values(plan, head, queries, keys, products):
    low, high = head_span(head)
    keep = head_mask(head)

    def gather(refs, number, slots):
        return stack([refs[slot][number][0, :, low:high] for slot in slots], 0)

    out = []
    for query_slots, key_slots, _ in plan:
        q = [gather(queries, number, query_slots) for number in range(products)]
        k = [gather(keys, number, key_slots) * keep for number in range(products)]
        out.append((q, k, [matmul(b, a, NT) for a, b in zip(q, k)]))
    return out, keep


def tiles_ahead(heads, plan, queries, keys, products):
    ready = tile_values(plan, 0, queries, keys, products)
    for head in range(heads):
        now = ready
        if head + 1 < heads:
            ready = tile_values(plan, head + 1, queries, keys, products)
        yield head, now


def pair_tile(lengths_ref, rows, me):
    mate = me + 1 - 2 * lax.rem(me, 2)
    return make_tile(lengths_ref, rows, ((0, me), (1, mate)), ((0, me), (1, me - 2)))


def third_tile(third, lengths_ref, rows, me):
    slots, keys, mask = make_tile(lengths_ref, rows, ((2, me + 1),), ((1, me - 2),))
    return slots, keys, mask & (me == third)


def lane_cut(value, number, rows):
    return value[:, number * rows : (number + 1) * rows]


def row_of(group, kinds, kind, head):
    return pl.ds((group * kinds + kind) * GROUP + head, 1)


def per_query(slots, kinds, kind, head, ref):
    return stack([ref[row_of(slot, kinds, kind, head), :] for slot in slots], 1)


def collect_stats(heads, power, step, plan, queries, keys, rows, out_ref, groups):
    for head, (tiles, _) in tiles_ahead(heads, plan, queries, keys, 1):
        for (query_slots, _, mask), (_, _, (raw,)) in zip(plan, tiles):
            raw = jnp.where(mask, raw, FLOOR)
            top = jnp.max(raw, axis=0, keepdims=True)
            sums = jnp.sum(jnp.exp2((raw - top) * power), axis=0, keepdims=True)
            for number, slot in enumerate(query_slots):
                at = step * heads + head
                out_ref[row_of(groups[slot], 2, 0, at), :] = lane_cut(top, number, rows)
                out_ref[row_of(groups[slot], 2, 1, at), :] = lane_cut(sums, number, rows)


def stats_kernel(
    heads, power, place_ref, lengths_ref, q_own, q_mate, k_own, k_back, o_own, v_own, o_copy, v_copy, out_ref
):
    rows, me, step = k_own.shape[1], place_ref[0], pl.program_id(0)
    o_copy[...], v_copy[...] = o_own[...], v_own[...]
    plan = [pair_tile(lengths_ref, rows, me)]
    queries, keys = ((q_own,), (q_mate,)), ((k_own,), (k_back,))
    collect_stats(heads, power, step, plan, queries, keys, rows, out_ref, (0, 1))


def third_stats_kernel(third, heads, power, place_ref, lengths_ref, q_third, k_back, out_ref):
    rows, me, step = k_back.shape[1], place_ref[0], pl.program_id(0)
    plan = [third_tile(third, lengths_ref, rows, me)]
    queries, keys = (None, None, (q_third,)), (None, (k_back,))
    collect_stats(heads, power, step, plan, queries, keys, rows, out_ref, (None, None, 0))


def part_of(ref, kinds, number):
    size = kinds * GROUP
    return ref[number * size : (number + 1) * size, :]


def group_parts(kinds, mine, sent, extra):
    own = [part_of(mine, kinds, 0), part_of(sent, kinds, 1)]
    mate = [part_of(mine, kinds, 1), part_of(sent, kinds, 0)]
    if extra:
        near, far = extra
        own, mate = own + [near[...]], mate + [far[...]]
    return [own, mate]


def merge_groups(scaling, shift_ref, refs):
    mine, sent, *extra = refs
    for number, parts in enumerate(group_parts(2, mine, sent, extra)):
        shift_ref[number * GROUP : (number + 1) * GROUP, :] = merge_stats(scaling, parts)


def merge_stats(scaling, parts):
    split = [(jnp.where(p[GROUP:] > 0, p[:GROUP], FLOOR), p[GROUP:]) for p in parts]
    top = functools.reduce(jnp.maximum, [s[0] for s in split])
    total = sum(jnp.exp((s[0] - top) * scaling) * s[1] for s in split)
    return top + jnp.log(jnp.where(total > 0, total, 1.0)) / scaling


class Emitter:
    def __init__(self, outs, base={}):
        self.outs, self.base, self.carry = outs, base, {}

    def put(self, name, start, stop, value):
        if name in self.base:
            value = value + self.base[name][0, :, start:stop].astype(jnp.float32)
        self.outs[name][0, :, start:stop] = value.astype(jnp.bfloat16)

    def emit(self, head, name, value):
        low, high = head_span(head)
        first, last = head * HEAD % LANES == 0, (head + 1) * HEAD % LANES == 0
        start, stop = low, high
        if not first:
            self.put(name, low, low + LANES, value[:, :LANES] + self.carry.pop(name))
            start = low + LANES
        if not last:
            self.carry[name] = value[:, high - LANES - low :]
            stop = high - LANES
        if stop > start:
            self.put(name, start, stop, value[:, start - low : stop - low])


def add_rows(sums, kind, slots, value, rows):
    for number, slot in enumerate(slots):
        piece = value[number * rows : (number + 1) * rows]
        name = (kind, slot)
        sums[name] = sums[name] + piece if name in sums else piece


def split_refs(refs):
    return ((refs[0:2], refs[2:4]), (refs[4:6], refs[6:8]), refs[8:])


def values_kernel(merge, heads, scaling, power, place_ref, lengths_ref, q0, o0, q1, o1, k0, k1, *refs):
    queries, keys = ((q0, o0), (q1, o1)), ((k0,), (k1,))
    if merge:
        *stats, value_own, value_back, shift_ref = refs
        merge_groups(scaling, shift_ref, stats)
    else:
        shift_ref, value_own, value_back = refs
    rows, me, step = k0.shape[1], place_ref[0], pl.program_id(0)
    plan = [pair_tile(lengths_ref, rows, me)]
    out = Emitter({("v", 0): value_own, ("v", 1): value_back})
    for head, (tiles, keep) in tiles_ahead(heads, plan, queries, keys, 1):
        low, high = head_span(head)
        sums = {}
        for (query_slots, key_slots, mask), (_, _, (raw,)) in zip(plan, tiles):
            shift = per_query(query_slots, 1, 0, step * heads + head, shift_ref)
            weight = jnp.where(mask, jnp.exp2((raw - shift) * power), 0.0).astype(jnp.bfloat16)
            o = stack([queries[slot][1][0, :, low:high] for slot in query_slots], 0) * keep
            add_rows(sums, "v", key_slots, matmul(weight, o, NN), rows)
        for name, value in sums.items():
            out.emit(head, name, value)


def dots_kernel(merge, heads, scaling, power, place_ref, lengths_ref, *refs):
    queries, keys, refs = split_refs(refs)
    if merge:
        *stats, bundle_ref, dots_ref, shift_ref = refs
        merge_groups(scaling, shift_ref, stats)
        bundle_ref[: 4 * GROUP] = stats[0][...]
    else:
        shift_ref, dots_ref = refs
    rows, me, step = keys[0][0].shape[1], place_ref[0], pl.program_id(0)
    plan = [pair_tile(lengths_ref, rows, me)]
    for head, (tiles, _) in tiles_ahead(heads, plan, queries, keys, 2):
        at = step * heads + head
        for (query_slots, _, mask), (_, _, (raw, grads)) in zip(plan, tiles):
            shift = per_query(query_slots, 1, 0, at, shift_ref)
            weight = jnp.where(mask, jnp.exp2((raw - shift) * power), 0.0)
            dots = jnp.sum(weight * grads, axis=0, keepdims=True)
            for number, slot in enumerate(query_slots):
                dots_ref[row_of(slot, 1, 0, at), :] = lane_cut(dots, number, rows)
                if merge:
                    bundle_ref[row_of(4 + slot, 1, 0, at), :] = lane_cut(dots, number, rows)


def keys_kernel(third, heads, scaling, power, place_ref, lengths_ref, *refs):
    queries, keys, refs = split_refs(refs)
    (*base, shift_ref, mine, sent), refs = (refs[:3], refs[3:]) if third is None else (refs[:4], refs[4:])
    *extra, key_own, key_back, query_own, query_mate, total_ref = refs
    rows, me, step = keys[0][0].shape[1], place_ref[0], pl.program_id(0)
    plan = [pair_tile(lengths_ref, rows, me)]
    for number, parts in enumerate(group_parts(1, mine, sent, extra)):
        total_ref[number * GROUP : (number + 1) * GROUP, :] = sum(parts)
    outs = {("k", 0): key_own, ("k", 1): key_back, ("q", 0): query_own, ("q", 1): query_mate}
    out = Emitter(outs, {("k", 1): ref for ref in base})
    for head, (tiles, keep) in tiles_ahead(heads, plan, queries, keys, 2):
        at = step * heads + head
        sums = {}
        for (query_slots, key_slots, mask), ((q, _), (k, _), (raw, grads)) in zip(plan, tiles):
            shift = per_query(query_slots, 1, 0, at, shift_ref)
            dots = per_query(query_slots, 1, 0, at, total_ref)
            weight = jnp.where(mask, jnp.exp2((raw - shift) * power), 0.0)
            slope = (weight * (grads - dots) * scaling).astype(jnp.bfloat16)
            add_rows(sums, "k", key_slots, matmul(slope, q * keep, NN), rows)
            add_rows(sums, "q", query_slots, matmul(slope, k, TN), rows)
        for name, value in sums.items():
            out.emit(head, name, value)


def third_kernel(
    third, heads, scaling, power, place_ref, lengths_ref, q_third, o_third, k_back, v_back, value_part,
    stats, even, odd, value_out, key_out, query_out, dots_ref, shift_ref,
):
    rows, me, step = k_back.shape[1], place_ref[0], pl.program_id(0)
    parts = [stats[...], part_of(even, 2, 0), part_of(odd, 2, 1)]
    shift_ref[...] = merge_stats(scaling, parts)
    slots, keys, mask = third_tile(third, lengths_ref, rows, me)
    queries, keys = (None, None, (q_third, o_third)), (None, (k_back, v_back))
    plan = [(slots, [1], mask)]
    out = Emitter({"v": value_out, "k": key_out, "q": query_out}, {"v": value_part})
    for head, (tiles, keep) in tiles_ahead(heads, plan, queries, keys, 2):
        (q, o), (k, _), (raw, grads) = tiles[0]
        at = step * heads + head
        weight = jnp.where(mask, jnp.exp2((raw - shift_ref[pl.ds(at, 1), :]) * power), 0.0)
        dots = jnp.sum(weight * grads, axis=0, keepdims=True)
        dots_ref[pl.ds(at, 1), :] = dots
        total = dots + even[row_of(4, 1, 0, at), :] + odd[row_of(5, 1, 0, at), :]
        slope = (weight * (grads - total) * scaling).astype(jnp.bfloat16)
        out.emit(head, "v", matmul(weight.astype(jnp.bfloat16), o * keep, NN))
        out.emit(head, "k", matmul(slope, q * keep, NN))
        out.emit(head, "q", matmul(slope, k, TN))


def add_refs(*refs):
    return sum(ref[...].astype(jnp.float32) for ref in refs)


def sums_kernel(key_part, key_sent, *refs):
    *query_parts, key_out, query_out = refs
    key_out[...] = add_refs(key_part, key_sent).astype(jnp.bfloat16)
    query_out[...] = add_refs(*query_parts).astype(jnp.bfloat16)


def halo_program(third, queries, key_vectors, value_vectors, out_grad, facts):
    _, rows, width = queries.shape
    seq_size = lax.axis_size("seq")
    me = lax.axis_index("seq").astype(jnp.int32)
    scaling = HEAD ** (-0.5)
    power = scaling * math.log2(math.e)
    steps = width // HEAD // 4
    part = width // steps
    heads = part // HEAD
    devices = range(seq_size)
    mates = [(s, s ^ 1) for s in devices]
    ring = third is None
    chain = [(s, s + 2) for s in devices if s + 2 < seq_size]
    ahead = [(s, (s + 2) % seq_size) for s in devices] if ring else chain
    behind = [(s, s - 2) for s in devices if s >= 2]
    if not ring:
        relay, to_odd = [(third + 2, third)], [(third, third + 2)]
        from_even, to_even = [(third + 1, third)], [(third, third + 1)]

    def send(value, pairs):
        return lax.ppermute(value, "seq", pairs)

    smem = pl.BlockSpec(memory_space=pltpu.SMEM)
    wide = pl.BlockSpec((1, rows, part), lambda step: (0, 0, step))
    wide_shape = jax.ShapeDtypeStruct((1, rows, width), jnp.bfloat16)

    def slim(groups, kinds):
        return pl.BlockSpec((groups * kinds * GROUP, rows), lambda step: (0, 0))

    def slim_shape(groups, kinds):
        return jax.ShapeDtypeStruct((groups * kinds * GROUP, rows), jnp.float32)

    def call(kernel, products, wides, slims, outs, slim_outs, plain=False, scratch=()):
        flops = 2 * products * 4 * rows * rows * width * 3 // 2
        lead = [] if plain else [me[None], facts]
        return pl.pallas_call(
            kernel,
            grid=(steps,),
            in_specs=[smem] * len(lead)
            + [wide] * len(wides)
            + [slim(groups, kinds) for groups, kinds, _ in slims],
            out_specs=[wide] * outs + [slim(*sizes) for sizes in slim_outs],
            out_shape=[wide_shape] * outs + [slim_shape(*sizes) for sizes in slim_outs],
            scratch_shapes=[pltpu.VMEM((groups * GROUP, rows), jnp.float32) for groups in scratch],
            compiler_params=pltpu.CompilerParams(vmem_limit_bytes=20 * 1024 * 1024),
            cost_estimate=pl.CostEstimate(
                flops=flops, bytes_accessed=20 * rows * width, transcendentals=0
            ),
        )(*lead, *wides, *[value for _, _, value in slims])

    query_mate = send(queries, mates)
    key_back = send(key_vectors, chain)
    grad_mate = send(out_grad, mates)
    value_back = send(value_vectors, ahead)
    grad_own, value_own, stats = call(
        functools.partial(stats_kernel, heads, power), 1,
        [queries, query_mate, key_vectors, key_back, out_grad, value_vectors], [], 2, [(2, 2)],
    )
    stats_mate = send(stats, mates)
    rows_in = [queries, grad_own, query_mate, grad_mate]
    tensors = rows_in + [key_vectors, value_own, key_back, value_back]
    constants = (heads, scaling, power)
    if ring:
        value_part, value_sent, shift = call(
            functools.partial(values_kernel, True, *constants), 2, rows_in + [key_vectors, key_back],
            [(2, 2, stats), (2, 2, stats_mate)], 2, [(2, 1)],
        )
        (dots,) = call(
            functools.partial(dots_kernel, False, *constants), 2, tensors, [(2, 1, shift)], 0, [(2, 1)]
        )
        dots_in = [(2, 1, shift), (2, 1, dots), (2, 1, send(dots, mates))]
        base = []
    else:
        query_third = send(query_mate, relay)
        held, stats_mate = lax.optimization_barrier((grad_mate, stats_mate))
        grad_third = send(held, relay)
        query_third, _ = lax.optimization_barrier((query_third, value_back))
        (third_stats,) = call(
            functools.partial(third_stats_kernel, third, heads, power), 1, [query_third, key_back], [],
            0, [(1, 2)],
        )
        stats_in = [(2, 2, stats), (2, 2, stats_mate)]
        stats_in += [(1, 2, send(third_stats, to_even)), (1, 2, send(third_stats, to_odd))]
        bundle, dots, shift = call(
            functools.partial(dots_kernel, True, *constants), 2, tensors, stats_in, 0,
            [(2, 3), (2, 1), (2, 1)],
        )
        even, odd, dots_mate = send(bundle, from_even), send(bundle, relay), send(dots, mates)
        value_part, value_back_part = call(
            functools.partial(values_kernel, False, *constants), 2, rows_in + [key_vectors, key_back],
            [(2, 1, shift)], 2, [],
        )
        value_back_part, dots_mate = lax.optimization_barrier((value_back_part, dots_mate))
        value_sent, key_third, query_extra, third_dots = call(
            functools.partial(third_kernel, third, *constants), 2,
            [query_third, grad_third, key_back, value_back, value_back_part],
            [(1, 2, third_stats), (2, 3, even), (2, 3, odd)],
            3, [(1, 1)], scratch=[1],
        )
        dots_in = [(2, 1, shift), (2, 1, dots), (2, 1, dots_mate)]
        dots_in += [(1, 1, send(third_dots, to_even)), (1, 1, send(third_dots, to_odd))]
        base = [key_third]
    value_received = send(value_sent, behind)
    key_part, key_sent, query_part, query_sent = call(
        functools.partial(keys_kernel, third, *constants), 4, tensors + base, dots_in, 4, [], scratch=[2],
    )
    key_received = send(key_sent, behind)
    query_received = [send(query_sent, mates)] + ([] if ring else [send(query_extra, to_even)])
    value_ready = (value_part.astype(jnp.float32) + value_received.astype(jnp.float32)).astype(jnp.bfloat16)
    key_ready, query_ready = call(
        sums_kernel, 0, [key_part, key_received, query_part, *query_received], [], 2, [], plain=True
    )
    return query_ready, key_ready, value_ready


def program_kernel(shift, lengths_ref, out_ref):
    start, found = jnp.int32(0), jnp.int32(0)
    for doc in range(lengths_ref.shape[0]):
        end = start + lengths_ref[doc]
        last = (end - 1) >> shift
        spans = (last - (start >> shift) >= 3) & (last & 1 == 0)
        found = jnp.where(spans, (last >> 1) - 1, found)
        out_ref[doc + 1] = lengths_ref[doc]
        start = end
    out_ref[0] = found


def program_facts(rows, doc_lengths):
    smem = pl.BlockSpec(memory_space=pltpu.SMEM)
    return pl.pallas_call(
        functools.partial(program_kernel, rows.bit_length() - 1),
        in_specs=[smem],
        out_specs=smem,
        out_shape=jax.ShapeDtypeStruct((doc_lengths.shape[0] + 1,), jnp.int32),
    )(doc_lengths)


def halo_shards(*arguments):
    *tensors, doc_lengths = arguments
    facts = program_facts(tensors[0].shape[1], doc_lengths)
    thirds = range(3, lax.axis_size("seq") - 2, 2)
    programs = [functools.partial(halo_program, third) for third in (None, *thirds)]
    return lax.switch(facts[0], programs, *tensors, facts)


def shards(queries, key_vectors, value_vectors, out_grad, doc_lengths):
    _, rows, width = queries.shape
    seq_size = lax.axis_size("seq")
    longest = rows * seq_size * 3 // 8
    fits = longest <= 3 * rows and seq_size % 2 == 0 and seq_size > 4 and rows == LANES
    heads = width // HEAD
    plan = halo_shards if fits and heads % 4 == 0 and heads <= GROUP else spread_shards
    return plan(queries, key_vectors, value_vectors, out_grad, doc_lengths)


def solution(mesh):
    return jax.shard_map(
        shards,
        mesh=mesh,
        in_specs=(
            P("section", "seq", "dp"),
            P("section", "seq", "dp"),
            P("section", "seq", "dp"),
            P("section", "seq", "dp"),
            P(),
        ),
        out_specs=(P("section", "seq", "dp"), P("section", "seq", "dp"), P("section", "seq", "dp")),
        check_vma=False,
    )
```

```python
import functools
import math
import jax
import jax.numpy as jnp
from jax import lax
from jax.experimental import pallas as pl
from jax.experimental.pallas import tpu as pltpu
from jax.sharding import PartitionSpec as P

HEAD = 224
LANES = 128
FLOOR = -1e30


def pick_slot(stacked, slot):
    return lax.dynamic_index_in_dim(stacked, slot, 0, keepdims=False)


def put_slot(stacked, update, slot):
    return lax.dynamic_update_index_in_dim(stacked, update, slot, 0)


def spread_shards(queries, key_vectors, value_vectors, out_grad, doc_lengths):
    local_rows = queries.shape[1]
    local_width = queries.shape[2]
    head_count = local_width // HEAD
    seq_size = lax.axis_size("seq")
    group = seq_size // head_count
    scaling = HEAD ** (-0.5)

    def spread(matrix):
        shaped = matrix.reshape(local_rows, head_count, 1, HEAD)
        copies = jnp.broadcast_to(shaped, (local_rows, head_count, group, HEAD))
        return copies.reshape(local_rows, seq_size * HEAD)

    query_head, key_head, value_head, cot_head = (
        lax.all_to_all(spread(queries), "seq", split_axis=1, concat_axis=0, tiled=True),
        lax.all_to_all(spread(key_vectors), "seq", split_axis=1, concat_axis=0, tiled=True),
        lax.all_to_all(spread(value_vectors), "seq", split_axis=1, concat_axis=0, tiled=True),
        lax.all_to_all(spread(out_grad), "seq", split_axis=1, concat_axis=0, tiled=True),
    )
    length = key_head.shape[0]
    member = lax.axis_index("seq") % group
    blocks = 2 * group
    block = length // blocks
    bounds = jnp.cumsum(doc_lengths)
    positions = jnp.arange(length, dtype=jnp.int32)
    doc_index = jnp.sum((positions[:, None] >= bounds[None, :]).astype(jnp.int32), axis=1)
    row_list = [member, blocks - 1 - member]
    query_list = []
    cot_list = []
    pos_list = []
    for which in range(2):
        offset = row_list[which] * block
        query_list.append(lax.dynamic_slice_in_dim(query_head, offset, block, 0))
        cot_list.append(lax.dynamic_slice_in_dim(cot_head, offset, block, 0))
        pos_list.append(offset + jnp.arange(block, dtype=jnp.int32))
    query_stack = jnp.stack(query_list)
    cot_stack = jnp.stack(cot_list)
    pos_stack = jnp.stack(pos_list)
    doc_stack = jnp.take(doc_index, pos_stack)
    plan = []
    for number in range(blocks + 1):
        first = number <= member
        slot = jnp.where(first, 0, 1).astype(jnp.int32)
        col_block = jnp.where(first, number, number - member - 1)
        flag = None
        plan.append((slot, col_block, flag))
    row_max = jnp.full((2, block), -jnp.inf, jnp.float32)
    row_sum = jnp.zeros((2, block), jnp.float32)
    stored = []
    for slot, col_block, flag in plan:

        def score_tile(carry, slot=slot, col_block=col_block):
            maxima, totals = carry
            query_rows = pick_slot(query_stack, slot)
            key_rows = lax.dynamic_slice_in_dim(key_head, col_block * block, block, 0)
            col_docs = lax.dynamic_slice_in_dim(doc_index, col_block * block, block, 0)
            col_positions = col_block * block + jnp.arange(block, dtype=jnp.int32)
            raw = jnp.dot(query_rows, key_rows.T, preferred_element_type=jnp.float32) * scaling
            allowed = (pick_slot(doc_stack, slot)[:, None] == col_docs[None, :]) & (
                pick_slot(pos_stack, slot)[:, None] >= col_positions[None, :]
            )
            scores = jnp.where(allowed, raw, -jnp.inf)
            before = pick_slot(maxima, slot)
            after = jnp.maximum(before, jnp.max(scores, axis=1))
            safe = jnp.where(jnp.isfinite(after), after, 0.0)
            total = pick_slot(totals, slot) * jnp.exp(before - safe) + jnp.sum(
                jnp.exp(scores - safe[:, None]), axis=1
            )
            return (scores, put_slot(maxima, after, slot), put_slot(totals, total, slot))

        scores, row_max, row_sum = score_tile((row_max, row_sum))
        stored.append(scores)

    def tile_weights(scores, slot):
        return (
            jnp.exp(scores - pick_slot(row_max, slot)[:, None]) / pick_slot(row_sum, slot)[:, None]
        )

    summed = jnp.zeros((2, block, HEAD), jnp.float32)
    for (slot, col_block, flag), scores in zip(plan, stored):

        def add_values(carry, slot=slot, col_block=col_block, scores=scores):
            rounded = tile_weights(scores, slot).astype(jnp.bfloat16)
            value_rows = lax.dynamic_slice_in_dim(value_head, col_block * block, block, 0)
            term = jnp.dot(rounded, value_rows, preferred_element_type=jnp.float32)
            return put_slot(carry, pick_slot(carry, slot) + term, slot)

        summed = add_values(summed)
    attended = summed.astype(jnp.bfloat16)
    row_dot = jnp.sum(cot_stack.astype(jnp.float32) * attended.astype(jnp.float32), axis=2)
    query_acc = jnp.zeros((2, block, HEAD), jnp.float32)
    key_acc = jnp.zeros((length, HEAD), jnp.float32)
    value_acc = jnp.zeros((length, HEAD), jnp.float32)
    for (slot, col_block, flag), scores in zip(plan, stored):

        def backward_tile(carry, slot=slot, col_block=col_block, scores=scores):
            query_sum, key_sum, value_sum = carry
            weights = tile_weights(scores, slot)
            rounded = weights.astype(jnp.bfloat16)
            query_rows = pick_slot(query_stack, slot)
            cot_rows = pick_slot(cot_stack, slot)
            start = col_block * block
            key_rows = lax.dynamic_slice_in_dim(key_head, start, block, 0)
            value_rows = lax.dynamic_slice_in_dim(value_head, start, block, 0)
            value_term = jnp.dot(rounded.T, cot_rows, preferred_element_type=jnp.float32)
            prob_grad = jnp.dot(cot_rows, value_rows.T, preferred_element_type=jnp.float32)
            score_grad = (
                weights * (prob_grad - pick_slot(row_dot, slot)[:, None]) * scaling
            ).astype(jnp.bfloat16)
            query_term = jnp.dot(score_grad, key_rows, preferred_element_type=jnp.float32)
            key_term = jnp.dot(score_grad.T, query_rows, preferred_element_type=jnp.float32)
            query_sum = put_slot(query_sum, pick_slot(query_sum, slot) + query_term, slot)
            key_sum = lax.dynamic_update_slice_in_dim(
                key_sum, lax.dynamic_slice_in_dim(key_sum, start, block, 0) + key_term, start, 0
            )
            value_sum = lax.dynamic_update_slice_in_dim(
                value_sum,
                lax.dynamic_slice_in_dim(value_sum, start, block, 0) + value_term,
                start,
                0,
            )
            return (query_sum, key_sum, value_sum)

        query_acc, key_acc, value_acc = backward_tile((query_acc, key_acc, value_acc))
    query_rounded = query_acc.astype(jnp.bfloat16)
    key_back, value_back = (
        lax.all_to_all(key_acc, "seq", split_axis=0, concat_axis=1, tiled=True),
        lax.all_to_all(value_acc, "seq", split_axis=0, concat_axis=1, tiled=True),
    )

    def settle(received):
        shaped = received.astype(jnp.float32).reshape(local_rows, head_count, group, HEAD)
        return jnp.sum(shaped, axis=2).reshape(1, local_rows, local_width).astype(jnp.bfloat16)

    query_full = jnp.zeros((length, HEAD), jnp.bfloat16)
    for which in range(2):
        query_full = lax.dynamic_update_slice_in_dim(
            query_full, query_rounded[which], row_list[which] * block, 0
        )
    query_back = lax.all_to_all(query_full, "seq", split_axis=0, concat_axis=1, tiled=True)
    query_out = settle(query_back)
    return (query_out, settle(key_back), settle(value_back))


NT = ((1,), (1,))
NN = ((1,), (0,))
TN = ((0,), (0,))
GROUP = 8


def head_span(head):
    low = head * HEAD // LANES * LANES
    high = -(-(head + 1) * HEAD // LANES) * LANES
    return low, high


def head_mask(head):
    low, high = head_span(head)
    lane = lax.broadcasted_iota(jnp.int32, (1, high - low), 1) + low
    inside = (lane >= head * HEAD) & (lane < (head + 1) * HEAD)
    return inside.astype(jnp.float32).astype(jnp.bfloat16)


def matmul(left, right, dims):
    return lax.dot_general(left, right, (dims, ((), ())), preferred_element_type=jnp.float32)


def stack(values, axis):
    return values[0] if len(values) == 1 else jnp.concatenate(values, axis=axis)


def allowed(lengths_ref, rows, query_block, key_block, columns=None):
    shape = (rows, columns or rows)
    position = query_block * rows + lax.broadcasted_iota(jnp.int32, shape, 1)
    keys = key_block * rows + lax.broadcasted_iota(jnp.int32, shape, 0)
    start = jnp.zeros_like(position)
    bound = jnp.int32(0)
    for doc in range(1, lengths_ref.shape[0] - 1):
        bound = bound + lengths_ref[doc]
        start = jnp.where(position >= bound, bound, start)
    return (keys >= start) & (keys <= position)


def make_tile(lengths_ref, rows, queries, keys):
    mask = stack(
        [stack([allowed(lengths_ref, rows, q, k) for _, q in queries], 1) for _, k in keys], 0
    )
    return [slot for slot, _ in queries], [slot for slot, _ in keys], mask


def tile_values(plan, head, queries, keys, products):
    low, high = head_span(head)
    keep = head_mask(head)

    def gather(refs, number, slots):
        return stack([refs[slot][number][0, :, low:high] for slot in slots], 0)

    out = []
    for query_slots, key_slots, _ in plan:
        q = [gather(queries, number, query_slots) for number in range(products)]
        k = [gather(keys, number, key_slots) * keep for number in range(products)]
        out.append((q, k, [matmul(b, a, NT) for a, b in zip(q, k)]))
    return out, keep


def tiles_ahead(heads, plan, queries, keys, products):
    ready = tile_values(plan, 0, queries, keys, products)
    for head in range(heads):
        now = ready
        if head + 1 < heads:
            ready = tile_values(plan, head + 1, queries, keys, products)
        yield head, now


def pair_tile(lengths_ref, rows, me):
    mate = me + 1 - 2 * lax.rem(me, 2)
    return make_tile(lengths_ref, rows, ((0, me), (1, mate)), ((0, me), (1, me - 2)))


def third_tile(facts_ref, rows, columns, me):
    mask = allowed(facts_ref, rows, me + 1, me - 2, columns)
    return [2], [1], mask & (me == facts_ref[facts_ref.shape[0] - 1])


def lane_cut(value, number, rows):
    return value[:, number * rows : (number + 1) * rows]


def row_of(group, kinds, kind, head):
    return pl.ds((group * kinds + kind) * GROUP + head, 1)


def per_query(slots, kinds, kind, head, ref):
    return stack([ref[row_of(slot, kinds, kind, head), :] for slot in slots], 1)


def collect_stats(heads, power, step, plan, queries, keys, rows, out_ref, groups):
    for head, (tiles, _) in tiles_ahead(heads, plan, queries, keys, 1):
        for (query_slots, _, mask), (_, _, (raw,)) in zip(plan, tiles):
            raw = jnp.where(mask, raw, FLOOR)
            top = jnp.max(raw, axis=0, keepdims=True)
            sums = jnp.sum(jnp.exp2((raw - top) * power), axis=0, keepdims=True)
            for number, slot in enumerate(query_slots):
                at = step * heads + head
                out_ref[row_of(groups[slot], 2, 0, at), :] = lane_cut(top, number, rows)
                out_ref[row_of(groups[slot], 2, 1, at), :] = lane_cut(sums, number, rows)


def stats_kernel(
    heads, power, place_ref, lengths_ref, q_own, q_mate, k_own, k_back, o_own, v_own, o_copy, v_copy, out_ref
):
    rows, me, step = k_own.shape[1], place_ref[0], pl.program_id(0)
    o_copy[...], v_copy[...] = o_own[...], v_own[...]
    plan = [pair_tile(lengths_ref, rows, me)]
    queries, keys = ((q_own,), (q_mate,)), ((k_own,), (k_back,))
    collect_stats(heads, power, step, plan, queries, keys, rows, out_ref, (0, 1))


def third_stats_kernel(heads, power, place_ref, lengths_ref, q_third, k_back, out_ref):
    rows, me, step = k_back.shape[1], place_ref[0], pl.program_id(0)
    plan = [third_tile(lengths_ref, rows, q_third.shape[1], me)]
    queries, keys = (None, None, (q_third,)), (None, (k_back,))
    collect_stats(heads, power, step, plan, queries, keys, rows, out_ref, (None, None, 0))


def part_of(ref, kinds, number):
    size = kinds * GROUP
    return ref[number * size : (number + 1) * size, :]


def fill_lanes(value, width):
    missing = width - value.shape[1]
    if missing == 0:
        return value
    return jnp.concatenate([value, jnp.zeros((value.shape[0], missing), jnp.float32)], axis=1)


def group_parts(kinds, mine, sent, extra):
    own = [part_of(mine, kinds, 0), part_of(sent, kinds, 1)]
    mate = [part_of(mine, kinds, 1), part_of(sent, kinds, 0)]
    if extra:
        near, far = (fill_lanes(ref[...], mine.shape[1]) for ref in extra)
        own, mate = own + [near], mate + [far]
    return [own, mate]


def merge_groups(scaling, shift_ref, refs):
    mine, sent, *extra = refs
    for number, parts in enumerate(group_parts(2, mine, sent, extra)):
        shift_ref[number * GROUP : (number + 1) * GROUP, :] = merge_stats(scaling, parts)


def merge_stats(scaling, parts):
    split = [(jnp.where(p[GROUP:] > 0, p[:GROUP], FLOOR), p[GROUP:]) for p in parts]
    top = functools.reduce(jnp.maximum, [s[0] for s in split])
    total = sum(jnp.exp((s[0] - top) * scaling) * s[1] for s in split)
    return top + jnp.log(jnp.where(total > 0, total, 1.0)) / scaling


class Emitter:
    def __init__(self, outs, base={}):
        self.outs, self.base, self.carry = outs, base, {}

    def put(self, name, start, stop, value):
        if name in self.base:
            value = value + self.base[name][0, :, start:stop].astype(jnp.float32)
        self.outs[name][0, :, start:stop] = value.astype(jnp.bfloat16)

    def emit(self, head, name, value):
        low, high = head_span(head)
        first, last = head * HEAD % LANES == 0, (head + 1) * HEAD % LANES == 0
        start, stop = low, high
        if not first:
            self.put(name, low, low + LANES, value[:, :LANES] + self.carry.pop(name))
            start = low + LANES
        if not last:
            self.carry[name] = value[:, high - LANES - low :]
            stop = high - LANES
        if stop > start:
            self.put(name, start, stop, value[:, start - low : stop - low])


def add_rows(sums, kind, slots, value, rows):
    for number, slot in enumerate(slots):
        piece = value[number * rows : (number + 1) * rows]
        name = (kind, slot)
        sums[name] = sums[name] + piece if name in sums else piece


def split_refs(refs):
    return ((refs[0:2], refs[2:4]), (refs[4:6], refs[6:8]), refs[8:])


def values_kernel(merge, heads, scaling, power, place_ref, lengths_ref, q0, o0, q1, o1, k0, k1, *refs):
    queries, keys = ((q0, o0), (q1, o1)), ((k0,), (k1,))
    if merge:
        *stats, value_own, value_back, shift_ref = refs
        merge_groups(scaling, shift_ref, stats)
    else:
        shift_ref, value_own, value_back = refs
    rows, me, step = k0.shape[1], place_ref[0], pl.program_id(0)
    plan = [pair_tile(lengths_ref, rows, me)]
    out = Emitter({("v", 0): value_own, ("v", 1): value_back})
    for head, (tiles, keep) in tiles_ahead(heads, plan, queries, keys, 1):
        low, high = head_span(head)
        sums = {}
        for (query_slots, key_slots, mask), (_, _, (raw,)) in zip(plan, tiles):
            shift = per_query(query_slots, 1, 0, step * heads + head, shift_ref)
            weight = jnp.where(mask, jnp.exp2((raw - shift) * power), 0.0).astype(jnp.bfloat16)
            o = stack([queries[slot][1][0, :, low:high] for slot in query_slots], 0) * keep
            add_rows(sums, "v", key_slots, matmul(weight, o, NN), rows)
        for name, value in sums.items():
            out.emit(head, name, value)


def dots_kernel(merge, heads, scaling, power, place_ref, lengths_ref, *refs):
    queries, keys, refs = split_refs(refs)
    if merge:
        *stats, bundle_ref, dots_ref, shift_ref = refs
        merge_groups(scaling, shift_ref, stats)
        bundle_ref[: 4 * GROUP] = stats[0][...]
    else:
        shift_ref, dots_ref = refs
    rows, me, step = keys[0][0].shape[1], place_ref[0], pl.program_id(0)
    plan = [pair_tile(lengths_ref, rows, me)]
    for head, (tiles, _) in tiles_ahead(heads, plan, queries, keys, 2):
        at = step * heads + head
        for (query_slots, _, mask), (_, _, (raw, grads)) in zip(plan, tiles):
            shift = per_query(query_slots, 1, 0, at, shift_ref)
            weight = jnp.where(mask, jnp.exp2((raw - shift) * power), 0.0)
            dots = jnp.sum(weight * grads, axis=0, keepdims=True)
            for number, slot in enumerate(query_slots):
                dots_ref[row_of(slot, 1, 0, at), :] = lane_cut(dots, number, rows)
                if merge:
                    bundle_ref[row_of(4 + slot, 1, 0, at), :] = lane_cut(dots, number, rows)


def keys_kernel(based, heads, scaling, power, place_ref, lengths_ref, *refs):
    queries, keys, refs = split_refs(refs)
    (*base, shift_ref, mine, sent), refs = (refs[:4], refs[4:]) if based else (refs[:3], refs[3:])
    *extra, key_own, key_back, query_own, query_mate, total_ref = refs
    rows, me, step = keys[0][0].shape[1], place_ref[0], pl.program_id(0)
    plan = [pair_tile(lengths_ref, rows, me)]
    for number, parts in enumerate(group_parts(1, mine, sent, extra)):
        total_ref[number * GROUP : (number + 1) * GROUP, :] = sum(parts)
    outs = {("k", 0): key_own, ("k", 1): key_back, ("q", 0): query_own, ("q", 1): query_mate}
    out = Emitter(outs, {("k", 1): ref for ref in base})
    for head, (tiles, keep) in tiles_ahead(heads, plan, queries, keys, 2):
        at = step * heads + head
        sums = {}
        for (query_slots, key_slots, mask), ((q, _), (k, _), (raw, grads)) in zip(plan, tiles):
            shift = per_query(query_slots, 1, 0, at, shift_ref)
            dots = per_query(query_slots, 1, 0, at, total_ref)
            weight = jnp.where(mask, jnp.exp2((raw - shift) * power), 0.0)
            slope = (weight * (grads - dots) * scaling).astype(jnp.bfloat16)
            add_rows(sums, "k", key_slots, matmul(slope, q * keep, NN), rows)
            add_rows(sums, "q", query_slots, matmul(slope, k, TN), rows)
        for name, value in sums.items():
            out.emit(head, name, value)


def third_kernel(
    heads, scaling, power, place_ref, lengths_ref, q_third, o_third, k_back, v_back, value_part,
    stats, even, odd, value_out, key_out, query_out, dots_ref, shift_ref,
):
    rows, me, step = k_back.shape[1], place_ref[0], pl.program_id(0)
    columns = q_third.shape[1]
    parts = [stats[...], part_of(even, 2, 0)[:, :columns], part_of(odd, 2, 1)[:, :columns]]
    shift_ref[...] = merge_stats(scaling, parts)
    plan = [third_tile(lengths_ref, rows, columns, me)]
    mask = plan[0][2]
    queries, keys = (None, None, (q_third, o_third)), (None, (k_back, v_back))
    out = Emitter({"v": value_out, "k": key_out, "q": query_out}, {"v": value_part})
    for head, (tiles, keep) in tiles_ahead(heads, plan, queries, keys, 2):
        (q, o), (k, _), (raw, grads) = tiles[0]
        at = step * heads + head
        weight = jnp.where(mask, jnp.exp2((raw - shift_ref[pl.ds(at, 1), :]) * power), 0.0)
        dots = jnp.sum(weight * grads, axis=0, keepdims=True)
        dots_ref[pl.ds(at, 1), :] = dots
        total = dots + even[row_of(4, 1, 0, at), :][:, :columns] + odd[row_of(5, 1, 0, at), :][:, :columns]
        slope = (weight * (grads - total) * scaling).astype(jnp.bfloat16)
        out.emit(head, "v", matmul(weight.astype(jnp.bfloat16), o * keep, NN))
        out.emit(head, "k", matmul(slope, q * keep, NN))
        out.emit(head, "q", matmul(slope, k, TN))


def add_refs(*refs):
    return sum(ref[...].astype(jnp.float32) for ref in refs)


def sums_kernel(key_part, key_sent, query_part, query_sent, *refs):
    *extra, key_out, query_out = refs
    key_out[...] = add_refs(key_part, key_sent).astype(jnp.bfloat16)
    total = add_refs(query_part, query_sent)
    if extra:
        count = extra[0].shape[1]
        query_out[:, :count] = (total[:, :count] + add_refs(*extra)).astype(jnp.bfloat16)
        total = total[:, count:]
    if total.shape[1]:
        query_out[:, query_out.shape[1] - total.shape[1] :] = total.astype(jnp.bfloat16)


def halo_program(columns, queries, key_vectors, value_vectors, out_grad, facts):
    _, rows, width = queries.shape
    seq_size = lax.axis_size("seq")
    me = lax.axis_index("seq").astype(jnp.int32)
    scaling = HEAD ** (-0.5)
    power = scaling * math.log2(math.e)
    steps = width // HEAD // 4
    part = width // steps
    heads = part // HEAD
    devices = range(seq_size)
    mates = [(s, s ^ 1) for s in devices]
    ring = columns is None
    chain = [(s, s + 2) for s in devices if s + 2 < seq_size]
    ahead = [(s, (s + 2) % seq_size) for s in devices] if ring else chain
    behind = [(s, s - 2) for s in devices if s >= 2]
    if not ring:
        thirds = range(3, seq_size - 2, 2)
        relay, to_odd = [(t + 2, t) for t in thirds], [(t, t + 2) for t in thirds]
        from_even, to_even = [(t + 1, t) for t in thirds], [(t, t + 1) for t in thirds]

    def send(value, pairs):
        return lax.ppermute(value, "seq", pairs)

    smem = pl.BlockSpec(memory_space=pltpu.SMEM)
    def wide(count):
        return pl.BlockSpec((1, count, part), lambda step: (0, 0, step))

    def slim(count, lanes=rows):
        return pl.BlockSpec((count * GROUP, lanes), lambda step: (0, 0))

    def slim_shape(count, lanes=rows):
        return jax.ShapeDtypeStruct((count * GROUP, lanes), jnp.float32)

    def call(kernel, products, wides, slims, outs, slim_outs, plain=False, scratch=()):
        flops = 2 * products * 4 * rows * rows * width * 3 // 2
        lead = [] if plain else [me[None], facts]
        wide_shapes = [jax.ShapeDtypeStruct((1, count, width), jnp.bfloat16) for count in outs]
        return pl.pallas_call(
            kernel,
            grid=(steps,),
            in_specs=[smem] * len(lead)
            + [wide(value.shape[1]) for value in wides]
            + [slim(value.shape[0] // GROUP, value.shape[1]) for value in slims],
            out_specs=[wide(count) for count in outs] + [slim(*sizes) for sizes in slim_outs],
            out_shape=wide_shapes + [slim_shape(*sizes) for sizes in slim_outs],
            scratch_shapes=[pltpu.VMEM((count * GROUP, lanes), jnp.float32) for count, lanes in scratch],
            compiler_params=pltpu.CompilerParams(vmem_limit_bytes=20 * 1024 * 1024),
            cost_estimate=pl.CostEstimate(
                flops=flops, bytes_accessed=20 * rows * width, transcendentals=0
            ),
        )(*lead, *wides, *slims)

    query_mate = send(queries, mates)
    key_back = send(key_vectors, chain)
    grad_mate = send(out_grad, mates)
    value_back = send(value_vectors, ahead)
    grad_own, value_own, stats = call(
        functools.partial(stats_kernel, heads, power), 1,
        [queries, query_mate, key_vectors, key_back, out_grad, value_vectors], [], [rows] * 2, [(4,)],
    )
    stats_mate = send(stats, mates)
    rows_in = [queries, grad_own, query_mate, grad_mate]
    tensors = rows_in + [key_vectors, value_own, key_back, value_back]
    constants = (heads, scaling, power)
    if ring:
        value_part, value_sent, shift = call(
            functools.partial(values_kernel, True, *constants), 2, rows_in + [key_vectors, key_back],
            [stats, stats_mate], [rows] * 2, [(2,)],
        )
        (dots,) = call(functools.partial(dots_kernel, False, *constants), 2, tensors, [shift], [], [(2,)])
        dots_in, base, extra = [shift, dots, send(dots, mates)], [], []
    else:
        query_third = send(query_mate[:, :columns], relay)
        held, stats_mate = lax.optimization_barrier((grad_mate[:, :columns], stats_mate))
        grad_third = send(held, relay)
        query_third, _ = lax.optimization_barrier((query_third, value_back))
        (third_stats,) = call(
            functools.partial(third_stats_kernel, heads, power), 1, [query_third, key_back], [], [],
            [(2, columns)],
        )
        stats_in = [stats, stats_mate, send(third_stats, to_even), send(third_stats, to_odd)]
        bundle, dots, shift = call(
            functools.partial(dots_kernel, True, *constants), 2, tensors, stats_in, [], [(6,), (2,), (2,)],
        )
        even, odd, dots_mate = send(bundle, from_even), send(bundle, relay), send(dots, mates)
        value_part, value_back_part = call(
            functools.partial(values_kernel, False, *constants), 2, rows_in + [key_vectors, key_back],
            [shift], [rows] * 2, [],
        )
        value_back_part, dots_mate = lax.optimization_barrier((value_back_part, dots_mate))
        value_sent, key_third, query_third_part, third_dots = call(
            functools.partial(third_kernel, *constants), 2,
            [query_third, grad_third, key_back, value_back, value_back_part], [third_stats, even, odd],
            [rows, rows, columns], [(1, columns)], scratch=[(1, columns)],
        )
        dots_in = [shift, dots, dots_mate, send(third_dots, to_even), send(third_dots, to_odd)]
        base, extra = [key_third], [send(query_third_part, to_even)]
    value_received = send(value_sent, behind)
    key_part, key_sent, query_part, query_sent = call(
        functools.partial(keys_kernel, bool(base), *constants), 4, tensors + base, dots_in, [rows] * 4, [],
        scratch=[(2, rows)],
    )
    key_received = send(key_sent, behind)
    query_received = send(query_sent, mates)
    value_ready = (value_part.astype(jnp.float32) + value_received.astype(jnp.float32)).astype(jnp.bfloat16)
    key_ready, query_ready = call(
        sums_kernel, 0, [key_part, key_received, query_part, query_received, *extra], [], [rows] * 2, [],
        plain=True,
    )
    return query_ready, key_ready, value_ready


def program_kernel(shift, lengths_ref, out_ref):
    count = lengths_ref.shape[0]
    start, found, third = jnp.int32(0), jnp.int32(0), jnp.int32(-1)
    half = 1 << (shift - 1)
    for doc in range(count):
        end = start + lengths_ref[doc]
        last = (end - 1) >> shift
        spans = (last - (start >> shift) >= 3) & (last & 1 == 0)
        found = jnp.where(spans, jnp.where(end - (last << shift) <= half, 1, 2), found)
        third = jnp.where(spans, last - 1, third)
        out_ref[doc + 1] = lengths_ref[doc]
        start = end
    out_ref[0], out_ref[count + 1] = found, third


def program_facts(rows, doc_lengths):
    smem = pl.BlockSpec(memory_space=pltpu.SMEM)
    return pl.pallas_call(
        functools.partial(program_kernel, rows.bit_length() - 1),
        in_specs=[smem],
        out_specs=smem,
        out_shape=jax.ShapeDtypeStruct((doc_lengths.shape[0] + 2,), jnp.int32),
    )(doc_lengths)


def halo_shards(*arguments):
    *tensors, doc_lengths = arguments
    rows = tensors[0].shape[1]
    facts = program_facts(rows, doc_lengths)
    programs = [functools.partial(halo_program, columns) for columns in (None, rows // 2, rows)]
    return lax.switch(facts[0], programs, *tensors, facts)


def shards(queries, key_vectors, value_vectors, out_grad, doc_lengths):
    _, rows, width = queries.shape
    seq_size = lax.axis_size("seq")
    longest = rows * seq_size * 3 // 8
    fits = longest <= 3 * rows and seq_size % 2 == 0 and seq_size > 4 and rows == LANES
    heads = width // HEAD
    plan = halo_shards if fits and heads % 4 == 0 and heads <= GROUP else spread_shards
    return plan(queries, key_vectors, value_vectors, out_grad, doc_lengths)


def solution(mesh):
    return jax.shard_map(
        shards,
        mesh=mesh,
        in_specs=(
            P("section", "seq", "dp"),
            P("section", "seq", "dp"),
            P("section", "seq", "dp"),
            P("section", "seq", "dp"),
            P(),
        ),
        out_specs=(P("section", "seq", "dp"), P("section", "seq", "dp"), P("section", "seq", "dp")),
        check_vma=False,
    )
```

```python
import functools
import math
import jax
import jax.numpy as jnp
from jax import lax
from jax.experimental import pallas as pl
from jax.experimental.pallas import tpu as pltpu
from jax.sharding import PartitionSpec as P

HEAD = 224
LANES = 128
FLOOR = -1e30


def pick_slot(stacked, slot):
    return lax.dynamic_index_in_dim(stacked, slot, 0, keepdims=False)


def put_slot(stacked, update, slot):
    return lax.dynamic_update_index_in_dim(stacked, update, slot, 0)


def spread_shards(queries, key_vectors, value_vectors, out_grad, doc_lengths):
    local_rows = queries.shape[1]
    local_width = queries.shape[2]
    head_count = local_width // HEAD
    seq_size = lax.axis_size("seq")
    group = seq_size // head_count
    scaling = HEAD ** (-0.5)

    def spread(matrix):
        shaped = matrix.reshape(local_rows, head_count, 1, HEAD)
        copies = jnp.broadcast_to(shaped, (local_rows, head_count, group, HEAD))
        return copies.reshape(local_rows, seq_size * HEAD)

    query_head, key_head, value_head, cot_head = (
        lax.all_to_all(spread(queries), "seq", split_axis=1, concat_axis=0, tiled=True),
        lax.all_to_all(spread(key_vectors), "seq", split_axis=1, concat_axis=0, tiled=True),
        lax.all_to_all(spread(value_vectors), "seq", split_axis=1, concat_axis=0, tiled=True),
        lax.all_to_all(spread(out_grad), "seq", split_axis=1, concat_axis=0, tiled=True),
    )
    length = key_head.shape[0]
    member = lax.axis_index("seq") % group
    blocks = 2 * group
    block = length // blocks
    bounds = jnp.cumsum(doc_lengths)
    positions = jnp.arange(length, dtype=jnp.int32)
    doc_index = jnp.sum((positions[:, None] >= bounds[None, :]).astype(jnp.int32), axis=1)
    row_list = [member, blocks - 1 - member]
    query_list = []
    cot_list = []
    pos_list = []
    for which in range(2):
        offset = row_list[which] * block
        query_list.append(lax.dynamic_slice_in_dim(query_head, offset, block, 0))
        cot_list.append(lax.dynamic_slice_in_dim(cot_head, offset, block, 0))
        pos_list.append(offset + jnp.arange(block, dtype=jnp.int32))
    query_stack = jnp.stack(query_list)
    cot_stack = jnp.stack(cot_list)
    pos_stack = jnp.stack(pos_list)
    doc_stack = jnp.take(doc_index, pos_stack)
    plan = []
    for number in range(blocks + 1):
        first = number <= member
        slot = jnp.where(first, 0, 1).astype(jnp.int32)
        col_block = jnp.where(first, number, number - member - 1)
        flag = None
        plan.append((slot, col_block, flag))
    row_max = jnp.full((2, block), -jnp.inf, jnp.float32)
    row_sum = jnp.zeros((2, block), jnp.float32)
    stored = []
    for slot, col_block, flag in plan:

        def score_tile(carry, slot=slot, col_block=col_block):
            maxima, totals = carry
            query_rows = pick_slot(query_stack, slot)
            key_rows = lax.dynamic_slice_in_dim(key_head, col_block * block, block, 0)
            col_docs = lax.dynamic_slice_in_dim(doc_index, col_block * block, block, 0)
            col_positions = col_block * block + jnp.arange(block, dtype=jnp.int32)
            raw = jnp.dot(query_rows, key_rows.T, preferred_element_type=jnp.float32) * scaling
            allowed = (pick_slot(doc_stack, slot)[:, None] == col_docs[None, :]) & (
                pick_slot(pos_stack, slot)[:, None] >= col_positions[None, :]
            )
            scores = jnp.where(allowed, raw, -jnp.inf)
            before = pick_slot(maxima, slot)
            after = jnp.maximum(before, jnp.max(scores, axis=1))
            safe = jnp.where(jnp.isfinite(after), after, 0.0)
            total = pick_slot(totals, slot) * jnp.exp(before - safe) + jnp.sum(
                jnp.exp(scores - safe[:, None]), axis=1
            )
            return (scores, put_slot(maxima, after, slot), put_slot(totals, total, slot))

        scores, row_max, row_sum = score_tile((row_max, row_sum))
        stored.append(scores)

    def tile_weights(scores, slot):
        return (
            jnp.exp(scores - pick_slot(row_max, slot)[:, None]) / pick_slot(row_sum, slot)[:, None]
        )

    summed = jnp.zeros((2, block, HEAD), jnp.float32)
    for (slot, col_block, flag), scores in zip(plan, stored):

        def add_values(carry, slot=slot, col_block=col_block, scores=scores):
            rounded = tile_weights(scores, slot).astype(jnp.bfloat16)
            value_rows = lax.dynamic_slice_in_dim(value_head, col_block * block, block, 0)
            term = jnp.dot(rounded, value_rows, preferred_element_type=jnp.float32)
            return put_slot(carry, pick_slot(carry, slot) + term, slot)

        summed = add_values(summed)
    attended = summed.astype(jnp.bfloat16)
    row_dot = jnp.sum(cot_stack.astype(jnp.float32) * attended.astype(jnp.float32), axis=2)
    query_acc = jnp.zeros((2, block, HEAD), jnp.float32)
    key_acc = jnp.zeros((length, HEAD), jnp.float32)
    value_acc = jnp.zeros((length, HEAD), jnp.float32)
    for (slot, col_block, flag), scores in zip(plan, stored):

        def backward_tile(carry, slot=slot, col_block=col_block, scores=scores):
            query_sum, key_sum, value_sum = carry
            weights = tile_weights(scores, slot)
            rounded = weights.astype(jnp.bfloat16)
            query_rows = pick_slot(query_stack, slot)
            cot_rows = pick_slot(cot_stack, slot)
            start = col_block * block
            key_rows = lax.dynamic_slice_in_dim(key_head, start, block, 0)
            value_rows = lax.dynamic_slice_in_dim(value_head, start, block, 0)
            value_term = jnp.dot(rounded.T, cot_rows, preferred_element_type=jnp.float32)
            prob_grad = jnp.dot(cot_rows, value_rows.T, preferred_element_type=jnp.float32)
            score_grad = (
                weights * (prob_grad - pick_slot(row_dot, slot)[:, None]) * scaling
            ).astype(jnp.bfloat16)
            query_term = jnp.dot(score_grad, key_rows, preferred_element_type=jnp.float32)
            key_term = jnp.dot(score_grad.T, query_rows, preferred_element_type=jnp.float32)
            query_sum = put_slot(query_sum, pick_slot(query_sum, slot) + query_term, slot)
            key_sum = lax.dynamic_update_slice_in_dim(
                key_sum, lax.dynamic_slice_in_dim(key_sum, start, block, 0) + key_term, start, 0
            )
            value_sum = lax.dynamic_update_slice_in_dim(
                value_sum,
                lax.dynamic_slice_in_dim(value_sum, start, block, 0) + value_term,
                start,
                0,
            )
            return (query_sum, key_sum, value_sum)

        query_acc, key_acc, value_acc = backward_tile((query_acc, key_acc, value_acc))
    query_rounded = query_acc.astype(jnp.bfloat16)
    key_back, value_back = (
        lax.all_to_all(key_acc, "seq", split_axis=0, concat_axis=1, tiled=True),
        lax.all_to_all(value_acc, "seq", split_axis=0, concat_axis=1, tiled=True),
    )

    def settle(received):
        shaped = received.astype(jnp.float32).reshape(local_rows, head_count, group, HEAD)
        return jnp.sum(shaped, axis=2).reshape(1, local_rows, local_width).astype(jnp.bfloat16)

    query_full = jnp.zeros((length, HEAD), jnp.bfloat16)
    for which in range(2):
        query_full = lax.dynamic_update_slice_in_dim(
            query_full, query_rounded[which], row_list[which] * block, 0
        )
    query_back = lax.all_to_all(query_full, "seq", split_axis=0, concat_axis=1, tiled=True)
    query_out = settle(query_back)
    return (query_out, settle(key_back), settle(value_back))


NT = ((1,), (1,))
NN = ((1,), (0,))
TN = ((0,), (0,))
GROUP = 8


def head_span(head):
    low = head * HEAD // LANES * LANES
    high = -(-(head + 1) * HEAD // LANES) * LANES
    return low, high


def head_mask(head):
    low, high = head_span(head)
    lane = lax.broadcasted_iota(jnp.int32, (1, high - low), 1) + low
    inside = (lane >= head * HEAD) & (lane < (head + 1) * HEAD)
    return inside.astype(jnp.float32).astype(jnp.bfloat16)


def matmul(left, right, dims):
    return lax.dot_general(left, right, (dims, ((), ())), preferred_element_type=jnp.float32)


def stack(values, axis):
    return values[0] if len(values) == 1 else jnp.concatenate(values, axis=axis)


def allowed(lengths_ref, rows, query_block, key_block, columns=None):
    shape = (rows, columns or rows)
    position = query_block * rows + lax.broadcasted_iota(jnp.int32, shape, 1)
    keys = key_block * rows + lax.broadcasted_iota(jnp.int32, shape, 0)
    start = jnp.zeros_like(position)
    bound = jnp.int32(0)
    for doc in range(1, lengths_ref.shape[0] - 1):
        bound = bound + lengths_ref[doc]
        start = jnp.where(position >= bound, bound, start)
    return (keys >= start) & (keys <= position)


def make_tile(lengths_ref, rows, queries, keys):
    mask = stack(
        [stack([allowed(lengths_ref, rows, q, k) for _, q in queries], 1) for _, k in keys], 0
    )
    return [slot for slot, _ in queries], [slot for slot, _ in keys], mask


def tile_values(plan, head, queries, keys, products):
    low, high = head_span(head)
    keep = head_mask(head)

    def gather(refs, number, slots):
        return stack([refs[slot][number][0, :, low:high] for slot in slots], 0)

    out = []
    for query_slots, key_slots, _ in plan:
        q = [gather(queries, number, query_slots) for number in range(products)]
        k = [gather(keys, number, key_slots) * keep for number in range(products)]
        out.append((q, k, [matmul(b, a, NT) for a, b in zip(q, k)]))
    return out, keep


def tiles_ahead(heads, plan, queries, keys, products):
    ready = tile_values(plan, 0, queries, keys, products)
    for head in range(heads):
        now = ready
        if head + 1 < heads:
            ready = tile_values(plan, head + 1, queries, keys, products)
        yield head, now


def pair_tile(lengths_ref, rows, me):
    mate = me + 1 - 2 * lax.rem(me, 2)
    return make_tile(lengths_ref, rows, ((0, me), (1, mate)), ((0, me), (1, me - 2)))


def third_tile(facts_ref, rows, columns, me):
    mask = allowed(facts_ref, rows, me + 1, me - 2, columns)
    return [2], [1], mask & (me == facts_ref[facts_ref.shape[0] - 1])


def lane_cut(value, number, rows):
    return value[:, number * rows : (number + 1) * rows]


def row_of(group, kinds, kind, head):
    return pl.ds((group * kinds + kind) * GROUP + head, 1)


def per_query(slots, kinds, kind, head, ref):
    return stack([ref[row_of(slot, kinds, kind, head), :] for slot in slots], 1)


def collect_stats(heads, power, step, plan, queries, keys, rows, out_ref, groups):
    for head, (tiles, _) in tiles_ahead(heads, plan, queries, keys, 1):
        for (query_slots, _, mask), (_, _, (raw,)) in zip(plan, tiles):
            raw = jnp.where(mask, raw, FLOOR)
            top = jnp.max(raw, axis=0, keepdims=True)
            sums = jnp.sum(jnp.exp2((raw - top) * power), axis=0, keepdims=True)
            for number, slot in enumerate(query_slots):
                at = step * heads + head
                out_ref[row_of(groups[slot], 2, 0, at), :] = lane_cut(top, number, rows)
                out_ref[row_of(groups[slot], 2, 1, at), :] = lane_cut(sums, number, rows)


def stats_kernel(
    heads, power, place_ref, lengths_ref, q_own, q_mate, k_own, k_back, o_own, v_own, o_copy, v_copy, out_ref
):
    rows, me, step = k_own.shape[1], place_ref[0], pl.program_id(0)
    o_copy[...], v_copy[...] = o_own[...], v_own[...]
    plan = [pair_tile(lengths_ref, rows, me)]
    queries, keys = ((q_own,), (q_mate,)), ((k_own,), (k_back,))
    collect_stats(heads, power, step, plan, queries, keys, rows, out_ref, (0, 1))


def third_stats_kernel(heads, power, place_ref, lengths_ref, q_third, k_back, out_ref):
    rows, me, step = k_back.shape[1], place_ref[0], pl.program_id(0)
    plan = [third_tile(lengths_ref, rows, q_third.shape[1], me)]
    queries, keys = (None, None, (q_third,)), (None, (k_back,))
    collect_stats(heads, power, step, plan, queries, keys, rows, out_ref, (None, None, 0))


def part_of(ref, kinds, number):
    size = kinds * GROUP
    return ref[number * size : (number + 1) * size, :]


def group_parts(kinds, mine, sent, extra):
    own = [part_of(mine, kinds, 0), part_of(sent, kinds, 1)]
    mate = [part_of(mine, kinds, 1), part_of(sent, kinds, 0)]
    if extra:
        own, mate = own + [part_of(sent, kinds, 2)], mate + [extra[0][...]]
    return [own, mate]


def merge_groups(scaling, shift_ref, refs):
    mine, sent, *extra = refs
    for number, parts in enumerate(group_parts(2, mine, sent, extra)):
        shift_ref[number * GROUP : (number + 1) * GROUP, :] = merge_stats(scaling, parts)


def merge_stats(scaling, parts):
    split = [(jnp.where(p[GROUP:] > 0, p[:GROUP], FLOOR), p[GROUP:]) for p in parts]
    top = functools.reduce(jnp.maximum, [s[0] for s in split])
    total = sum(jnp.exp((s[0] - top) * scaling) * s[1] for s in split)
    return top + jnp.log(jnp.where(total > 0, total, 1.0)) / scaling


class Emitter:
    def __init__(self, outs, base={}):
        self.outs, self.base, self.carry = outs, base, {}

    def put(self, name, start, stop, value):
        if name in self.base:
            value = value + self.base[name][0, :, start:stop].astype(jnp.float32)
        self.outs[name][0, :, start:stop] = value.astype(jnp.bfloat16)

    def emit(self, head, name, value):
        low, high = head_span(head)
        first, last = head * HEAD % LANES == 0, (head + 1) * HEAD % LANES == 0
        start, stop = low, high
        if not first:
            self.put(name, low, low + LANES, value[:, :LANES] + self.carry.pop(name))
            start = low + LANES
        if not last:
            self.carry[name] = value[:, high - LANES - low :]
            stop = high - LANES
        if stop > start:
            self.put(name, start, stop, value[:, start - low : stop - low])


def add_rows(sums, kind, slots, value, rows):
    for number, slot in enumerate(slots):
        piece = value[number * rows : (number + 1) * rows]
        name = (kind, slot)
        sums[name] = sums[name] + piece if name in sums else piece


def split_refs(refs):
    return ((refs[0:2], refs[2:4]), (refs[4:6], refs[6:8]), refs[8:])


def values_kernel(merge, heads, scaling, power, place_ref, lengths_ref, q0, o0, q1, o1, k0, k1, *refs):
    queries, keys = ((q0, o0), (q1, o1)), ((k0,), (k1,))
    if merge:
        *stats, value_own, value_back, shift_ref = refs
        merge_groups(scaling, shift_ref, stats)
    else:
        shift_ref, value_own, value_back = refs
    rows, me, step = k0.shape[1], place_ref[0], pl.program_id(0)
    plan = [pair_tile(lengths_ref, rows, me)]
    out = Emitter({("v", 0): value_own, ("v", 1): value_back})
    for head, (tiles, keep) in tiles_ahead(heads, plan, queries, keys, 1):
        low, high = head_span(head)
        sums = {}
        for (query_slots, key_slots, mask), (_, _, (raw,)) in zip(plan, tiles):
            shift = per_query(query_slots, 1, 0, step * heads + head, shift_ref)
            weight = jnp.where(mask, jnp.exp2((raw - shift) * power), 0.0).astype(jnp.bfloat16)
            o = stack([queries[slot][1][0, :, low:high] for slot in query_slots], 0) * keep
            add_rows(sums, "v", key_slots, matmul(weight, o, NN), rows)
        for name, value in sums.items():
            out.emit(head, name, value)


def dots_kernel(merge, heads, scaling, power, place_ref, lengths_ref, *refs):
    queries, keys, refs = split_refs(refs)
    if merge:
        *stats, bundle_ref, dots_ref, shift_ref = refs
        merge_groups(scaling, shift_ref, stats)
        bundle_ref[: 4 * GROUP] = stats[0][...]
    else:
        shift_ref, dots_ref = refs
    rows, me, step = keys[0][0].shape[1], place_ref[0], pl.program_id(0)
    plan = [pair_tile(lengths_ref, rows, me)]
    for head, (tiles, _) in tiles_ahead(heads, plan, queries, keys, 2):
        at = step * heads + head
        for (query_slots, _, mask), (_, _, (raw, grads)) in zip(plan, tiles):
            shift = per_query(query_slots, 1, 0, at, shift_ref)
            weight = jnp.where(mask, jnp.exp2((raw - shift) * power), 0.0)
            dots = jnp.sum(weight * grads, axis=0, keepdims=True)
            for number, slot in enumerate(query_slots):
                dots_ref[row_of(slot, 1, 0, at), :] = lane_cut(dots, number, rows)
                if merge:
                    bundle_ref[row_of(4 + slot, 1, 0, at), :] = lane_cut(dots, number, rows)


def keys_kernel(based, heads, scaling, power, place_ref, lengths_ref, *refs):
    queries, keys, refs = split_refs(refs)
    (*base, shift_ref, mine, sent), refs = (refs[:4], refs[4:]) if based else (refs[:3], refs[3:])
    *extra, key_own, key_back, query_own, query_mate, total_ref = refs
    rows, me, step = keys[0][0].shape[1], place_ref[0], pl.program_id(0)
    plan = [pair_tile(lengths_ref, rows, me)]
    for number, parts in enumerate(group_parts(1, mine, sent, extra)):
        total_ref[number * GROUP : (number + 1) * GROUP, :] = sum(parts)
    outs = {("k", 0): key_own, ("k", 1): key_back, ("q", 0): query_own, ("q", 1): query_mate}
    out = Emitter(outs, {("k", 1): ref for ref in base})
    for head, (tiles, keep) in tiles_ahead(heads, plan, queries, keys, 2):
        at = step * heads + head
        sums = {}
        for (query_slots, key_slots, mask), ((q, _), (k, _), (raw, grads)) in zip(plan, tiles):
            shift = per_query(query_slots, 1, 0, at, shift_ref)
            dots = per_query(query_slots, 1, 0, at, total_ref)
            weight = jnp.where(mask, jnp.exp2((raw - shift) * power), 0.0)
            slope = (weight * (grads - dots) * scaling).astype(jnp.bfloat16)
            add_rows(sums, "k", key_slots, matmul(slope, q * keep, NN), rows)
            add_rows(sums, "q", query_slots, matmul(slope, k, TN), rows)
        for name, value in sums.items():
            out.emit(head, name, value)


def third_kernel(
    heads, scaling, power, place_ref, lengths_ref, q_third, o_third, k_back, v_back, value_part,
    stats, even, odd, value_out, key_out, query_out, dots_ref, shift_ref,
):
    rows, me, step = k_back.shape[1], place_ref[0], pl.program_id(0)
    columns = q_third.shape[1]
    parts = [stats[...], part_of(even, 2, 0)[:, :columns], part_of(odd, 2, 1)[:, :columns]]
    shift_ref[...] = merge_stats(scaling, parts)
    plan = [third_tile(lengths_ref, rows, columns, me)]
    mask = plan[0][2]
    queries, keys = (None, None, (q_third, o_third)), (None, (k_back, v_back))
    out = Emitter({"v": value_out, "k": key_out, "q": query_out}, {"v": value_part})
    for head, (tiles, keep) in tiles_ahead(heads, plan, queries, keys, 2):
        (q, o), (k, _), (raw, grads) = tiles[0]
        at = step * heads + head
        weight = jnp.where(mask, jnp.exp2((raw - shift_ref[pl.ds(at, 1), :]) * power), 0.0)
        dots = jnp.sum(weight * grads, axis=0, keepdims=True)
        dots_ref[pl.ds(at, 1), :] = dots
        total = dots + even[row_of(4, 1, 0, at), :][:, :columns] + odd[row_of(5, 1, 0, at), :][:, :columns]
        slope = (weight * (grads - total) * scaling).astype(jnp.bfloat16)
        out.emit(head, "v", matmul(weight.astype(jnp.bfloat16), o * keep, NN))
        out.emit(head, "k", matmul(slope, q * keep, NN))
        out.emit(head, "q", matmul(slope, k, TN))


def add_refs(*refs):
    return sum(ref[...].astype(jnp.float32) for ref in refs)


def sums_kernel(key_part, key_sent, query_part, query_sent, *refs):
    *extra, key_out, query_out = refs
    key_out[...] = add_refs(key_part, key_sent).astype(jnp.bfloat16)
    total = add_refs(query_part, query_sent)
    if extra:
        count = extra[0].shape[1]
        query_out[:, :count] = (total[:, :count] + add_refs(*extra)).astype(jnp.bfloat16)
        total = total[:, count:]
    if total.shape[1]:
        query_out[:, query_out.shape[1] - total.shape[1] :] = total.astype(jnp.bfloat16)


def halo_program(columns, queries, key_vectors, value_vectors, out_grad, facts):
    _, rows, width = queries.shape
    seq_size = lax.axis_size("seq")
    me = lax.axis_index("seq").astype(jnp.int32)
    scaling = HEAD ** (-0.5)
    power = scaling * math.log2(math.e)
    steps = width // HEAD // 4
    part = width // steps
    heads = part // HEAD
    devices = range(seq_size)
    def send(value, pairs):
        return lax.ppermute(value, "seq", pairs)

    mates = [(s, s ^ 1) for s in devices]
    ring = columns is None
    chain = [(s, s + 2) for s in devices if s + 2 < seq_size]
    ahead = [(s, (s + 2) % seq_size) for s in devices] if ring else chain
    behind = [(s, s - 2) for s in devices if s >= 2]
    if not ring:
        thirds = range(3, seq_size - 2, 2)
        relay, to_odd = [(t + 2, t) for t in thirds], [(t, t + 2) for t in thirds]
        from_even, to_even = [(t + 1, t) for t in thirds], [(t, t + 1) for t in thirds]

    def pass_on(value, terms):
        terms = jnp.pad(terms, ((0, 0), (0, rows - terms.shape[1])))
        far = send(terms, to_odd)
        return send(jnp.concatenate([value, far]), mates), far

    smem = pl.BlockSpec(memory_space=pltpu.SMEM)
    def wide(count):
        return pl.BlockSpec((1, count, part), lambda step: (0, 0, step))

    def slim(count, lanes=rows):
        return pl.BlockSpec((count * GROUP, lanes), lambda step: (0, 0))

    def slim_shape(count, lanes=rows):
        return jax.ShapeDtypeStruct((count * GROUP, lanes), jnp.float32)

    def call(kernel, products, wides, slims, outs, slim_outs, plain=False, scratch=()):
        flops = 2 * products * 4 * rows * rows * width * 3 // 2
        lead = [] if plain else [me[None], facts]
        wide_shapes = [jax.ShapeDtypeStruct((1, count, width), jnp.bfloat16) for count in outs]
        return pl.pallas_call(
            kernel,
            grid=(steps,),
            in_specs=[smem] * len(lead)
            + [wide(value.shape[1]) for value in wides]
            + [slim(value.shape[0] // GROUP, value.shape[1]) for value in slims],
            out_specs=[wide(count) for count in outs] + [slim(*sizes) for sizes in slim_outs],
            out_shape=wide_shapes + [slim_shape(*sizes) for sizes in slim_outs],
            scratch_shapes=[pltpu.VMEM((count * GROUP, lanes), jnp.float32) for count, lanes in scratch],
            compiler_params=pltpu.CompilerParams(vmem_limit_bytes=20 * 1024 * 1024),
            cost_estimate=pl.CostEstimate(
                flops=flops, bytes_accessed=20 * rows * width, transcendentals=0
            ),
        )(*lead, *wides, *slims)

    query_mate = send(queries, mates)
    key_back = send(key_vectors, chain)
    grad_mate = send(out_grad, mates)
    value_back = send(value_vectors, ahead)
    grad_own, value_own, stats = call(
        functools.partial(stats_kernel, heads, power), 1,
        [queries, query_mate, key_vectors, key_back, out_grad, value_vectors], [], [rows] * 2, [(4,)],
    )
    rows_in = [queries, grad_own, query_mate, grad_mate]
    tensors = rows_in + [key_vectors, value_own, key_back, value_back]
    constants = (heads, scaling, power)
    if ring:
        value_part, value_sent, shift = call(
            functools.partial(values_kernel, True, *constants), 2, rows_in + [key_vectors, key_back],
            [stats, send(stats, mates)], [rows] * 2, [(2,)],
        )
        (dots,) = call(functools.partial(dots_kernel, False, *constants), 2, tensors, [shift], [], [(2,)])
        dots_in, base, extra = [shift, dots, send(dots, mates)], [], []
    else:
        query_third = send(query_mate[:, :columns], relay)
        held, _ = lax.optimization_barrier((grad_mate[:, :columns], stats))
        grad_third = send(held, relay)
        query_third, *_ = lax.optimization_barrier((query_third, value_back, stats, held))
        (third_stats,) = call(
            functools.partial(third_stats_kernel, heads, power), 1, [query_third, key_back], [], [],
            [(2, columns)],
        )
        stats_in = [stats, *pass_on(stats, third_stats)]
        bundle, dots, shift = call(
            functools.partial(dots_kernel, True, *constants), 2, tensors, stats_in, [], [(6,), (2,), (2,)],
        )
        even, odd = send(bundle, from_even), send(bundle, relay)
        value_part, value_back_part = call(
            functools.partial(values_kernel, False, *constants), 2, rows_in + [key_vectors, key_back],
            [shift], [rows] * 2, [],
        )
        value_sent, key_third, query_third_part, third_dots = call(
            functools.partial(third_kernel, *constants), 2,
            [query_third, grad_third, key_back, value_back, value_back_part], [third_stats, even, odd],
            [rows, rows, columns], [(1, columns)], scratch=[(1, columns)],
        )
        dots_in = [shift, dots, *pass_on(dots, third_dots)]
        base, extra = [key_third], [send(query_third_part, to_even)]
    value_received = send(value_sent, behind)
    key_part, key_sent, query_part, query_sent = call(
        functools.partial(keys_kernel, bool(base), *constants), 4, tensors + base, dots_in, [rows] * 4, [],
        scratch=[(2, rows)],
    )
    key_received = send(key_sent, behind)
    query_received = send(query_sent, mates)
    value_ready = (value_part.astype(jnp.float32) + value_received.astype(jnp.float32)).astype(jnp.bfloat16)
    key_ready, query_ready = call(
        sums_kernel, 0, [key_part, key_received, query_part, query_received, *extra], [], [rows] * 2, [],
        plain=True,
    )
    return query_ready, key_ready, value_ready


def program_kernel(shift, lengths_ref, out_ref):
    count = lengths_ref.shape[0]
    start, found, third = jnp.int32(0), jnp.int32(0), jnp.int32(-1)
    half = 1 << (shift - 1)
    for doc in range(count):
        end = start + lengths_ref[doc]
        last = (end - 1) >> shift
        spans = (last - (start >> shift) >= 3) & (last & 1 == 0)
        found = jnp.where(spans, jnp.where(end - (last << shift) <= half, 1, 2), found)
        third = jnp.where(spans, last - 1, third)
        out_ref[doc + 1] = lengths_ref[doc]
        start = end
    out_ref[0], out_ref[count + 1] = found, third


def program_facts(rows, doc_lengths):
    smem = pl.BlockSpec(memory_space=pltpu.SMEM)
    return pl.pallas_call(
        functools.partial(program_kernel, rows.bit_length() - 1),
        in_specs=[smem],
        out_specs=smem,
        out_shape=jax.ShapeDtypeStruct((doc_lengths.shape[0] + 2,), jnp.int32),
    )(doc_lengths)


def halo_shards(*arguments):
    *tensors, doc_lengths = arguments
    rows = tensors[0].shape[1]
    facts = program_facts(rows, doc_lengths)
    programs = [functools.partial(halo_program, columns) for columns in (None, rows // 2, rows)]
    return lax.switch(facts[0], programs, *tensors, facts)


def shards(queries, key_vectors, value_vectors, out_grad, doc_lengths):
    _, rows, width = queries.shape
    seq_size = lax.axis_size("seq")
    longest = rows * seq_size * 3 // 8
    fits = longest <= 3 * rows and seq_size % 2 == 0 and seq_size > 4 and rows == LANES
    heads = width // HEAD
    plan = halo_shards if fits and heads % 4 == 0 and heads <= GROUP else spread_shards
    return plan(queries, key_vectors, value_vectors, out_grad, doc_lengths)


def solution(mesh):
    return jax.shard_map(
        shards,
        mesh=mesh,
        in_specs=(
            P("section", "seq", "dp"),
            P("section", "seq", "dp"),
            P("section", "seq", "dp"),
            P("section", "seq", "dp"),
            P(),
        ),
        out_specs=(P("section", "seq", "dp"), P("section", "seq", "dp"), P("section", "seq", "dp")),
        check_vma=False,
    )
```

```python
import functools
import math
import jax
import jax.numpy as jnp
from jax import lax
from jax.experimental import pallas as pl
from jax.experimental.pallas import tpu as pltpu
from jax.sharding import PartitionSpec as P

HEAD = 224
LANES = 128
FLOOR = -1e30


def pick_slot(stacked, slot):
    return lax.dynamic_index_in_dim(stacked, slot, 0, keepdims=False)


def put_slot(stacked, update, slot):
    return lax.dynamic_update_index_in_dim(stacked, update, slot, 0)


def spread_shards(queries, key_vectors, value_vectors, out_grad, doc_lengths):
    local_rows = queries.shape[1]
    local_width = queries.shape[2]
    head_count = local_width // HEAD
    seq_size = lax.axis_size("seq")
    group = seq_size // head_count
    scaling = HEAD ** (-0.5)

    def spread(matrix):
        shaped = matrix.reshape(local_rows, head_count, 1, HEAD)
        copies = jnp.broadcast_to(shaped, (local_rows, head_count, group, HEAD))
        return copies.reshape(local_rows, seq_size * HEAD)

    query_head, key_head, value_head, cot_head = (
        lax.all_to_all(spread(queries), "seq", split_axis=1, concat_axis=0, tiled=True),
        lax.all_to_all(spread(key_vectors), "seq", split_axis=1, concat_axis=0, tiled=True),
        lax.all_to_all(spread(value_vectors), "seq", split_axis=1, concat_axis=0, tiled=True),
        lax.all_to_all(spread(out_grad), "seq", split_axis=1, concat_axis=0, tiled=True),
    )
    length = key_head.shape[0]
    member = lax.axis_index("seq") % group
    blocks = 2 * group
    block = length // blocks
    bounds = jnp.cumsum(doc_lengths)
    positions = jnp.arange(length, dtype=jnp.int32)
    doc_index = jnp.sum((positions[:, None] >= bounds[None, :]).astype(jnp.int32), axis=1)
    row_list = [member, blocks - 1 - member]
    query_list = []
    cot_list = []
    pos_list = []
    for which in range(2):
        offset = row_list[which] * block
        query_list.append(lax.dynamic_slice_in_dim(query_head, offset, block, 0))
        cot_list.append(lax.dynamic_slice_in_dim(cot_head, offset, block, 0))
        pos_list.append(offset + jnp.arange(block, dtype=jnp.int32))
    query_stack = jnp.stack(query_list)
    cot_stack = jnp.stack(cot_list)
    pos_stack = jnp.stack(pos_list)
    doc_stack = jnp.take(doc_index, pos_stack)
    plan = []
    for number in range(blocks + 1):
        first = number <= member
        slot = jnp.where(first, 0, 1).astype(jnp.int32)
        col_block = jnp.where(first, number, number - member - 1)
        flag = None
        plan.append((slot, col_block, flag))
    row_max = jnp.full((2, block), -jnp.inf, jnp.float32)
    row_sum = jnp.zeros((2, block), jnp.float32)
    stored = []
    for slot, col_block, flag in plan:

        def score_tile(carry, slot=slot, col_block=col_block):
            maxima, totals = carry
            query_rows = pick_slot(query_stack, slot)
            key_rows = lax.dynamic_slice_in_dim(key_head, col_block * block, block, 0)
            col_docs = lax.dynamic_slice_in_dim(doc_index, col_block * block, block, 0)
            col_positions = col_block * block + jnp.arange(block, dtype=jnp.int32)
            raw = jnp.dot(query_rows, key_rows.T, preferred_element_type=jnp.float32) * scaling
            allowed = (pick_slot(doc_stack, slot)[:, None] == col_docs[None, :]) & (
                pick_slot(pos_stack, slot)[:, None] >= col_positions[None, :]
            )
            scores = jnp.where(allowed, raw, -jnp.inf)
            before = pick_slot(maxima, slot)
            after = jnp.maximum(before, jnp.max(scores, axis=1))
            safe = jnp.where(jnp.isfinite(after), after, 0.0)
            total = pick_slot(totals, slot) * jnp.exp(before - safe) + jnp.sum(
                jnp.exp(scores - safe[:, None]), axis=1
            )
            return (scores, put_slot(maxima, after, slot), put_slot(totals, total, slot))

        scores, row_max, row_sum = score_tile((row_max, row_sum))
        stored.append(scores)

    def tile_weights(scores, slot):
        return (
            jnp.exp(scores - pick_slot(row_max, slot)[:, None]) / pick_slot(row_sum, slot)[:, None]
        )

    summed = jnp.zeros((2, block, HEAD), jnp.float32)
    for (slot, col_block, flag), scores in zip(plan, stored):

        def add_values(carry, slot=slot, col_block=col_block, scores=scores):
            rounded = tile_weights(scores, slot).astype(jnp.bfloat16)
            value_rows = lax.dynamic_slice_in_dim(value_head, col_block * block, block, 0)
            term = jnp.dot(rounded, value_rows, preferred_element_type=jnp.float32)
            return put_slot(carry, pick_slot(carry, slot) + term, slot)

        summed = add_values(summed)
    attended = summed.astype(jnp.bfloat16)
    row_dot = jnp.sum(cot_stack.astype(jnp.float32) * attended.astype(jnp.float32), axis=2)
    query_acc = jnp.zeros((2, block, HEAD), jnp.float32)
    key_acc = jnp.zeros((length, HEAD), jnp.float32)
    value_acc = jnp.zeros((length, HEAD), jnp.float32)
    for (slot, col_block, flag), scores in zip(plan, stored):

        def backward_tile(carry, slot=slot, col_block=col_block, scores=scores):
            query_sum, key_sum, value_sum = carry
            weights = tile_weights(scores, slot)
            rounded = weights.astype(jnp.bfloat16)
            query_rows = pick_slot(query_stack, slot)
            cot_rows = pick_slot(cot_stack, slot)
            start = col_block * block
            key_rows = lax.dynamic_slice_in_dim(key_head, start, block, 0)
            value_rows = lax.dynamic_slice_in_dim(value_head, start, block, 0)
            value_term = jnp.dot(rounded.T, cot_rows, preferred_element_type=jnp.float32)
            prob_grad = jnp.dot(cot_rows, value_rows.T, preferred_element_type=jnp.float32)
            score_grad = (
                weights * (prob_grad - pick_slot(row_dot, slot)[:, None]) * scaling
            ).astype(jnp.bfloat16)
            query_term = jnp.dot(score_grad, key_rows, preferred_element_type=jnp.float32)
            key_term = jnp.dot(score_grad.T, query_rows, preferred_element_type=jnp.float32)
            query_sum = put_slot(query_sum, pick_slot(query_sum, slot) + query_term, slot)
            key_sum = lax.dynamic_update_slice_in_dim(
                key_sum, lax.dynamic_slice_in_dim(key_sum, start, block, 0) + key_term, start, 0
            )
            value_sum = lax.dynamic_update_slice_in_dim(
                value_sum,
                lax.dynamic_slice_in_dim(value_sum, start, block, 0) + value_term,
                start,
                0,
            )
            return (query_sum, key_sum, value_sum)

        query_acc, key_acc, value_acc = backward_tile((query_acc, key_acc, value_acc))
    query_rounded = query_acc.astype(jnp.bfloat16)
    key_back, value_back = (
        lax.all_to_all(key_acc, "seq", split_axis=0, concat_axis=1, tiled=True),
        lax.all_to_all(value_acc, "seq", split_axis=0, concat_axis=1, tiled=True),
    )

    def settle(received):
        shaped = received.astype(jnp.float32).reshape(local_rows, head_count, group, HEAD)
        return jnp.sum(shaped, axis=2).reshape(1, local_rows, local_width).astype(jnp.bfloat16)

    query_full = jnp.zeros((length, HEAD), jnp.bfloat16)
    for which in range(2):
        query_full = lax.dynamic_update_slice_in_dim(
            query_full, query_rounded[which], row_list[which] * block, 0
        )
    query_back = lax.all_to_all(query_full, "seq", split_axis=0, concat_axis=1, tiled=True)
    query_out = settle(query_back)
    return (query_out, settle(key_back), settle(value_back))


NT = ((1,), (1,))
NN = ((1,), (0,))
TN = ((0,), (0,))
GROUP = 8


def head_span(head):
    low = head * HEAD // LANES * LANES
    high = -(-(head + 1) * HEAD // LANES) * LANES
    return low, high


def head_mask(head):
    low, high = head_span(head)
    lane = lax.broadcasted_iota(jnp.int32, (1, high - low), 1) + low
    inside = (lane >= head * HEAD) & (lane < (head + 1) * HEAD)
    return inside.astype(jnp.float32).astype(jnp.bfloat16)


def matmul(left, right, dims):
    return lax.dot_general(left, right, (dims, ((), ())), preferred_element_type=jnp.float32)


def stack(values, axis):
    return values[0] if len(values) == 1 else jnp.concatenate(values, axis=axis)


def allowed(lengths_ref, rows, query_block, key_block, columns=None):
    shape = (rows, columns or rows)
    position = query_block * rows + lax.broadcasted_iota(jnp.int32, shape, 1)
    keys = key_block * rows + lax.broadcasted_iota(jnp.int32, shape, 0)
    start = jnp.zeros_like(position)
    bound = jnp.int32(0)
    for doc in range(1, lengths_ref.shape[0] - 1):
        bound = bound + lengths_ref[doc]
        start = jnp.where(position >= bound, bound, start)
    return (keys >= start) & (keys <= position)


def make_tile(lengths_ref, rows, queries, keys):
    mask = stack(
        [stack([allowed(lengths_ref, rows, q, k) for _, q in queries], 1) for _, k in keys], 0
    )
    return [slot for slot, _ in queries], [slot for slot, _ in keys], mask


def tile_values(plan, head, queries, keys, products):
    low, high = head_span(head)
    keep = head_mask(head)

    def gather(refs, number, slots):
        return stack([refs[slot][number][0, :, low:high] for slot in slots], 0)

    out = []
    for query_slots, key_slots, _ in plan:
        q = [gather(queries, number, query_slots) for number in range(products)]
        k = [gather(keys, number, key_slots) * keep for number in range(products)]
        out.append((q, k, [matmul(b, a, NT) for a, b in zip(q, k)]))
    return out, keep


def tiles_ahead(heads, plan, queries, keys, products):
    ready = tile_values(plan, 0, queries, keys, products)
    for head in range(heads):
        now = ready
        if head + 1 < heads:
            ready = tile_values(plan, head + 1, queries, keys, products)
        yield head, now


def pair_tile(lengths_ref, rows, me):
    mate = me + 1 - 2 * lax.rem(me, 2)
    return make_tile(lengths_ref, rows, ((0, me), (1, mate)), ((0, me), (1, me - 2)))


def third_tile(facts_ref, rows, columns, me):
    mask = allowed(facts_ref, rows, me + 1, me - 2, columns)
    return [2], [1], mask & (me == facts_ref[facts_ref.shape[0] - 1])


def lane_cut(value, number, rows):
    return value[:, number * rows : (number + 1) * rows]


def row_of(group, kinds, kind, head):
    return pl.ds((group * kinds + kind) * GROUP + head, 1)


def per_query(slots, kinds, kind, head, ref):
    return stack([ref[row_of(slot, kinds, kind, head), :] for slot in slots], 1)


def collect_stats(heads, power, step, plan, queries, keys, rows, out_ref, groups):
    for head, (tiles, _) in tiles_ahead(heads, plan, queries, keys, 1):
        for (query_slots, _, mask), (_, _, (raw,)) in zip(plan, tiles):
            raw = jnp.where(mask, raw, FLOOR)
            top = jnp.max(raw, axis=0, keepdims=True)
            sums = jnp.sum(jnp.exp2((raw - top) * power), axis=0, keepdims=True)
            for number, slot in enumerate(query_slots):
                at = step * heads + head
                out_ref[row_of(groups[slot], 2, 0, at), :] = lane_cut(top, number, rows)
                out_ref[row_of(groups[slot], 2, 1, at), :] = lane_cut(sums, number, rows)


def stats_kernel(
    heads, power, place_ref, lengths_ref, q_own, q_mate, k_own, k_back, o_own, v_own, o_copy, v_copy, out_ref
):
    rows, me, step = k_own.shape[1], place_ref[0], pl.program_id(0)
    o_copy[...], v_copy[...] = o_own[...], v_own[...]
    plan = [pair_tile(lengths_ref, rows, me)]
    queries, keys = ((q_own,), (q_mate,)), ((k_own,), (k_back,))
    collect_stats(heads, power, step, plan, queries, keys, rows, out_ref, (0, 1))


def third_stats_kernel(heads, power, place_ref, lengths_ref, q_third, k_back, out_ref):
    rows, me, step = k_back.shape[1], place_ref[0], pl.program_id(0)
    plan = [third_tile(lengths_ref, rows, q_third.shape[1], me)]
    queries, keys = (None, None, (q_third,)), (None, (k_back,))
    collect_stats(heads, power, step, plan, queries, keys, rows, out_ref, (None, None, 0))


def part_of(ref, kinds, number):
    size = kinds * GROUP
    return ref[number * size : (number + 1) * size, :]


def group_parts(kinds, mine, sent, extra):
    own = [part_of(mine, kinds, 0), part_of(sent, kinds, 1)]
    mate = [part_of(mine, kinds, 1), part_of(sent, kinds, 0)]
    if extra:
        own, mate = own + [part_of(sent, kinds, 2)], mate + [extra[0][...]]
    return [own, mate]


def merge_groups(scaling, shift_ref, refs):
    mine, sent, *extra = refs
    for number, parts in enumerate(group_parts(2, mine, sent, extra)):
        shift_ref[number * GROUP : (number + 1) * GROUP, :] = merge_stats(scaling, parts)


def merge_stats(scaling, parts):
    split = [(jnp.where(p[GROUP:] > 0, p[:GROUP], FLOOR), p[GROUP:]) for p in parts]
    top = functools.reduce(jnp.maximum, [s[0] for s in split])
    total = sum(jnp.exp((s[0] - top) * scaling) * s[1] for s in split)
    return top + jnp.log(jnp.where(total > 0, total, 1.0)) / scaling


class Emitter:
    def __init__(self, outs, base={}):
        self.outs, self.base, self.carry = outs, base, {}

    def put(self, name, start, stop, value):
        if name in self.base:
            value = value + self.base[name][0, :, start:stop].astype(jnp.float32)
        self.outs[name][0, :, start:stop] = value.astype(jnp.bfloat16)

    def emit(self, head, name, value):
        low, high = head_span(head)
        first, last = head * HEAD % LANES == 0, (head + 1) * HEAD % LANES == 0
        start, stop = low, high
        if not first:
            self.put(name, low, low + LANES, value[:, :LANES] + self.carry.pop(name))
            start = low + LANES
        if not last:
            self.carry[name] = value[:, high - LANES - low :]
            stop = high - LANES
        if stop > start:
            self.put(name, start, stop, value[:, start - low : stop - low])


def add_rows(sums, kind, slots, value, rows):
    for number, slot in enumerate(slots):
        piece = value[number * rows : (number + 1) * rows]
        name = (kind, slot)
        sums[name] = sums[name] + piece if name in sums else piece


def split_refs(refs):
    return ((refs[0:2], refs[2:4]), (refs[4:6], refs[6:8]), refs[8:])


def values_kernel(merge, heads, scaling, power, place_ref, lengths_ref, q0, o0, q1, o1, k0, k1, *refs):
    queries, keys = ((q0, o0), (q1, o1)), ((k0,), (k1,))
    if merge:
        *stats, value_own, value_back, shift_ref = refs
        merge_groups(scaling, shift_ref, stats)
    else:
        shift_ref, value_own, value_back = refs
    rows, me, step = k0.shape[1], place_ref[0], pl.program_id(0)
    plan = [pair_tile(lengths_ref, rows, me)]
    out = Emitter({("v", 0): value_own, ("v", 1): value_back})
    for head, (tiles, keep) in tiles_ahead(heads, plan, queries, keys, 1):
        low, high = head_span(head)
        sums = {}
        for (query_slots, key_slots, mask), (_, _, (raw,)) in zip(plan, tiles):
            shift = per_query(query_slots, 1, 0, step * heads + head, shift_ref)
            weight = jnp.where(mask, jnp.exp2((raw - shift) * power), 0.0).astype(jnp.bfloat16)
            o = stack([queries[slot][1][0, :, low:high] for slot in query_slots], 0) * keep
            add_rows(sums, "v", key_slots, matmul(weight, o, NN), rows)
        for name, value in sums.items():
            out.emit(head, name, value)


def dots_kernel(merge, heads, scaling, power, place_ref, lengths_ref, *refs):
    queries, keys, refs = split_refs(refs)
    if merge:
        *stats, bundle_ref, dots_ref, shift_ref = refs
        merge_groups(scaling, shift_ref, stats)
        bundle_ref[: 4 * GROUP] = stats[0][...]
    else:
        shift_ref, dots_ref = refs
    rows, me, step = keys[0][0].shape[1], place_ref[0], pl.program_id(0)
    plan = [pair_tile(lengths_ref, rows, me)]
    for head, (tiles, _) in tiles_ahead(heads, plan, queries, keys, 2):
        at = step * heads + head
        for (query_slots, _, mask), (_, _, (raw, grads)) in zip(plan, tiles):
            shift = per_query(query_slots, 1, 0, at, shift_ref)
            weight = jnp.where(mask, jnp.exp2((raw - shift) * power), 0.0)
            dots = jnp.sum(weight * grads, axis=0, keepdims=True)
            for number, slot in enumerate(query_slots):
                dots_ref[row_of(slot, 1, 0, at), :] = lane_cut(dots, number, rows)
                if merge:
                    bundle_ref[row_of(4 + slot, 1, 0, at), :] = lane_cut(dots, number, rows)


def keys_kernel(heads, scaling, power, place_ref, lengths_ref, *refs):
    queries, keys, refs = split_refs(refs)
    base, shift_ref, mine, sent, far, key_own, key_back, query_own, query_mate, total_ref = refs
    rows, me, step = keys[0][0].shape[1], place_ref[0], pl.program_id(0)
    plan = [pair_tile(lengths_ref, rows, me)]
    for number, parts in enumerate(group_parts(1, mine, sent, [far])):
        total_ref[number * GROUP : (number + 1) * GROUP, :] = sum(parts)
    outs = {("k", 0): key_own, ("k", 1): key_back, ("q", 0): query_own, ("q", 1): query_mate}
    out = Emitter(outs, {("k", 1): base})
    for head, (tiles, keep) in tiles_ahead(heads, plan, queries, keys, 2):
        at = step * heads + head
        sums = {}
        for (query_slots, key_slots, mask), ((q, _), (k, _), (raw, grads)) in zip(plan, tiles):
            shift = per_query(query_slots, 1, 0, at, shift_ref)
            dots = per_query(query_slots, 1, 0, at, total_ref)
            weight = jnp.where(mask, jnp.exp2((raw - shift) * power), 0.0)
            slope = (weight * (grads - dots) * scaling).astype(jnp.bfloat16)
            add_rows(sums, "k", key_slots, matmul(slope, q * keep, NN), rows)
            add_rows(sums, "q", query_slots, matmul(slope, k, TN), rows)
        for name, value in sums.items():
            out.emit(head, name, value)


def weights_kernel(heads, power, place_ref, lengths_ref, *refs):
    queries, keys, (shift_ref, _, weight_ref, product_ref) = split_refs(refs)
    rows, me, step = keys[0][0].shape[1], place_ref[0], pl.program_id(0)
    plan = [pair_tile(lengths_ref, rows, me)]
    for head, (tiles, _) in tiles_ahead(heads, plan, queries, keys, 2):
        (query_slots, _, mask), (_, _, (raw, grads)) = plan[0], tiles[0]
        shift = per_query(query_slots, 1, 0, step * heads + head, shift_ref)
        weight = jnp.where(mask, jnp.exp2((raw - shift) * power), 0.0)
        weight_ref[head] = weight.astype(jnp.bfloat16)
        product_ref[head] = (weight * grads).astype(jnp.bfloat16)


def split_keys_kernel(
    heads, scaling, q0, q1, k0, k1, weight_ref, product_ref, mine, sent, key_own, key_back, query_own,
    query_mate, total_ref,
):
    rows, step = k0.shape[1], pl.program_id(0)
    for number, parts in enumerate(group_parts(1, mine, sent, [])):
        total_ref[number * GROUP : (number + 1) * GROUP, :] = sum(parts)
    outs = {("k", 0): key_own, ("k", 1): key_back, ("q", 0): query_own, ("q", 1): query_mate}
    out = Emitter(outs)
    for head in range(heads):
        low, high = head_span(head)
        keep = head_mask(head)
        q = stack([ref[0, :, low:high] for ref in (q0, q1)], 0) * keep
        k = stack([ref[0, :, low:high] for ref in (k0, k1)], 0) * keep
        dots = per_query((0, 1), 1, 0, step * heads + head, total_ref)
        weight, product = weight_ref[head].astype(jnp.float32), product_ref[head].astype(jnp.float32)
        slope = ((product - weight * dots) * scaling).astype(jnp.bfloat16)
        sums = {}
        add_rows(sums, "k", (0, 1), matmul(slope, q, NN), rows)
        add_rows(sums, "q", (0, 1), matmul(slope, k, TN), rows)
        for name, value in sums.items():
            out.emit(head, name, value)


def third_kernel(
    heads, scaling, power, place_ref, lengths_ref, q_third, o_third, k_back, v_back, value_part,
    stats, even, odd, value_out, key_out, query_out, dots_ref, shift_ref,
):
    rows, me, step = k_back.shape[1], place_ref[0], pl.program_id(0)
    columns = q_third.shape[1]
    parts = [stats[...], part_of(even, 2, 0)[:, :columns], part_of(odd, 2, 1)[:, :columns]]
    shift_ref[...] = merge_stats(scaling, parts)
    plan = [third_tile(lengths_ref, rows, columns, me)]
    mask = plan[0][2]
    queries, keys = (None, None, (q_third, o_third)), (None, (k_back, v_back))
    out = Emitter({"v": value_out, "k": key_out, "q": query_out}, {"v": value_part})
    for head, (tiles, keep) in tiles_ahead(heads, plan, queries, keys, 2):
        (q, o), (k, _), (raw, grads) = tiles[0]
        at = step * heads + head
        weight = jnp.where(mask, jnp.exp2((raw - shift_ref[pl.ds(at, 1), :]) * power), 0.0)
        dots = jnp.sum(weight * grads, axis=0, keepdims=True)
        dots_ref[pl.ds(at, 1), :] = dots
        total = dots + even[row_of(4, 1, 0, at), :][:, :columns] + odd[row_of(5, 1, 0, at), :][:, :columns]
        slope = (weight * (grads - total) * scaling).astype(jnp.bfloat16)
        out.emit(head, "v", matmul(weight.astype(jnp.bfloat16), o * keep, NN))
        out.emit(head, "k", matmul(slope, q * keep, NN))
        out.emit(head, "q", matmul(slope, k, TN))


def add_refs(*refs):
    return sum(ref[...].astype(jnp.float32) for ref in refs)


def sums_kernel(key_part, key_sent, query_part, query_sent, *refs):
    *extra, key_out, query_out = refs
    key_out[...] = add_refs(key_part, key_sent).astype(jnp.bfloat16)
    total = add_refs(query_part, query_sent)
    if extra:
        count = extra[0].shape[1]
        query_out[:, :count] = (total[:, :count] + add_refs(*extra)).astype(jnp.bfloat16)
        total = total[:, count:]
    if total.shape[1]:
        query_out[:, query_out.shape[1] - total.shape[1] :] = total.astype(jnp.bfloat16)


def halo_program(columns, queries, key_vectors, value_vectors, out_grad, facts):
    _, rows, width = queries.shape
    seq_size = lax.axis_size("seq")
    me = lax.axis_index("seq").astype(jnp.int32)
    scaling = HEAD ** (-0.5)
    power = scaling * math.log2(math.e)
    steps = width // HEAD // 4
    part = width // steps
    heads = part // HEAD
    devices = range(seq_size)
    def send(value, pairs):
        return lax.ppermute(value, "seq", pairs)

    mates = [(s, s ^ 1) for s in devices]
    ring = columns is None
    chain = [(s, s + 2) for s in devices if s + 2 < seq_size]
    ahead = [(s, (s + 2) % seq_size) for s in devices] if ring else chain
    behind = [(s, s - 2) for s in devices if s >= 2]
    if not ring:
        thirds = range(3, seq_size - 2, 2)
        relay, to_odd = [(t + 2, t) for t in thirds], [(t, t + 2) for t in thirds]
        from_even, to_even = [(t + 1, t) for t in thirds], [(t, t + 1) for t in thirds]

    def pass_on(value, terms):
        terms = jnp.pad(terms, ((0, 0), (0, rows - terms.shape[1])))
        far = send(terms, to_odd)
        return send(jnp.concatenate([value, far]), mates), far

    smem = pl.BlockSpec(memory_space=pltpu.SMEM)
    def wide(count):
        return pl.BlockSpec((1, count, part), lambda step: (0, 0, step))

    def slim(count, lanes=rows):
        return pl.BlockSpec((count * GROUP, lanes), lambda step: (0, 0))

    def slim_shape(count, lanes=rows):
        return jax.ShapeDtypeStruct((count * GROUP, lanes), jnp.float32)

    cube = pl.BlockSpec((heads, 2 * rows, 2 * rows), lambda step: (step, 0, 0))
    cube_shape = jax.ShapeDtypeStruct((steps * heads, 2 * rows, 2 * rows), jnp.bfloat16)
    anywhere = pl.BlockSpec(memory_space=pl.ANY)

    def call(
        kernel, products, wides, slims, outs, slim_outs, plain=False, scratch=(), cubes=(), after=(), cube_outs=0
    ):
        flops = 2 * products * 4 * rows * rows * width * 3 // 2
        lead = [] if plain else [me[None], facts]
        wide_shapes = [jax.ShapeDtypeStruct((1, count, width), jnp.bfloat16) for count in outs]
        return pl.pallas_call(
            kernel,
            grid=(steps,),
            in_specs=[smem] * len(lead)
            + [wide(value.shape[1]) for value in wides]
            + [cube] * len(cubes)
            + [slim(value.shape[0] // GROUP, value.shape[1]) for value in slims]
            + [anywhere] * len(after),
            out_specs=[wide(count) for count in outs] + [slim(*sizes) for sizes in slim_outs] + [cube] * cube_outs,
            out_shape=wide_shapes + [slim_shape(*sizes) for sizes in slim_outs] + [cube_shape] * cube_outs,
            scratch_shapes=[pltpu.VMEM((count * GROUP, lanes), jnp.float32) for count, lanes in scratch],
            compiler_params=pltpu.CompilerParams(vmem_limit_bytes=20 * 1024 * 1024),
            cost_estimate=pl.CostEstimate(
                flops=flops, bytes_accessed=20 * rows * width, transcendentals=0
            ),
        )(*lead, *wides, *cubes, *slims, *after)

    query_mate = send(queries, mates)
    key_back = send(key_vectors, chain)
    grad_mate = send(out_grad, mates)
    value_back = send(value_vectors, ahead)
    grad_own, value_own, stats = call(
        functools.partial(stats_kernel, heads, power), 1,
        [queries, query_mate, key_vectors, key_back, out_grad, value_vectors], [], [rows] * 2, [(4,)],
    )
    rows_in = [queries, grad_own, query_mate, grad_mate]
    tensors = rows_in + [key_vectors, value_own, key_back, value_back]
    constants = (heads, scaling, power)
    if ring:
        value_part, value_sent, shift = call(
            functools.partial(values_kernel, True, *constants), 2, rows_in + [key_vectors, key_back],
            [stats, send(stats, mates)], [rows] * 2, [(2,)],
        )
        (dots,) = call(functools.partial(dots_kernel, False, *constants), 2, tensors, [shift], [], [(2,)])
        dots_mate, extra = send(dots, mates), []
        cubes = call(
            functools.partial(weights_kernel, heads, power), 2, tensors, [shift], [], [], after=[dots], cube_outs=2
        )
        key_part, key_sent, query_part, query_sent = call(
            functools.partial(split_keys_kernel, heads, scaling), 2,
            [queries, query_mate, key_vectors, key_back], [dots, dots_mate], [rows] * 4, [],
            plain=True, scratch=[(2, rows)], cubes=cubes,
        )
    else:
        query_third = send(query_mate[:, :columns], relay)
        held, _ = lax.optimization_barrier((grad_mate[:, :columns], stats))
        grad_third = send(held, relay)
        query_third, *_ = lax.optimization_barrier((query_third, value_back, stats, held))
        (third_stats,) = call(
            functools.partial(third_stats_kernel, heads, power), 1, [query_third, key_back], [], [],
            [(2, columns)],
        )
        stats_in = [stats, *pass_on(stats, third_stats)]
        bundle, dots, shift = call(
            functools.partial(dots_kernel, True, *constants), 2, tensors, stats_in, [], [(6,), (2,), (2,)],
        )
        even, odd = send(bundle, from_even), send(bundle, relay)
        value_part, value_back_part = call(
            functools.partial(values_kernel, False, *constants), 2, rows_in + [key_vectors, key_back],
            [shift], [rows] * 2, [],
        )
        value_sent, key_third, query_third_part, third_dots = call(
            functools.partial(third_kernel, *constants), 2,
            [query_third, grad_third, key_back, value_back, value_back_part], [third_stats, even, odd],
            [rows, rows, columns], [(1, columns)], scratch=[(1, columns)],
        )
        dots_in = [shift, dots, *pass_on(dots, third_dots)]
        extra = [send(query_third_part, to_even)]
        key_part, key_sent, query_part, query_sent = call(
            functools.partial(keys_kernel, *constants), 4, tensors + [key_third], dots_in, [rows] * 4, [],
            scratch=[(2, rows)],
        )
    value_received = send(value_sent, behind)
    key_received = send(key_sent, behind)
    query_received = send(query_sent, mates)
    value_ready = (value_part.astype(jnp.float32) + value_received.astype(jnp.float32)).astype(jnp.bfloat16)
    key_ready, query_ready = call(
        sums_kernel, 0, [key_part, key_received, query_part, query_received, *extra], [], [rows] * 2, [],
        plain=True,
    )
    return query_ready, key_ready, value_ready


def program_kernel(shift, lengths_ref, out_ref):
    count = lengths_ref.shape[0]
    start, found, third = jnp.int32(0), jnp.int32(0), jnp.int32(-1)
    half = 1 << (shift - 1)
    for doc in range(count):
        end = start + lengths_ref[doc]
        last = (end - 1) >> shift
        spans = (last - (start >> shift) >= 3) & (last & 1 == 0)
        found = jnp.where(spans, jnp.where(end - (last << shift) <= half, 1, 2), found)
        third = jnp.where(spans, last - 1, third)
        out_ref[doc + 1] = lengths_ref[doc]
        start = end
    out_ref[0], out_ref[count + 1] = found, third


def program_facts(rows, doc_lengths):
    smem = pl.BlockSpec(memory_space=pltpu.SMEM)
    return pl.pallas_call(
        functools.partial(program_kernel, rows.bit_length() - 1),
        in_specs=[smem],
        out_specs=smem,
        out_shape=jax.ShapeDtypeStruct((doc_lengths.shape[0] + 2,), jnp.int32),
    )(doc_lengths)


def halo_shards(*arguments):
    *tensors, doc_lengths = arguments
    rows = tensors[0].shape[1]
    facts = program_facts(rows, doc_lengths)
    programs = [functools.partial(halo_program, columns) for columns in (None, rows // 2, rows)]
    return lax.switch(facts[0], programs, *tensors, facts)


def shards(queries, key_vectors, value_vectors, out_grad, doc_lengths):
    _, rows, width = queries.shape
    seq_size = lax.axis_size("seq")
    longest = rows * seq_size * 3 // 8
    fits = longest <= 3 * rows and seq_size % 2 == 0 and seq_size > 4 and rows == LANES
    heads = width // HEAD
    plan = halo_shards if fits and heads % 4 == 0 and heads <= GROUP else spread_shards
    return plan(queries, key_vectors, value_vectors, out_grad, doc_lengths)


def solution(mesh):
    return jax.shard_map(
        shards,
        mesh=mesh,
        in_specs=(
            P("section", "seq", "dp"),
            P("section", "seq", "dp"),
            P("section", "seq", "dp"),
            P("section", "seq", "dp"),
            P(),
        ),
        out_specs=(P("section", "seq", "dp"), P("section", "seq", "dp"), P("section", "seq", "dp")),
        check_vma=False,
    )
```

```python
import functools
import math
import jax
import jax.numpy as jnp
from jax import lax
from jax.experimental import pallas as pl
from jax.experimental.pallas import tpu as pltpu
from jax.sharding import PartitionSpec as P

HEAD = 224
LANES = 128
FLOOR = -1e30


def pick_slot(stacked, slot):
    return lax.dynamic_index_in_dim(stacked, slot, 0, keepdims=False)


def put_slot(stacked, update, slot):
    return lax.dynamic_update_index_in_dim(stacked, update, slot, 0)


def spread_shards(queries, key_vectors, value_vectors, out_grad, doc_lengths):
    local_rows = queries.shape[1]
    local_width = queries.shape[2]
    head_count = local_width // HEAD
    seq_size = lax.axis_size("seq")
    group = seq_size // head_count
    scaling = HEAD ** (-0.5)

    def spread(matrix):
        shaped = matrix.reshape(local_rows, head_count, 1, HEAD)
        copies = jnp.broadcast_to(shaped, (local_rows, head_count, group, HEAD))
        return copies.reshape(local_rows, seq_size * HEAD)

    query_head, key_head, value_head, cot_head = (
        lax.all_to_all(spread(queries), "seq", split_axis=1, concat_axis=0, tiled=True),
        lax.all_to_all(spread(key_vectors), "seq", split_axis=1, concat_axis=0, tiled=True),
        lax.all_to_all(spread(value_vectors), "seq", split_axis=1, concat_axis=0, tiled=True),
        lax.all_to_all(spread(out_grad), "seq", split_axis=1, concat_axis=0, tiled=True),
    )
    length = key_head.shape[0]
    member = lax.axis_index("seq") % group
    blocks = 2 * group
    block = length // blocks
    bounds = jnp.cumsum(doc_lengths)
    positions = jnp.arange(length, dtype=jnp.int32)
    doc_index = jnp.sum((positions[:, None] >= bounds[None, :]).astype(jnp.int32), axis=1)
    row_list = [member, blocks - 1 - member]
    query_list = []
    cot_list = []
    pos_list = []
    for which in range(2):
        offset = row_list[which] * block
        query_list.append(lax.dynamic_slice_in_dim(query_head, offset, block, 0))
        cot_list.append(lax.dynamic_slice_in_dim(cot_head, offset, block, 0))
        pos_list.append(offset + jnp.arange(block, dtype=jnp.int32))
    query_stack = jnp.stack(query_list)
    cot_stack = jnp.stack(cot_list)
    pos_stack = jnp.stack(pos_list)
    doc_stack = jnp.take(doc_index, pos_stack)
    plan = []
    for number in range(blocks + 1):
        first = number <= member
        slot = jnp.where(first, 0, 1).astype(jnp.int32)
        col_block = jnp.where(first, number, number - member - 1)
        flag = None
        plan.append((slot, col_block, flag))
    row_max = jnp.full((2, block), -jnp.inf, jnp.float32)
    row_sum = jnp.zeros((2, block), jnp.float32)
    stored = []
    for slot, col_block, flag in plan:

        def score_tile(carry, slot=slot, col_block=col_block):
            maxima, totals = carry
            query_rows = pick_slot(query_stack, slot)
            key_rows = lax.dynamic_slice_in_dim(key_head, col_block * block, block, 0)
            col_docs = lax.dynamic_slice_in_dim(doc_index, col_block * block, block, 0)
            col_positions = col_block * block + jnp.arange(block, dtype=jnp.int32)
            raw = jnp.dot(query_rows, key_rows.T, preferred_element_type=jnp.float32) * scaling
            allowed = (pick_slot(doc_stack, slot)[:, None] == col_docs[None, :]) & (
                pick_slot(pos_stack, slot)[:, None] >= col_positions[None, :]
            )
            scores = jnp.where(allowed, raw, -jnp.inf)
            before = pick_slot(maxima, slot)
            after = jnp.maximum(before, jnp.max(scores, axis=1))
            safe = jnp.where(jnp.isfinite(after), after, 0.0)
            total = pick_slot(totals, slot) * jnp.exp(before - safe) + jnp.sum(
                jnp.exp(scores - safe[:, None]), axis=1
            )
            return (scores, put_slot(maxima, after, slot), put_slot(totals, total, slot))

        scores, row_max, row_sum = score_tile((row_max, row_sum))
        stored.append(scores)

    def tile_weights(scores, slot):
        return (
            jnp.exp(scores - pick_slot(row_max, slot)[:, None]) / pick_slot(row_sum, slot)[:, None]
        )

    summed = jnp.zeros((2, block, HEAD), jnp.float32)
    for (slot, col_block, flag), scores in zip(plan, stored):

        def add_values(carry, slot=slot, col_block=col_block, scores=scores):
            rounded = tile_weights(scores, slot).astype(jnp.bfloat16)
            value_rows = lax.dynamic_slice_in_dim(value_head, col_block * block, block, 0)
            term = jnp.dot(rounded, value_rows, preferred_element_type=jnp.float32)
            return put_slot(carry, pick_slot(carry, slot) + term, slot)

        summed = add_values(summed)
    attended = summed.astype(jnp.bfloat16)
    row_dot = jnp.sum(cot_stack.astype(jnp.float32) * attended.astype(jnp.float32), axis=2)
    query_acc = jnp.zeros((2, block, HEAD), jnp.float32)
    key_acc = jnp.zeros((length, HEAD), jnp.float32)
    value_acc = jnp.zeros((length, HEAD), jnp.float32)
    for (slot, col_block, flag), scores in zip(plan, stored):

        def backward_tile(carry, slot=slot, col_block=col_block, scores=scores):
            query_sum, key_sum, value_sum = carry
            weights = tile_weights(scores, slot)
            rounded = weights.astype(jnp.bfloat16)
            query_rows = pick_slot(query_stack, slot)
            cot_rows = pick_slot(cot_stack, slot)
            start = col_block * block
            key_rows = lax.dynamic_slice_in_dim(key_head, start, block, 0)
            value_rows = lax.dynamic_slice_in_dim(value_head, start, block, 0)
            value_term = jnp.dot(rounded.T, cot_rows, preferred_element_type=jnp.float32)
            prob_grad = jnp.dot(cot_rows, value_rows.T, preferred_element_type=jnp.float32)
            score_grad = (
                weights * (prob_grad - pick_slot(row_dot, slot)[:, None]) * scaling
            ).astype(jnp.bfloat16)
            query_term = jnp.dot(score_grad, key_rows, preferred_element_type=jnp.float32)
            key_term = jnp.dot(score_grad.T, query_rows, preferred_element_type=jnp.float32)
            query_sum = put_slot(query_sum, pick_slot(query_sum, slot) + query_term, slot)
            key_sum = lax.dynamic_update_slice_in_dim(
                key_sum, lax.dynamic_slice_in_dim(key_sum, start, block, 0) + key_term, start, 0
            )
            value_sum = lax.dynamic_update_slice_in_dim(
                value_sum,
                lax.dynamic_slice_in_dim(value_sum, start, block, 0) + value_term,
                start,
                0,
            )
            return (query_sum, key_sum, value_sum)

        query_acc, key_acc, value_acc = backward_tile((query_acc, key_acc, value_acc))
    query_rounded = query_acc.astype(jnp.bfloat16)
    key_back, value_back = (
        lax.all_to_all(key_acc, "seq", split_axis=0, concat_axis=1, tiled=True),
        lax.all_to_all(value_acc, "seq", split_axis=0, concat_axis=1, tiled=True),
    )

    def settle(received):
        shaped = received.astype(jnp.float32).reshape(local_rows, head_count, group, HEAD)
        return jnp.sum(shaped, axis=2).reshape(1, local_rows, local_width).astype(jnp.bfloat16)

    query_full = jnp.zeros((length, HEAD), jnp.bfloat16)
    for which in range(2):
        query_full = lax.dynamic_update_slice_in_dim(
            query_full, query_rounded[which], row_list[which] * block, 0
        )
    query_back = lax.all_to_all(query_full, "seq", split_axis=0, concat_axis=1, tiled=True)
    query_out = settle(query_back)
    return (query_out, settle(key_back), settle(value_back))


NT = ((1,), (1,))
NN = ((1,), (0,))
TN = ((0,), (0,))
GROUP = 8


def head_span(head):
    low = head * HEAD // LANES * LANES
    high = -(-(head + 1) * HEAD // LANES) * LANES
    return low, high


def head_mask(head):
    low, high = head_span(head)
    lane = lax.broadcasted_iota(jnp.int32, (1, high - low), 1) + low
    inside = (lane >= head * HEAD) & (lane < (head + 1) * HEAD)
    return inside.astype(jnp.float32).astype(jnp.bfloat16)


def matmul(left, right, dims):
    return lax.dot_general(left, right, (dims, ((), ())), preferred_element_type=jnp.float32)


def stack(values, axis):
    return values[0] if len(values) == 1 else jnp.concatenate(values, axis=axis)


def allowed(lengths_ref, rows, query_block, key_block, columns=None):
    shape = (rows, columns or rows)
    position = query_block * rows + lax.broadcasted_iota(jnp.int32, shape, 1)
    keys = key_block * rows + lax.broadcasted_iota(jnp.int32, shape, 0)
    start = jnp.zeros_like(position)
    bound = jnp.int32(0)
    for doc in range(1, lengths_ref.shape[0] - 1):
        bound = bound + lengths_ref[doc]
        start = jnp.where(position >= bound, bound, start)
    return (keys >= start) & (keys <= position)


def make_tile(lengths_ref, rows, queries, keys):
    mask = stack(
        [stack([allowed(lengths_ref, rows, q, k) for _, q in queries], 1) for _, k in keys], 0
    )
    return [slot for slot, _ in queries], [slot for slot, _ in keys], mask


def tile_values(plan, head, queries, keys, products):
    low, high = head_span(head)
    keep = head_mask(head)

    def gather(refs, number, slots):
        return stack([refs[slot][number][0, :, low:high] for slot in slots], 0)

    out = []
    for query_slots, key_slots, _ in plan:
        q = [gather(queries, number, query_slots) for number in range(products)]
        k = [gather(keys, number, key_slots) * keep for number in range(products)]
        out.append((q, k, [matmul(b, a, NT) for a, b in zip(q, k)]))
    return out, keep


def tiles_ahead(heads, plan, queries, keys, products):
    ready = tile_values(plan, 0, queries, keys, products)
    for head in range(heads):
        now = ready
        if head + 1 < heads:
            ready = tile_values(plan, head + 1, queries, keys, products)
        yield head, now


def pair_tile(lengths_ref, rows, me):
    mate = me + 1 - 2 * lax.rem(me, 2)
    return make_tile(lengths_ref, rows, ((0, me), (1, mate)), ((0, me), (1, me - 2)))


def third_tile(facts_ref, rows, columns, me):
    mask = allowed(facts_ref, rows, me + 1, me - 2, columns)
    return [2], [1], mask & (me == facts_ref[facts_ref.shape[0] - 1])


def lane_cut(value, number, rows):
    return value[:, number * rows : (number + 1) * rows]


def row_of(group, kinds, kind, head):
    return pl.ds((group * kinds + kind) * GROUP + head, 1)


def per_query(slots, kinds, kind, head, ref):
    return stack([ref[row_of(slot, kinds, kind, head), :] for slot in slots], 1)


def collect_stats(heads, power, step, plan, queries, keys, rows, out_ref, groups):
    for head, (tiles, _) in tiles_ahead(heads, plan, queries, keys, 1):
        for (query_slots, _, mask), (_, _, (raw,)) in zip(plan, tiles):
            raw = jnp.where(mask, raw, FLOOR)
            top = jnp.max(raw, axis=0, keepdims=True)
            sums = jnp.sum(jnp.exp2((raw - top) * power), axis=0, keepdims=True)
            for number, slot in enumerate(query_slots):
                at = step * heads + head
                out_ref[row_of(groups[slot], 2, 0, at), :] = lane_cut(top, number, rows)
                out_ref[row_of(groups[slot], 2, 1, at), :] = lane_cut(sums, number, rows)


def stats_kernel(
    heads, power, place_ref, lengths_ref, q_own, q_mate, k_own, k_back, o_own, v_own, o_copy, v_copy, out_ref
):
    rows, me, step = k_own.shape[1], place_ref[0], pl.program_id(0)
    o_copy[...], v_copy[...] = o_own[...], v_own[...]
    plan = [pair_tile(lengths_ref, rows, me)]
    queries, keys = ((q_own,), (q_mate,)), ((k_own,), (k_back,))
    collect_stats(heads, power, step, plan, queries, keys, rows, out_ref, (0, 1))


def third_stats_kernel(heads, power, place_ref, lengths_ref, q_third, k_back, out_ref):
    rows, me, step = k_back.shape[1], place_ref[0], pl.program_id(0)
    plan = [third_tile(lengths_ref, rows, q_third.shape[1], me)]
    queries, keys = (None, None, (q_third,)), (None, (k_back,))
    collect_stats(heads, power, step, plan, queries, keys, rows, out_ref, (None, None, 0))


def part_of(ref, kinds, number):
    size = kinds * GROUP
    return ref[number * size : (number + 1) * size, :]


def group_parts(kinds, mine, sent, extra):
    own = [part_of(mine, kinds, 0), part_of(sent, kinds, 1)]
    mate = [part_of(mine, kinds, 1), part_of(sent, kinds, 0)]
    if extra:
        own, mate = own + [part_of(sent, kinds, 2)], mate + [extra[0][...]]
    return [own, mate]


def merge_groups(scaling, shift_ref, refs):
    mine, sent, *extra = refs
    for number, parts in enumerate(group_parts(2, mine, sent, extra)):
        shift_ref[number * GROUP : (number + 1) * GROUP, :] = merge_stats(scaling, parts)


def merge_stats(scaling, parts):
    split = [(jnp.where(p[GROUP:] > 0, p[:GROUP], FLOOR), p[GROUP:]) for p in parts]
    top = functools.reduce(jnp.maximum, [s[0] for s in split])
    total = sum(jnp.exp((s[0] - top) * scaling) * s[1] for s in split)
    return top + jnp.log(jnp.where(total > 0, total, 1.0)) / scaling


class Emitter:
    def __init__(self, outs, base={}):
        self.outs, self.base, self.carry = outs, base, {}

    def put(self, name, start, stop, value):
        if name in self.base:
            value = value + self.base[name][0, :, start:stop].astype(jnp.float32)
        self.outs[name][0, :, start:stop] = value.astype(jnp.bfloat16)

    def emit(self, head, name, value):
        low, high = head_span(head)
        first, last = head * HEAD % LANES == 0, (head + 1) * HEAD % LANES == 0
        start, stop = low, high
        if not first:
            self.put(name, low, low + LANES, value[:, :LANES] + self.carry.pop(name))
            start = low + LANES
        if not last:
            self.carry[name] = value[:, high - LANES - low :]
            stop = high - LANES
        if stop > start:
            self.put(name, start, stop, value[:, start - low : stop - low])


def add_rows(sums, kind, slots, value, rows):
    for number, slot in enumerate(slots):
        piece = value[number * rows : (number + 1) * rows]
        name = (kind, slot)
        sums[name] = sums[name] + piece if name in sums else piece


def split_refs(refs):
    return ((refs[0:2], refs[2:4]), (refs[4:6], refs[6:8]), refs[8:])


def values_kernel(merge, heads, scaling, power, place_ref, lengths_ref, q0, o0, q1, o1, k0, k1, *refs):
    queries, keys = ((q0, o0), (q1, o1)), ((k0,), (k1,))
    if merge:
        *stats, value_own, value_back, shift_ref = refs
        merge_groups(scaling, shift_ref, stats)
    else:
        shift_ref, value_own, value_back = refs
    rows, me, step = k0.shape[1], place_ref[0], pl.program_id(0)
    plan = [pair_tile(lengths_ref, rows, me)]
    out = Emitter({("v", 0): value_own, ("v", 1): value_back})
    for head, (tiles, keep) in tiles_ahead(heads, plan, queries, keys, 1):
        low, high = head_span(head)
        sums = {}
        for (query_slots, key_slots, mask), (_, _, (raw,)) in zip(plan, tiles):
            shift = per_query(query_slots, 1, 0, step * heads + head, shift_ref)
            weight = jnp.where(mask, jnp.exp2((raw - shift) * power), 0.0).astype(jnp.bfloat16)
            o = stack([queries[slot][1][0, :, low:high] for slot in query_slots], 0) * keep
            add_rows(sums, "v", key_slots, matmul(weight, o, NN), rows)
        for name, value in sums.items():
            out.emit(head, name, value)


def dots_kernel(merge, heads, scaling, power, place_ref, lengths_ref, *refs):
    queries, keys, refs = split_refs(refs)
    if merge:
        *stats, bundle_ref, dots_ref, shift_ref = refs
        merge_groups(scaling, shift_ref, stats)
        bundle_ref[: 4 * GROUP] = stats[0][...]
    else:
        shift_ref, dots_ref = refs
    rows, me, step = keys[0][0].shape[1], place_ref[0], pl.program_id(0)
    plan = [pair_tile(lengths_ref, rows, me)]
    for head, (tiles, _) in tiles_ahead(heads, plan, queries, keys, 2):
        at = step * heads + head
        for (query_slots, _, mask), (_, _, (raw, grads)) in zip(plan, tiles):
            shift = per_query(query_slots, 1, 0, at, shift_ref)
            weight = jnp.where(mask, jnp.exp2((raw - shift) * power), 0.0)
            dots = jnp.sum(weight * grads, axis=0, keepdims=True)
            for number, slot in enumerate(query_slots):
                dots_ref[row_of(slot, 1, 0, at), :] = lane_cut(dots, number, rows)
                if merge:
                    bundle_ref[row_of(4 + slot, 1, 0, at), :] = lane_cut(dots, number, rows)


def keys_kernel(heads, scaling, power, place_ref, lengths_ref, *refs):
    queries, keys, refs = split_refs(refs)
    base, shift_ref, mine, sent, far, key_own, key_back, query_own, query_mate, total_ref = refs
    rows, me, step = keys[0][0].shape[1], place_ref[0], pl.program_id(0)
    plan = [pair_tile(lengths_ref, rows, me)]
    for number, parts in enumerate(group_parts(1, mine, sent, [far])):
        total_ref[number * GROUP : (number + 1) * GROUP, :] = sum(parts)
    outs = {("k", 0): key_own, ("k", 1): key_back, ("q", 0): query_own, ("q", 1): query_mate}
    out = Emitter(outs, {("k", 1): base})
    for head, (tiles, keep) in tiles_ahead(heads, plan, queries, keys, 2):
        at = step * heads + head
        sums = {}
        for (query_slots, key_slots, mask), ((q, _), (k, _), (raw, grads)) in zip(plan, tiles):
            shift = per_query(query_slots, 1, 0, at, shift_ref)
            dots = per_query(query_slots, 1, 0, at, total_ref)
            weight = jnp.where(mask, jnp.exp2((raw - shift) * power), 0.0)
            slope = (weight * (grads - dots) * scaling).astype(jnp.bfloat16)
            add_rows(sums, "k", key_slots, matmul(slope, q * keep, NN), rows)
            add_rows(sums, "q", query_slots, matmul(slope, k, TN), rows)
        for name, value in sums.items():
            out.emit(head, name, value)


def weights_kernel(heads, power, place_ref, lengths_ref, *refs):
    queries, keys, (shift_ref, _, weight_ref, product_ref) = split_refs(refs)
    rows, me, step = keys[0][0].shape[1], place_ref[0], pl.program_id(0)
    plan = [pair_tile(lengths_ref, rows, me)]
    for head, (tiles, _) in tiles_ahead(heads, plan, queries, keys, 2):
        (query_slots, _, mask), (_, _, (raw, grads)) = plan[0], tiles[0]
        shift = per_query(query_slots, 1, 0, step * heads + head, shift_ref)
        weight = jnp.where(mask, jnp.exp2((raw - shift) * power), 0.0)
        weight_ref[head] = weight.astype(jnp.bfloat16)
        product_ref[head] = (weight * grads).astype(jnp.bfloat16)


def split_keys_kernel(
    heads, scaling, q0, q1, k0, k1, weight_ref, product_ref, mine, sent, key_own, key_back, query_own,
    query_mate, total_ref,
):
    rows, step = k0.shape[1], pl.program_id(0)
    for number, parts in enumerate(group_parts(1, mine, sent, [])):
        total_ref[number * GROUP : (number + 1) * GROUP, :] = sum(parts)
    outs = {("k", 0): key_own, ("k", 1): key_back, ("q", 0): query_own, ("q", 1): query_mate}
    out = Emitter(outs)
    for head in range(heads):
        low, high = head_span(head)
        keep = head_mask(head)
        q = stack([ref[0, :, low:high] for ref in (q0, q1)], 0) * keep
        k = stack([ref[0, :, low:high] for ref in (k0, k1)], 0) * keep
        dots = per_query((0, 1), 1, 0, step * heads + head, total_ref)
        weight, product = weight_ref[head].astype(jnp.float32), product_ref[head].astype(jnp.float32)
        slope = ((product - weight * dots) * scaling).astype(jnp.bfloat16)
        sums = {}
        add_rows(sums, "k", (0, 1), matmul(slope, q, NN), rows)
        add_rows(sums, "q", (0, 1), matmul(slope, k, TN), rows)
        for name, value in sums.items():
            out.emit(head, name, value)


def third_kernel(
    heads, scaling, power, place_ref, lengths_ref, q_third, o_third, k_back, v_back, value_part,
    stats, even, odd, value_out, key_out, query_out, dots_ref, shift_ref,
):
    rows, me, step = k_back.shape[1], place_ref[0], pl.program_id(0)
    columns = q_third.shape[1]
    parts = [stats[...], part_of(even, 2, 0)[:, :columns], part_of(odd, 2, 1)[:, :columns]]
    shift_ref[...] = merge_stats(scaling, parts)
    plan = [third_tile(lengths_ref, rows, columns, me)]
    mask = plan[0][2]
    queries, keys = (None, None, (q_third, o_third)), (None, (k_back, v_back))
    out = Emitter({"v": value_out, "k": key_out, "q": query_out}, {"v": value_part})
    for head, (tiles, keep) in tiles_ahead(heads, plan, queries, keys, 2):
        (q, o), (k, _), (raw, grads) = tiles[0]
        at = step * heads + head
        weight = jnp.where(mask, jnp.exp2((raw - shift_ref[pl.ds(at, 1), :]) * power), 0.0)
        dots = jnp.sum(weight * grads, axis=0, keepdims=True)
        dots_ref[pl.ds(at, 1), :] = dots
        total = dots + even[row_of(4, 1, 0, at), :][:, :columns] + odd[row_of(5, 1, 0, at), :][:, :columns]
        slope = (weight * (grads - total) * scaling).astype(jnp.bfloat16)
        out.emit(head, "v", matmul(weight.astype(jnp.bfloat16), o * keep, NN))
        out.emit(head, "k", matmul(slope, q * keep, NN))
        out.emit(head, "q", matmul(slope, k, TN))


def add_refs(*refs):
    return sum(ref[...].astype(jnp.float32) for ref in refs)


def sums_kernel(key_part, key_sent, query_part, query_sent, *refs):
    *extra, key_out, query_out = refs
    key_out[...] = add_refs(key_part, key_sent).astype(jnp.bfloat16)
    total = add_refs(query_part, query_sent)
    if extra:
        count = extra[0].shape[1]
        query_out[:, :count] = (total[:, :count] + add_refs(*extra)).astype(jnp.bfloat16)
        total = total[:, count:]
    if total.shape[1]:
        query_out[:, query_out.shape[1] - total.shape[1] :] = total.astype(jnp.bfloat16)


def halo_program(columns, queries, key_vectors, value_vectors, out_grad, facts):
    _, rows, width = queries.shape
    seq_size = lax.axis_size("seq")
    me = lax.axis_index("seq").astype(jnp.int32)
    scaling = HEAD ** (-0.5)
    power = scaling * math.log2(math.e)
    steps = width // HEAD // 4
    part = width // steps
    heads = part // HEAD
    devices = range(seq_size)
    def send(value, pairs):
        return lax.ppermute(value, "seq", pairs)

    mates = [(s, s ^ 1) for s in devices]
    ring = columns is None
    chain = [(s, s + 2) for s in devices if s + 2 < seq_size]
    ahead = [(s, (s + 2) % seq_size) for s in devices] if ring else chain
    behind = [(s, s - 2) for s in devices if s >= 2]
    if not ring:
        thirds = range(3, seq_size - 2, 2)
        relay, to_odd = [(t + 2, t) for t in thirds], [(t, t + 2) for t in thirds]
        from_even, to_even = [(t + 1, t) for t in thirds], [(t, t + 1) for t in thirds]

    def pass_on(value, terms):
        terms = jnp.pad(terms, ((0, 0), (0, rows - terms.shape[1])))
        far = send(terms, to_odd)
        return send(jnp.concatenate([value, far]), mates), far

    smem = pl.BlockSpec(memory_space=pltpu.SMEM)
    def wide(count):
        return pl.BlockSpec((1, count, part), lambda step: (0, 0, step))

    def slim(count, lanes=rows):
        return pl.BlockSpec((count * GROUP, lanes), lambda step: (0, 0))

    def slim_shape(count, lanes=rows):
        return jax.ShapeDtypeStruct((count * GROUP, lanes), jnp.float32)

    cube = pl.BlockSpec((heads, 2 * rows, 2 * rows), lambda step: (step, 0, 0))
    cube_shape = jax.ShapeDtypeStruct((steps * heads, 2 * rows, 2 * rows), jnp.bfloat16)
    anywhere = pl.BlockSpec(memory_space=pl.ANY)

    def call(
        kernel, products, wides, slims, outs, slim_outs, plain=False, scratch=(), cubes=(), after=(), cube_outs=0
    ):
        flops = 2 * products * 4 * rows * rows * width * 3 // 2
        lead = [] if plain else [me[None], facts]
        wide_shapes = [jax.ShapeDtypeStruct((1, count, width), jnp.bfloat16) for count in outs]
        return pl.pallas_call(
            kernel,
            grid=(steps,),
            in_specs=[smem] * len(lead)
            + [wide(value.shape[1]) for value in wides]
            + [cube] * len(cubes)
            + [slim(value.shape[0] // GROUP, value.shape[1]) for value in slims]
            + [anywhere] * len(after),
            out_specs=[wide(count) for count in outs] + [slim(*sizes) for sizes in slim_outs] + [cube] * cube_outs,
            out_shape=wide_shapes + [slim_shape(*sizes) for sizes in slim_outs] + [cube_shape] * cube_outs,
            scratch_shapes=[pltpu.VMEM((count * GROUP, lanes), jnp.float32) for count, lanes in scratch],
            compiler_params=pltpu.CompilerParams(vmem_limit_bytes=20 * 1024 * 1024),
            cost_estimate=pl.CostEstimate(
                flops=flops, bytes_accessed=20 * rows * width, transcendentals=0
            ),
        )(*lead, *wides, *cubes, *slims, *after)

    query_mate = send(queries, mates)
    key_back = send(key_vectors, chain)
    grad_mate = send(out_grad, mates)
    value_back = send(value_vectors, ahead)
    grad_own, value_own, stats = call(
        functools.partial(stats_kernel, heads, power), 1,
        [queries, query_mate, key_vectors, key_back, out_grad, value_vectors], [], [rows] * 2, [(4,)],
    )
    rows_in = [queries, grad_own, query_mate, grad_mate]
    tensors = rows_in + [key_vectors, value_own, key_back, value_back]
    constants = (heads, scaling, power)
    if ring:
        value_part, value_sent, shift = call(
            functools.partial(values_kernel, True, *constants), 2, rows_in + [key_vectors, key_back],
            [stats, send(stats, mates)], [rows] * 2, [(2,)],
        )
        (dots,) = call(functools.partial(dots_kernel, False, *constants), 2, tensors, [shift], [], [(2,)])
        dots_mate, extra = send(dots, mates), []
        cubes = call(
            functools.partial(weights_kernel, heads, power), 2, tensors, [shift], [], [], after=[dots], cube_outs=2
        )
        key_part, key_sent, query_part, query_sent = call(
            functools.partial(split_keys_kernel, heads, scaling), 2,
            [queries, query_mate, key_vectors, key_back], [dots, dots_mate], [rows] * 4, [],
            plain=True, scratch=[(2, rows)], cubes=cubes,
        )
    else:
        query_third = send(query_mate[:, :columns], relay)
        held, _ = lax.optimization_barrier((grad_mate[:, :columns], stats))
        grad_third = send(held, relay)
        query_third, *_ = lax.optimization_barrier((query_third, value_back, stats, held))
        (third_stats,) = call(
            functools.partial(third_stats_kernel, heads, power), 1, [query_third, key_back], [], [],
            [(2, columns)],
        )
        stats_in = [stats, *pass_on(stats, third_stats)]
        bundle, dots, shift = call(
            functools.partial(dots_kernel, True, *constants), 2, tensors, stats_in, [], [(6,), (2,), (2,)],
        )
        even, odd = send(bundle, from_even), send(bundle, relay)
        value_part, value_back_part = call(
            functools.partial(values_kernel, False, *constants), 2, rows_in + [key_vectors, key_back],
            [shift], [rows] * 2, [],
        )
        value_sent, key_third, query_third_part, third_dots = call(
            functools.partial(third_kernel, *constants), 2,
            [query_third, grad_third, key_back, value_back, value_back_part], [third_stats, even, odd],
            [rows, rows, columns], [(1, columns)], scratch=[(1, columns)],
        )
        dots_in = [shift, dots, *pass_on(dots, third_dots)]
        extra = [send(query_third_part, to_even)]
        key_part, key_sent, query_part, query_sent = call(
            functools.partial(keys_kernel, *constants), 4, tensors + [key_third], dots_in, [rows] * 4, [],
            scratch=[(2, rows)],
        )
    value_received = send(value_sent, [(s, (s - 2) % seq_size) for s in devices] if ring else behind)
    key_received = send(key_sent, behind)
    query_received = send(query_sent, mates)
    value_ready = (value_part.astype(jnp.float32) + value_received.astype(jnp.float32)).astype(jnp.bfloat16)
    key_ready, query_ready = call(
        sums_kernel, 0, [key_part, key_received, query_part, query_received, *extra], [], [rows] * 2, [],
        plain=True,
    )
    return query_ready, key_ready, value_ready


def program_kernel(shift, lengths_ref, out_ref):
    count = lengths_ref.shape[0]
    start, found, third = jnp.int32(0), jnp.int32(0), jnp.int32(-1)
    half = 1 << (shift - 1)
    for doc in range(count):
        end = start + lengths_ref[doc]
        last = (end - 1) >> shift
        spans = (last - (start >> shift) >= 3) & (last & 1 == 0)
        found = jnp.where(spans, jnp.where(end - (last << shift) <= half, 1, 2), found)
        third = jnp.where(spans, last - 1, third)
        out_ref[doc + 1] = lengths_ref[doc]
        start = end
    out_ref[0], out_ref[count + 1] = found, third


def program_facts(rows, doc_lengths):
    smem = pl.BlockSpec(memory_space=pltpu.SMEM)
    return pl.pallas_call(
        functools.partial(program_kernel, rows.bit_length() - 1),
        in_specs=[smem],
        out_specs=smem,
        out_shape=jax.ShapeDtypeStruct((doc_lengths.shape[0] + 2,), jnp.int32),
    )(doc_lengths)


def halo_shards(*arguments):
    *tensors, doc_lengths = arguments
    rows = tensors[0].shape[1]
    facts = program_facts(rows, doc_lengths)
    programs = [functools.partial(halo_program, columns) for columns in (None, rows // 2, rows)]
    return lax.switch(facts[0], programs, *tensors, facts)


def shards(queries, key_vectors, value_vectors, out_grad, doc_lengths):
    _, rows, width = queries.shape
    seq_size = lax.axis_size("seq")
    longest = rows * seq_size * 3 // 8
    fits = longest <= 3 * rows and seq_size % 2 == 0 and seq_size > 4 and rows == LANES
    heads = width // HEAD
    plan = halo_shards if fits and heads % 4 == 0 and heads <= GROUP else spread_shards
    return plan(queries, key_vectors, value_vectors, out_grad, doc_lengths)


def solution(mesh):
    return jax.shard_map(
        shards,
        mesh=mesh,
        in_specs=(
            P("section", "seq", "dp"),
            P("section", "seq", "dp"),
            P("section", "seq", "dp"),
            P("section", "seq", "dp"),
            P(),
        ),
        out_specs=(P("section", "seq", "dp"), P("section", "seq", "dp"), P("section", "seq", "dp")),
        check_vma=False,
    )
```

```python
import functools
import math
import jax
import jax.numpy as jnp
from jax import lax
from jax.experimental import pallas as pl
from jax.experimental.pallas import tpu as pltpu
from jax.sharding import PartitionSpec as P

HEAD = 224
LANES = 128
FLOOR = -1e30


def pick_slot(stacked, slot):
    return lax.dynamic_index_in_dim(stacked, slot, 0, keepdims=False)


def put_slot(stacked, update, slot):
    return lax.dynamic_update_index_in_dim(stacked, update, slot, 0)


def spread_shards(queries, key_vectors, value_vectors, out_grad, doc_lengths):
    local_rows = queries.shape[1]
    local_width = queries.shape[2]
    head_count = local_width // HEAD
    seq_size = lax.axis_size("seq")
    group = seq_size // head_count
    scaling = HEAD ** (-0.5)

    def spread(matrix):
        shaped = matrix.reshape(local_rows, head_count, 1, HEAD)
        copies = jnp.broadcast_to(shaped, (local_rows, head_count, group, HEAD))
        return copies.reshape(local_rows, seq_size * HEAD)

    query_head, key_head, value_head, cot_head = (
        lax.all_to_all(spread(queries), "seq", split_axis=1, concat_axis=0, tiled=True),
        lax.all_to_all(spread(key_vectors), "seq", split_axis=1, concat_axis=0, tiled=True),
        lax.all_to_all(spread(value_vectors), "seq", split_axis=1, concat_axis=0, tiled=True),
        lax.all_to_all(spread(out_grad), "seq", split_axis=1, concat_axis=0, tiled=True),
    )
    length = key_head.shape[0]
    member = lax.axis_index("seq") % group
    blocks = 2 * group
    block = length // blocks
    bounds = jnp.cumsum(doc_lengths)
    positions = jnp.arange(length, dtype=jnp.int32)
    doc_index = jnp.sum((positions[:, None] >= bounds[None, :]).astype(jnp.int32), axis=1)
    row_list = [member, blocks - 1 - member]
    query_list = []
    cot_list = []
    pos_list = []
    for which in range(2):
        offset = row_list[which] * block
        query_list.append(lax.dynamic_slice_in_dim(query_head, offset, block, 0))
        cot_list.append(lax.dynamic_slice_in_dim(cot_head, offset, block, 0))
        pos_list.append(offset + jnp.arange(block, dtype=jnp.int32))
    query_stack = jnp.stack(query_list)
    cot_stack = jnp.stack(cot_list)
    pos_stack = jnp.stack(pos_list)
    doc_stack = jnp.take(doc_index, pos_stack)
    plan = []
    for number in range(blocks + 1):
        first = number <= member
        slot = jnp.where(first, 0, 1).astype(jnp.int32)
        col_block = jnp.where(first, number, number - member - 1)
        flag = None
        plan.append((slot, col_block, flag))
    row_max = jnp.full((2, block), -jnp.inf, jnp.float32)
    row_sum = jnp.zeros((2, block), jnp.float32)
    stored = []
    for slot, col_block, flag in plan:

        def score_tile(carry, slot=slot, col_block=col_block):
            maxima, totals = carry
            query_rows = pick_slot(query_stack, slot)
            key_rows = lax.dynamic_slice_in_dim(key_head, col_block * block, block, 0)
            col_docs = lax.dynamic_slice_in_dim(doc_index, col_block * block, block, 0)
            col_positions = col_block * block + jnp.arange(block, dtype=jnp.int32)
            raw = jnp.dot(query_rows, key_rows.T, preferred_element_type=jnp.float32) * scaling
            allowed = (pick_slot(doc_stack, slot)[:, None] == col_docs[None, :]) & (
                pick_slot(pos_stack, slot)[:, None] >= col_positions[None, :]
            )
            scores = jnp.where(allowed, raw, -jnp.inf)
            before = pick_slot(maxima, slot)
            after = jnp.maximum(before, jnp.max(scores, axis=1))
            safe = jnp.where(jnp.isfinite(after), after, 0.0)
            total = pick_slot(totals, slot) * jnp.exp(before - safe) + jnp.sum(
                jnp.exp(scores - safe[:, None]), axis=1
            )
            return (scores, put_slot(maxima, after, slot), put_slot(totals, total, slot))

        scores, row_max, row_sum = score_tile((row_max, row_sum))
        stored.append(scores)

    def tile_weights(scores, slot):
        return (
            jnp.exp(scores - pick_slot(row_max, slot)[:, None]) / pick_slot(row_sum, slot)[:, None]
        )

    summed = jnp.zeros((2, block, HEAD), jnp.float32)
    for (slot, col_block, flag), scores in zip(plan, stored):

        def add_values(carry, slot=slot, col_block=col_block, scores=scores):
            rounded = tile_weights(scores, slot).astype(jnp.bfloat16)
            value_rows = lax.dynamic_slice_in_dim(value_head, col_block * block, block, 0)
            term = jnp.dot(rounded, value_rows, preferred_element_type=jnp.float32)
            return put_slot(carry, pick_slot(carry, slot) + term, slot)

        summed = add_values(summed)
    attended = summed.astype(jnp.bfloat16)
    row_dot = jnp.sum(cot_stack.astype(jnp.float32) * attended.astype(jnp.float32), axis=2)
    query_acc = jnp.zeros((2, block, HEAD), jnp.float32)
    key_acc = jnp.zeros((length, HEAD), jnp.float32)
    value_acc = jnp.zeros((length, HEAD), jnp.float32)
    for (slot, col_block, flag), scores in zip(plan, stored):

        def backward_tile(carry, slot=slot, col_block=col_block, scores=scores):
            query_sum, key_sum, value_sum = carry
            weights = tile_weights(scores, slot)
            rounded = weights.astype(jnp.bfloat16)
            query_rows = pick_slot(query_stack, slot)
            cot_rows = pick_slot(cot_stack, slot)
            start = col_block * block
            key_rows = lax.dynamic_slice_in_dim(key_head, start, block, 0)
            value_rows = lax.dynamic_slice_in_dim(value_head, start, block, 0)
            value_term = jnp.dot(rounded.T, cot_rows, preferred_element_type=jnp.float32)
            prob_grad = jnp.dot(cot_rows, value_rows.T, preferred_element_type=jnp.float32)
            score_grad = (
                weights * (prob_grad - pick_slot(row_dot, slot)[:, None]) * scaling
            ).astype(jnp.bfloat16)
            query_term = jnp.dot(score_grad, key_rows, preferred_element_type=jnp.float32)
            key_term = jnp.dot(score_grad.T, query_rows, preferred_element_type=jnp.float32)
            query_sum = put_slot(query_sum, pick_slot(query_sum, slot) + query_term, slot)
            key_sum = lax.dynamic_update_slice_in_dim(
                key_sum, lax.dynamic_slice_in_dim(key_sum, start, block, 0) + key_term, start, 0
            )
            value_sum = lax.dynamic_update_slice_in_dim(
                value_sum,
                lax.dynamic_slice_in_dim(value_sum, start, block, 0) + value_term,
                start,
                0,
            )
            return (query_sum, key_sum, value_sum)

        query_acc, key_acc, value_acc = backward_tile((query_acc, key_acc, value_acc))
    query_rounded = query_acc.astype(jnp.bfloat16)
    key_back, value_back = (
        lax.all_to_all(key_acc, "seq", split_axis=0, concat_axis=1, tiled=True),
        lax.all_to_all(value_acc, "seq", split_axis=0, concat_axis=1, tiled=True),
    )

    def settle(received):
        shaped = received.astype(jnp.float32).reshape(local_rows, head_count, group, HEAD)
        return jnp.sum(shaped, axis=2).reshape(1, local_rows, local_width).astype(jnp.bfloat16)

    query_full = jnp.zeros((length, HEAD), jnp.bfloat16)
    for which in range(2):
        query_full = lax.dynamic_update_slice_in_dim(
            query_full, query_rounded[which], row_list[which] * block, 0
        )
    query_back = lax.all_to_all(query_full, "seq", split_axis=0, concat_axis=1, tiled=True)
    query_out = settle(query_back)
    return (query_out, settle(key_back), settle(value_back))


NT = ((1,), (1,))
NN = ((1,), (0,))
TN = ((0,), (0,))
GROUP = 8


def head_span(head):
    low = head * HEAD // LANES * LANES
    high = -(-(head + 1) * HEAD // LANES) * LANES
    return low, high


def head_mask(head):
    low, high = head_span(head)
    lane = lax.broadcasted_iota(jnp.int32, (1, high - low), 1) + low
    inside = (lane >= head * HEAD) & (lane < (head + 1) * HEAD)
    return inside.astype(jnp.float32).astype(jnp.bfloat16)


def matmul(left, right, dims):
    return lax.dot_general(left, right, (dims, ((), ())), preferred_element_type=jnp.float32)


def stack(values, axis):
    return values[0] if len(values) == 1 else jnp.concatenate(values, axis=axis)


def allowed(lengths_ref, rows, query_block, key_block, columns=None):
    shape = (rows, columns or rows)
    position = query_block * rows + lax.broadcasted_iota(jnp.int32, shape, 1)
    keys = key_block * rows + lax.broadcasted_iota(jnp.int32, shape, 0)
    start = jnp.zeros_like(position)
    bound = jnp.int32(0)
    for doc in range(1, lengths_ref.shape[0] - 1):
        bound = bound + lengths_ref[doc]
        start = jnp.where(position >= bound, bound, start)
    return (keys >= start) & (keys <= position)


def make_tile(lengths_ref, rows, queries, keys):
    mask = stack(
        [stack([allowed(lengths_ref, rows, q, k) for _, q in queries], 1) for _, k in keys], 0
    )
    return [slot for slot, _ in queries], [slot for slot, _ in keys], mask


def tile_values(plan, head, queries, keys, products):
    low, high = head_span(head)
    keep = head_mask(head)

    def gather(refs, number, slots):
        return stack([refs[slot][number][0, :, low:high] for slot in slots], 0)

    out = []
    for query_slots, key_slots, _ in plan:
        q = [gather(queries, number, query_slots) for number in range(products)]
        k = [gather(keys, number, key_slots) * keep for number in range(products)]
        out.append((q, k, [matmul(b, a, NT) for a, b in zip(q, k)]))
    return out, keep


def tiles_ahead(heads, plan, queries, keys, products):
    ready = tile_values(plan, 0, queries, keys, products)
    for head in range(heads):
        now = ready
        if head + 1 < heads:
            ready = tile_values(plan, head + 1, queries, keys, products)
        yield head, now


def pair_tile(lengths_ref, rows, me):
    mate = me + 1 - 2 * lax.rem(me, 2)
    return make_tile(lengths_ref, rows, ((0, me), (1, mate)), ((0, me), (1, me - 2)))


def third_tile(facts_ref, rows, columns, me):
    mask = allowed(facts_ref, rows, me + 1, me - 2, columns)
    return [2], [1], mask & (me == facts_ref[facts_ref.shape[0] - 1])


def lane_cut(value, number, rows):
    return value[:, number * rows : (number + 1) * rows]


def row_of(group, kinds, kind, head):
    return pl.ds((group * kinds + kind) * GROUP + head, 1)


def per_query(slots, kinds, kind, head, ref):
    return stack([ref[row_of(slot, kinds, kind, head), :] for slot in slots], 1)


def collect_stats(heads, power, step, plan, queries, keys, rows, out_ref, groups):
    for head, (tiles, _) in tiles_ahead(heads, plan, queries, keys, 1):
        for (query_slots, _, mask), (_, _, (raw,)) in zip(plan, tiles):
            raw = jnp.where(mask, raw, FLOOR)
            top = jnp.max(raw, axis=0, keepdims=True)
            sums = jnp.sum(jnp.exp2((raw - top) * power), axis=0, keepdims=True)
            for number, slot in enumerate(query_slots):
                at = step * heads + head
                out_ref[row_of(groups[slot], 2, 0, at), :] = lane_cut(top, number, rows)
                out_ref[row_of(groups[slot], 2, 1, at), :] = lane_cut(sums, number, rows)


def stats_kernel(
    heads, power, place_ref, lengths_ref, q_own, q_mate, k_own, k_back, o_own, v_own, o_copy, v_copy, out_ref
):
    rows, me, step = k_own.shape[1], place_ref[0], pl.program_id(0)
    o_copy[...], v_copy[...] = o_own[...], v_own[...]
    plan = [pair_tile(lengths_ref, rows, me)]
    queries, keys = ((q_own,), (q_mate,)), ((k_own,), (k_back,))
    collect_stats(heads, power, step, plan, queries, keys, rows, out_ref, (0, 1))


def third_stats_kernel(heads, power, place_ref, lengths_ref, q_third, k_back, out_ref):
    rows, me, step = k_back.shape[1], place_ref[0], pl.program_id(0)
    plan = [third_tile(lengths_ref, rows, q_third.shape[1], me)]
    queries, keys = (None, None, (q_third,)), (None, (k_back,))
    collect_stats(heads, power, step, plan, queries, keys, rows, out_ref, (None, None, 0))


def part_of(ref, kinds, number):
    size = kinds * GROUP
    return ref[number * size : (number + 1) * size, :]


def group_parts(kinds, mine, sent, extra):
    own = [part_of(mine, kinds, 0), part_of(sent, kinds, 1)]
    mate = [part_of(mine, kinds, 1), part_of(sent, kinds, 0)]
    if extra:
        own, mate = own + [part_of(sent, kinds, 2)], mate + [extra[0][...]]
    return [own, mate]


def merge_groups(scaling, shift_ref, refs):
    mine, sent, *extra = refs
    for number, parts in enumerate(group_parts(2, mine, sent, extra)):
        shift_ref[number * GROUP : (number + 1) * GROUP, :] = merge_stats(scaling, parts)


def merge_stats(scaling, parts):
    split = [(jnp.where(p[GROUP:] > 0, p[:GROUP], FLOOR), p[GROUP:]) for p in parts]
    top = functools.reduce(jnp.maximum, [s[0] for s in split])
    total = sum(jnp.exp((s[0] - top) * scaling) * s[1] for s in split)
    return top + jnp.log(jnp.where(total > 0, total, 1.0)) / scaling


class Emitter:
    def __init__(self, outs, base={}):
        self.outs, self.base, self.carry = outs, base, {}

    def put(self, name, start, stop, value):
        if name in self.base:
            value = value + self.base[name][0, :, start:stop].astype(jnp.float32)
        self.outs[name][0, :, start:stop] = value.astype(jnp.bfloat16)

    def emit(self, head, name, value):
        low, high = head_span(head)
        first, last = head * HEAD % LANES == 0, (head + 1) * HEAD % LANES == 0
        start, stop = low, high
        if not first:
            self.put(name, low, low + LANES, value[:, :LANES] + self.carry.pop(name))
            start = low + LANES
        if not last:
            self.carry[name] = value[:, high - LANES - low :]
            stop = high - LANES
        if stop > start:
            self.put(name, start, stop, value[:, start - low : stop - low])


def add_rows(sums, kind, slots, value, rows):
    for number, slot in enumerate(slots):
        piece = value[number * rows : (number + 1) * rows]
        name = (kind, slot)
        sums[name] = sums[name] + piece if name in sums else piece


def split_refs(refs):
    return ((refs[0:2], refs[2:4]), (refs[4:6], refs[6:8]), refs[8:])


def values_kernel(merge, heads, scaling, power, place_ref, lengths_ref, q0, o0, q1, o1, k0, k1, *refs):
    queries, keys = ((q0, o0), (q1, o1)), ((k0,), (k1,))
    if merge:
        *stats, value_own, value_back, shift_ref = refs
        merge_groups(scaling, shift_ref, stats)
    else:
        shift_ref, value_own, value_back = refs
    rows, me, step = k0.shape[1], place_ref[0], pl.program_id(0)
    plan = [pair_tile(lengths_ref, rows, me)]
    out = Emitter({("v", 0): value_own, ("v", 1): value_back})
    for head, (tiles, keep) in tiles_ahead(heads, plan, queries, keys, 1):
        low, high = head_span(head)
        sums = {}
        for (query_slots, key_slots, mask), (_, _, (raw,)) in zip(plan, tiles):
            shift = per_query(query_slots, 1, 0, step * heads + head, shift_ref)
            weight = jnp.where(mask, jnp.exp2((raw - shift) * power), 0.0).astype(jnp.bfloat16)
            o = stack([queries[slot][1][0, :, low:high] for slot in query_slots], 0) * keep
            add_rows(sums, "v", key_slots, matmul(weight, o, NN), rows)
        for name, value in sums.items():
            out.emit(head, name, value)


def dots_kernel(merge, heads, scaling, power, place_ref, lengths_ref, *refs):
    queries, keys, refs = split_refs(refs)
    if merge:
        *stats, bundle_ref, dots_ref, shift_ref = refs
        merge_groups(scaling, shift_ref, stats)
        bundle_ref[: 4 * GROUP] = stats[0][...]
    else:
        shift_ref, dots_ref = refs
    rows, me, step = keys[0][0].shape[1], place_ref[0], pl.program_id(0)
    plan = [pair_tile(lengths_ref, rows, me)]
    for head, (tiles, _) in tiles_ahead(heads, plan, queries, keys, 2):
        at = step * heads + head
        for (query_slots, _, mask), (_, _, (raw, grads)) in zip(plan, tiles):
            shift = per_query(query_slots, 1, 0, at, shift_ref)
            weight = jnp.where(mask, jnp.exp2((raw - shift) * power), 0.0)
            dots = jnp.sum(weight * grads, axis=0, keepdims=True)
            for number, slot in enumerate(query_slots):
                dots_ref[row_of(slot, 1, 0, at), :] = lane_cut(dots, number, rows)
                if merge:
                    bundle_ref[row_of(4 + slot, 1, 0, at), :] = lane_cut(dots, number, rows)


def keys_kernel(heads, scaling, power, place_ref, lengths_ref, *refs):
    queries, keys, refs = split_refs(refs)
    base, shift_ref, mine, sent, far, key_own, key_back, query_own, query_mate, total_ref = refs
    rows, me, step = keys[0][0].shape[1], place_ref[0], pl.program_id(0)
    plan = [pair_tile(lengths_ref, rows, me)]
    for number, parts in enumerate(group_parts(1, mine, sent, [far])):
        total_ref[number * GROUP : (number + 1) * GROUP, :] = sum(parts)
    outs = {("k", 0): key_own, ("k", 1): key_back, ("q", 0): query_own, ("q", 1): query_mate}
    out = Emitter(outs, {("k", 1): base})
    for head, (tiles, keep) in tiles_ahead(heads, plan, queries, keys, 2):
        at = step * heads + head
        sums = {}
        for (query_slots, key_slots, mask), ((q, _), (k, _), (raw, grads)) in zip(plan, tiles):
            shift = per_query(query_slots, 1, 0, at, shift_ref)
            dots = per_query(query_slots, 1, 0, at, total_ref)
            weight = jnp.where(mask, jnp.exp2((raw - shift) * power), 0.0)
            slope = (weight * (grads - dots) * scaling).astype(jnp.bfloat16)
            add_rows(sums, "k", key_slots, matmul(slope, q * keep, NN), rows)
            add_rows(sums, "q", query_slots, matmul(slope, k, TN), rows)
        for name, value in sums.items():
            out.emit(head, name, value)


def weights_kernel(heads, power, place_ref, lengths_ref, *refs):
    queries, keys, (shift_ref, _, weight_ref, product_ref) = split_refs(refs)
    rows, me, step = keys[0][0].shape[1], place_ref[0], pl.program_id(0)
    plan = [pair_tile(lengths_ref, rows, me)]
    for head, (tiles, _) in tiles_ahead(heads, plan, queries, keys, 2):
        (query_slots, _, mask), (_, _, (raw, grads)) = plan[0], tiles[0]
        shift = per_query(query_slots, 1, 0, step * heads + head, shift_ref)
        weight = jnp.where(mask, jnp.exp2((raw - shift) * power), 0.0)
        weight_ref[head] = weight.astype(jnp.bfloat16)
        product_ref[head] = (weight * grads).astype(jnp.bfloat16)


def split_keys_kernel(
    heads, scaling, q0, q1, k0, k1, weight_ref, product_ref, mine, sent, key_own, key_back, query_own,
    query_mate, total_ref,
):
    rows, step = k0.shape[1], pl.program_id(0)
    for number, parts in enumerate(group_parts(1, mine, sent, [])):
        total_ref[number * GROUP : (number + 1) * GROUP, :] = sum(parts)
    outs = {("k", 0): key_own, ("k", 1): key_back, ("q", 0): query_own, ("q", 1): query_mate}
    out = Emitter(outs)
    for head in range(heads):
        low, high = head_span(head)
        keep = head_mask(head)
        q = stack([ref[0, :, low:high] for ref in (q0, q1)], 0) * keep
        k = stack([ref[0, :, low:high] for ref in (k0, k1)], 0) * keep
        dots = per_query((0, 1), 1, 0, step * heads + head, total_ref)
        weight, product = weight_ref[head].astype(jnp.float32), product_ref[head].astype(jnp.float32)
        slope = ((product - weight * dots) * scaling).astype(jnp.bfloat16)
        sums = {}
        add_rows(sums, "k", (0, 1), matmul(slope, q, NN), rows)
        add_rows(sums, "q", (0, 1), matmul(slope, k, TN), rows)
        for name, value in sums.items():
            out.emit(head, name, value)


def third_kernel(
    heads, scaling, power, place_ref, lengths_ref, q_third, o_third, k_back, v_back, value_part,
    stats, even, odd, value_out, key_out, query_out, dots_ref, shift_ref,
):
    rows, me, step = k_back.shape[1], place_ref[0], pl.program_id(0)
    columns = q_third.shape[1]
    parts = [stats[...], part_of(even, 2, 0)[:, :columns], part_of(odd, 2, 1)[:, :columns]]
    shift_ref[...] = merge_stats(scaling, parts)
    plan = [third_tile(lengths_ref, rows, columns, me)]
    mask = plan[0][2]
    queries, keys = (None, None, (q_third, o_third)), (None, (k_back, v_back))
    out = Emitter({"v": value_out, "k": key_out, "q": query_out}, {"v": value_part})
    for head, (tiles, keep) in tiles_ahead(heads, plan, queries, keys, 2):
        (q, o), (k, _), (raw, grads) = tiles[0]
        at = step * heads + head
        weight = jnp.where(mask, jnp.exp2((raw - shift_ref[pl.ds(at, 1), :]) * power), 0.0)
        dots = jnp.sum(weight * grads, axis=0, keepdims=True)
        dots_ref[pl.ds(at, 1), :] = dots
        total = dots + even[row_of(4, 1, 0, at), :][:, :columns] + odd[row_of(5, 1, 0, at), :][:, :columns]
        slope = (weight * (grads - total) * scaling).astype(jnp.bfloat16)
        out.emit(head, "v", matmul(weight.astype(jnp.bfloat16), o * keep, NN))
        out.emit(head, "k", matmul(slope, q * keep, NN))
        out.emit(head, "q", matmul(slope, k, TN))


def add_refs(*refs):
    return sum(ref[...].astype(jnp.float32) for ref in refs)


def sums_kernel(key_part, key_sent, query_part, query_sent, *refs):
    *extra, key_out, query_out = refs
    key_out[...] = add_refs(key_part, key_sent).astype(jnp.bfloat16)
    total = add_refs(query_part, query_sent)
    if extra:
        count = extra[0].shape[1]
        query_out[:, :count] = (total[:, :count] + add_refs(*extra)).astype(jnp.bfloat16)
        total = total[:, count:]
    if total.shape[1]:
        query_out[:, query_out.shape[1] - total.shape[1] :] = total.astype(jnp.bfloat16)


def halo_program(third, queries, key_vectors, value_vectors, out_grad, facts):
    _, rows, width = queries.shape
    seq_size = lax.axis_size("seq")
    me = lax.axis_index("seq").astype(jnp.int32)
    scaling = HEAD ** (-0.5)
    power = scaling * math.log2(math.e)
    steps = width // HEAD // 4
    part = width // steps
    heads = part // HEAD
    devices = range(seq_size)
    def send(value, pairs):
        return lax.ppermute(value, "seq", pairs)

    mates = [(s, s ^ 1) for s in devices]
    ring, columns = third is None, rows
    chain = [(s, s + 2) for s in devices if s + 2 < seq_size]
    ahead = [(s, (s + 2) % seq_size) for s in devices] if ring else chain
    behind = [(s, s - 2) for s in devices if s >= 2]
    if not ring:
        relay, to_odd = [(third + 2, third)], [(third, third + 2)]
        from_even, to_even = [(third + 1, third)], [(third, third + 1)]

    def pass_on(value, terms):
        terms = jnp.pad(terms, ((0, 0), (0, rows - terms.shape[1])))
        far = send(terms, to_odd)
        return send(jnp.concatenate([value, far]), mates), far

    smem = pl.BlockSpec(memory_space=pltpu.SMEM)
    def wide(count):
        return pl.BlockSpec((1, count, part), lambda step: (0, 0, step))

    def slim(count, lanes=rows):
        return pl.BlockSpec((count * GROUP, lanes), lambda step: (0, 0))

    def slim_shape(count, lanes=rows):
        return jax.ShapeDtypeStruct((count * GROUP, lanes), jnp.float32)

    cube = pl.BlockSpec((heads, 2 * rows, 2 * rows), lambda step: (step, 0, 0))
    cube_shape = jax.ShapeDtypeStruct((steps * heads, 2 * rows, 2 * rows), jnp.bfloat16)
    anywhere = pl.BlockSpec(memory_space=pl.ANY)

    def call(
        kernel, products, wides, slims, outs, slim_outs, plain=False, scratch=(), cubes=(), after=(), cube_outs=0
    ):
        flops = 2 * products * 4 * rows * rows * width * 3 // 2
        lead = [] if plain else [me[None], facts]
        wide_shapes = [jax.ShapeDtypeStruct((1, count, width), jnp.bfloat16) for count in outs]
        return pl.pallas_call(
            kernel,
            grid=(steps,),
            in_specs=[smem] * len(lead)
            + [wide(value.shape[1]) for value in wides]
            + [cube] * len(cubes)
            + [slim(value.shape[0] // GROUP, value.shape[1]) for value in slims]
            + [anywhere] * len(after),
            out_specs=[wide(count) for count in outs] + [slim(*sizes) for sizes in slim_outs] + [cube] * cube_outs,
            out_shape=wide_shapes + [slim_shape(*sizes) for sizes in slim_outs] + [cube_shape] * cube_outs,
            scratch_shapes=[pltpu.VMEM((count * GROUP, lanes), jnp.float32) for count, lanes in scratch],
            compiler_params=pltpu.CompilerParams(vmem_limit_bytes=20 * 1024 * 1024),
            cost_estimate=pl.CostEstimate(
                flops=flops, bytes_accessed=20 * rows * width, transcendentals=0
            ),
        )(*lead, *wides, *cubes, *slims, *after)

    query_mate = send(queries, mates)
    key_back = send(key_vectors, chain)
    grad_mate = send(out_grad, mates)
    value_back = send(value_vectors, ahead)
    grad_own, value_own, stats = call(
        functools.partial(stats_kernel, heads, power), 1,
        [queries, query_mate, key_vectors, key_back, out_grad, value_vectors], [], [rows] * 2, [(4,)],
    )
    rows_in = [queries, grad_own, query_mate, grad_mate]
    tensors = rows_in + [key_vectors, value_own, key_back, value_back]
    constants = (heads, scaling, power)
    if ring:
        value_part, value_sent, shift = call(
            functools.partial(values_kernel, True, *constants), 2, rows_in + [key_vectors, key_back],
            [stats, send(stats, mates)], [rows] * 2, [(2,)],
        )
        (dots,) = call(functools.partial(dots_kernel, False, *constants), 2, tensors, [shift], [], [(2,)])
        dots_mate, extra = send(dots, mates), []
        cubes = call(
            functools.partial(weights_kernel, heads, power), 2, tensors, [shift], [], [], after=[dots], cube_outs=2
        )
        key_part, key_sent, query_part, query_sent = call(
            functools.partial(split_keys_kernel, heads, scaling), 2,
            [queries, query_mate, key_vectors, key_back], [dots, dots_mate], [rows] * 4, [],
            plain=True, scratch=[(2, rows)], cubes=cubes,
        )
    else:
        query_third = send(query_mate[:, :columns], relay)
        held, _ = lax.optimization_barrier((grad_mate[:, :columns], stats))
        grad_third = send(held, relay)
        query_third, *_ = lax.optimization_barrier((query_third, value_back, stats, held))
        (third_stats,) = call(
            functools.partial(third_stats_kernel, heads, power), 1, [query_third, key_back], [], [],
            [(2, columns)],
        )
        stats_in = [stats, *pass_on(stats, third_stats)]
        bundle, dots, shift = call(
            functools.partial(dots_kernel, True, *constants), 2, tensors, stats_in, [], [(6,), (2,), (2,)],
        )
        even, odd = send(bundle, from_even), send(bundle, relay)
        value_part, value_back_part = call(
            functools.partial(values_kernel, False, *constants), 2, rows_in + [key_vectors, key_back],
            [shift], [rows] * 2, [],
        )
        value_sent, key_third, query_third_part, third_dots = call(
            functools.partial(third_kernel, *constants), 2,
            [query_third, grad_third, key_back, value_back, value_back_part], [third_stats, even, odd],
            [rows, rows, columns], [(1, columns)], scratch=[(1, columns)],
        )
        dots_in = [shift, dots, *pass_on(dots, third_dots)]
        extra = [send(query_third_part, to_even)]
        key_part, key_sent, query_part, query_sent = call(
            functools.partial(keys_kernel, *constants), 4, tensors + [key_third], dots_in, [rows] * 4, [],
            scratch=[(2, rows)],
        )
    value_received = send(value_sent, behind)
    key_received = send(key_sent, behind)
    query_received = send(query_sent, mates)
    value_ready = (value_part.astype(jnp.float32) + value_received.astype(jnp.float32)).astype(jnp.bfloat16)
    key_ready, query_ready = call(
        sums_kernel, 0, [key_part, key_received, query_part, query_received, *extra], [], [rows] * 2, [],
        plain=True,
    )
    return query_ready, key_ready, value_ready


def program_kernel(shift, lengths_ref, out_ref):
    count = lengths_ref.shape[0]
    start, third = jnp.int32(0), jnp.int32(-1)
    for doc in range(count):
        end = start + lengths_ref[doc]
        last = (end - 1) >> shift
        spans = (last - (start >> shift) >= 3) & (last & 1 == 0)
        third = jnp.where(spans, last - 1, third)
        out_ref[doc + 1] = lengths_ref[doc]
        start = end
    out_ref[0] = jnp.where(third < 0, 0, (third - 1) >> 1)
    out_ref[count + 1] = third


def program_facts(rows, doc_lengths):
    smem = pl.BlockSpec(memory_space=pltpu.SMEM)
    return pl.pallas_call(
        functools.partial(program_kernel, rows.bit_length() - 1),
        in_specs=[smem],
        out_specs=smem,
        out_shape=jax.ShapeDtypeStruct((doc_lengths.shape[0] + 2,), jnp.int32),
    )(doc_lengths)


def halo_shards(*arguments):
    *tensors, doc_lengths = arguments
    facts = program_facts(tensors[0].shape[1], doc_lengths)
    thirds = range(3, lax.axis_size("seq") - 2, 2)
    programs = [functools.partial(halo_program, third) for third in (None, *thirds)]
    return lax.switch(facts[0], programs, *tensors, facts)


def shards(queries, key_vectors, value_vectors, out_grad, doc_lengths):
    _, rows, width = queries.shape
    seq_size = lax.axis_size("seq")
    longest = rows * seq_size * 3 // 8
    fits = longest <= 3 * rows and seq_size % 2 == 0 and seq_size > 4 and rows == LANES
    heads = width // HEAD
    plan = halo_shards if fits and heads % 4 == 0 and heads <= GROUP else spread_shards
    return plan(queries, key_vectors, value_vectors, out_grad, doc_lengths)


def solution(mesh):
    return jax.shard_map(
        shards,
        mesh=mesh,
        in_specs=(
            P("section", "seq", "dp"),
            P("section", "seq", "dp"),
            P("section", "seq", "dp"),
            P("section", "seq", "dp"),
            P(),
        ),
        out_specs=(P("section", "seq", "dp"), P("section", "seq", "dp"), P("section", "seq", "dp")),
        check_vma=False,
    )
```

```python
import functools
import math
import jax
import jax.numpy as jnp
from jax import lax
from jax.experimental import pallas as pl
from jax.experimental.pallas import tpu as pltpu
from jax.sharding import PartitionSpec as P

HEAD = 224
LANES = 128
FLOOR = -1e30


def pick_slot(stacked, slot):
    return lax.dynamic_index_in_dim(stacked, slot, 0, keepdims=False)


def put_slot(stacked, update, slot):
    return lax.dynamic_update_index_in_dim(stacked, update, slot, 0)


def spread_shards(queries, key_vectors, value_vectors, out_grad, doc_lengths):
    local_rows = queries.shape[1]
    local_width = queries.shape[2]
    head_count = local_width // HEAD
    seq_size = lax.axis_size("seq")
    group = seq_size // head_count
    scaling = HEAD ** (-0.5)

    def spread(matrix):
        shaped = matrix.reshape(local_rows, head_count, 1, HEAD)
        copies = jnp.broadcast_to(shaped, (local_rows, head_count, group, HEAD))
        return copies.reshape(local_rows, seq_size * HEAD)

    query_head, key_head, value_head, cot_head = (
        lax.all_to_all(spread(queries), "seq", split_axis=1, concat_axis=0, tiled=True),
        lax.all_to_all(spread(key_vectors), "seq", split_axis=1, concat_axis=0, tiled=True),
        lax.all_to_all(spread(value_vectors), "seq", split_axis=1, concat_axis=0, tiled=True),
        lax.all_to_all(spread(out_grad), "seq", split_axis=1, concat_axis=0, tiled=True),
    )
    length = key_head.shape[0]
    member = lax.axis_index("seq") % group
    blocks = 2 * group
    block = length // blocks
    bounds = jnp.cumsum(doc_lengths)
    positions = jnp.arange(length, dtype=jnp.int32)
    doc_index = jnp.sum((positions[:, None] >= bounds[None, :]).astype(jnp.int32), axis=1)
    row_list = [member, blocks - 1 - member]
    query_list = []
    cot_list = []
    pos_list = []
    for which in range(2):
        offset = row_list[which] * block
        query_list.append(lax.dynamic_slice_in_dim(query_head, offset, block, 0))
        cot_list.append(lax.dynamic_slice_in_dim(cot_head, offset, block, 0))
        pos_list.append(offset + jnp.arange(block, dtype=jnp.int32))
    query_stack = jnp.stack(query_list)
    cot_stack = jnp.stack(cot_list)
    pos_stack = jnp.stack(pos_list)
    doc_stack = jnp.take(doc_index, pos_stack)
    plan = []
    for number in range(blocks + 1):
        first = number <= member
        slot = jnp.where(first, 0, 1).astype(jnp.int32)
        col_block = jnp.where(first, number, number - member - 1)
        flag = None
        plan.append((slot, col_block, flag))
    row_max = jnp.full((2, block), -jnp.inf, jnp.float32)
    row_sum = jnp.zeros((2, block), jnp.float32)
    stored = []
    for slot, col_block, flag in plan:

        def score_tile(carry, slot=slot, col_block=col_block):
            maxima, totals = carry
            query_rows = pick_slot(query_stack, slot)
            key_rows = lax.dynamic_slice_in_dim(key_head, col_block * block, block, 0)
            col_docs = lax.dynamic_slice_in_dim(doc_index, col_block * block, block, 0)
            col_positions = col_block * block + jnp.arange(block, dtype=jnp.int32)
            raw = jnp.dot(query_rows, key_rows.T, preferred_element_type=jnp.float32) * scaling
            allowed = (pick_slot(doc_stack, slot)[:, None] == col_docs[None, :]) & (
                pick_slot(pos_stack, slot)[:, None] >= col_positions[None, :]
            )
            scores = jnp.where(allowed, raw, -jnp.inf)
            before = pick_slot(maxima, slot)
            after = jnp.maximum(before, jnp.max(scores, axis=1))
            safe = jnp.where(jnp.isfinite(after), after, 0.0)
            total = pick_slot(totals, slot) * jnp.exp(before - safe) + jnp.sum(
                jnp.exp(scores - safe[:, None]), axis=1
            )
            return (scores, put_slot(maxima, after, slot), put_slot(totals, total, slot))

        scores, row_max, row_sum = score_tile((row_max, row_sum))
        stored.append(scores)

    def tile_weights(scores, slot):
        return (
            jnp.exp(scores - pick_slot(row_max, slot)[:, None]) / pick_slot(row_sum, slot)[:, None]
        )

    summed = jnp.zeros((2, block, HEAD), jnp.float32)
    for (slot, col_block, flag), scores in zip(plan, stored):

        def add_values(carry, slot=slot, col_block=col_block, scores=scores):
            rounded = tile_weights(scores, slot).astype(jnp.bfloat16)
            value_rows = lax.dynamic_slice_in_dim(value_head, col_block * block, block, 0)
            term = jnp.dot(rounded, value_rows, preferred_element_type=jnp.float32)
            return put_slot(carry, pick_slot(carry, slot) + term, slot)

        summed = add_values(summed)
    attended = summed.astype(jnp.bfloat16)
    row_dot = jnp.sum(cot_stack.astype(jnp.float32) * attended.astype(jnp.float32), axis=2)
    query_acc = jnp.zeros((2, block, HEAD), jnp.float32)
    key_acc = jnp.zeros((length, HEAD), jnp.float32)
    value_acc = jnp.zeros((length, HEAD), jnp.float32)
    for (slot, col_block, flag), scores in zip(plan, stored):

        def backward_tile(carry, slot=slot, col_block=col_block, scores=scores):
            query_sum, key_sum, value_sum = carry
            weights = tile_weights(scores, slot)
            rounded = weights.astype(jnp.bfloat16)
            query_rows = pick_slot(query_stack, slot)
            cot_rows = pick_slot(cot_stack, slot)
            start = col_block * block
            key_rows = lax.dynamic_slice_in_dim(key_head, start, block, 0)
            value_rows = lax.dynamic_slice_in_dim(value_head, start, block, 0)
            value_term = jnp.dot(rounded.T, cot_rows, preferred_element_type=jnp.float32)
            prob_grad = jnp.dot(cot_rows, value_rows.T, preferred_element_type=jnp.float32)
            score_grad = (
                weights * (prob_grad - pick_slot(row_dot, slot)[:, None]) * scaling
            ).astype(jnp.bfloat16)
            query_term = jnp.dot(score_grad, key_rows, preferred_element_type=jnp.float32)
            key_term = jnp.dot(score_grad.T, query_rows, preferred_element_type=jnp.float32)
            query_sum = put_slot(query_sum, pick_slot(query_sum, slot) + query_term, slot)
            key_sum = lax.dynamic_update_slice_in_dim(
                key_sum, lax.dynamic_slice_in_dim(key_sum, start, block, 0) + key_term, start, 0
            )
            value_sum = lax.dynamic_update_slice_in_dim(
                value_sum,
                lax.dynamic_slice_in_dim(value_sum, start, block, 0) + value_term,
                start,
                0,
            )
            return (query_sum, key_sum, value_sum)

        query_acc, key_acc, value_acc = backward_tile((query_acc, key_acc, value_acc))
    query_rounded = query_acc.astype(jnp.bfloat16)
    key_back, value_back = (
        lax.all_to_all(key_acc, "seq", split_axis=0, concat_axis=1, tiled=True),
        lax.all_to_all(value_acc, "seq", split_axis=0, concat_axis=1, tiled=True),
    )

    def settle(received):
        shaped = received.astype(jnp.float32).reshape(local_rows, head_count, group, HEAD)
        return jnp.sum(shaped, axis=2).reshape(1, local_rows, local_width).astype(jnp.bfloat16)

    query_full = jnp.zeros((length, HEAD), jnp.bfloat16)
    for which in range(2):
        query_full = lax.dynamic_update_slice_in_dim(
            query_full, query_rounded[which], row_list[which] * block, 0
        )
    query_back = lax.all_to_all(query_full, "seq", split_axis=0, concat_axis=1, tiled=True)
    query_out = settle(query_back)
    return (query_out, settle(key_back), settle(value_back))


NT = ((1,), (1,))
NN = ((1,), (0,))
TN = ((0,), (0,))
GROUP = 8


def head_span(head):
    low = head * HEAD // LANES * LANES
    high = -(-(head + 1) * HEAD // LANES) * LANES
    return low, high


def head_mask(head):
    low, high = head_span(head)
    lane = lax.broadcasted_iota(jnp.int32, (1, high - low), 1) + low
    inside = (lane >= head * HEAD) & (lane < (head + 1) * HEAD)
    return inside.astype(jnp.float32).astype(jnp.bfloat16)


def matmul(left, right, dims):
    return lax.dot_general(left, right, (dims, ((), ())), preferred_element_type=jnp.float32)


def stack(values, axis):
    return values[0] if len(values) == 1 else jnp.concatenate(values, axis=axis)


def allowed(lengths_ref, rows, query_block, key_block):
    shape = (rows, rows)
    position = query_block * rows + lax.broadcasted_iota(jnp.int32, shape, 1)
    keys = key_block * rows + lax.broadcasted_iota(jnp.int32, shape, 0)
    start = jnp.zeros_like(position)
    bound = jnp.int32(0)
    for doc in range(1, lengths_ref.shape[0]):
        bound = bound + lengths_ref[doc]
        start = jnp.where(position >= bound, bound, start)
    return (keys >= start) & (keys <= position)


def make_tile(lengths_ref, rows, queries, keys):
    mask = stack(
        [stack([allowed(lengths_ref, rows, q, k) for _, q in queries], 1) for _, k in keys], 0
    )
    return [slot for slot, _ in queries], [slot for slot, _ in keys], mask


def tile_values(plan, head, queries, keys, products):
    low, high = head_span(head)
    keep = head_mask(head)

    def gather(refs, number, slots):
        return stack([refs[slot][number][0, :, low:high] for slot in slots], 0)

    out = []
    for query_slots, key_slots, _ in plan:
        q = [gather(queries, number, query_slots) for number in range(products)]
        k = [gather(keys, number, key_slots) * keep for number in range(products)]
        out.append((q, k, [matmul(b, a, NT) for a, b in zip(q, k)]))
    return out, keep


def tiles_ahead(heads, plan, queries, keys, products):
    ready = tile_values(plan, 0, queries, keys, products)
    for head in range(heads):
        now = ready
        if head + 1 < heads:
            ready = tile_values(plan, head + 1, queries, keys, products)
        yield head, now


def pair_tile(lengths_ref, rows, me, slots=(0, 1)):
    mate = me + 1 - 2 * lax.rem(me, 2)
    return make_tile(lengths_ref, rows, ((0, me), (1, mate)), [(slot, me - 2 * slot) for slot in slots])


def third_tile(third, lengths_ref, rows, me):
    slots, keys, mask = make_tile(lengths_ref, rows, ((2, me + 1),), ((1, me - 2),))
    return slots, keys, mask & (me == third)


def lane_cut(value, number, rows):
    return value[:, number * rows : (number + 1) * rows]


def row_of(group, kinds, kind, head):
    return pl.ds((group * kinds + kind) * GROUP + head, 1)


def per_query(slots, kinds, kind, head, ref):
    return stack([ref[row_of(slot, kinds, kind, head), :] for slot in slots], 1)


def collect_stats(heads, power, step, plan, queries, keys, rows, out_ref, groups):
    for head, (tiles, _) in tiles_ahead(heads, plan, queries, keys, 1):
        for (query_slots, _, mask), (_, _, (raw,)) in zip(plan, tiles):
            raw = jnp.where(mask, raw, FLOOR)
            top = jnp.max(raw, axis=0, keepdims=True)
            sums = jnp.sum(jnp.exp2((raw - top) * power), axis=0, keepdims=True)
            for number, slot in enumerate(query_slots):
                at = step * heads + head
                out_ref[row_of(groups[slot], 2, 0, at), :] = lane_cut(top, number, rows)
                out_ref[row_of(groups[slot], 2, 1, at), :] = lane_cut(sums, number, rows)


def stats_kernel(
    heads, power, place_ref, lengths_ref, q_own, q_mate, k_own, k_back, o_own, v_own, o_copy, v_copy, out_ref
):
    rows, me, step = k_own.shape[1], place_ref[0], pl.program_id(0)
    o_copy[...], v_copy[...] = o_own[...], v_own[...]
    plan = [pair_tile(lengths_ref, rows, me)]
    queries, keys = ((q_own,), (q_mate,)), ((k_own,), (k_back,))
    collect_stats(heads, power, step, plan, queries, keys, rows, out_ref, (0, 1))


def third_stats_kernel(third, heads, power, place_ref, lengths_ref, q_third, k_back, out_ref):
    rows, me, step = k_back.shape[1], place_ref[0], pl.program_id(0)
    plan = [third_tile(third, lengths_ref, rows, me)]
    queries, keys = (None, None, (q_third,)), (None, (k_back,))
    collect_stats(heads, power, step, plan, queries, keys, rows, out_ref, (None, None, 0))


def part_of(ref, kinds, number):
    size = kinds * GROUP
    return ref[number * size : (number + 1) * size, :]


def group_parts(kinds, mine, sent, extra):
    own = [part_of(mine, kinds, 0), part_of(sent, kinds, 1)]
    mate = [part_of(mine, kinds, 1), part_of(sent, kinds, 0)]
    if extra:
        near, far = extra
        own, mate = own + [near[...]], mate + [far[...]]
    return [own, mate]


def merge_groups(scaling, shift_ref, refs):
    mine, sent, *extra = refs
    for number, parts in enumerate(group_parts(2, mine, sent, extra)):
        shift_ref[number * GROUP : (number + 1) * GROUP, :] = merge_stats(scaling, parts)


def merge_stats(scaling, parts):
    split = [(jnp.where(p[GROUP:] > 0, p[:GROUP], FLOOR), p[GROUP:]) for p in parts]
    top = functools.reduce(jnp.maximum, [s[0] for s in split])
    total = sum(jnp.exp((s[0] - top) * scaling) * s[1] for s in split)
    return top + jnp.log(jnp.where(total > 0, total, 1.0)) / scaling


class Emitter:
    def __init__(self, outs, base={}):
        self.outs, self.base, self.carry = outs, base, {}

    def put(self, name, start, stop, value):
        if name in self.base:
            value = value + self.base[name][0, :, start:stop].astype(jnp.float32)
        self.outs[name][0, :, start:stop] = value.astype(jnp.bfloat16)

    def emit(self, head, name, value):
        low, high = head_span(head)
        first, last = head * HEAD % LANES == 0, (head + 1) * HEAD % LANES == 0
        start, stop = low, high
        if not first:
            self.put(name, low, low + LANES, value[:, :LANES] + self.carry.pop(name))
            start = low + LANES
        if not last:
            self.carry[name] = value[:, high - LANES - low :]
            stop = high - LANES
        if stop > start:
            self.put(name, start, stop, value[:, start - low : stop - low])


def add_rows(sums, kind, slots, value, rows):
    for number, slot in enumerate(slots):
        piece = value[number * rows : (number + 1) * rows]
        name = (kind, slot)
        sums[name] = sums[name] + piece if name in sums else piece


def split_refs(refs):
    return ((refs[0:2], refs[2:4]), (refs[4:6], refs[6:8]), refs[8:])


def values_kernel(merge, slots, heads, scaling, power, place_ref, lengths_ref, q0, o0, q1, o1, *refs):
    key_refs, refs = refs[: len(slots)], refs[len(slots) :]
    queries, keys = ((q0, o0), (q1, o1)), {slot: (ref,) for slot, ref in zip(slots, key_refs)}
    if merge:
        *refs, shift_ref = refs
        stats, value_refs = refs[: -len(slots)], refs[-len(slots) :]
        merge_groups(scaling, shift_ref, stats)
    else:
        shift_ref, value_refs = refs[0], refs[-len(slots) :]
    rows, me, step = q0.shape[1], place_ref[0], pl.program_id(0)
    plan = [pair_tile(lengths_ref, rows, me, slots)]
    out = Emitter({("v", slot): ref for slot, ref in zip(slots, value_refs)})
    for head, (tiles, keep) in tiles_ahead(heads, plan, queries, keys, 1):
        low, high = head_span(head)
        sums = {}
        for (query_slots, key_slots, mask), (_, _, (raw,)) in zip(plan, tiles):
            shift = per_query(query_slots, 1, 0, step * heads + head, shift_ref)
            weight = jnp.where(mask, jnp.exp2((raw - shift) * power), 0.0).astype(jnp.bfloat16)
            o = stack([queries[slot][1][0, :, low:high] for slot in query_slots], 0) * keep
            add_rows(sums, "v", key_slots, matmul(weight, o, NN), rows)
        for name, value in sums.items():
            out.emit(head, name, value)


def dots_kernel(merge, heads, scaling, power, place_ref, lengths_ref, *refs):
    queries, keys, refs = split_refs(refs)
    if merge:
        *stats, bundle_ref, dots_ref, shift_ref = refs
        merge_groups(scaling, shift_ref, stats)
        bundle_ref[: 4 * GROUP] = stats[0][...]
    else:
        shift_ref, dots_ref = refs
    rows, me, step = keys[0][0].shape[1], place_ref[0], pl.program_id(0)
    plan = [pair_tile(lengths_ref, rows, me)]
    for head, (tiles, _) in tiles_ahead(heads, plan, queries, keys, 2):
        at = step * heads + head
        for (query_slots, _, mask), (_, _, (raw, grads)) in zip(plan, tiles):
            shift = per_query(query_slots, 1, 0, at, shift_ref)
            weight = jnp.where(mask, jnp.exp2((raw - shift) * power), 0.0)
            dots = jnp.sum(weight * grads, axis=0, keepdims=True)
            for number, slot in enumerate(query_slots):
                dots_ref[row_of(slot, 1, 0, at), :] = lane_cut(dots, number, rows)
                if merge:
                    bundle_ref[row_of(4 + slot, 1, 0, at), :] = lane_cut(dots, number, rows)


def keys_kernel(third, heads, scaling, power, place_ref, lengths_ref, *refs):
    queries, keys, refs = split_refs(refs)
    (*base, shift_ref, mine, sent), refs = (refs[:3], refs[3:]) if third is None else (refs[:4], refs[4:])
    *extra, key_own, key_back, query_own, query_mate, total_ref = refs
    rows, me, step = keys[0][0].shape[1], place_ref[0], pl.program_id(0)
    plan = [pair_tile(lengths_ref, rows, me)]
    for number, parts in enumerate(group_parts(1, mine, sent, extra)):
        total_ref[number * GROUP : (number + 1) * GROUP, :] = sum(parts)
    outs = {("k", 0): key_own, ("k", 1): key_back, ("q", 0): query_own, ("q", 1): query_mate}
    out = Emitter(outs, {("k", 1): ref for ref in base})
    for head, (tiles, keep) in tiles_ahead(heads, plan, queries, keys, 2):
        at = step * heads + head
        sums = {}
        for (query_slots, key_slots, mask), ((q, _), (k, _), (raw, grads)) in zip(plan, tiles):
            shift = per_query(query_slots, 1, 0, at, shift_ref)
            dots = per_query(query_slots, 1, 0, at, total_ref)
            weight = jnp.where(mask, jnp.exp2((raw - shift) * power), 0.0)
            slope = (weight * (grads - dots) * scaling).astype(jnp.bfloat16)
            add_rows(sums, "k", key_slots, matmul(slope, q * keep, NN), rows)
            add_rows(sums, "q", query_slots, matmul(slope, k, TN), rows)
        for name, value in sums.items():
            out.emit(head, name, value)


def third_kernel(
    third, heads, scaling, power, place_ref, lengths_ref, q_third, o_third, k_back, v_back, value_part,
    stats, even, odd, value_out, key_out, query_out, dots_ref, shift_ref,
):
    rows, me, step = k_back.shape[1], place_ref[0], pl.program_id(0)
    parts = [stats[...], part_of(even, 2, 0), part_of(odd, 2, 1)]
    shift_ref[...] = merge_stats(scaling, parts)
    slots, keys, mask = third_tile(third, lengths_ref, rows, me)
    queries, keys = (None, None, (q_third, o_third)), (None, (k_back, v_back))
    plan = [(slots, [1], mask)]
    out = Emitter({"v": value_out, "k": key_out, "q": query_out}, {"v": value_part})
    for head, (tiles, keep) in tiles_ahead(heads, plan, queries, keys, 2):
        (q, o), (k, _), (raw, grads) = tiles[0]
        at = step * heads + head
        weight = jnp.where(mask, jnp.exp2((raw - shift_ref[pl.ds(at, 1), :]) * power), 0.0)
        dots = jnp.sum(weight * grads, axis=0, keepdims=True)
        dots_ref[pl.ds(at, 1), :] = dots
        total = dots + even[row_of(4, 1, 0, at), :] + odd[row_of(5, 1, 0, at), :]
        slope = (weight * (grads - total) * scaling).astype(jnp.bfloat16)
        out.emit(head, "v", matmul(weight.astype(jnp.bfloat16), o * keep, NN))
        out.emit(head, "k", matmul(slope, q * keep, NN))
        out.emit(head, "q", matmul(slope, k, TN))


def add_refs(*refs):
    return sum(ref[...].astype(jnp.float32) for ref in refs)


def sums_kernel(key_part, key_sent, *refs):
    *query_parts, key_out, query_out = refs
    key_out[...] = add_refs(key_part, key_sent).astype(jnp.bfloat16)
    query_out[...] = add_refs(*query_parts).astype(jnp.bfloat16)


def halo_program(third, queries, key_vectors, value_vectors, out_grad, facts):
    _, rows, width = queries.shape
    seq_size = lax.axis_size("seq")
    me = lax.axis_index("seq").astype(jnp.int32)
    scaling = HEAD ** (-0.5)
    power = scaling * math.log2(math.e)
    steps = width // HEAD // 4
    part = width // steps
    heads = part // HEAD
    devices = range(seq_size)
    mates = [(s, s ^ 1) for s in devices]
    ring = third is None
    chain = [(s, s + 2) for s in devices if s + 2 < seq_size]
    ahead = [(s, (s + 2) % seq_size) for s in devices] if ring else chain
    behind = [(s, s - 2) for s in devices if s >= 2]
    if not ring:
        relay, to_odd = [(third + 2, third)], [(third, third + 2)]
        from_even, to_even = [(third + 1, third)], [(third, third + 1)]

    def send(value, pairs):
        return lax.ppermute(value, "seq", pairs)

    smem = pl.BlockSpec(memory_space=pltpu.SMEM)
    wide = pl.BlockSpec((1, rows, part), lambda step: (0, 0, step))
    wide_shape = jax.ShapeDtypeStruct((1, rows, width), jnp.bfloat16)

    def slim(groups, kinds):
        return pl.BlockSpec((groups * kinds * GROUP, rows), lambda step: (0, 0))

    def slim_shape(groups, kinds):
        return jax.ShapeDtypeStruct((groups * kinds * GROUP, rows), jnp.float32)

    def call(kernel, products, wides, slims, outs, slim_outs, plain=False, scratch=(), after=()):
        flops = 2 * products * 4 * rows * rows * width * 3 // 2
        lead = [] if plain else [me[None], facts]
        return pl.pallas_call(
            kernel,
            grid=(steps,),
            in_specs=[smem] * len(lead)
            + [wide] * len(wides)
            + [slim(groups, kinds) for groups, kinds, _ in slims]
            + [pl.BlockSpec(memory_space=pl.ANY)] * len(after),
            out_specs=[wide] * outs + [slim(*sizes) for sizes in slim_outs],
            out_shape=[wide_shape] * outs + [slim_shape(*sizes) for sizes in slim_outs],
            scratch_shapes=[pltpu.VMEM((groups * GROUP, rows), jnp.float32) for groups in scratch],
            compiler_params=pltpu.CompilerParams(vmem_limit_bytes=20 * 1024 * 1024),
            cost_estimate=pl.CostEstimate(
                flops=flops, bytes_accessed=20 * rows * width, transcendentals=0
            ),
        )(*lead, *wides, *[value for _, _, value in slims], *after)

    query_mate = send(queries, mates)
    key_back = send(key_vectors, chain)
    grad_mate = send(out_grad, mates)
    value_back = send(value_vectors, ahead)
    grad_own, value_own, stats = call(
        functools.partial(stats_kernel, heads, power), 1,
        [queries, query_mate, key_vectors, key_back, out_grad, value_vectors], [], 2, [(2, 2)],
    )
    stats_mate = send(stats, mates)
    rows_in = [queries, grad_own, query_mate, grad_mate]
    tensors = rows_in + [key_vectors, value_own, key_back, value_back]
    constants = (heads, scaling, power)
    if ring:
        value_sent, shift = call(
            functools.partial(values_kernel, True, (1,), *constants), 1, rows_in + [key_back],
            [(2, 2, stats), (2, 2, stats_mate)], 1, [(2, 1)],
        )
        (dots,) = call(
            functools.partial(dots_kernel, False, *constants), 2, tensors, [(2, 1, shift)], 0, [(2, 1)]
        )
        dots_in = [(2, 1, shift), (2, 1, dots), (2, 1, send(dots, mates))]
        (value_part,) = call(
            functools.partial(values_kernel, False, (0,), *constants), 1, rows_in + [key_vectors],
            [(2, 1, shift)], 1, [], after=[dots],
        )
        base = []
    else:
        query_third = send(query_mate, relay)
        held, stats_mate = lax.optimization_barrier((grad_mate, stats_mate))
        grad_third = send(held, relay)
        query_third, _ = lax.optimization_barrier((query_third, value_back))
        (third_stats,) = call(
            functools.partial(third_stats_kernel, third, heads, power), 1, [query_third, key_back], [],
            0, [(1, 2)],
        )
        stats_in = [(2, 2, stats), (2, 2, stats_mate)]
        stats_in += [(1, 2, send(third_stats, to_even)), (1, 2, send(third_stats, to_odd))]
        bundle, dots, shift = call(
            functools.partial(dots_kernel, True, *constants), 2, tensors, stats_in, 0,
            [(2, 3), (2, 1), (2, 1)],
        )
        even, odd, dots_mate = send(bundle, from_even), send(bundle, relay), send(dots, mates)
        value_part, value_back_part = call(
            functools.partial(values_kernel, False, (0, 1), *constants), 2, rows_in + [key_vectors, key_back],
            [(2, 1, shift)], 2, [],
        )
        value_back_part, dots_mate = lax.optimization_barrier((value_back_part, dots_mate))
        value_sent, key_third, query_extra, third_dots = call(
            functools.partial(third_kernel, third, *constants), 2,
            [query_third, grad_third, key_back, value_back, value_back_part],
            [(1, 2, third_stats), (2, 3, even), (2, 3, odd)],
            3, [(1, 1)], scratch=[1],
        )
        dots_in = [(2, 1, shift), (2, 1, dots), (2, 1, dots_mate)]
        dots_in += [(1, 1, send(third_dots, to_even)), (1, 1, send(third_dots, to_odd))]
        base = [key_third]
    value_received = send(value_sent, behind)
    key_part, key_sent, query_part, query_sent = call(
        functools.partial(keys_kernel, third, *constants), 4, tensors + base, dots_in, 4, [], scratch=[2],
    )
    key_received = send(key_sent, behind)
    query_received = [send(query_sent, mates)] + ([] if ring else [send(query_extra, to_even)])
    value_ready = (value_part.astype(jnp.float32) + value_received.astype(jnp.float32)).astype(jnp.bfloat16)
    key_ready, query_ready = call(
        sums_kernel, 0, [key_part, key_received, query_part, *query_received], [], 2, [], plain=True
    )
    return query_ready, key_ready, value_ready


def program_kernel(shift, lengths_ref, out_ref):
    start, found = jnp.int32(0), jnp.int32(0)
    for doc in range(lengths_ref.shape[0]):
        end = start + lengths_ref[doc]
        last = (end - 1) >> shift
        spans = (last - (start >> shift) >= 3) & (last & 1 == 0)
        found = jnp.where(spans, (last >> 1) - 1, found)
        out_ref[doc + 1] = lengths_ref[doc]
        start = end
    out_ref[0] = found


def program_facts(rows, doc_lengths):
    smem = pl.BlockSpec(memory_space=pltpu.SMEM)
    return pl.pallas_call(
        functools.partial(program_kernel, rows.bit_length() - 1),
        in_specs=[smem],
        out_specs=smem,
        out_shape=jax.ShapeDtypeStruct((doc_lengths.shape[0] + 1,), jnp.int32),
    )(doc_lengths)


def halo_shards(*arguments):
    *tensors, doc_lengths = arguments
    facts = program_facts(tensors[0].shape[1], doc_lengths)
    thirds = range(3, lax.axis_size("seq") - 2, 2)
    programs = [functools.partial(halo_program, third) for third in (None, *thirds)]
    return lax.switch(facts[0], programs, *tensors, facts)


def shards(queries, key_vectors, value_vectors, out_grad, doc_lengths):
    _, rows, width = queries.shape
    seq_size = lax.axis_size("seq")
    longest = rows * seq_size * 3 // 8
    fits = longest <= 3 * rows and seq_size % 2 == 0 and seq_size > 4 and rows == LANES
    heads = width // HEAD
    plan = halo_shards if fits and heads % 4 == 0 and heads <= GROUP else spread_shards
    return plan(queries, key_vectors, value_vectors, out_grad, doc_lengths)


def solution(mesh):
    return jax.shard_map(
        shards,
        mesh=mesh,
        in_specs=(
            P("section", "seq", "dp"),
            P("section", "seq", "dp"),
            P("section", "seq", "dp"),
            P("section", "seq", "dp"),
            P(),
        ),
        out_specs=(P("section", "seq", "dp"), P("section", "seq", "dp"), P("section", "seq", "dp")),
        check_vma=False,
    )
```

```python
import functools
import math
import jax
import jax.numpy as jnp
from jax import lax
from jax.experimental import pallas as pl
from jax.experimental.pallas import tpu as pltpu
from jax.sharding import PartitionSpec as P

HEAD = 224
LANES = 128
FLOOR = -1e30


def pick_slot(stacked, slot):
    return lax.dynamic_index_in_dim(stacked, slot, 0, keepdims=False)


def put_slot(stacked, update, slot):
    return lax.dynamic_update_index_in_dim(stacked, update, slot, 0)


def spread_shards(queries, key_vectors, value_vectors, out_grad, doc_lengths):
    local_rows = queries.shape[1]
    local_width = queries.shape[2]
    head_count = local_width // HEAD
    seq_size = lax.axis_size("seq")
    group = seq_size // head_count
    scaling = HEAD ** (-0.5)

    def spread(matrix):
        shaped = matrix.reshape(local_rows, head_count, 1, HEAD)
        copies = jnp.broadcast_to(shaped, (local_rows, head_count, group, HEAD))
        return copies.reshape(local_rows, seq_size * HEAD)

    query_head, key_head, value_head, cot_head = (
        lax.all_to_all(spread(queries), "seq", split_axis=1, concat_axis=0, tiled=True),
        lax.all_to_all(spread(key_vectors), "seq", split_axis=1, concat_axis=0, tiled=True),
        lax.all_to_all(spread(value_vectors), "seq", split_axis=1, concat_axis=0, tiled=True),
        lax.all_to_all(spread(out_grad), "seq", split_axis=1, concat_axis=0, tiled=True),
    )
    length = key_head.shape[0]
    member = lax.axis_index("seq") % group
    blocks = 2 * group
    block = length // blocks
    bounds = jnp.cumsum(doc_lengths)
    positions = jnp.arange(length, dtype=jnp.int32)
    doc_index = jnp.sum((positions[:, None] >= bounds[None, :]).astype(jnp.int32), axis=1)
    row_list = [member, blocks - 1 - member]
    query_list = []
    cot_list = []
    pos_list = []
    for which in range(2):
        offset = row_list[which] * block
        query_list.append(lax.dynamic_slice_in_dim(query_head, offset, block, 0))
        cot_list.append(lax.dynamic_slice_in_dim(cot_head, offset, block, 0))
        pos_list.append(offset + jnp.arange(block, dtype=jnp.int32))
    query_stack = jnp.stack(query_list)
    cot_stack = jnp.stack(cot_list)
    pos_stack = jnp.stack(pos_list)
    doc_stack = jnp.take(doc_index, pos_stack)
    plan = []
    for number in range(blocks + 1):
        first = number <= member
        slot = jnp.where(first, 0, 1).astype(jnp.int32)
        col_block = jnp.where(first, number, number - member - 1)
        flag = None
        plan.append((slot, col_block, flag))
    row_max = jnp.full((2, block), -jnp.inf, jnp.float32)
    row_sum = jnp.zeros((2, block), jnp.float32)
    stored = []
    for slot, col_block, flag in plan:

        def score_tile(carry, slot=slot, col_block=col_block):
            maxima, totals = carry
            query_rows = pick_slot(query_stack, slot)
            key_rows = lax.dynamic_slice_in_dim(key_head, col_block * block, block, 0)
            col_docs = lax.dynamic_slice_in_dim(doc_index, col_block * block, block, 0)
            col_positions = col_block * block + jnp.arange(block, dtype=jnp.int32)
            raw = jnp.dot(query_rows, key_rows.T, preferred_element_type=jnp.float32) * scaling
            allowed = (pick_slot(doc_stack, slot)[:, None] == col_docs[None, :]) & (
                pick_slot(pos_stack, slot)[:, None] >= col_positions[None, :]
            )
            scores = jnp.where(allowed, raw, -jnp.inf)
            before = pick_slot(maxima, slot)
            after = jnp.maximum(before, jnp.max(scores, axis=1))
            safe = jnp.where(jnp.isfinite(after), after, 0.0)
            total = pick_slot(totals, slot) * jnp.exp(before - safe) + jnp.sum(
                jnp.exp(scores - safe[:, None]), axis=1
            )
            return (scores, put_slot(maxima, after, slot), put_slot(totals, total, slot))

        scores, row_max, row_sum = score_tile((row_max, row_sum))
        stored.append(scores)

    def tile_weights(scores, slot):
        return (
            jnp.exp(scores - pick_slot(row_max, slot)[:, None]) / pick_slot(row_sum, slot)[:, None]
        )

    summed = jnp.zeros((2, block, HEAD), jnp.float32)
    for (slot, col_block, flag), scores in zip(plan, stored):

        def add_values(carry, slot=slot, col_block=col_block, scores=scores):
            rounded = tile_weights(scores, slot).astype(jnp.bfloat16)
            value_rows = lax.dynamic_slice_in_dim(value_head, col_block * block, block, 0)
            term = jnp.dot(rounded, value_rows, preferred_element_type=jnp.float32)
            return put_slot(carry, pick_slot(carry, slot) + term, slot)

        summed = add_values(summed)
    attended = summed.astype(jnp.bfloat16)
    row_dot = jnp.sum(cot_stack.astype(jnp.float32) * attended.astype(jnp.float32), axis=2)
    query_acc = jnp.zeros((2, block, HEAD), jnp.float32)
    key_acc = jnp.zeros((length, HEAD), jnp.float32)
    value_acc = jnp.zeros((length, HEAD), jnp.float32)
    for (slot, col_block, flag), scores in zip(plan, stored):

        def backward_tile(carry, slot=slot, col_block=col_block, scores=scores):
            query_sum, key_sum, value_sum = carry
            weights = tile_weights(scores, slot)
            rounded = weights.astype(jnp.bfloat16)
            query_rows = pick_slot(query_stack, slot)
            cot_rows = pick_slot(cot_stack, slot)
            start = col_block * block
            key_rows = lax.dynamic_slice_in_dim(key_head, start, block, 0)
            value_rows = lax.dynamic_slice_in_dim(value_head, start, block, 0)
            value_term = jnp.dot(rounded.T, cot_rows, preferred_element_type=jnp.float32)
            prob_grad = jnp.dot(cot_rows, value_rows.T, preferred_element_type=jnp.float32)
            score_grad = (
                weights * (prob_grad - pick_slot(row_dot, slot)[:, None]) * scaling
            ).astype(jnp.bfloat16)
            query_term = jnp.dot(score_grad, key_rows, preferred_element_type=jnp.float32)
            key_term = jnp.dot(score_grad.T, query_rows, preferred_element_type=jnp.float32)
            query_sum = put_slot(query_sum, pick_slot(query_sum, slot) + query_term, slot)
            key_sum = lax.dynamic_update_slice_in_dim(
                key_sum, lax.dynamic_slice_in_dim(key_sum, start, block, 0) + key_term, start, 0
            )
            value_sum = lax.dynamic_update_slice_in_dim(
                value_sum,
                lax.dynamic_slice_in_dim(value_sum, start, block, 0) + value_term,
                start,
                0,
            )
            return (query_sum, key_sum, value_sum)

        query_acc, key_acc, value_acc = backward_tile((query_acc, key_acc, value_acc))
    query_rounded = query_acc.astype(jnp.bfloat16)
    key_back, value_back = (
        lax.all_to_all(key_acc, "seq", split_axis=0, concat_axis=1, tiled=True),
        lax.all_to_all(value_acc, "seq", split_axis=0, concat_axis=1, tiled=True),
    )

    def settle(received):
        shaped = received.astype(jnp.float32).reshape(local_rows, head_count, group, HEAD)
        return jnp.sum(shaped, axis=2).reshape(1, local_rows, local_width).astype(jnp.bfloat16)

    query_full = jnp.zeros((length, HEAD), jnp.bfloat16)
    for which in range(2):
        query_full = lax.dynamic_update_slice_in_dim(
            query_full, query_rounded[which], row_list[which] * block, 0
        )
    query_back = lax.all_to_all(query_full, "seq", split_axis=0, concat_axis=1, tiled=True)
    query_out = settle(query_back)
    return (query_out, settle(key_back), settle(value_back))


NT = ((1,), (1,))
NN = ((1,), (0,))
TN = ((0,), (0,))
GROUP = 8


def head_span(head):
    low = head * HEAD // LANES * LANES
    high = -(-(head + 1) * HEAD // LANES) * LANES
    return low, high


def head_mask(head):
    low, high = head_span(head)
    lane = lax.broadcasted_iota(jnp.int32, (1, high - low), 1) + low
    inside = (lane >= head * HEAD) & (lane < (head + 1) * HEAD)
    return inside.astype(jnp.float32).astype(jnp.bfloat16)


def matmul(left, right, dims):
    return lax.dot_general(left, right, (dims, ((), ())), preferred_element_type=jnp.float32)


def stack(values, axis):
    return values[0] if len(values) == 1 else jnp.concatenate(values, axis=axis)


def allowed(lengths_ref, rows, query_block, key_block):
    shape = (rows, rows)
    position = query_block * rows + lax.broadcasted_iota(jnp.int32, shape, 1)
    keys = key_block * rows + lax.broadcasted_iota(jnp.int32, shape, 0)
    start = jnp.zeros_like(position)
    bound = jnp.int32(0)
    for doc in range(1, lengths_ref.shape[0]):
        bound = bound + lengths_ref[doc]
        start = jnp.where(position >= bound, bound, start)
    return (keys >= start) & (keys <= position)


def make_tile(lengths_ref, rows, queries, keys):
    mask = stack(
        [stack([allowed(lengths_ref, rows, q, k) for _, q in queries], 1) for _, k in keys], 0
    )
    return [slot for slot, _ in queries], [slot for slot, _ in keys], mask


def tile_values(plan, head, queries, keys, products):
    low, high = head_span(head)
    keep = head_mask(head)

    def gather(refs, number, slots):
        return stack([refs[slot][number][0, :, low:high] for slot in slots], 0)

    out = []
    for query_slots, key_slots, _ in plan:
        q = [gather(queries, number, query_slots) for number in range(products)]
        k = [gather(keys, number, key_slots) * keep for number in range(products)]
        out.append((q, k, [matmul(b, a, NT) for a, b in zip(q, k)]))
    return out, keep


def tiles_ahead(heads, plan, queries, keys, products):
    ready = tile_values(plan, 0, queries, keys, products)
    for head in range(heads):
        now = ready
        if head + 1 < heads:
            ready = tile_values(plan, head + 1, queries, keys, products)
        yield head, now


def pair_tile(lengths_ref, rows, me, slots=(0, 1)):
    mate = me + 1 - 2 * lax.rem(me, 2)
    return make_tile(lengths_ref, rows, ((0, me), (1, mate)), [(slot, me - 2 * slot) for slot in slots])


def third_tile(third, lengths_ref, rows, me):
    slots, keys, mask = make_tile(lengths_ref, rows, ((2, me + 1),), ((1, me - 2),))
    return slots, keys, mask & (me == third)


def lane_cut(value, number, rows):
    return value[:, number * rows : (number + 1) * rows]


def row_of(group, kinds, kind, head):
    return pl.ds((group * kinds + kind) * GROUP + head, 1)


def per_query(slots, kinds, kind, head, ref):
    return stack([ref[row_of(slot, kinds, kind, head), :] for slot in slots], 1)


def collect_stats(heads, power, step, plan, queries, keys, rows, out_ref, groups):
    for head, (tiles, _) in tiles_ahead(heads, plan, queries, keys, 1):
        for (query_slots, _, mask), (_, _, (raw,)) in zip(plan, tiles):
            raw = jnp.where(mask, raw, FLOOR)
            top = jnp.max(raw, axis=0, keepdims=True)
            sums = jnp.sum(jnp.exp2((raw - top) * power), axis=0, keepdims=True)
            for number, slot in enumerate(query_slots):
                at = step * heads + head
                out_ref[row_of(groups[slot], 2, 0, at), :] = lane_cut(top, number, rows)
                out_ref[row_of(groups[slot], 2, 1, at), :] = lane_cut(sums, number, rows)


def stats_kernel(
    heads, power, place_ref, lengths_ref, q_own, q_mate, k_own, k_back, o_own, v_own, o_copy, v_copy, out_ref
):
    rows, me, step = k_own.shape[1], place_ref[0], place_ref[1]
    o_copy[...], v_copy[...] = o_own[...], v_own[...]
    plan = [pair_tile(lengths_ref, rows, me)]
    queries, keys = ((q_own,), (q_mate,)), ((k_own,), (k_back,))
    collect_stats(heads, power, step, plan, queries, keys, rows, out_ref, (0, 1))


def third_stats_kernel(third, heads, power, place_ref, lengths_ref, q_third, k_back, out_ref):
    rows, me, step = k_back.shape[1], place_ref[0], place_ref[1]
    plan = [third_tile(third, lengths_ref, rows, me)]
    queries, keys = (None, None, (q_third,)), (None, (k_back,))
    collect_stats(heads, power, step, plan, queries, keys, rows, out_ref, (None, None, 0))


def part_of(ref, kinds, number):
    size = kinds * GROUP
    return ref[number * size : (number + 1) * size, :]


def group_parts(kinds, mine, sent, extra):
    own = [part_of(mine, kinds, 0), part_of(sent, kinds, 1)]
    mate = [part_of(mine, kinds, 1), part_of(sent, kinds, 0)]
    if extra:
        near, far = extra
        own, mate = own + [near[...]], mate + [far[...]]
    return [own, mate]


def merge_groups(scaling, shift_ref, refs):
    mine, sent, *extra = refs
    for number, parts in enumerate(group_parts(2, mine, sent, extra)):
        shift_ref[number * GROUP : (number + 1) * GROUP, :] = merge_stats(scaling, parts)


def merge_stats(scaling, parts):
    split = [(jnp.where(p[GROUP:] > 0, p[:GROUP], FLOOR), p[GROUP:]) for p in parts]
    top = functools.reduce(jnp.maximum, [s[0] for s in split])
    total = sum(jnp.exp((s[0] - top) * scaling) * s[1] for s in split)
    return top + jnp.log(jnp.where(total > 0, total, 1.0)) / scaling


class Emitter:
    def __init__(self, outs, base={}):
        self.outs, self.base, self.carry = outs, base, {}

    def put(self, name, start, stop, value):
        if name in self.base:
            value = value + self.base[name][0, :, start:stop].astype(jnp.float32)
        self.outs[name][0, :, start:stop] = value.astype(jnp.bfloat16)

    def emit(self, head, name, value):
        low, high = head_span(head)
        first, last = head * HEAD % LANES == 0, (head + 1) * HEAD % LANES == 0
        start, stop = low, high
        if not first:
            self.put(name, low, low + LANES, value[:, :LANES] + self.carry.pop(name))
            start = low + LANES
        if not last:
            self.carry[name] = value[:, high - LANES - low :]
            stop = high - LANES
        if stop > start:
            self.put(name, start, stop, value[:, start - low : stop - low])


def add_rows(sums, kind, slots, value, rows):
    for number, slot in enumerate(slots):
        piece = value[number * rows : (number + 1) * rows]
        name = (kind, slot)
        sums[name] = sums[name] + piece if name in sums else piece


def split_refs(refs):
    return ((refs[0:2], refs[2:4]), (refs[4:6], refs[6:8]), refs[8:])


def values_kernel(merge, slots, heads, scaling, power, place_ref, lengths_ref, q0, o0, q1, o1, *refs):
    key_refs, refs = refs[: len(slots)], refs[len(slots) :]
    queries, keys = ((q0, o0), (q1, o1)), {slot: (ref,) for slot, ref in zip(slots, key_refs)}
    if merge:
        *refs, shift_ref = refs
        stats, value_refs = refs[: -len(slots)], refs[-len(slots) :]
        merge_groups(scaling, shift_ref, stats)
    else:
        shift_ref, value_refs = refs[0], refs[-len(slots) :]
    rows, me, step = q0.shape[1], place_ref[0], place_ref[1]
    plan = [pair_tile(lengths_ref, rows, me, slots)]
    out = Emitter({("v", slot): ref for slot, ref in zip(slots, value_refs)})
    for head, (tiles, keep) in tiles_ahead(heads, plan, queries, keys, 1):
        low, high = head_span(head)
        sums = {}
        for (query_slots, key_slots, mask), (_, _, (raw,)) in zip(plan, tiles):
            shift = per_query(query_slots, 1, 0, step * heads + head, shift_ref)
            weight = jnp.where(mask, jnp.exp2((raw - shift) * power), 0.0).astype(jnp.bfloat16)
            o = stack([queries[slot][1][0, :, low:high] for slot in query_slots], 0) * keep
            add_rows(sums, "v", key_slots, matmul(weight, o, NN), rows)
        for name, value in sums.items():
            out.emit(head, name, value)


def dots_kernel(merge, heads, scaling, power, place_ref, lengths_ref, *refs):
    queries, keys, refs = split_refs(refs)
    if merge:
        *stats, bundle_ref, dots_ref, shift_ref = refs
        merge_groups(scaling, shift_ref, stats)
        bundle_ref[: 4 * GROUP] = stats[0][...]
    else:
        shift_ref, dots_ref = refs
    rows, me, step = keys[0][0].shape[1], place_ref[0], place_ref[1]
    plan = [pair_tile(lengths_ref, rows, me)]
    for head, (tiles, _) in tiles_ahead(heads, plan, queries, keys, 2):
        at = step * heads + head
        for (query_slots, _, mask), (_, _, (raw, grads)) in zip(plan, tiles):
            shift = per_query(query_slots, 1, 0, at, shift_ref)
            weight = jnp.where(mask, jnp.exp2((raw - shift) * power), 0.0)
            dots = jnp.sum(weight * grads, axis=0, keepdims=True)
            for number, slot in enumerate(query_slots):
                dots_ref[row_of(slot, 1, 0, at), :] = lane_cut(dots, number, rows)
                if merge:
                    bundle_ref[row_of(4 + slot, 1, 0, at), :] = lane_cut(dots, number, rows)


def keys_kernel(third, heads, scaling, power, place_ref, lengths_ref, *refs):
    queries, keys, refs = split_refs(refs)
    (*base, shift_ref, mine, sent), refs = (refs[:3], refs[3:]) if third is None else (refs[:4], refs[4:])
    *extra, key_own, key_back, query_own, query_mate, total_ref = refs
    rows, me, step = keys[0][0].shape[1], place_ref[0], place_ref[1]
    plan = [pair_tile(lengths_ref, rows, me)]
    for number, parts in enumerate(group_parts(1, mine, sent, extra)):
        total_ref[number * GROUP : (number + 1) * GROUP, :] = sum(parts)
    outs = {("k", 0): key_own, ("k", 1): key_back, ("q", 0): query_own, ("q", 1): query_mate}
    out = Emitter(outs, {("k", 1): ref for ref in base})
    for head, (tiles, keep) in tiles_ahead(heads, plan, queries, keys, 2):
        at = step * heads + head
        sums = {}
        for (query_slots, key_slots, mask), ((q, _), (k, _), (raw, grads)) in zip(plan, tiles):
            shift = per_query(query_slots, 1, 0, at, shift_ref)
            dots = per_query(query_slots, 1, 0, at, total_ref)
            weight = jnp.where(mask, jnp.exp2((raw - shift) * power), 0.0)
            slope = (weight * (grads - dots) * scaling).astype(jnp.bfloat16)
            add_rows(sums, "k", key_slots, matmul(slope, q * keep, NN), rows)
            add_rows(sums, "q", query_slots, matmul(slope, k, TN), rows)
        for name, value in sums.items():
            out.emit(head, name, value)


def third_kernel(
    third, heads, scaling, power, place_ref, lengths_ref, q_third, o_third, k_back, v_back, value_part,
    stats, even, odd, value_out, key_out, query_out, dots_ref, shift_ref,
):
    rows, me, step = k_back.shape[1], place_ref[0], place_ref[1]
    parts = [stats[...], part_of(even, 2, 0), part_of(odd, 2, 1)]
    shift_ref[...] = merge_stats(scaling, parts)
    slots, keys, mask = third_tile(third, lengths_ref, rows, me)
    queries, keys = (None, None, (q_third, o_third)), (None, (k_back, v_back))
    plan = [(slots, [1], mask)]
    out = Emitter({"v": value_out, "k": key_out, "q": query_out}, {"v": value_part})
    for head, (tiles, keep) in tiles_ahead(heads, plan, queries, keys, 2):
        (q, o), (k, _), (raw, grads) = tiles[0]
        at = step * heads + head
        weight = jnp.where(mask, jnp.exp2((raw - shift_ref[pl.ds(at, 1), :]) * power), 0.0)
        dots = jnp.sum(weight * grads, axis=0, keepdims=True)
        dots_ref[pl.ds(at, 1), :] = dots
        total = dots + even[row_of(4, 1, 0, at), :] + odd[row_of(5, 1, 0, at), :]
        slope = (weight * (grads - total) * scaling).astype(jnp.bfloat16)
        out.emit(head, "v", matmul(weight.astype(jnp.bfloat16), o * keep, NN))
        out.emit(head, "k", matmul(slope, q * keep, NN))
        out.emit(head, "q", matmul(slope, k, TN))


def add_refs(*refs):
    return sum(ref[...].astype(jnp.float32) for ref in refs)


def sums_kernel(key_part, key_sent, *refs):
    *query_parts, key_out, query_out = refs
    key_out[...] = add_refs(key_part, key_sent).astype(jnp.bfloat16)
    query_out[...] = add_refs(*query_parts).astype(jnp.bfloat16)


def halo_program(third, queries, key_vectors, value_vectors, out_grad, facts):
    _, rows, width = queries.shape
    seq_size = lax.axis_size("seq")
    me = lax.axis_index("seq").astype(jnp.int32)
    scaling = HEAD ** (-0.5)
    power = scaling * math.log2(math.e)
    steps = width // HEAD // 4
    part = width // steps
    heads = part // HEAD
    devices = range(seq_size)
    mates = [(s, s ^ 1) for s in devices]
    ring = third is None
    chain = [(s, s + 2) for s in devices if s + 2 < seq_size]
    ahead = [(s, (s + 2) % seq_size) for s in devices] if ring else chain
    behind = [(s, s - 2) for s in devices if s >= 2]
    if not ring:
        relay, to_odd = [(third + 2, third)], [(third, third + 2)]
        from_even, to_even = [(third + 1, third)], [(third, third + 1)]

    def send(value, pairs):
        return lax.ppermute(value, "seq", pairs)

    smem = pl.BlockSpec(memory_space=pltpu.SMEM)
    vmem = pl.BlockSpec(memory_space=pltpu.VMEM)
    wide_shape = jax.ShapeDtypeStruct((1, rows, width), jnp.bfloat16)

    def slim_shape(groups, kinds):
        return jax.ShapeDtypeStruct((groups * kinds * GROUP, rows), jnp.float32)

    def call(kernel, products, wides, slims, outs, slim_outs, plain=False, scratch=(), after=()):
        flops = 2 * products * 4 * rows * rows * width * 3 // 2
        lead = [] if plain else [me[None], facts]
        inputs = len(lead) + len(wides) + len(slims) + len(after)
        columns = {*range(len(lead), len(lead) + len(wides)), *range(inputs, inputs + outs)}

        def body(*refs):
            def half(step, carry):
                cut = pl.ds(pl.multiple_of(step * part, LANES), part)
                views = [ref.at[:, :, cut] if n in columns else ref for n, ref in enumerate(refs)]
                if not plain:
                    views[0] = (refs[0][0], step)
                kernel(*views)
                return carry

            lax.fori_loop(0, steps, half, 0)

        return pl.pallas_call(
            body,
            in_specs=[smem] * len(lead)
            + [vmem] * (len(wides) + len(slims))
            + [pl.BlockSpec(memory_space=pl.ANY)] * len(after),
            out_specs=[vmem] * (outs + len(slim_outs)),
            out_shape=[wide_shape] * outs + [slim_shape(*sizes) for sizes in slim_outs],
            scratch_shapes=[pltpu.VMEM((groups * GROUP, rows), jnp.float32) for groups in scratch],
            compiler_params=pltpu.CompilerParams(vmem_limit_bytes=20 * 1024 * 1024),
            cost_estimate=pl.CostEstimate(
                flops=flops, bytes_accessed=20 * rows * width, transcendentals=0
            ),
        )(*lead, *wides, *[value for _, _, value in slims], *after)

    query_mate = send(queries, mates)
    key_back = send(key_vectors, chain)
    grad_mate = send(out_grad, mates)
    value_back = send(value_vectors, ahead)
    grad_own, value_own, stats = call(
        functools.partial(stats_kernel, heads, power), 1,
        [queries, query_mate, key_vectors, key_back, out_grad, value_vectors], [], 2, [(2, 2)],
    )
    stats_mate = send(stats, mates)
    rows_in = [queries, grad_own, query_mate, grad_mate]
    tensors = rows_in + [key_vectors, value_own, key_back, value_back]
    constants = (heads, scaling, power)
    if ring:
        value_sent, shift = call(
            functools.partial(values_kernel, True, (1,), *constants), 1, rows_in + [key_back],
            [(2, 2, stats), (2, 2, stats_mate)], 1, [(2, 1)],
        )
        (dots,) = call(
            functools.partial(dots_kernel, False, *constants), 2, tensors, [(2, 1, shift)], 0, [(2, 1)]
        )
        dots_in = [(2, 1, shift), (2, 1, dots), (2, 1, send(dots, mates))]
        (value_part,) = call(
            functools.partial(values_kernel, False, (0,), *constants), 1, rows_in + [key_vectors],
            [(2, 1, shift)], 1, [], after=[dots],
        )
        base = []
    else:
        query_third = send(query_mate, relay)
        held, stats_mate = lax.optimization_barrier((grad_mate, stats_mate))
        grad_third = send(held, relay)
        query_third, _ = lax.optimization_barrier((query_third, value_back))
        (third_stats,) = call(
            functools.partial(third_stats_kernel, third, heads, power), 1, [query_third, key_back], [],
            0, [(1, 2)],
        )
        stats_in = [(2, 2, stats), (2, 2, stats_mate)]
        stats_in += [(1, 2, send(third_stats, to_even)), (1, 2, send(third_stats, to_odd))]
        bundle, dots, shift = call(
            functools.partial(dots_kernel, True, *constants), 2, tensors, stats_in, 0,
            [(2, 3), (2, 1), (2, 1)],
        )
        even, odd, dots_mate = send(bundle, from_even), send(bundle, relay), send(dots, mates)
        value_part, value_back_part = call(
            functools.partial(values_kernel, False, (0, 1), *constants), 2, rows_in + [key_vectors, key_back],
            [(2, 1, shift)], 2, [],
        )
        value_back_part, dots_mate = lax.optimization_barrier((value_back_part, dots_mate))
        value_sent, key_third, query_extra, third_dots = call(
            functools.partial(third_kernel, third, *constants), 2,
            [query_third, grad_third, key_back, value_back, value_back_part],
            [(1, 2, third_stats), (2, 3, even), (2, 3, odd)],
            3, [(1, 1)], scratch=[1],
        )
        dots_in = [(2, 1, shift), (2, 1, dots), (2, 1, dots_mate)]
        dots_in += [(1, 1, send(third_dots, to_even)), (1, 1, send(third_dots, to_odd))]
        base = [key_third]
    value_received = send(value_sent, behind)
    key_part, key_sent, query_part, query_sent = call(
        functools.partial(keys_kernel, third, *constants), 4, tensors + base, dots_in, 4, [], scratch=[2],
    )
    key_received = send(key_sent, behind)
    query_received = [send(query_sent, mates)] + ([] if ring else [send(query_extra, to_even)])
    value_ready = (value_part.astype(jnp.float32) + value_received.astype(jnp.float32)).astype(jnp.bfloat16)
    key_ready, query_ready = call(
        sums_kernel, 0, [key_part, key_received, query_part, *query_received], [], 2, [], plain=True
    )
    return query_ready, key_ready, value_ready


def program_kernel(shift, lengths_ref, out_ref):
    start, found = jnp.int32(0), jnp.int32(0)
    for doc in range(lengths_ref.shape[0]):
        end = start + lengths_ref[doc]
        last = (end - 1) >> shift
        spans = (last - (start >> shift) >= 3) & (last & 1 == 0)
        found = jnp.where(spans, (last >> 1) - 1, found)
        out_ref[doc + 1] = lengths_ref[doc]
        start = end
    out_ref[0] = found


def program_facts(rows, doc_lengths):
    smem = pl.BlockSpec(memory_space=pltpu.SMEM)
    return pl.pallas_call(
        functools.partial(program_kernel, rows.bit_length() - 1),
        in_specs=[smem],
        out_specs=smem,
        out_shape=jax.ShapeDtypeStruct((doc_lengths.shape[0] + 1,), jnp.int32),
    )(doc_lengths)


def halo_shards(*arguments):
    *tensors, doc_lengths = arguments
    facts = program_facts(tensors[0].shape[1], doc_lengths)
    thirds = range(3, lax.axis_size("seq") - 2, 2)
    programs = [functools.partial(halo_program, third) for third in (None, *thirds)]
    return lax.switch(facts[0], programs, *tensors, facts)


def shards(queries, key_vectors, value_vectors, out_grad, doc_lengths):
    _, rows, width = queries.shape
    seq_size = lax.axis_size("seq")
    longest = rows * seq_size * 3 // 8
    fits = longest <= 3 * rows and seq_size % 2 == 0 and seq_size > 4 and rows == LANES
    heads = width // HEAD
    plan = halo_shards if fits and heads % 4 == 0 and heads <= GROUP else spread_shards
    return plan(queries, key_vectors, value_vectors, out_grad, doc_lengths)


def solution(mesh):
    return jax.shard_map(
        shards,
        mesh=mesh,
        in_specs=(
            P("section", "seq", "dp"),
            P("section", "seq", "dp"),
            P("section", "seq", "dp"),
            P("section", "seq", "dp"),
            P(),
        ),
        out_specs=(P("section", "seq", "dp"), P("section", "seq", "dp"), P("section", "seq", "dp")),
        check_vma=False,
    )
```

```python
import functools
import math
import jax
import jax.numpy as jnp
from jax import lax
from jax.experimental import pallas as pl
from jax.experimental.pallas import tpu as pltpu
from jax.sharding import PartitionSpec as P

HEAD = 224
LANES = 128
FLOOR = -1e30


def pick_slot(stacked, slot):
    return lax.dynamic_index_in_dim(stacked, slot, 0, keepdims=False)


def put_slot(stacked, update, slot):
    return lax.dynamic_update_index_in_dim(stacked, update, slot, 0)


def spread_shards(queries, key_vectors, value_vectors, out_grad, doc_lengths):
    local_rows = queries.shape[1]
    local_width = queries.shape[2]
    head_count = local_width // HEAD
    seq_size = lax.axis_size("seq")
    group = seq_size // head_count
    scaling = HEAD ** (-0.5)

    def spread(matrix):
        shaped = matrix.reshape(local_rows, head_count, 1, HEAD)
        copies = jnp.broadcast_to(shaped, (local_rows, head_count, group, HEAD))
        return copies.reshape(local_rows, seq_size * HEAD)

    query_head, key_head, value_head, cot_head = (
        lax.all_to_all(spread(queries), "seq", split_axis=1, concat_axis=0, tiled=True),
        lax.all_to_all(spread(key_vectors), "seq", split_axis=1, concat_axis=0, tiled=True),
        lax.all_to_all(spread(value_vectors), "seq", split_axis=1, concat_axis=0, tiled=True),
        lax.all_to_all(spread(out_grad), "seq", split_axis=1, concat_axis=0, tiled=True),
    )
    length = key_head.shape[0]
    member = lax.axis_index("seq") % group
    blocks = 2 * group
    block = length // blocks
    bounds = jnp.cumsum(doc_lengths)
    positions = jnp.arange(length, dtype=jnp.int32)
    doc_index = jnp.sum((positions[:, None] >= bounds[None, :]).astype(jnp.int32), axis=1)
    row_list = [member, blocks - 1 - member]
    query_list = []
    cot_list = []
    pos_list = []
    for which in range(2):
        offset = row_list[which] * block
        query_list.append(lax.dynamic_slice_in_dim(query_head, offset, block, 0))
        cot_list.append(lax.dynamic_slice_in_dim(cot_head, offset, block, 0))
        pos_list.append(offset + jnp.arange(block, dtype=jnp.int32))
    query_stack = jnp.stack(query_list)
    cot_stack = jnp.stack(cot_list)
    pos_stack = jnp.stack(pos_list)
    doc_stack = jnp.take(doc_index, pos_stack)
    plan = []
    for number in range(blocks + 1):
        first = number <= member
        slot = jnp.where(first, 0, 1).astype(jnp.int32)
        col_block = jnp.where(first, number, number - member - 1)
        flag = None
        plan.append((slot, col_block, flag))
    row_max = jnp.full((2, block), -jnp.inf, jnp.float32)
    row_sum = jnp.zeros((2, block), jnp.float32)
    stored = []
    for slot, col_block, flag in plan:

        def score_tile(carry, slot=slot, col_block=col_block):
            maxima, totals = carry
            query_rows = pick_slot(query_stack, slot)
            key_rows = lax.dynamic_slice_in_dim(key_head, col_block * block, block, 0)
            col_docs = lax.dynamic_slice_in_dim(doc_index, col_block * block, block, 0)
            col_positions = col_block * block + jnp.arange(block, dtype=jnp.int32)
            raw = jnp.dot(query_rows, key_rows.T, preferred_element_type=jnp.float32) * scaling
            allowed = (pick_slot(doc_stack, slot)[:, None] == col_docs[None, :]) & (
                pick_slot(pos_stack, slot)[:, None] >= col_positions[None, :]
            )
            scores = jnp.where(allowed, raw, -jnp.inf)
            before = pick_slot(maxima, slot)
            after = jnp.maximum(before, jnp.max(scores, axis=1))
            safe = jnp.where(jnp.isfinite(after), after, 0.0)
            total = pick_slot(totals, slot) * jnp.exp(before - safe) + jnp.sum(
                jnp.exp(scores - safe[:, None]), axis=1
            )
            return (scores, put_slot(maxima, after, slot), put_slot(totals, total, slot))

        scores, row_max, row_sum = score_tile((row_max, row_sum))
        stored.append(scores)

    def tile_weights(scores, slot):
        return (
            jnp.exp(scores - pick_slot(row_max, slot)[:, None]) / pick_slot(row_sum, slot)[:, None]
        )

    summed = jnp.zeros((2, block, HEAD), jnp.float32)
    for (slot, col_block, flag), scores in zip(plan, stored):

        def add_values(carry, slot=slot, col_block=col_block, scores=scores):
            rounded = tile_weights(scores, slot).astype(jnp.bfloat16)
            value_rows = lax.dynamic_slice_in_dim(value_head, col_block * block, block, 0)
            term = jnp.dot(rounded, value_rows, preferred_element_type=jnp.float32)
            return put_slot(carry, pick_slot(carry, slot) + term, slot)

        summed = add_values(summed)
    attended = summed.astype(jnp.bfloat16)
    row_dot = jnp.sum(cot_stack.astype(jnp.float32) * attended.astype(jnp.float32), axis=2)
    query_acc = jnp.zeros((2, block, HEAD), jnp.float32)
    key_acc = jnp.zeros((length, HEAD), jnp.float32)
    value_acc = jnp.zeros((length, HEAD), jnp.float32)
    for (slot, col_block, flag), scores in zip(plan, stored):

        def backward_tile(carry, slot=slot, col_block=col_block, scores=scores):
            query_sum, key_sum, value_sum = carry
            weights = tile_weights(scores, slot)
            rounded = weights.astype(jnp.bfloat16)
            query_rows = pick_slot(query_stack, slot)
            cot_rows = pick_slot(cot_stack, slot)
            start = col_block * block
            key_rows = lax.dynamic_slice_in_dim(key_head, start, block, 0)
            value_rows = lax.dynamic_slice_in_dim(value_head, start, block, 0)
            value_term = jnp.dot(rounded.T, cot_rows, preferred_element_type=jnp.float32)
            prob_grad = jnp.dot(cot_rows, value_rows.T, preferred_element_type=jnp.float32)
            score_grad = (
                weights * (prob_grad - pick_slot(row_dot, slot)[:, None]) * scaling
            ).astype(jnp.bfloat16)
            query_term = jnp.dot(score_grad, key_rows, preferred_element_type=jnp.float32)
            key_term = jnp.dot(score_grad.T, query_rows, preferred_element_type=jnp.float32)
            query_sum = put_slot(query_sum, pick_slot(query_sum, slot) + query_term, slot)
            key_sum = lax.dynamic_update_slice_in_dim(
                key_sum, lax.dynamic_slice_in_dim(key_sum, start, block, 0) + key_term, start, 0
            )
            value_sum = lax.dynamic_update_slice_in_dim(
                value_sum,
                lax.dynamic_slice_in_dim(value_sum, start, block, 0) + value_term,
                start,
                0,
            )
            return (query_sum, key_sum, value_sum)

        query_acc, key_acc, value_acc = backward_tile((query_acc, key_acc, value_acc))
    query_rounded = query_acc.astype(jnp.bfloat16)
    key_back, value_back = (
        lax.all_to_all(key_acc, "seq", split_axis=0, concat_axis=1, tiled=True),
        lax.all_to_all(value_acc, "seq", split_axis=0, concat_axis=1, tiled=True),
    )

    def settle(received):
        shaped = received.astype(jnp.float32).reshape(local_rows, head_count, group, HEAD)
        return jnp.sum(shaped, axis=2).reshape(1, local_rows, local_width).astype(jnp.bfloat16)

    query_full = jnp.zeros((length, HEAD), jnp.bfloat16)
    for which in range(2):
        query_full = lax.dynamic_update_slice_in_dim(
            query_full, query_rounded[which], row_list[which] * block, 0
        )
    query_back = lax.all_to_all(query_full, "seq", split_axis=0, concat_axis=1, tiled=True)
    query_out = settle(query_back)
    return (query_out, settle(key_back), settle(value_back))


NT = ((1,), (1,))
NN = ((1,), (0,))
TN = ((0,), (0,))
GROUP = 8


def head_span(head):
    low = head * HEAD // LANES * LANES
    high = -(-(head + 1) * HEAD // LANES) * LANES
    return low, high


def head_mask(head):
    low, high = head_span(head)
    lane = lax.broadcasted_iota(jnp.int32, (1, high - low), 1) + low
    inside = (lane >= head * HEAD) & (lane < (head + 1) * HEAD)
    return inside.astype(jnp.float32).astype(jnp.bfloat16)


def matmul(left, right, dims):
    return lax.dot_general(left, right, (dims, ((), ())), preferred_element_type=jnp.float32)


def stack(values, axis):
    return values[0] if len(values) == 1 else jnp.concatenate(values, axis=axis)


def allowed(lengths_ref, rows, query_block, key_block):
    shape = (rows, rows)
    position = query_block * rows + lax.broadcasted_iota(jnp.int32, shape, 1)
    keys = key_block * rows + lax.broadcasted_iota(jnp.int32, shape, 0)
    start = jnp.zeros_like(position)
    bound = jnp.int32(0)
    for doc in range(1, lengths_ref.shape[0]):
        bound = bound + lengths_ref[doc]
        start = jnp.where(position >= bound, bound, start)
    return (keys >= start) & (keys <= position)


def make_tile(lengths_ref, rows, queries, keys):
    mask = stack(
        [stack([allowed(lengths_ref, rows, q, k) for _, q in queries], 1) for _, k in keys], 0
    )
    return [slot for slot, _ in queries], [slot for slot, _ in keys], mask


def tile_values(plan, head, queries, keys, products):
    low, high = head_span(head)
    keep = head_mask(head)

    def gather(refs, number, slots):
        return stack([refs[slot][number][0, :, low:high] for slot in slots], 0)

    out = []
    for query_slots, key_slots, _ in plan:
        q = [gather(queries, number, query_slots) for number in range(products)]
        k = [gather(keys, number, key_slots) * keep for number in range(products)]
        out.append((q, k, [matmul(b, a, NT) for a, b in zip(q, k)]))
    return out, keep


def tiles_ahead(heads, plan, queries, keys, products):
    yield from enumerate([tile_values(plan, head, queries, keys, products) for head in range(heads)])


def pair_tile(lengths_ref, rows, me, slots=(0, 1)):
    mate = me + 1 - 2 * lax.rem(me, 2)
    return make_tile(lengths_ref, rows, ((0, me), (1, mate)), [(slot, me - 2 * slot) for slot in slots])


def third_tile(third, lengths_ref, rows, me):
    slots, keys, mask = make_tile(lengths_ref, rows, ((2, me + 1),), ((1, me - 2),))
    return slots, keys, mask & (me == third)


def lane_cut(value, number, rows):
    return value[:, number * rows : (number + 1) * rows]


def row_of(group, kinds, kind, head):
    return pl.ds((group * kinds + kind) * GROUP + head, 1)


def per_query(slots, kinds, kind, head, ref):
    return stack([ref[row_of(slot, kinds, kind, head), :] for slot in slots], 1)


def collect_stats(heads, power, step, plan, queries, keys, rows, out_ref, groups):
    for head, (tiles, _) in tiles_ahead(heads, plan, queries, keys, 1):
        for (query_slots, _, mask), (_, _, (raw,)) in zip(plan, tiles):
            raw = jnp.where(mask, raw, FLOOR)
            top = jnp.max(raw, axis=0, keepdims=True)
            sums = jnp.sum(jnp.exp2((raw - top) * power), axis=0, keepdims=True)
            for number, slot in enumerate(query_slots):
                at = step * heads + head
                out_ref[row_of(groups[slot], 2, 0, at), :] = lane_cut(top, number, rows)
                out_ref[row_of(groups[slot], 2, 1, at), :] = lane_cut(sums, number, rows)


def stats_kernel(
    heads, power, place_ref, lengths_ref, q_own, q_mate, k_own, k_back, o_own, v_own, o_copy, v_copy, out_ref
):
    rows, me, step = k_own.shape[1], place_ref[0], place_ref[1]
    o_copy[...], v_copy[...] = o_own[...], v_own[...]
    plan = [pair_tile(lengths_ref, rows, me)]
    queries, keys = ((q_own,), (q_mate,)), ((k_own,), (k_back,))
    collect_stats(heads, power, step, plan, queries, keys, rows, out_ref, (0, 1))


def third_stats_kernel(third, heads, power, place_ref, lengths_ref, q_third, k_back, out_ref):
    rows, me, step = k_back.shape[1], place_ref[0], place_ref[1]
    plan = [third_tile(third, lengths_ref, rows, me)]
    queries, keys = (None, None, (q_third,)), (None, (k_back,))
    collect_stats(heads, power, step, plan, queries, keys, rows, out_ref, (None, None, 0))


def part_of(ref, kinds, number):
    size = kinds * GROUP
    return ref[number * size : (number + 1) * size, :]


def group_parts(kinds, mine, sent, extra):
    own = [part_of(mine, kinds, 0), part_of(sent, kinds, 1)]
    mate = [part_of(mine, kinds, 1), part_of(sent, kinds, 0)]
    if extra:
        near, far = extra
        own, mate = own + [near[...]], mate + [far[...]]
    return [own, mate]


def merge_groups(scaling, shift_ref, refs):
    mine, sent, *extra = refs
    for number, parts in enumerate(group_parts(2, mine, sent, extra)):
        shift_ref[number * GROUP : (number + 1) * GROUP, :] = merge_stats(scaling, parts)


def merge_stats(scaling, parts):
    split = [(jnp.where(p[GROUP:] > 0, p[:GROUP], FLOOR), p[GROUP:]) for p in parts]
    top = functools.reduce(jnp.maximum, [s[0] for s in split])
    total = sum(jnp.exp((s[0] - top) * scaling) * s[1] for s in split)
    return top + jnp.log(jnp.where(total > 0, total, 1.0)) / scaling


class Emitter:
    def __init__(self, outs, base={}):
        self.outs, self.base, self.carry = outs, base, {}

    def put(self, name, start, stop, value):
        if name in self.base:
            value = value + self.base[name][0, :, start:stop].astype(jnp.float32)
        self.outs[name][0, :, start:stop] = value.astype(jnp.bfloat16)

    def emit(self, head, name, value):
        low, high = head_span(head)
        first, last = head * HEAD % LANES == 0, (head + 1) * HEAD % LANES == 0
        start, stop = low, high
        if not first:
            self.put(name, low, low + LANES, value[:, :LANES] + self.carry.pop(name))
            start = low + LANES
        if not last:
            self.carry[name] = value[:, high - LANES - low :]
            stop = high - LANES
        if stop > start:
            self.put(name, start, stop, value[:, start - low : stop - low])


def add_rows(sums, kind, slots, value, rows):
    for number, slot in enumerate(slots):
        piece = value[number * rows : (number + 1) * rows]
        name = (kind, slot)
        sums[name] = sums[name] + piece if name in sums else piece


def split_refs(refs):
    return ((refs[0:2], refs[2:4]), (refs[4:6], refs[6:8]), refs[8:])


def values_kernel(merge, slots, heads, scaling, power, place_ref, lengths_ref, q0, o0, q1, o1, *refs):
    key_refs, refs = refs[: len(slots)], refs[len(slots) :]
    queries, keys = ((q0, o0), (q1, o1)), {slot: (ref,) for slot, ref in zip(slots, key_refs)}
    if merge:
        *refs, shift_ref = refs
        stats, value_refs = refs[: -len(slots)], refs[-len(slots) :]
        merge_groups(scaling, shift_ref, stats)
    else:
        shift_ref, value_refs = refs[0], refs[-len(slots) :]
    rows, me, step = q0.shape[1], place_ref[0], place_ref[1]
    plan = [pair_tile(lengths_ref, rows, me, slots)]
    out = Emitter({("v", slot): ref for slot, ref in zip(slots, value_refs)})
    weights = []
    for head, (tiles, keep) in tiles_ahead(heads, plan, queries, keys, 1):
        (query_slots, key_slots, mask), (_, _, (raw,)) = plan[0], tiles[0]
        shift = per_query(query_slots, 1, 0, step * heads + head, shift_ref)
        weight = jnp.where(mask, jnp.exp2((raw - shift) * power), 0.0)
        weights.append((weight.astype(jnp.bfloat16), keep))
    for head, (weight, keep) in enumerate(weights):
        low, high = head_span(head)
        o = stack([queries[slot][1][0, :, low:high] for slot in query_slots], 0) * keep
        sums = {}
        add_rows(sums, "v", key_slots, matmul(weight, o, NN), rows)
        for name, value in sums.items():
            out.emit(head, name, value)


def dots_kernel(merge, heads, scaling, power, place_ref, lengths_ref, *refs):
    queries, keys, refs = split_refs(refs)
    if merge:
        *stats, bundle_ref, dots_ref, shift_ref = refs
        merge_groups(scaling, shift_ref, stats)
        bundle_ref[: 4 * GROUP] = stats[0][...]
    else:
        shift_ref, dots_ref = refs
    rows, me, step = keys[0][0].shape[1], place_ref[0], place_ref[1]
    plan = [pair_tile(lengths_ref, rows, me)]
    for head, (tiles, _) in tiles_ahead(heads, plan, queries, keys, 2):
        at = step * heads + head
        for (query_slots, _, mask), (_, _, (raw, grads)) in zip(plan, tiles):
            shift = per_query(query_slots, 1, 0, at, shift_ref)
            weight = jnp.where(mask, jnp.exp2((raw - shift) * power), 0.0)
            dots = jnp.sum(weight * grads, axis=0, keepdims=True)
            for number, slot in enumerate(query_slots):
                dots_ref[row_of(slot, 1, 0, at), :] = lane_cut(dots, number, rows)
                if merge:
                    bundle_ref[row_of(4 + slot, 1, 0, at), :] = lane_cut(dots, number, rows)


def keys_kernel(third, heads, scaling, power, place_ref, lengths_ref, *refs):
    queries, keys, refs = split_refs(refs)
    (*base, shift_ref, mine, sent), refs = (refs[:3], refs[3:]) if third is None else (refs[:4], refs[4:])
    *extra, key_own, key_back, query_own, query_mate, total_ref = refs
    rows, me, step = keys[0][0].shape[1], place_ref[0], place_ref[1]
    plan = [pair_tile(lengths_ref, rows, me)]
    for number, parts in enumerate(group_parts(1, mine, sent, extra)):
        total_ref[number * GROUP : (number + 1) * GROUP, :] = sum(parts)
    outs = {("k", 0): key_own, ("k", 1): key_back, ("q", 0): query_own, ("q", 1): query_mate}
    out = Emitter(outs, {("k", 1): ref for ref in base})
    slopes = []
    for head, (tiles, keep) in tiles_ahead(heads, plan, queries, keys, 2):
        at = step * heads + head
        (query_slots, key_slots, mask), ((q, _), (k, _), (raw, grads)) = plan[0], tiles[0]
        shift = per_query(query_slots, 1, 0, at, shift_ref)
        dots = per_query(query_slots, 1, 0, at, total_ref)
        weight = jnp.where(mask, jnp.exp2((raw - shift) * power), 0.0)
        slope = (weight * (grads - dots) * scaling).astype(jnp.bfloat16)
        slopes.append((slope, q * keep, k))
    for head, (slope, q, k) in enumerate(slopes):
        sums = {}
        add_rows(sums, "k", key_slots, matmul(slope, q, NN), rows)
        add_rows(sums, "q", query_slots, matmul(slope, k, TN), rows)
        for name, value in sums.items():
            out.emit(head, name, value)


def third_kernel(
    third, heads, scaling, power, place_ref, lengths_ref, q_third, o_third, k_back, v_back, value_part,
    stats, even, odd, value_out, key_out, query_out, dots_ref, shift_ref,
):
    rows, me, step = k_back.shape[1], place_ref[0], place_ref[1]
    parts = [stats[...], part_of(even, 2, 0), part_of(odd, 2, 1)]
    shift_ref[...] = merge_stats(scaling, parts)
    slots, keys, mask = third_tile(third, lengths_ref, rows, me)
    queries, keys = (None, None, (q_third, o_third)), (None, (k_back, v_back))
    plan = [(slots, [1], mask)]
    out = Emitter({"v": value_out, "k": key_out, "q": query_out}, {"v": value_part})
    for head, (tiles, keep) in tiles_ahead(heads, plan, queries, keys, 2):
        (q, o), (k, _), (raw, grads) = tiles[0]
        at = step * heads + head
        weight = jnp.where(mask, jnp.exp2((raw - shift_ref[pl.ds(at, 1), :]) * power), 0.0)
        dots = jnp.sum(weight * grads, axis=0, keepdims=True)
        dots_ref[pl.ds(at, 1), :] = dots
        total = dots + even[row_of(4, 1, 0, at), :] + odd[row_of(5, 1, 0, at), :]
        slope = (weight * (grads - total) * scaling).astype(jnp.bfloat16)
        out.emit(head, "v", matmul(weight.astype(jnp.bfloat16), o * keep, NN))
        out.emit(head, "k", matmul(slope, q * keep, NN))
        out.emit(head, "q", matmul(slope, k, TN))


def add_refs(*refs):
    return sum(ref[...].astype(jnp.float32) for ref in refs)


def sums_kernel(key_part, key_sent, *refs):
    *query_parts, key_out, query_out = refs
    key_out[...] = add_refs(key_part, key_sent).astype(jnp.bfloat16)
    query_out[...] = add_refs(*query_parts).astype(jnp.bfloat16)


def halo_program(third, queries, key_vectors, value_vectors, out_grad, facts):
    _, rows, width = queries.shape
    seq_size = lax.axis_size("seq")
    me = lax.axis_index("seq").astype(jnp.int32)
    scaling = HEAD ** (-0.5)
    power = scaling * math.log2(math.e)
    steps = width // HEAD // 4
    part = width // steps
    heads = part // HEAD
    devices = range(seq_size)
    mates = [(s, s ^ 1) for s in devices]
    ring = third is None
    chain = [(s, s + 2) for s in devices if s + 2 < seq_size]
    ahead = [(s, (s + 2) % seq_size) for s in devices] if ring else chain
    behind = [(s, s - 2) for s in devices if s >= 2]
    if not ring:
        relay, to_odd = [(third + 2, third)], [(third, third + 2)]
        from_even, to_even = [(third + 1, third)], [(third, third + 1)]

    def send(value, pairs):
        return lax.ppermute(value, "seq", pairs)

    smem = pl.BlockSpec(memory_space=pltpu.SMEM)
    vmem = pl.BlockSpec(memory_space=pltpu.VMEM)
    wide_shape = jax.ShapeDtypeStruct((1, rows, width), jnp.bfloat16)

    def slim_shape(groups, kinds):
        return jax.ShapeDtypeStruct((groups * kinds * GROUP, rows), jnp.float32)

    def call(kernel, products, wides, slims, outs, slim_outs, plain=False, scratch=(), after=()):
        flops = 2 * products * 4 * rows * rows * width * 3 // 2
        lead = [] if plain else [me[None], facts]
        inputs = len(lead) + len(wides) + len(slims) + len(after)
        columns = {*range(len(lead), len(lead) + len(wides)), *range(inputs, inputs + outs)}

        def body(*refs):
            def half(step, carry):
                cut = pl.ds(pl.multiple_of(step * part, LANES), part)
                views = [ref.at[:, :, cut] if n in columns else ref for n, ref in enumerate(refs)]
                if not plain:
                    views[0] = (refs[0][0], step)
                kernel(*views)
                return carry

            lax.fori_loop(0, steps, half, 0)

        return pl.pallas_call(
            body,
            in_specs=[smem] * len(lead)
            + [vmem] * (len(wides) + len(slims))
            + [pl.BlockSpec(memory_space=pl.ANY)] * len(after),
            out_specs=[vmem] * (outs + len(slim_outs)),
            out_shape=[wide_shape] * outs + [slim_shape(*sizes) for sizes in slim_outs],
            scratch_shapes=[pltpu.VMEM((groups * GROUP, rows), jnp.float32) for groups in scratch],
            compiler_params=pltpu.CompilerParams(vmem_limit_bytes=20 * 1024 * 1024),
            cost_estimate=pl.CostEstimate(
                flops=flops, bytes_accessed=20 * rows * width, transcendentals=0
            ),
        )(*lead, *wides, *[value for _, _, value in slims], *after)

    query_mate = send(queries, mates)
    key_back = send(key_vectors, chain)
    grad_mate = send(out_grad, mates)
    value_back = send(value_vectors, ahead)
    grad_own, value_own, stats = call(
        functools.partial(stats_kernel, heads, power), 1,
        [queries, query_mate, key_vectors, key_back, out_grad, value_vectors], [], 2, [(2, 2)],
    )
    stats_mate = send(stats, mates)
    rows_in = [queries, grad_own, query_mate, grad_mate]
    tensors = rows_in + [key_vectors, value_own, key_back, value_back]
    constants = (heads, scaling, power)
    if ring:
        value_sent, shift = call(
            functools.partial(values_kernel, True, (1,), *constants), 1, rows_in + [key_back],
            [(2, 2, stats), (2, 2, stats_mate)], 1, [(2, 1)],
        )
        (dots,) = call(
            functools.partial(dots_kernel, False, *constants), 2, tensors, [(2, 1, shift)], 0, [(2, 1)]
        )
        dots_in = [(2, 1, shift), (2, 1, dots), (2, 1, send(dots, mates))]
        (value_part,) = call(
            functools.partial(values_kernel, False, (0,), *constants), 1, rows_in + [key_vectors],
            [(2, 1, shift)], 1, [], after=[dots],
        )
        base = []
    else:
        query_third = send(query_mate, relay)
        held, stats_mate = lax.optimization_barrier((grad_mate, stats_mate))
        grad_third = send(held, relay)
        query_third, _ = lax.optimization_barrier((query_third, value_back))
        (third_stats,) = call(
            functools.partial(third_stats_kernel, third, heads, power), 1, [query_third, key_back], [],
            0, [(1, 2)],
        )
        stats_in = [(2, 2, stats), (2, 2, stats_mate)]
        stats_in += [(1, 2, send(third_stats, to_even)), (1, 2, send(third_stats, to_odd))]
        bundle, dots, shift = call(
            functools.partial(dots_kernel, True, *constants), 2, tensors, stats_in, 0,
            [(2, 3), (2, 1), (2, 1)],
        )
        even, odd, dots_mate = send(bundle, from_even), send(bundle, relay), send(dots, mates)
        value_part, value_back_part = call(
            functools.partial(values_kernel, False, (0, 1), *constants), 2, rows_in + [key_vectors, key_back],
            [(2, 1, shift)], 2, [],
        )
        value_back_part, dots_mate = lax.optimization_barrier((value_back_part, dots_mate))
        value_sent, key_third, query_extra, third_dots = call(
            functools.partial(third_kernel, third, *constants), 2,
            [query_third, grad_third, key_back, value_back, value_back_part],
            [(1, 2, third_stats), (2, 3, even), (2, 3, odd)],
            3, [(1, 1)], scratch=[1],
        )
        dots_in = [(2, 1, shift), (2, 1, dots), (2, 1, dots_mate)]
        dots_in += [(1, 1, send(third_dots, to_even)), (1, 1, send(third_dots, to_odd))]
        base = [key_third]
    value_received = send(value_sent, behind)
    key_part, key_sent, query_part, query_sent = call(
        functools.partial(keys_kernel, third, *constants), 4, tensors + base, dots_in, 4, [], scratch=[2],
    )
    key_received = send(key_sent, behind)
    query_received = [send(query_sent, mates)] + ([] if ring else [send(query_extra, to_even)])
    value_ready = (value_part.astype(jnp.float32) + value_received.astype(jnp.float32)).astype(jnp.bfloat16)
    key_ready, query_ready = call(
        sums_kernel, 0, [key_part, key_received, query_part, *query_received], [], 2, [], plain=True
    )
    return query_ready, key_ready, value_ready


def program_kernel(shift, lengths_ref, out_ref):
    start, found = jnp.int32(0), jnp.int32(0)
    for doc in range(lengths_ref.shape[0]):
        end = start + lengths_ref[doc]
        last = (end - 1) >> shift
        spans = (last - (start >> shift) >= 3) & (last & 1 == 0)
        found = jnp.where(spans, (last >> 1) - 1, found)
        out_ref[doc + 1] = lengths_ref[doc]
        start = end
    out_ref[0] = found


def program_facts(rows, doc_lengths):
    smem = pl.BlockSpec(memory_space=pltpu.SMEM)
    return pl.pallas_call(
        functools.partial(program_kernel, rows.bit_length() - 1),
        in_specs=[smem],
        out_specs=smem,
        out_shape=jax.ShapeDtypeStruct((doc_lengths.shape[0] + 1,), jnp.int32),
    )(doc_lengths)


def halo_shards(*arguments):
    *tensors, doc_lengths = arguments
    facts = program_facts(tensors[0].shape[1], doc_lengths)
    thirds = range(3, lax.axis_size("seq") - 2, 2)
    programs = [functools.partial(halo_program, third) for third in (None, *thirds)]
    return lax.switch(facts[0], programs, *tensors, facts)


def shards(queries, key_vectors, value_vectors, out_grad, doc_lengths):
    _, rows, width = queries.shape
    seq_size = lax.axis_size("seq")
    longest = rows * seq_size * 3 // 8
    fits = longest <= 3 * rows and seq_size % 2 == 0 and seq_size > 4 and rows == LANES
    heads = width // HEAD
    plan = halo_shards if fits and heads % 4 == 0 and heads <= GROUP else spread_shards
    return plan(queries, key_vectors, value_vectors, out_grad, doc_lengths)


def solution(mesh):
    return jax.shard_map(
        shards,
        mesh=mesh,
        in_specs=(
            P("section", "seq", "dp"),
            P("section", "seq", "dp"),
            P("section", "seq", "dp"),
            P("section", "seq", "dp"),
            P(),
        ),
        out_specs=(P("section", "seq", "dp"), P("section", "seq", "dp"), P("section", "seq", "dp")),
        check_vma=False,
    )
```

```python
import functools
import math
import jax
import jax.numpy as jnp
from jax import lax
from jax.experimental import pallas as pl
from jax.experimental.pallas import tpu as pltpu
from jax.sharding import PartitionSpec as P

HEAD = 224
LANES = 128
FLOOR = -1e30


def pick_slot(stacked, slot):
    return lax.dynamic_index_in_dim(stacked, slot, 0, keepdims=False)


def put_slot(stacked, update, slot):
    return lax.dynamic_update_index_in_dim(stacked, update, slot, 0)


def spread_shards(queries, key_vectors, value_vectors, out_grad, doc_lengths):
    local_rows = queries.shape[1]
    local_width = queries.shape[2]
    head_count = local_width // HEAD
    seq_size = lax.axis_size("seq")
    group = seq_size // head_count
    scaling = HEAD ** (-0.5)

    def spread(matrix):
        shaped = matrix.reshape(local_rows, head_count, 1, HEAD)
        copies = jnp.broadcast_to(shaped, (local_rows, head_count, group, HEAD))
        return copies.reshape(local_rows, seq_size * HEAD)

    query_head, key_head, value_head, cot_head = (
        lax.all_to_all(spread(queries), "seq", split_axis=1, concat_axis=0, tiled=True),
        lax.all_to_all(spread(key_vectors), "seq", split_axis=1, concat_axis=0, tiled=True),
        lax.all_to_all(spread(value_vectors), "seq", split_axis=1, concat_axis=0, tiled=True),
        lax.all_to_all(spread(out_grad), "seq", split_axis=1, concat_axis=0, tiled=True),
    )
    length = key_head.shape[0]
    member = lax.axis_index("seq") % group
    blocks = 2 * group
    block = length // blocks
    bounds = jnp.cumsum(doc_lengths)
    positions = jnp.arange(length, dtype=jnp.int32)
    doc_index = jnp.sum((positions[:, None] >= bounds[None, :]).astype(jnp.int32), axis=1)
    row_list = [member, blocks - 1 - member]
    query_list = []
    cot_list = []
    pos_list = []
    for which in range(2):
        offset = row_list[which] * block
        query_list.append(lax.dynamic_slice_in_dim(query_head, offset, block, 0))
        cot_list.append(lax.dynamic_slice_in_dim(cot_head, offset, block, 0))
        pos_list.append(offset + jnp.arange(block, dtype=jnp.int32))
    query_stack = jnp.stack(query_list)
    cot_stack = jnp.stack(cot_list)
    pos_stack = jnp.stack(pos_list)
    doc_stack = jnp.take(doc_index, pos_stack)
    plan = []
    for number in range(blocks + 1):
        first = number <= member
        slot = jnp.where(first, 0, 1).astype(jnp.int32)
        col_block = jnp.where(first, number, number - member - 1)
        flag = None
        plan.append((slot, col_block, flag))
    row_max = jnp.full((2, block), -jnp.inf, jnp.float32)
    row_sum = jnp.zeros((2, block), jnp.float32)
    stored = []
    for slot, col_block, flag in plan:

        def score_tile(carry, slot=slot, col_block=col_block):
            maxima, totals = carry
            query_rows = pick_slot(query_stack, slot)
            key_rows = lax.dynamic_slice_in_dim(key_head, col_block * block, block, 0)
            col_docs = lax.dynamic_slice_in_dim(doc_index, col_block * block, block, 0)
            col_positions = col_block * block + jnp.arange(block, dtype=jnp.int32)
            raw = jnp.dot(query_rows, key_rows.T, preferred_element_type=jnp.float32) * scaling
            allowed = (pick_slot(doc_stack, slot)[:, None] == col_docs[None, :]) & (
                pick_slot(pos_stack, slot)[:, None] >= col_positions[None, :]
            )
            scores = jnp.where(allowed, raw, -jnp.inf)
            before = pick_slot(maxima, slot)
            after = jnp.maximum(before, jnp.max(scores, axis=1))
            safe = jnp.where(jnp.isfinite(after), after, 0.0)
            total = pick_slot(totals, slot) * jnp.exp(before - safe) + jnp.sum(
                jnp.exp(scores - safe[:, None]), axis=1
            )
            return (scores, put_slot(maxima, after, slot), put_slot(totals, total, slot))

        scores, row_max, row_sum = score_tile((row_max, row_sum))
        stored.append(scores)

    def tile_weights(scores, slot):
        return (
            jnp.exp(scores - pick_slot(row_max, slot)[:, None]) / pick_slot(row_sum, slot)[:, None]
        )

    summed = jnp.zeros((2, block, HEAD), jnp.float32)
    for (slot, col_block, flag), scores in zip(plan, stored):

        def add_values(carry, slot=slot, col_block=col_block, scores=scores):
            rounded = tile_weights(scores, slot).astype(jnp.bfloat16)
            value_rows = lax.dynamic_slice_in_dim(value_head, col_block * block, block, 0)
            term = jnp.dot(rounded, value_rows, preferred_element_type=jnp.float32)
            return put_slot(carry, pick_slot(carry, slot) + term, slot)

        summed = add_values(summed)
    attended = summed.astype(jnp.bfloat16)
    row_dot = jnp.sum(cot_stack.astype(jnp.float32) * attended.astype(jnp.float32), axis=2)
    query_acc = jnp.zeros((2, block, HEAD), jnp.float32)
    key_acc = jnp.zeros((length, HEAD), jnp.float32)
    value_acc = jnp.zeros((length, HEAD), jnp.float32)
    for (slot, col_block, flag), scores in zip(plan, stored):

        def backward_tile(carry, slot=slot, col_block=col_block, scores=scores):
            query_sum, key_sum, value_sum = carry
            weights = tile_weights(scores, slot)
            rounded = weights.astype(jnp.bfloat16)
            query_rows = pick_slot(query_stack, slot)
            cot_rows = pick_slot(cot_stack, slot)
            start = col_block * block
            key_rows = lax.dynamic_slice_in_dim(key_head, start, block, 0)
            value_rows = lax.dynamic_slice_in_dim(value_head, start, block, 0)
            value_term = jnp.dot(rounded.T, cot_rows, preferred_element_type=jnp.float32)
            prob_grad = jnp.dot(cot_rows, value_rows.T, preferred_element_type=jnp.float32)
            score_grad = (
                weights * (prob_grad - pick_slot(row_dot, slot)[:, None]) * scaling
            ).astype(jnp.bfloat16)
            query_term = jnp.dot(score_grad, key_rows, preferred_element_type=jnp.float32)
            key_term = jnp.dot(score_grad.T, query_rows, preferred_element_type=jnp.float32)
            query_sum = put_slot(query_sum, pick_slot(query_sum, slot) + query_term, slot)
            key_sum = lax.dynamic_update_slice_in_dim(
                key_sum, lax.dynamic_slice_in_dim(key_sum, start, block, 0) + key_term, start, 0
            )
            value_sum = lax.dynamic_update_slice_in_dim(
                value_sum,
                lax.dynamic_slice_in_dim(value_sum, start, block, 0) + value_term,
                start,
                0,
            )
            return (query_sum, key_sum, value_sum)

        query_acc, key_acc, value_acc = backward_tile((query_acc, key_acc, value_acc))
    query_rounded = query_acc.astype(jnp.bfloat16)
    key_back, value_back = (
        lax.all_to_all(key_acc, "seq", split_axis=0, concat_axis=1, tiled=True),
        lax.all_to_all(value_acc, "seq", split_axis=0, concat_axis=1, tiled=True),
    )

    def settle(received):
        shaped = received.astype(jnp.float32).reshape(local_rows, head_count, group, HEAD)
        return jnp.sum(shaped, axis=2).reshape(1, local_rows, local_width).astype(jnp.bfloat16)

    query_full = jnp.zeros((length, HEAD), jnp.bfloat16)
    for which in range(2):
        query_full = lax.dynamic_update_slice_in_dim(
            query_full, query_rounded[which], row_list[which] * block, 0
        )
    query_back = lax.all_to_all(query_full, "seq", split_axis=0, concat_axis=1, tiled=True)
    query_out = settle(query_back)
    return (query_out, settle(key_back), settle(value_back))


NT = ((1,), (1,))
NN = ((1,), (0,))
TN = ((0,), (0,))
GROUP = 8


def head_span(head):
    low = head * HEAD // LANES * LANES
    high = -(-(head + 1) * HEAD // LANES) * LANES
    return low, high


def head_mask(head):
    low, high = head_span(head)
    lane = lax.broadcasted_iota(jnp.int32, (1, high - low), 1) + low
    inside = (lane >= head * HEAD) & (lane < (head + 1) * HEAD)
    return inside.astype(jnp.float32).astype(jnp.bfloat16)


def matmul(left, right, dims):
    return lax.dot_general(left, right, (dims, ((), ())), preferred_element_type=jnp.float32)


def stack(values, axis):
    return values[0] if len(values) == 1 else jnp.concatenate(values, axis=axis)


def allowed(lengths_ref, rows, query_block, key_block):
    position = query_block * rows + lax.broadcasted_iota(jnp.int32, (1, rows), 1)
    keys = key_block * rows + lax.broadcasted_iota(jnp.int32, (rows, rows), 0)
    start = jnp.zeros_like(position)
    bound = jnp.int32(0)
    for doc in range(1, lengths_ref.shape[0]):
        bound = bound + lengths_ref[doc]
        start = jnp.where(position >= bound, bound, start)
    return (keys >= start) & (keys <= position)


def make_tile(lengths_ref, rows, queries, keys):
    mask = stack(
        [stack([allowed(lengths_ref, rows, q, k) for _, q in queries], 1) for _, k in keys], 0
    )
    return [slot for slot, _ in queries], [slot for slot, _ in keys], mask


def tile_values(plan, head, queries, keys, products):
    low, high = head_span(head)
    keep = head_mask(head)

    def gather(refs, number, slots):
        return stack([refs[slot][number][0, :, low:high] for slot in slots], 0)

    out = []
    for query_slots, key_slots, _ in plan:
        q = [gather(queries, number, query_slots) for number in range(products)]
        k = [gather(keys, number, key_slots) * keep for number in range(products)]
        out.append((q, k, [matmul(b, a, NT) for a, b in zip(q, k)]))
    return out, keep


def tiles_ahead(heads, plan, queries, keys, products):
    yield from enumerate([tile_values(plan, head, queries, keys, products) for head in range(heads)])


def pair_tile(lengths_ref, rows, me, slots=(0, 1)):
    mate = me + 1 - 2 * lax.rem(me, 2)
    return make_tile(lengths_ref, rows, ((0, me), (1, mate)), [(slot, me - 2 * slot) for slot in slots])


def third_tile(third, lengths_ref, rows, me):
    slots, keys, mask = make_tile(lengths_ref, rows, ((2, me + 1),), ((1, me - 2),))
    return slots, keys, mask & (me == third)


def lane_cut(value, number, rows):
    return value[:, number * rows : (number + 1) * rows]


def row_of(group, kinds, kind, head):
    return pl.ds((group * kinds + kind) * GROUP + head, 1)


def per_query(slots, kinds, kind, head, ref):
    return stack([ref[row_of(slot, kinds, kind, head), :] for slot in slots], 1)


def collect_stats(heads, power, step, plan, queries, keys, rows, out_ref, groups):
    for head, (tiles, _) in tiles_ahead(heads, plan, queries, keys, 1):
        for (query_slots, _, mask), (_, _, (raw,)) in zip(plan, tiles):
            raw = jnp.where(mask, raw, FLOOR)
            top = jnp.max(raw, axis=0, keepdims=True)
            sums = jnp.sum(jnp.exp2((raw - top) * power), axis=0, keepdims=True)
            for number, slot in enumerate(query_slots):
                at = step * heads + head
                out_ref[row_of(groups[slot], 2, 0, at), :] = lane_cut(top, number, rows)
                out_ref[row_of(groups[slot], 2, 1, at), :] = lane_cut(sums, number, rows)


def stats_kernel(
    heads, power, place_ref, lengths_ref, q_own, q_mate, k_own, k_back, o_own, v_own, o_copy, v_copy, out_ref
):
    rows, me, step = k_own.shape[1], place_ref[0], place_ref[1]
    o_copy[...], v_copy[...] = o_own[...], v_own[...]
    plan = [pair_tile(lengths_ref, rows, me)]
    queries, keys = ((q_own,), (q_mate,)), ((k_own,), (k_back,))
    collect_stats(heads, power, step, plan, queries, keys, rows, out_ref, (0, 1))


def third_stats_kernel(third, heads, power, place_ref, lengths_ref, q_third, k_back, out_ref):
    rows, me, step = k_back.shape[1], place_ref[0], place_ref[1]
    plan = [third_tile(third, lengths_ref, rows, me)]
    queries, keys = (None, None, (q_third,)), (None, (k_back,))
    collect_stats(heads, power, step, plan, queries, keys, rows, out_ref, (None, None, 0))


def part_of(ref, kinds, number):
    size = kinds * GROUP
    return ref[number * size : (number + 1) * size, :]


def group_parts(kinds, mine, sent, extra):
    own = [part_of(mine, kinds, 0), part_of(sent, kinds, 1)]
    mate = [part_of(mine, kinds, 1), part_of(sent, kinds, 0)]
    if extra:
        near, far = extra
        own, mate = own + [near[...]], mate + [far[...]]
    return [own, mate]


def merge_groups(scaling, shift_ref, refs):
    mine, sent, *extra = refs
    for number, parts in enumerate(group_parts(2, mine, sent, extra)):
        shift_ref[number * GROUP : (number + 1) * GROUP, :] = merge_stats(scaling, parts)


def merge_stats(scaling, parts):
    split = [(jnp.where(p[GROUP:] > 0, p[:GROUP], FLOOR), p[GROUP:]) for p in parts]
    top = functools.reduce(jnp.maximum, [s[0] for s in split])
    total = sum(jnp.exp((s[0] - top) * scaling) * s[1] for s in split)
    return top + jnp.log(jnp.where(total > 0, total, 1.0)) / scaling


class Emitter:
    def __init__(self, outs, base={}):
        self.outs, self.base, self.carry = outs, base, {}

    def put(self, name, start, stop, value):
        if name in self.base:
            value = value + self.base[name][0, :, start:stop].astype(jnp.float32)
        self.outs[name][0, :, start:stop] = value.astype(jnp.bfloat16)

    def emit(self, head, name, value):
        low, high = head_span(head)
        first, last = head * HEAD % LANES == 0, (head + 1) * HEAD % LANES == 0
        start, stop = low, high
        if not first:
            self.put(name, low, low + LANES, value[:, :LANES] + self.carry.pop(name))
            start = low + LANES
        if not last:
            self.carry[name] = value[:, high - LANES - low :]
            stop = high - LANES
        if stop > start:
            self.put(name, start, stop, value[:, start - low : stop - low])


def add_rows(sums, kind, slots, value, rows):
    for number, slot in enumerate(slots):
        piece = value[number * rows : (number + 1) * rows]
        name = (kind, slot)
        sums[name] = sums[name] + piece if name in sums else piece


def split_refs(refs):
    return ((refs[0:2], refs[2:4]), (refs[4:6], refs[6:8]), refs[8:])


def values_kernel(merge, slots, heads, scaling, power, place_ref, lengths_ref, q0, o0, q1, o1, *refs):
    key_refs, refs = refs[: len(slots)], refs[len(slots) :]
    queries, keys = ((q0, o0), (q1, o1)), {slot: (ref,) for slot, ref in zip(slots, key_refs)}
    if merge:
        *refs, shift_ref = refs
        stats, value_refs = refs[: -len(slots)], refs[-len(slots) :]
        merge_groups(scaling, shift_ref, stats)
    else:
        shift_ref, value_refs = refs[0], refs[-len(slots) :]
    rows, me, step = q0.shape[1], place_ref[0], place_ref[1]
    plan = [pair_tile(lengths_ref, rows, me, slots)]
    out = Emitter({("v", slot): ref for slot, ref in zip(slots, value_refs)})
    weights = []
    for head, (tiles, keep) in tiles_ahead(heads, plan, queries, keys, 1):
        (query_slots, key_slots, mask), (_, _, (raw,)) = plan[0], tiles[0]
        shift = per_query(query_slots, 1, 0, step * heads + head, shift_ref)
        weight = jnp.where(mask, jnp.exp2((raw - shift) * power), 0.0)
        weights.append((weight.astype(jnp.bfloat16), keep))
    for head, (weight, keep) in enumerate(weights):
        low, high = head_span(head)
        o = stack([queries[slot][1][0, :, low:high] for slot in query_slots], 0) * keep
        sums = {}
        add_rows(sums, "v", key_slots, matmul(weight, o, NN), rows)
        for name, value in sums.items():
            out.emit(head, name, value)


def dots_kernel(merge, heads, scaling, power, place_ref, lengths_ref, *refs):
    queries, keys, refs = split_refs(refs)
    if merge:
        *stats, bundle_ref, dots_ref, shift_ref = refs
        merge_groups(scaling, shift_ref, stats)
        bundle_ref[: 4 * GROUP] = stats[0][...]
    else:
        shift_ref, dots_ref = refs
    rows, me, step = keys[0][0].shape[1], place_ref[0], place_ref[1]
    plan = [pair_tile(lengths_ref, rows, me)]
    for head, (tiles, _) in tiles_ahead(heads, plan, queries, keys, 2):
        at = step * heads + head
        for (query_slots, _, mask), (_, _, (raw, grads)) in zip(plan, tiles):
            shift = per_query(query_slots, 1, 0, at, shift_ref)
            weight = jnp.where(mask, jnp.exp2((raw - shift) * power), 0.0)
            dots = jnp.sum(weight * grads, axis=0, keepdims=True)
            for number, slot in enumerate(query_slots):
                dots_ref[row_of(slot, 1, 0, at), :] = lane_cut(dots, number, rows)
                if merge:
                    bundle_ref[row_of(4 + slot, 1, 0, at), :] = lane_cut(dots, number, rows)


def keys_kernel(third, heads, scaling, power, place_ref, lengths_ref, *refs):
    queries, keys, refs = split_refs(refs)
    (*base, shift_ref, mine, sent), refs = (refs[:3], refs[3:]) if third is None else (refs[:4], refs[4:])
    *extra, key_own, key_back, query_own, query_mate, total_ref = refs
    rows, me, step = keys[0][0].shape[1], place_ref[0], place_ref[1]
    plan = [pair_tile(lengths_ref, rows, me)]
    for number, parts in enumerate(group_parts(1, mine, sent, extra)):
        total_ref[number * GROUP : (number + 1) * GROUP, :] = sum(parts)
    outs = {("k", 0): key_own, ("k", 1): key_back, ("q", 0): query_own, ("q", 1): query_mate}
    out = Emitter(outs, {("k", 1): ref for ref in base})
    slopes = []
    for head, (tiles, keep) in tiles_ahead(heads, plan, queries, keys, 2):
        at = step * heads + head
        (query_slots, key_slots, mask), ((q, _), (k, _), (raw, grads)) = plan[0], tiles[0]
        shift = per_query(query_slots, 1, 0, at, shift_ref)
        dots = per_query(query_slots, 1, 0, at, total_ref)
        weight = jnp.where(mask, jnp.exp2((raw - shift) * power), 0.0)
        slope = (weight * (grads - dots) * scaling).astype(jnp.bfloat16)
        slopes.append((slope, q * keep, k))
    for head, (slope, q, k) in enumerate(slopes):
        sums = {}
        add_rows(sums, "k", key_slots, matmul(slope, q, NN), rows)
        add_rows(sums, "q", query_slots, matmul(slope, k, TN), rows)
        for name, value in sums.items():
            out.emit(head, name, value)


def third_kernel(
    third, heads, scaling, power, place_ref, lengths_ref, q_third, o_third, k_back, v_back, value_part,
    stats, even, odd, value_out, key_out, query_out, dots_ref, shift_ref,
):
    rows, me, step = k_back.shape[1], place_ref[0], place_ref[1]
    parts = [stats[...], part_of(even, 2, 0), part_of(odd, 2, 1)]
    shift_ref[...] = merge_stats(scaling, parts)
    slots, keys, mask = third_tile(third, lengths_ref, rows, me)
    queries, keys = (None, None, (q_third, o_third)), (None, (k_back, v_back))
    plan = [(slots, [1], mask)]
    out = Emitter({"v": value_out, "k": key_out, "q": query_out}, {"v": value_part})
    for head, (tiles, keep) in tiles_ahead(heads, plan, queries, keys, 2):
        (q, o), (k, _), (raw, grads) = tiles[0]
        at = step * heads + head
        weight = jnp.where(mask, jnp.exp2((raw - shift_ref[pl.ds(at, 1), :]) * power), 0.0)
        dots = jnp.sum(weight * grads, axis=0, keepdims=True)
        dots_ref[pl.ds(at, 1), :] = dots
        total = dots + even[row_of(4, 1, 0, at), :] + odd[row_of(5, 1, 0, at), :]
        slope = (weight * (grads - total) * scaling).astype(jnp.bfloat16)
        out.emit(head, "v", matmul(weight.astype(jnp.bfloat16), o * keep, NN))
        out.emit(head, "k", matmul(slope, q * keep, NN))
        out.emit(head, "q", matmul(slope, k, TN))


def add_refs(*refs):
    return sum(ref[...].astype(jnp.float32) for ref in refs)


def sums_kernel(key_part, key_sent, *refs):
    *query_parts, key_out, query_out = refs
    key_out[...] = add_refs(key_part, key_sent).astype(jnp.bfloat16)
    query_out[...] = add_refs(*query_parts).astype(jnp.bfloat16)


def halo_program(third, queries, key_vectors, value_vectors, out_grad, facts):
    _, rows, width = queries.shape
    seq_size = lax.axis_size("seq")
    me = lax.axis_index("seq").astype(jnp.int32)
    scaling = HEAD ** (-0.5)
    power = scaling * math.log2(math.e)
    steps = width // HEAD // 4
    part = width // steps
    heads = part // HEAD
    devices = range(seq_size)
    mates = [(s, s ^ 1) for s in devices]
    ring = third is None
    chain = [(s, s + 2) for s in devices if s + 2 < seq_size]
    ahead = [(s, (s + 2) % seq_size) for s in devices] if ring else chain
    behind = [(s, s - 2) for s in devices if s >= 2]
    if not ring:
        relay, to_odd = [(third + 2, third)], [(third, third + 2)]
        from_even, to_even = [(third + 1, third)], [(third, third + 1)]

    def send(value, pairs):
        return lax.ppermute(value, "seq", pairs)

    smem = pl.BlockSpec(memory_space=pltpu.SMEM)
    vmem = pl.BlockSpec(memory_space=pltpu.VMEM)
    wide_shape = jax.ShapeDtypeStruct((1, rows, width), jnp.bfloat16)

    def slim_shape(groups, kinds):
        return jax.ShapeDtypeStruct((groups * kinds * GROUP, rows), jnp.float32)

    def call(kernel, products, wides, slims, outs, slim_outs, plain=False, scratch=(), after=()):
        flops = 2 * products * 4 * rows * rows * width * 3 // 2
        lead = [] if plain else [me[None], facts]
        inputs = len(lead) + len(wides) + len(slims) + len(after)
        columns = {*range(len(lead), len(lead) + len(wides)), *range(inputs, inputs + outs)}

        def body(*refs):
            def half(step, carry):
                cut = pl.ds(pl.multiple_of(step * part, LANES), part)
                views = [ref.at[:, :, cut] if n in columns else ref for n, ref in enumerate(refs)]
                if not plain:
                    views[0] = (refs[0][0], step)
                kernel(*views)
                return carry

            lax.fori_loop(0, steps, half, 0)

        return pl.pallas_call(
            body,
            in_specs=[smem] * len(lead)
            + [vmem] * (len(wides) + len(slims))
            + [pl.BlockSpec(memory_space=pl.ANY)] * len(after),
            out_specs=[vmem] * (outs + len(slim_outs)),
            out_shape=[wide_shape] * outs + [slim_shape(*sizes) for sizes in slim_outs],
            scratch_shapes=[pltpu.VMEM((groups * GROUP, rows), jnp.float32) for groups in scratch],
            compiler_params=pltpu.CompilerParams(vmem_limit_bytes=20 * 1024 * 1024),
            cost_estimate=pl.CostEstimate(
                flops=flops, bytes_accessed=20 * rows * width, transcendentals=0
            ),
        )(*lead, *wides, *[value for _, _, value in slims], *after)

    query_mate = send(queries, mates)
    key_back = send(key_vectors, chain)
    grad_mate = send(out_grad, mates)
    value_back = send(value_vectors, ahead)
    grad_own, value_own, stats = call(
        functools.partial(stats_kernel, heads, power), 1,
        [queries, query_mate, key_vectors, key_back, out_grad, value_vectors], [], 2, [(2, 2)],
    )
    stats_mate = send(stats, mates)
    rows_in = [queries, grad_own, query_mate, grad_mate]
    tensors = rows_in + [key_vectors, value_own, key_back, value_back]
    constants = (heads, scaling, power)
    if ring:
        value_sent, shift = call(
            functools.partial(values_kernel, True, (1,), *constants), 1, rows_in + [key_back],
            [(2, 2, stats), (2, 2, stats_mate)], 1, [(2, 1)],
        )
        (dots,) = call(
            functools.partial(dots_kernel, False, *constants), 2, tensors, [(2, 1, shift)], 0, [(2, 1)]
        )
        dots_in = [(2, 1, shift), (2, 1, dots), (2, 1, send(dots, mates))]
        (value_part,) = call(
            functools.partial(values_kernel, False, (0,), *constants), 1, rows_in + [key_vectors],
            [(2, 1, shift)], 1, [], after=[dots],
        )
        base = []
    else:
        query_third = send(query_mate, relay)
        held, stats_mate = lax.optimization_barrier((grad_mate, stats_mate))
        grad_third = send(held, relay)
        query_third, _ = lax.optimization_barrier((query_third, value_back))
        (third_stats,) = call(
            functools.partial(third_stats_kernel, third, heads, power), 1, [query_third, key_back], [],
            0, [(1, 2)],
        )
        stats_in = [(2, 2, stats), (2, 2, stats_mate)]
        stats_in += [(1, 2, send(third_stats, to_even)), (1, 2, send(third_stats, to_odd))]
        bundle, dots, shift = call(
            functools.partial(dots_kernel, True, *constants), 2, tensors, stats_in, 0,
            [(2, 3), (2, 1), (2, 1)],
        )
        even, odd, dots_mate = send(bundle, from_even), send(bundle, relay), send(dots, mates)
        value_part, value_back_part = call(
            functools.partial(values_kernel, False, (0, 1), *constants), 2, rows_in + [key_vectors, key_back],
            [(2, 1, shift)], 2, [],
        )
        value_back_part, dots_mate = lax.optimization_barrier((value_back_part, dots_mate))
        value_sent, key_third, query_extra, third_dots = call(
            functools.partial(third_kernel, third, *constants), 2,
            [query_third, grad_third, key_back, value_back, value_back_part],
            [(1, 2, third_stats), (2, 3, even), (2, 3, odd)],
            3, [(1, 1)], scratch=[1],
        )
        dots_in = [(2, 1, shift), (2, 1, dots), (2, 1, dots_mate)]
        dots_in += [(1, 1, send(third_dots, to_even)), (1, 1, send(third_dots, to_odd))]
        base = [key_third]
    value_received = send(value_sent, behind)
    key_part, key_sent, query_part, query_sent = call(
        functools.partial(keys_kernel, third, *constants), 4, tensors + base, dots_in, 4, [], scratch=[2],
    )
    key_received = send(key_sent, behind)
    query_received = [send(query_sent, mates)] + ([] if ring else [send(query_extra, to_even)])
    value_ready = (value_part.astype(jnp.float32) + value_received.astype(jnp.float32)).astype(jnp.bfloat16)
    key_ready, query_ready = call(
        sums_kernel, 0, [key_part, key_received, query_part, *query_received], [], 2, [], plain=True
    )
    return query_ready, key_ready, value_ready


def program_kernel(shift, lengths_ref, out_ref):
    start, found = jnp.int32(0), jnp.int32(0)
    for doc in range(lengths_ref.shape[0]):
        end = start + lengths_ref[doc]
        last = (end - 1) >> shift
        spans = (last - (start >> shift) >= 3) & (last & 1 == 0)
        found = jnp.where(spans, (last >> 1) - 1, found)
        out_ref[doc + 1] = lengths_ref[doc]
        start = end
    out_ref[0] = found


def program_facts(rows, doc_lengths):
    smem = pl.BlockSpec(memory_space=pltpu.SMEM)
    return pl.pallas_call(
        functools.partial(program_kernel, rows.bit_length() - 1),
        in_specs=[smem],
        out_specs=smem,
        out_shape=jax.ShapeDtypeStruct((doc_lengths.shape[0] + 1,), jnp.int32),
    )(doc_lengths)


def halo_shards(*arguments):
    *tensors, doc_lengths = arguments
    facts = program_facts(tensors[0].shape[1], doc_lengths)
    thirds = range(3, lax.axis_size("seq") - 2, 2)
    programs = [functools.partial(halo_program, third) for third in (None, *thirds)]
    return lax.switch(facts[0], programs, *tensors, facts)


def shards(queries, key_vectors, value_vectors, out_grad, doc_lengths):
    _, rows, width = queries.shape
    seq_size = lax.axis_size("seq")
    longest = rows * seq_size * 3 // 8
    fits = longest <= 3 * rows and seq_size % 2 == 0 and seq_size > 4 and rows == LANES
    heads = width // HEAD
    plan = halo_shards if fits and heads % 4 == 0 and heads <= GROUP else spread_shards
    return plan(queries, key_vectors, value_vectors, out_grad, doc_lengths)


def solution(mesh):
    return jax.shard_map(
        shards,
        mesh=mesh,
        in_specs=(
            P("section", "seq", "dp"),
            P("section", "seq", "dp"),
            P("section", "seq", "dp"),
            P("section", "seq", "dp"),
            P(),
        ),
        out_specs=(P("section", "seq", "dp"), P("section", "seq", "dp"), P("section", "seq", "dp")),
        check_vma=False,
    )
```

```python
import functools
import math
import jax
import jax.numpy as jnp
from jax import lax
from jax.experimental import pallas as pl
from jax.experimental.pallas import tpu as pltpu
from jax.sharding import PartitionSpec as P

HEAD = 224
LANES = 128
FLOOR = -1e30


def pick_slot(stacked, slot):
    return lax.dynamic_index_in_dim(stacked, slot, 0, keepdims=False)


def put_slot(stacked, update, slot):
    return lax.dynamic_update_index_in_dim(stacked, update, slot, 0)


def spread_shards(queries, key_vectors, value_vectors, out_grad, doc_lengths):
    local_rows = queries.shape[1]
    local_width = queries.shape[2]
    head_count = local_width // HEAD
    seq_size = lax.axis_size("seq")
    group = seq_size // head_count
    scaling = HEAD ** (-0.5)

    def spread(matrix):
        shaped = matrix.reshape(local_rows, head_count, 1, HEAD)
        copies = jnp.broadcast_to(shaped, (local_rows, head_count, group, HEAD))
        return copies.reshape(local_rows, seq_size * HEAD)

    query_head, key_head, value_head, cot_head = (
        lax.all_to_all(spread(queries), "seq", split_axis=1, concat_axis=0, tiled=True),
        lax.all_to_all(spread(key_vectors), "seq", split_axis=1, concat_axis=0, tiled=True),
        lax.all_to_all(spread(value_vectors), "seq", split_axis=1, concat_axis=0, tiled=True),
        lax.all_to_all(spread(out_grad), "seq", split_axis=1, concat_axis=0, tiled=True),
    )
    length = key_head.shape[0]
    member = lax.axis_index("seq") % group
    blocks = 2 * group
    block = length // blocks
    bounds = jnp.cumsum(doc_lengths)
    positions = jnp.arange(length, dtype=jnp.int32)
    doc_index = jnp.sum((positions[:, None] >= bounds[None, :]).astype(jnp.int32), axis=1)
    row_list = [member, blocks - 1 - member]
    query_list = []
    cot_list = []
    pos_list = []
    for which in range(2):
        offset = row_list[which] * block
        query_list.append(lax.dynamic_slice_in_dim(query_head, offset, block, 0))
        cot_list.append(lax.dynamic_slice_in_dim(cot_head, offset, block, 0))
        pos_list.append(offset + jnp.arange(block, dtype=jnp.int32))
    query_stack = jnp.stack(query_list)
    cot_stack = jnp.stack(cot_list)
    pos_stack = jnp.stack(pos_list)
    doc_stack = jnp.take(doc_index, pos_stack)
    plan = []
    for number in range(blocks + 1):
        first = number <= member
        slot = jnp.where(first, 0, 1).astype(jnp.int32)
        col_block = jnp.where(first, number, number - member - 1)
        flag = None
        plan.append((slot, col_block, flag))
    row_max = jnp.full((2, block), -jnp.inf, jnp.float32)
    row_sum = jnp.zeros((2, block), jnp.float32)
    stored = []
    for slot, col_block, flag in plan:

        def score_tile(carry, slot=slot, col_block=col_block):
            maxima, totals = carry
            query_rows = pick_slot(query_stack, slot)
            key_rows = lax.dynamic_slice_in_dim(key_head, col_block * block, block, 0)
            col_docs = lax.dynamic_slice_in_dim(doc_index, col_block * block, block, 0)
            col_positions = col_block * block + jnp.arange(block, dtype=jnp.int32)
            raw = jnp.dot(query_rows, key_rows.T, preferred_element_type=jnp.float32) * scaling
            allowed = (pick_slot(doc_stack, slot)[:, None] == col_docs[None, :]) & (
                pick_slot(pos_stack, slot)[:, None] >= col_positions[None, :]
            )
            scores = jnp.where(allowed, raw, -jnp.inf)
            before = pick_slot(maxima, slot)
            after = jnp.maximum(before, jnp.max(scores, axis=1))
            safe = jnp.where(jnp.isfinite(after), after, 0.0)
            total = pick_slot(totals, slot) * jnp.exp(before - safe) + jnp.sum(
                jnp.exp(scores - safe[:, None]), axis=1
            )
            return (scores, put_slot(maxima, after, slot), put_slot(totals, total, slot))

        scores, row_max, row_sum = score_tile((row_max, row_sum))
        stored.append(scores)

    def tile_weights(scores, slot):
        return (
            jnp.exp(scores - pick_slot(row_max, slot)[:, None]) / pick_slot(row_sum, slot)[:, None]
        )

    summed = jnp.zeros((2, block, HEAD), jnp.float32)
    for (slot, col_block, flag), scores in zip(plan, stored):

        def add_values(carry, slot=slot, col_block=col_block, scores=scores):
            rounded = tile_weights(scores, slot).astype(jnp.bfloat16)
            value_rows = lax.dynamic_slice_in_dim(value_head, col_block * block, block, 0)
            term = jnp.dot(rounded, value_rows, preferred_element_type=jnp.float32)
            return put_slot(carry, pick_slot(carry, slot) + term, slot)

        summed = add_values(summed)
    attended = summed.astype(jnp.bfloat16)
    row_dot = jnp.sum(cot_stack.astype(jnp.float32) * attended.astype(jnp.float32), axis=2)
    query_acc = jnp.zeros((2, block, HEAD), jnp.float32)
    key_acc = jnp.zeros((length, HEAD), jnp.float32)
    value_acc = jnp.zeros((length, HEAD), jnp.float32)
    for (slot, col_block, flag), scores in zip(plan, stored):

        def backward_tile(carry, slot=slot, col_block=col_block, scores=scores):
            query_sum, key_sum, value_sum = carry
            weights = tile_weights(scores, slot)
            rounded = weights.astype(jnp.bfloat16)
            query_rows = pick_slot(query_stack, slot)
            cot_rows = pick_slot(cot_stack, slot)
            start = col_block * block
            key_rows = lax.dynamic_slice_in_dim(key_head, start, block, 0)
            value_rows = lax.dynamic_slice_in_dim(value_head, start, block, 0)
            value_term = jnp.dot(rounded.T, cot_rows, preferred_element_type=jnp.float32)
            prob_grad = jnp.dot(cot_rows, value_rows.T, preferred_element_type=jnp.float32)
            score_grad = (
                weights * (prob_grad - pick_slot(row_dot, slot)[:, None]) * scaling
            ).astype(jnp.bfloat16)
            query_term = jnp.dot(score_grad, key_rows, preferred_element_type=jnp.float32)
            key_term = jnp.dot(score_grad.T, query_rows, preferred_element_type=jnp.float32)
            query_sum = put_slot(query_sum, pick_slot(query_sum, slot) + query_term, slot)
            key_sum = lax.dynamic_update_slice_in_dim(
                key_sum, lax.dynamic_slice_in_dim(key_sum, start, block, 0) + key_term, start, 0
            )
            value_sum = lax.dynamic_update_slice_in_dim(
                value_sum,
                lax.dynamic_slice_in_dim(value_sum, start, block, 0) + value_term,
                start,
                0,
            )
            return (query_sum, key_sum, value_sum)

        query_acc, key_acc, value_acc = backward_tile((query_acc, key_acc, value_acc))
    query_rounded = query_acc.astype(jnp.bfloat16)
    key_back, value_back = (
        lax.all_to_all(key_acc, "seq", split_axis=0, concat_axis=1, tiled=True),
        lax.all_to_all(value_acc, "seq", split_axis=0, concat_axis=1, tiled=True),
    )

    def settle(received):
        shaped = received.astype(jnp.float32).reshape(local_rows, head_count, group, HEAD)
        return jnp.sum(shaped, axis=2).reshape(1, local_rows, local_width).astype(jnp.bfloat16)

    query_full = jnp.zeros((length, HEAD), jnp.bfloat16)
    for which in range(2):
        query_full = lax.dynamic_update_slice_in_dim(
            query_full, query_rounded[which], row_list[which] * block, 0
        )
    query_back = lax.all_to_all(query_full, "seq", split_axis=0, concat_axis=1, tiled=True)
    query_out = settle(query_back)
    return (query_out, settle(key_back), settle(value_back))


NT = ((1,), (1,))
NN = ((1,), (0,))
TN = ((0,), (0,))
GROUP = 8


def head_span(head):
    low = head * HEAD // LANES * LANES
    high = -(-(head + 1) * HEAD // LANES) * LANES
    return low, high


def head_mask(head):
    low, high = head_span(head)
    lane = lax.broadcasted_iota(jnp.int32, (1, high - low), 1) + low
    inside = (lane >= head * HEAD) & (lane < (head + 1) * HEAD)
    return inside.astype(jnp.float32).astype(jnp.bfloat16)


def matmul(left, right, dims):
    return lax.dot_general(left, right, (dims, ((), ())), preferred_element_type=jnp.float32)


def stack(values, axis):
    return values[0] if len(values) == 1 else jnp.concatenate(values, axis=axis)


def allowed(lengths_ref, rows, query_block, key_block):
    position = query_block * rows + lax.broadcasted_iota(jnp.int32, (1, rows), 1)
    keys = key_block * rows + lax.broadcasted_iota(jnp.int32, (rows, rows), 0)
    start = jnp.zeros_like(position)
    bound = jnp.int32(0)
    for doc in range(1, lengths_ref.shape[0]):
        bound = bound + lengths_ref[doc]
        start = jnp.where(position >= bound, bound, start)
    return (keys >= start) & (keys <= position)


def make_tile(lengths_ref, rows, queries, keys):
    mask = stack(
        [stack([allowed(lengths_ref, rows, q, k) for _, q in queries], 1) for _, k in keys], 0
    )
    return [slot for slot, _ in queries], [slot for slot, _ in keys], mask


def tile_values(plan, head, queries, keys, products):
    low, high = head_span(head)
    keep = head_mask(head)

    def gather(refs, number, slots):
        return stack([refs[slot][number][0, :, low:high] for slot in slots], 0)

    out = []
    for query_slots, key_slots, _ in plan:
        q = [gather(queries, number, query_slots) for number in range(products)]
        k = [gather(keys, number, key_slots) * keep for number in range(products)]
        out.append((q, k, [matmul(b, a, NT) for a, b in zip(q, k)]))
    return out, keep


def tiles_ahead(heads, plan, queries, keys, products):
    yield from enumerate([tile_values(plan, head, queries, keys, products) for head in range(heads)])


def pair_tile(lengths_ref, rows, me, slots=(0, 1)):
    mate = me + 1 - 2 * lax.rem(me, 2)
    return make_tile(lengths_ref, rows, ((0, me), (1, mate)), [(slot, me - 2 * slot) for slot in slots])


def third_tile(third, lengths_ref, rows, me):
    slots, keys, mask = make_tile(lengths_ref, rows, ((2, me + 1),), ((1, me - 2),))
    return slots, keys, mask & (me == third)


def lane_cut(value, number, rows):
    return value[:, number * rows : (number + 1) * rows]


def row_of(group, kinds, kind, head):
    return pl.ds((group * kinds + kind) * GROUP + head, 1)


def per_query(slots, kinds, kind, head, ref):
    return stack([ref[row_of(slot, kinds, kind, head), :] for slot in slots], 1)


def collect_stats(heads, power, step, plan, queries, keys, rows, out_ref, groups):
    for head, (tiles, _) in tiles_ahead(heads, plan, queries, keys, 1):
        for (query_slots, _, mask), (_, _, (raw,)) in zip(plan, tiles):
            raw = jnp.where(mask, raw, FLOOR)
            top = jnp.max(raw, axis=0, keepdims=True)
            sums = jnp.sum(jnp.exp2((raw - top) * power), axis=0, keepdims=True)
            for number, slot in enumerate(query_slots):
                at = step * heads + head
                out_ref[row_of(groups[slot], 2, 0, at), :] = lane_cut(top, number, rows)
                out_ref[row_of(groups[slot], 2, 1, at), :] = lane_cut(sums, number, rows)


def stats_kernel(
    heads, power, place_ref, lengths_ref, q_own, q_mate, k_own, k_back, o_own, v_own, o_copy, v_copy, out_ref
):
    rows, me, step = k_own.shape[1], place_ref[0], place_ref[1]
    o_copy[...], v_copy[...] = o_own[...], v_own[...]
    plan = [pair_tile(lengths_ref, rows, me)]
    queries, keys = ((q_own,), (q_mate,)), ((k_own,), (k_back,))
    collect_stats(heads, power, step, plan, queries, keys, rows, out_ref, (0, 1))


def third_stats_kernel(third, heads, power, place_ref, lengths_ref, q_third, k_back, out_ref):
    rows, me, step = k_back.shape[1], place_ref[0], place_ref[1]
    plan = [third_tile(third, lengths_ref, rows, me)]
    queries, keys = (None, None, (q_third,)), (None, (k_back,))
    collect_stats(heads, power, step, plan, queries, keys, rows, out_ref, (None, None, 0))


def part_of(ref, kinds, number):
    size = kinds * GROUP
    return ref[number * size : (number + 1) * size, :]


def group_parts(kinds, mine, sent, extra):
    own = [part_of(mine, kinds, 0), part_of(sent, kinds, 1)]
    mate = [part_of(mine, kinds, 1), part_of(sent, kinds, 0)]
    if extra:
        near, far = extra
        own, mate = own + [near[...]], mate + [far[...]]
    return [own, mate]


def merge_groups(scaling, shift_ref, refs):
    mine, sent, *extra = refs
    for number, parts in enumerate(group_parts(2, mine, sent, extra)):
        shift_ref[number * GROUP : (number + 1) * GROUP, :] = merge_stats(scaling, parts)


def merge_stats(scaling, parts):
    split = [(jnp.where(p[GROUP:] > 0, p[:GROUP], FLOOR), p[GROUP:]) for p in parts]
    top = functools.reduce(jnp.maximum, [s[0] for s in split])
    total = sum(jnp.exp((s[0] - top) * scaling) * s[1] for s in split)
    return top + jnp.log(jnp.where(total > 0, total, 1.0)) / scaling


class Emitter:
    def __init__(self, outs, base={}):
        self.outs, self.base, self.carry = outs, base, {}

    def put(self, name, start, stop, value):
        if name in self.base:
            value = value + self.base[name][0, :, start:stop].astype(jnp.float32)
        self.outs[name][0, :, start:stop] = value.astype(jnp.bfloat16)

    def emit(self, head, name, value):
        low, high = head_span(head)
        first, last = head * HEAD % LANES == 0, (head + 1) * HEAD % LANES == 0
        start, stop = low, high
        if not first:
            self.put(name, low, low + LANES, value[:, :LANES] + self.carry.pop(name))
            start = low + LANES
        if not last:
            self.carry[name] = value[:, high - LANES - low :]
            stop = high - LANES
        if stop > start:
            self.put(name, start, stop, value[:, start - low : stop - low])


def add_rows(sums, kind, slots, value, rows):
    for number, slot in enumerate(slots):
        piece = value[number * rows : (number + 1) * rows]
        name = (kind, slot)
        sums[name] = sums[name] + piece if name in sums else piece


def split_refs(refs):
    return ((refs[0:2], refs[2:4]), (refs[4:6], refs[6:8]), refs[8:])


def values_kernel(merge, slots, heads, scaling, power, place_ref, lengths_ref, q0, o0, q1, o1, *refs):
    key_refs, refs = refs[: len(slots)], refs[len(slots) :]
    queries, keys = ((q0, o0), (q1, o1)), {slot: (ref,) for slot, ref in zip(slots, key_refs)}
    if merge:
        *refs, shift_ref = refs
        stats, value_refs = refs[: -len(slots)], refs[-len(slots) :]
        merge_groups(scaling, shift_ref, stats)
    else:
        shift_ref, value_refs = refs[0], refs[-len(slots) :]
    rows, me, step = q0.shape[1], place_ref[0], place_ref[1]
    plan = [pair_tile(lengths_ref, rows, me, slots)]
    out = Emitter({("v", slot): ref for slot, ref in zip(slots, value_refs)})
    weights = []
    for head, (tiles, keep) in tiles_ahead(heads, plan, queries, keys, 1):
        (query_slots, key_slots, mask), (_, _, (raw,)) = plan[0], tiles[0]
        shift = per_query(query_slots, 1, 0, step * heads + head, shift_ref)
        weight = jnp.where(mask, jnp.exp2((raw - shift) * power), 0.0)
        weights.append((weight.astype(jnp.bfloat16), keep))
    for head, (weight, keep) in enumerate(weights):
        low, high = head_span(head)
        o = stack([queries[slot][1][0, :, low:high] for slot in query_slots], 0) * keep
        sums = {}
        add_rows(sums, "v", key_slots, matmul(weight, o, NN), rows)
        for name, value in sums.items():
            out.emit(head, name, value)


def dots_kernel(merge, heads, scaling, power, place_ref, lengths_ref, *refs):
    queries, keys, refs = split_refs(refs)
    if merge:
        *stats, bundle_ref, dots_ref, shift_ref = refs
        merge_groups(scaling, shift_ref, stats)
        bundle_ref[: 4 * GROUP] = stats[0][...]
    else:
        shift_ref, dots_ref = refs
    rows, me, step = keys[0][0].shape[1], place_ref[0], place_ref[1]
    plan = [pair_tile(lengths_ref, rows, me)]
    for head, (tiles, _) in tiles_ahead(heads, plan, queries, keys, 2):
        at = step * heads + head
        for (query_slots, _, mask), (_, _, (raw, grads)) in zip(plan, tiles):
            shift = per_query(query_slots, 1, 0, at, shift_ref)
            weight = jnp.where(mask, jnp.exp2((raw - shift) * power), 0.0)
            dots = jnp.sum(weight * grads, axis=0, keepdims=True)
            for number, slot in enumerate(query_slots):
                dots_ref[row_of(slot, 1, 0, at), :] = lane_cut(dots, number, rows)
                if merge:
                    bundle_ref[row_of(4 + slot, 1, 0, at), :] = lane_cut(dots, number, rows)


def keys_kernel(third, heads, scaling, power, place_ref, lengths_ref, *refs):
    queries, keys, refs = split_refs(refs)
    (*base, shift_ref, mine, sent), refs = (refs[:3], refs[3:]) if third is None else (refs[:4], refs[4:])
    *extra, key_own, key_back, query_own, query_mate, total_ref = refs
    rows, me, step = keys[0][0].shape[1], place_ref[0], place_ref[1]
    plan = [pair_tile(lengths_ref, rows, me)]
    for number, parts in enumerate(group_parts(1, mine, sent, extra)):
        total_ref[number * GROUP : (number + 1) * GROUP, :] = sum(parts)
    outs = {("k", 0): key_own, ("k", 1): key_back, ("q", 0): query_own, ("q", 1): query_mate}
    out = Emitter(outs, {("k", 1): ref for ref in base})
    slopes = []
    for head, (tiles, keep) in tiles_ahead(heads, plan, queries, keys, 2):
        at = step * heads + head
        (query_slots, key_slots, mask), ((q, _), (k, _), (raw, grads)) = plan[0], tiles[0]
        shift = per_query(query_slots, 1, 0, at, shift_ref)
        dots = per_query(query_slots, 1, 0, at, total_ref)
        weight = jnp.where(mask, jnp.exp2((raw - shift) * power), 0.0)
        slope = (weight * (grads - dots) * scaling).astype(jnp.bfloat16)
        slopes.append((slope, q * keep, k))
    for head, (slope, q, k) in enumerate(slopes):
        sums = {}
        add_rows(sums, "k", key_slots, matmul(slope, q, NN), rows)
        add_rows(sums, "q", query_slots, matmul(slope, k, TN), rows)
        for name, value in sums.items():
            out.emit(head, name, value)


def third_kernel(
    third, heads, scaling, power, place_ref, lengths_ref, q_third, o_third, k_back, v_back, value_part,
    stats, even, odd, value_out, key_out, query_out, dots_ref, shift_ref,
):
    rows, me, step = k_back.shape[1], place_ref[0], place_ref[1]
    parts = [stats[...], part_of(even, 2, 0), part_of(odd, 2, 1)]
    shift_ref[...] = merge_stats(scaling, parts)
    slots, keys, mask = third_tile(third, lengths_ref, rows, me)
    queries, keys = (None, None, (q_third, o_third)), (None, (k_back, v_back))
    plan = [(slots, [1], mask)]
    out = Emitter({"v": value_out, "k": key_out, "q": query_out}, {"v": value_part})
    for head, (tiles, keep) in tiles_ahead(heads, plan, queries, keys, 2):
        (q, o), (k, _), (raw, grads) = tiles[0]
        at = step * heads + head
        weight = jnp.where(mask, jnp.exp2((raw - shift_ref[pl.ds(at, 1), :]) * power), 0.0)
        dots = jnp.sum(weight * grads, axis=0, keepdims=True)
        dots_ref[pl.ds(at, 1), :] = dots
        total = dots + even[row_of(4, 1, 0, at), :] + odd[row_of(5, 1, 0, at), :]
        slope = (weight * (grads - total) * scaling).astype(jnp.bfloat16)
        out.emit(head, "v", matmul(weight.astype(jnp.bfloat16), o * keep, NN))
        out.emit(head, "k", matmul(slope, q * keep, NN))
        out.emit(head, "q", matmul(slope, k, TN))


def add_refs(*refs):
    return sum(ref[...].astype(jnp.float32) for ref in refs)


def sums_kernel(key_part, key_sent, *refs):
    *query_parts, key_out, query_out = refs
    key_out[...] = add_refs(key_part, key_sent).astype(jnp.bfloat16)
    query_out[...] = add_refs(*query_parts).astype(jnp.bfloat16)


def halo_program(third, queries, key_vectors, value_vectors, out_grad, facts):
    _, rows, width = queries.shape
    seq_size = lax.axis_size("seq")
    me = lax.axis_index("seq").astype(jnp.int32)
    scaling = HEAD ** (-0.5)
    power = scaling * math.log2(math.e)
    steps = width // HEAD // 4
    part = width // steps
    heads = part // HEAD
    devices = range(seq_size)
    mates = [(s, s ^ 1) for s in devices]
    ring = third is None
    chain = [(s, s + 2) for s in devices if s + 2 < seq_size]
    ahead = [(s, (s + 2) % seq_size) for s in devices] if ring else chain
    behind = [(s, s - 2) for s in devices if s >= 2]
    if not ring:
        relay, to_odd = [(third + 2, third)], [(third, third + 2)]
        from_even, to_even = [(third + 1, third)], [(third, third + 1)]

    def send(value, pairs):
        return lax.ppermute(value, "seq", pairs)

    smem = pl.BlockSpec(memory_space=pltpu.SMEM)
    vmem = pl.BlockSpec(memory_space=pltpu.VMEM)
    wide_shape = jax.ShapeDtypeStruct((1, rows, width), jnp.bfloat16)

    def slim_shape(groups, kinds):
        return jax.ShapeDtypeStruct((groups * kinds * GROUP, rows), jnp.float32)

    def call(kernel, products, wides, slims, outs, slim_outs, plain=False, scratch=(), after=()):
        flops = 2 * products * 4 * rows * rows * width * 3 // 2
        lead = [] if plain else [me[None], facts]
        inputs = len(lead) + len(wides) + len(slims) + len(after)
        columns = {*range(len(lead), len(lead) + len(wides)), *range(inputs, inputs + outs)}

        def body(*refs):
            def half(step, carry):
                start = step * part
                cut = pl.ds(start if ring else pl.multiple_of(start, LANES), part)
                views = [ref.at[:, :, cut] if n in columns else ref for n, ref in enumerate(refs)]
                if not plain:
                    views[0] = (refs[0][0], step)
                kernel(*views)
                return carry

            if ring:
                for step in range(steps):
                    half(step, 0)
            else:
                lax.fori_loop(0, steps, half, 0)

        return pl.pallas_call(
            body,
            in_specs=[smem] * len(lead)
            + [vmem] * (len(wides) + len(slims))
            + [pl.BlockSpec(memory_space=pl.ANY)] * len(after),
            out_specs=[vmem] * (outs + len(slim_outs)),
            out_shape=[wide_shape] * outs + [slim_shape(*sizes) for sizes in slim_outs],
            scratch_shapes=[pltpu.VMEM((groups * GROUP, rows), jnp.float32) for groups in scratch],
            compiler_params=pltpu.CompilerParams(vmem_limit_bytes=20 * 1024 * 1024),
            cost_estimate=pl.CostEstimate(
                flops=flops, bytes_accessed=20 * rows * width, transcendentals=0
            ),
        )(*lead, *wides, *[value for _, _, value in slims], *after)

    query_mate = send(queries, mates)
    key_back = send(key_vectors, chain)
    grad_mate = send(out_grad, mates)
    value_back = send(value_vectors, ahead)
    grad_own, value_own, stats = call(
        functools.partial(stats_kernel, heads, power), 1,
        [queries, query_mate, key_vectors, key_back, out_grad, value_vectors], [], 2, [(2, 2)],
    )
    stats_mate = send(stats, mates)
    rows_in = [queries, grad_own, query_mate, grad_mate]
    tensors = rows_in + [key_vectors, value_own, key_back, value_back]
    constants = (heads, scaling, power)
    if ring:
        value_sent, shift = call(
            functools.partial(values_kernel, True, (1,), *constants), 1, rows_in + [key_back],
            [(2, 2, stats), (2, 2, stats_mate)], 1, [(2, 1)],
        )
        (dots,) = call(
            functools.partial(dots_kernel, False, *constants), 2, tensors, [(2, 1, shift)], 0, [(2, 1)]
        )
        dots_in = [(2, 1, shift), (2, 1, dots), (2, 1, send(dots, mates))]
        (value_part,) = call(
            functools.partial(values_kernel, False, (0,), *constants), 1, rows_in + [key_vectors],
            [(2, 1, shift)], 1, [], after=[dots],
        )
        base = []
    else:
        query_third = send(query_mate, relay)
        held, stats_mate = lax.optimization_barrier((grad_mate, stats_mate))
        grad_third = send(held, relay)
        query_third, _ = lax.optimization_barrier((query_third, value_back))
        (third_stats,) = call(
            functools.partial(third_stats_kernel, third, heads, power), 1, [query_third, key_back], [],
            0, [(1, 2)],
        )
        stats_in = [(2, 2, stats), (2, 2, stats_mate)]
        stats_in += [(1, 2, send(third_stats, to_even)), (1, 2, send(third_stats, to_odd))]
        bundle, dots, shift = call(
            functools.partial(dots_kernel, True, *constants), 2, tensors, stats_in, 0,
            [(2, 3), (2, 1), (2, 1)],
        )
        even, odd, dots_mate = send(bundle, from_even), send(bundle, relay), send(dots, mates)
        value_part, value_back_part = call(
            functools.partial(values_kernel, False, (0, 1), *constants), 2, rows_in + [key_vectors, key_back],
            [(2, 1, shift)], 2, [],
        )
        value_back_part, dots_mate = lax.optimization_barrier((value_back_part, dots_mate))
        value_sent, key_third, query_extra, third_dots = call(
            functools.partial(third_kernel, third, *constants), 2,
            [query_third, grad_third, key_back, value_back, value_back_part],
            [(1, 2, third_stats), (2, 3, even), (2, 3, odd)],
            3, [(1, 1)], scratch=[1],
        )
        dots_in = [(2, 1, shift), (2, 1, dots), (2, 1, dots_mate)]
        dots_in += [(1, 1, send(third_dots, to_even)), (1, 1, send(third_dots, to_odd))]
        base = [key_third]
    value_received = send(value_sent, behind)
    key_part, key_sent, query_part, query_sent = call(
        functools.partial(keys_kernel, third, *constants), 4, tensors + base, dots_in, 4, [], scratch=[2],
    )
    key_received = send(key_sent, behind)
    query_received = [send(query_sent, mates)] + ([] if ring else [send(query_extra, to_even)])
    value_ready = (value_part.astype(jnp.float32) + value_received.astype(jnp.float32)).astype(jnp.bfloat16)
    key_ready, query_ready = call(
        sums_kernel, 0, [key_part, key_received, query_part, *query_received], [], 2, [], plain=True
    )
    return query_ready, key_ready, value_ready


def program_kernel(shift, lengths_ref, out_ref):
    start, found = jnp.int32(0), jnp.int32(0)
    for doc in range(lengths_ref.shape[0]):
        end = start + lengths_ref[doc]
        last = (end - 1) >> shift
        spans = (last - (start >> shift) >= 3) & (last & 1 == 0)
        found = jnp.where(spans, (last >> 1) - 1, found)
        out_ref[doc + 1] = lengths_ref[doc]
        start = end
    out_ref[0] = found


def program_facts(rows, doc_lengths):
    smem = pl.BlockSpec(memory_space=pltpu.SMEM)
    return pl.pallas_call(
        functools.partial(program_kernel, rows.bit_length() - 1),
        in_specs=[smem],
        out_specs=smem,
        out_shape=jax.ShapeDtypeStruct((doc_lengths.shape[0] + 1,), jnp.int32),
    )(doc_lengths)


def halo_shards(*arguments):
    *tensors, doc_lengths = arguments
    facts = program_facts(tensors[0].shape[1], doc_lengths)
    thirds = range(3, lax.axis_size("seq") - 2, 2)
    programs = [functools.partial(halo_program, third) for third in (None, *thirds)]
    return lax.switch(facts[0], programs, *tensors, facts)


def shards(queries, key_vectors, value_vectors, out_grad, doc_lengths):
    _, rows, width = queries.shape
    seq_size = lax.axis_size("seq")
    longest = rows * seq_size * 3 // 8
    fits = longest <= 3 * rows and seq_size % 2 == 0 and seq_size > 4 and rows == LANES
    heads = width // HEAD
    plan = halo_shards if fits and heads % 4 == 0 and heads <= GROUP else spread_shards
    return plan(queries, key_vectors, value_vectors, out_grad, doc_lengths)


def solution(mesh):
    return jax.shard_map(
        shards,
        mesh=mesh,
        in_specs=(
            P("section", "seq", "dp"),
            P("section", "seq", "dp"),
            P("section", "seq", "dp"),
            P("section", "seq", "dp"),
            P(),
        ),
        out_specs=(P("section", "seq", "dp"), P("section", "seq", "dp"), P("section", "seq", "dp")),
        check_vma=False,
    )
```

```python
import functools
import math
import jax
import jax.numpy as jnp
from jax import lax
from jax.experimental import pallas as pl
from jax.experimental.pallas import tpu as pltpu
from jax.sharding import PartitionSpec as P

HEAD = 224
LANES = 128
FLOOR = -1e30


def pick_slot(stacked, slot):
    return lax.dynamic_index_in_dim(stacked, slot, 0, keepdims=False)


def put_slot(stacked, update, slot):
    return lax.dynamic_update_index_in_dim(stacked, update, slot, 0)


def spread_shards(queries, key_vectors, value_vectors, out_grad, doc_lengths):
    local_rows = queries.shape[1]
    local_width = queries.shape[2]
    head_count = local_width // HEAD
    seq_size = lax.axis_size("seq")
    group = seq_size // head_count
    scaling = HEAD ** (-0.5)

    def spread(matrix):
        shaped = matrix.reshape(local_rows, head_count, 1, HEAD)
        copies = jnp.broadcast_to(shaped, (local_rows, head_count, group, HEAD))
        return copies.reshape(local_rows, seq_size * HEAD)

    query_head, key_head, value_head, cot_head = (
        lax.all_to_all(spread(queries), "seq", split_axis=1, concat_axis=0, tiled=True),
        lax.all_to_all(spread(key_vectors), "seq", split_axis=1, concat_axis=0, tiled=True),
        lax.all_to_all(spread(value_vectors), "seq", split_axis=1, concat_axis=0, tiled=True),
        lax.all_to_all(spread(out_grad), "seq", split_axis=1, concat_axis=0, tiled=True),
    )
    length = key_head.shape[0]
    member = lax.axis_index("seq") % group
    blocks = 2 * group
    block = length // blocks
    bounds = jnp.cumsum(doc_lengths)
    positions = jnp.arange(length, dtype=jnp.int32)
    doc_index = jnp.sum((positions[:, None] >= bounds[None, :]).astype(jnp.int32), axis=1)
    row_list = [member, blocks - 1 - member]
    query_list = []
    cot_list = []
    pos_list = []
    for which in range(2):
        offset = row_list[which] * block
        query_list.append(lax.dynamic_slice_in_dim(query_head, offset, block, 0))
        cot_list.append(lax.dynamic_slice_in_dim(cot_head, offset, block, 0))
        pos_list.append(offset + jnp.arange(block, dtype=jnp.int32))
    query_stack = jnp.stack(query_list)
    cot_stack = jnp.stack(cot_list)
    pos_stack = jnp.stack(pos_list)
    doc_stack = jnp.take(doc_index, pos_stack)
    plan = []
    for number in range(blocks + 1):
        first = number <= member
        slot = jnp.where(first, 0, 1).astype(jnp.int32)
        col_block = jnp.where(first, number, number - member - 1)
        flag = None
        plan.append((slot, col_block, flag))
    row_max = jnp.full((2, block), -jnp.inf, jnp.float32)
    row_sum = jnp.zeros((2, block), jnp.float32)
    stored = []
    for slot, col_block, flag in plan:

        def score_tile(carry, slot=slot, col_block=col_block):
            maxima, totals = carry
            query_rows = pick_slot(query_stack, slot)
            key_rows = lax.dynamic_slice_in_dim(key_head, col_block * block, block, 0)
            col_docs = lax.dynamic_slice_in_dim(doc_index, col_block * block, block, 0)
            col_positions = col_block * block + jnp.arange(block, dtype=jnp.int32)
            raw = jnp.dot(query_rows, key_rows.T, preferred_element_type=jnp.float32) * scaling
            allowed = (pick_slot(doc_stack, slot)[:, None] == col_docs[None, :]) & (
                pick_slot(pos_stack, slot)[:, None] >= col_positions[None, :]
            )
            scores = jnp.where(allowed, raw, -jnp.inf)
            before = pick_slot(maxima, slot)
            after = jnp.maximum(before, jnp.max(scores, axis=1))
            safe = jnp.where(jnp.isfinite(after), after, 0.0)
            total = pick_slot(totals, slot) * jnp.exp(before - safe) + jnp.sum(
                jnp.exp(scores - safe[:, None]), axis=1
            )
            return (scores, put_slot(maxima, after, slot), put_slot(totals, total, slot))

        scores, row_max, row_sum = score_tile((row_max, row_sum))
        stored.append(scores)

    def tile_weights(scores, slot):
        return (
            jnp.exp(scores - pick_slot(row_max, slot)[:, None]) / pick_slot(row_sum, slot)[:, None]
        )

    summed = jnp.zeros((2, block, HEAD), jnp.float32)
    for (slot, col_block, flag), scores in zip(plan, stored):

        def add_values(carry, slot=slot, col_block=col_block, scores=scores):
            rounded = tile_weights(scores, slot).astype(jnp.bfloat16)
            value_rows = lax.dynamic_slice_in_dim(value_head, col_block * block, block, 0)
            term = jnp.dot(rounded, value_rows, preferred_element_type=jnp.float32)
            return put_slot(carry, pick_slot(carry, slot) + term, slot)

        summed = add_values(summed)
    attended = summed.astype(jnp.bfloat16)
    row_dot = jnp.sum(cot_stack.astype(jnp.float32) * attended.astype(jnp.float32), axis=2)
    query_acc = jnp.zeros((2, block, HEAD), jnp.float32)
    key_acc = jnp.zeros((length, HEAD), jnp.float32)
    value_acc = jnp.zeros((length, HEAD), jnp.float32)
    for (slot, col_block, flag), scores in zip(plan, stored):

        def backward_tile(carry, slot=slot, col_block=col_block, scores=scores):
            query_sum, key_sum, value_sum = carry
            weights = tile_weights(scores, slot)
            rounded = weights.astype(jnp.bfloat16)
            query_rows = pick_slot(query_stack, slot)
            cot_rows = pick_slot(cot_stack, slot)
            start = col_block * block
            key_rows = lax.dynamic_slice_in_dim(key_head, start, block, 0)
            value_rows = lax.dynamic_slice_in_dim(value_head, start, block, 0)
            value_term = jnp.dot(rounded.T, cot_rows, preferred_element_type=jnp.float32)
            prob_grad = jnp.dot(cot_rows, value_rows.T, preferred_element_type=jnp.float32)
            score_grad = (
                weights * (prob_grad - pick_slot(row_dot, slot)[:, None]) * scaling
            ).astype(jnp.bfloat16)
            query_term = jnp.dot(score_grad, key_rows, preferred_element_type=jnp.float32)
            key_term = jnp.dot(score_grad.T, query_rows, preferred_element_type=jnp.float32)
            query_sum = put_slot(query_sum, pick_slot(query_sum, slot) + query_term, slot)
            key_sum = lax.dynamic_update_slice_in_dim(
                key_sum, lax.dynamic_slice_in_dim(key_sum, start, block, 0) + key_term, start, 0
            )
            value_sum = lax.dynamic_update_slice_in_dim(
                value_sum,
                lax.dynamic_slice_in_dim(value_sum, start, block, 0) + value_term,
                start,
                0,
            )
            return (query_sum, key_sum, value_sum)

        query_acc, key_acc, value_acc = backward_tile((query_acc, key_acc, value_acc))
    query_rounded = query_acc.astype(jnp.bfloat16)
    key_back, value_back = (
        lax.all_to_all(key_acc, "seq", split_axis=0, concat_axis=1, tiled=True),
        lax.all_to_all(value_acc, "seq", split_axis=0, concat_axis=1, tiled=True),
    )

    def settle(received):
        shaped = received.astype(jnp.float32).reshape(local_rows, head_count, group, HEAD)
        return jnp.sum(shaped, axis=2).reshape(1, local_rows, local_width).astype(jnp.bfloat16)

    query_full = jnp.zeros((length, HEAD), jnp.bfloat16)
    for which in range(2):
        query_full = lax.dynamic_update_slice_in_dim(
            query_full, query_rounded[which], row_list[which] * block, 0
        )
    query_back = lax.all_to_all(query_full, "seq", split_axis=0, concat_axis=1, tiled=True)
    query_out = settle(query_back)
    return (query_out, settle(key_back), settle(value_back))


NT = ((1,), (1,))
NN = ((1,), (0,))
TN = ((0,), (0,))
GROUP = 8


def head_span(head):
    low = head * HEAD // LANES * LANES
    high = -(-(head + 1) * HEAD // LANES) * LANES
    return low, high


def head_mask(head):
    low, high = head_span(head)
    lane = lax.broadcasted_iota(jnp.int32, (1, high - low), 1) + low
    inside = (lane >= head * HEAD) & (lane < (head + 1) * HEAD)
    return inside.astype(jnp.float32).astype(jnp.bfloat16)


def matmul(left, right, dims):
    return lax.dot_general(left, right, (dims, ((), ())), preferred_element_type=jnp.float32)


def stack(values, axis):
    return values[0] if len(values) == 1 else jnp.concatenate(values, axis=axis)


def allowed(lengths_ref, rows, query_block, key_block):
    position = query_block * rows + lax.broadcasted_iota(jnp.int32, (1, rows), 1)
    keys = key_block * rows + lax.broadcasted_iota(jnp.int32, (rows, rows), 0)
    start = jnp.zeros_like(position)
    bound = jnp.int32(0)
    for doc in range(1, lengths_ref.shape[0]):
        bound = bound + lengths_ref[doc]
        start = jnp.where(position >= bound, bound, start)
    return (keys >= start) & (keys <= position)


def make_tile(lengths_ref, rows, queries, keys):
    mask = stack(
        [stack([allowed(lengths_ref, rows, q, k) for _, q in queries], 1) for _, k in keys], 0
    )
    return [slot for slot, _ in queries], [slot for slot, _ in keys], mask


def tile_values(plan, head, queries, keys, products):
    low, high = head_span(head)
    keep = head_mask(head)

    def gather(refs, number, slots):
        return stack([refs[slot][number][0, :, low:high] for slot in slots], 0)

    out = []
    for query_slots, key_slots, _ in plan:
        q = [gather(queries, number, query_slots) for number in range(products)]
        k = [gather(keys, number, key_slots) * keep for number in range(products)]
        out.append((q, k, [matmul(b, a, NT) for a, b in zip(q, k)]))
    return out, keep


def tiles_ahead(heads, plan, queries, keys, products):
    yield from enumerate([tile_values(plan, head, queries, keys, products) for head in range(heads)])


def pair_tile(lengths_ref, rows, me, slots=(0, 1)):
    mate = me + 1 - 2 * lax.rem(me, 2)
    return make_tile(lengths_ref, rows, ((0, me), (1, mate)), [(slot, me - 2 * slot) for slot in slots])


def third_tile(third, lengths_ref, rows, me):
    slots, keys, mask = make_tile(lengths_ref, rows, ((2, me + 1),), ((1, me - 2),))
    return slots, keys, mask & (me == third)


def lane_cut(value, number, rows):
    return value[:, number * rows : (number + 1) * rows]


def row_of(group, kinds, kind, head):
    return pl.ds((group * kinds + kind) * GROUP + head, 1)


def per_query(slots, kinds, kind, head, ref):
    return stack([ref[row_of(slot, kinds, kind, head), :] for slot in slots], 1)


def collect_stats(heads, power, step, plan, queries, keys, rows, out_ref, groups):
    for head, (tiles, _) in tiles_ahead(heads, plan, queries, keys, 1):
        for (query_slots, _, mask), (_, _, (raw,)) in zip(plan, tiles):
            raw = jnp.where(mask, raw, FLOOR)
            top = jnp.max(raw, axis=0, keepdims=True)
            sums = jnp.sum(jnp.exp2((raw - top) * power), axis=0, keepdims=True)
            for number, slot in enumerate(query_slots):
                at = step * heads + head
                out_ref[row_of(groups[slot], 2, 0, at), :] = lane_cut(top, number, rows)
                out_ref[row_of(groups[slot], 2, 1, at), :] = lane_cut(sums, number, rows)


def stats_kernel(
    heads, power, place_ref, lengths_ref, q_own, q_mate, k_own, k_back, o_own, v_own, o_copy, v_copy, out_ref
):
    rows, me, step = k_own.shape[1], place_ref[0], place_ref[1]
    o_copy[...], v_copy[...] = o_own[...], v_own[...]
    plan = [pair_tile(lengths_ref, rows, me)]
    queries, keys = ((q_own,), (q_mate,)), ((k_own,), (k_back,))
    collect_stats(heads, power, step, plan, queries, keys, rows, out_ref, (0, 1))


def third_stats_kernel(third, heads, power, place_ref, lengths_ref, q_third, k_back, out_ref):
    rows, me, step = k_back.shape[1], place_ref[0], place_ref[1]
    plan = [third_tile(third, lengths_ref, rows, me)]
    queries, keys = (None, None, (q_third,)), (None, (k_back,))
    collect_stats(heads, power, step, plan, queries, keys, rows, out_ref, (None, None, 0))


def part_of(ref, kinds, number):
    size = kinds * GROUP
    return ref[number * size : (number + 1) * size, :]


def group_parts(kinds, mine, sent, extra):
    own = [part_of(mine, kinds, 0), part_of(sent, kinds, 1)]
    mate = [part_of(mine, kinds, 1), part_of(sent, kinds, 0)]
    if extra:
        near, far = extra
        own, mate = own + [near[...]], mate + [far[...]]
    return [own, mate]


def merge_groups(scaling, shift_ref, refs):
    mine, sent, *extra = refs
    for number, parts in enumerate(group_parts(2, mine, sent, extra)):
        shift_ref[number * GROUP : (number + 1) * GROUP, :] = merge_stats(scaling, parts)


def merge_stats(scaling, parts):
    split = [(jnp.where(p[GROUP:] > 0, p[:GROUP], FLOOR), p[GROUP:]) for p in parts]
    top = functools.reduce(jnp.maximum, [s[0] for s in split])
    total = sum(jnp.exp((s[0] - top) * scaling) * s[1] for s in split)
    return top + jnp.log(jnp.where(total > 0, total, 1.0)) / scaling


class Emitter:
    def __init__(self, outs, base={}):
        self.outs, self.base, self.carry = outs, base, {}

    def put(self, name, start, stop, value):
        if name in self.base:
            value = value + self.base[name][0, :, start:stop].astype(jnp.float32)
        self.outs[name][0, :, start:stop] = value.astype(jnp.bfloat16)

    def emit(self, head, name, value):
        low, high = head_span(head)
        first, last = head * HEAD % LANES == 0, (head + 1) * HEAD % LANES == 0
        start, stop = low, high
        if not first:
            self.put(name, low, low + LANES, value[:, :LANES] + self.carry.pop(name))
            start = low + LANES
        if not last:
            self.carry[name] = value[:, high - LANES - low :]
            stop = high - LANES
        if stop > start:
            self.put(name, start, stop, value[:, start - low : stop - low])


def add_rows(sums, kind, slots, value, rows):
    for number, slot in enumerate(slots):
        piece = value[number * rows : (number + 1) * rows]
        name = (kind, slot)
        sums[name] = sums[name] + piece if name in sums else piece


def split_refs(refs):
    return ((refs[0:2], refs[2:4]), (refs[4:6], refs[6:8]), refs[8:])


def values_kernel(merge, slots, heads, scaling, power, place_ref, lengths_ref, q0, o0, q1, o1, *refs):
    key_refs, refs = refs[: len(slots)], refs[len(slots) :]
    queries, keys = ((q0, o0), (q1, o1)), {slot: (ref,) for slot, ref in zip(slots, key_refs)}
    if merge:
        *refs, shift_ref = refs
        stats, value_refs = refs[: -len(slots)], refs[-len(slots) :]
        merge_groups(scaling, shift_ref, stats)
    else:
        shift_ref, value_refs = refs[0], refs[-len(slots) :]
    rows, me, step = q0.shape[1], place_ref[0], place_ref[1]
    plan = [pair_tile(lengths_ref, rows, me, slots)]
    out = Emitter({("v", slot): ref for slot, ref in zip(slots, value_refs)})
    weights = []
    for head, (tiles, keep) in tiles_ahead(heads, plan, queries, keys, 1):
        (query_slots, key_slots, mask), (_, _, (raw,)) = plan[0], tiles[0]
        shift = per_query(query_slots, 1, 0, step * heads + head, shift_ref)
        weight = jnp.where(mask, jnp.exp2((raw - shift) * power), 0.0)
        weights.append((weight.astype(jnp.bfloat16), keep))
    for head, (weight, keep) in enumerate(weights):
        low, high = head_span(head)
        o = stack([queries[slot][1][0, :, low:high] for slot in query_slots], 0) * keep
        sums = {}
        add_rows(sums, "v", key_slots, matmul(weight, o, NN), rows)
        for name, value in sums.items():
            out.emit(head, name, value)


def dots_kernel(merge, heads, scaling, power, place_ref, lengths_ref, *refs):
    queries, keys, refs = split_refs(refs)
    if merge:
        *stats, bundle_ref, dots_ref, shift_ref = refs
        merge_groups(scaling, shift_ref, stats)
        bundle_ref[: 4 * GROUP] = stats[0][...]
    else:
        shift_ref, dots_ref = refs
    rows, me, step = keys[0][0].shape[1], place_ref[0], place_ref[1]
    plan = [pair_tile(lengths_ref, rows, me)]
    for head, (tiles, _) in tiles_ahead(heads, plan, queries, keys, 2):
        at = step * heads + head
        for (query_slots, _, mask), (_, _, (raw, grads)) in zip(plan, tiles):
            shift = per_query(query_slots, 1, 0, at, shift_ref)
            weight = jnp.where(mask, jnp.exp2((raw - shift) * power), 0.0)
            dots = jnp.sum(weight * grads, axis=0, keepdims=True)
            for number, slot in enumerate(query_slots):
                dots_ref[row_of(slot, 1, 0, at), :] = lane_cut(dots, number, rows)
                if merge:
                    bundle_ref[row_of(4 + slot, 1, 0, at), :] = lane_cut(dots, number, rows)


def keys_kernel(third, heads, scaling, power, place_ref, lengths_ref, *refs):
    queries, keys, refs = split_refs(refs)
    (*base, shift_ref, mine, sent), refs = (refs[:3], refs[3:]) if third is None else (refs[:4], refs[4:])
    *extra, key_own, key_back, query_own, query_mate, total_ref = refs
    rows, me, step = keys[0][0].shape[1], place_ref[0], place_ref[1]
    plan = [pair_tile(lengths_ref, rows, me)]
    for number, parts in enumerate(group_parts(1, mine, sent, extra)):
        total_ref[number * GROUP : (number + 1) * GROUP, :] = sum(parts)
    outs = {("k", 0): key_own, ("k", 1): key_back, ("q", 0): query_own, ("q", 1): query_mate}
    out = Emitter(outs, {("k", 1): ref for ref in base})
    slopes = []
    for head, (tiles, keep) in tiles_ahead(heads, plan, queries, keys, 2):
        at = step * heads + head
        (query_slots, key_slots, mask), ((q, _), (k, _), (raw, grads)) = plan[0], tiles[0]
        shift = per_query(query_slots, 1, 0, at, shift_ref)
        dots = per_query(query_slots, 1, 0, at, total_ref)
        weight = jnp.where(mask, jnp.exp2((raw - shift) * power), 0.0)
        slope = (weight * (grads - dots) * scaling).astype(jnp.bfloat16)
        slopes.append((slope, q * keep, k))
    for head, (slope, q, k) in enumerate(slopes):
        sums = {}
        add_rows(sums, "k", key_slots, matmul(slope, q, NN), rows)
        add_rows(sums, "q", query_slots, matmul(slope, k, TN), rows)
        for name, value in sums.items():
            out.emit(head, name, value)


def third_kernel(
    third, heads, scaling, power, place_ref, lengths_ref, q_third, o_third, k_back, v_back, value_part,
    stats, even, odd, value_out, key_out, query_out, dots_ref, shift_ref,
):
    rows, me, step = k_back.shape[1], place_ref[0], place_ref[1]
    parts = [stats[...], part_of(even, 2, 0), part_of(odd, 2, 1)]
    shift_ref[...] = merge_stats(scaling, parts)
    slots, keys, mask = third_tile(third, lengths_ref, rows, me)
    queries, keys = (None, None, (q_third, o_third)), (None, (k_back, v_back))
    plan = [(slots, [1], mask)]
    out = Emitter({"v": value_out, "k": key_out, "q": query_out}, {"v": value_part})
    for head, (tiles, keep) in tiles_ahead(heads, plan, queries, keys, 2):
        (q, o), (k, _), (raw, grads) = tiles[0]
        at = step * heads + head
        weight = jnp.where(mask, jnp.exp2((raw - shift_ref[pl.ds(at, 1), :]) * power), 0.0)
        dots = jnp.sum(weight * grads, axis=0, keepdims=True)
        dots_ref[pl.ds(at, 1), :] = dots
        total = dots + even[row_of(4, 1, 0, at), :] + odd[row_of(5, 1, 0, at), :]
        slope = (weight * (grads - total) * scaling).astype(jnp.bfloat16)
        out.emit(head, "v", matmul(weight.astype(jnp.bfloat16), o * keep, NN))
        out.emit(head, "k", matmul(slope, q * keep, NN))
        out.emit(head, "q", matmul(slope, k, TN))


def add_refs(*refs):
    return sum(ref[...].astype(jnp.float32) for ref in refs)


def sums_kernel(key_part, key_sent, *refs):
    *query_parts, key_out, query_out = refs
    key_out[...] = add_refs(key_part, key_sent).astype(jnp.bfloat16)
    query_out[...] = add_refs(*query_parts).astype(jnp.bfloat16)


def halo_program(third, queries, key_vectors, value_vectors, out_grad, facts):
    _, rows, width = queries.shape
    seq_size = lax.axis_size("seq")
    me = lax.axis_index("seq").astype(jnp.int32)
    scaling = HEAD ** (-0.5)
    power = scaling * math.log2(math.e)
    steps = width // HEAD // 4
    part = width // steps
    heads = part // HEAD
    devices = range(seq_size)
    mates = [(s, s ^ 1) for s in devices]
    ring = third is None
    chain = [(s, s + 2) for s in devices if s + 2 < seq_size]
    ahead = [(s, (s + 2) % seq_size) for s in devices] if ring else chain
    behind = [(s, s - 2) for s in devices if s >= 2]
    if not ring:
        relay, to_odd = [(third + 2, third)], [(third, third + 2)]
        from_even, to_even = [(third + 1, third)], [(third, third + 1)]

    def send(value, pairs):
        return lax.ppermute(value, "seq", pairs)

    smem = pl.BlockSpec(memory_space=pltpu.SMEM)
    vmem = pl.BlockSpec(memory_space=pltpu.VMEM)
    wide_shape = jax.ShapeDtypeStruct((1, rows, width), jnp.bfloat16)

    def slim_shape(groups, kinds):
        return jax.ShapeDtypeStruct((groups * kinds * GROUP, rows), jnp.float32)

    def call(kernel, products, wides, slims, outs, slim_outs, plain=False, scratch=(), after=()):
        flops = 2 * products * 4 * rows * rows * width * 3 // 2
        lead = [] if plain else [me[None], facts]
        inputs = len(lead) + len(wides) + len(slims) + len(after)
        columns = {*range(len(lead), len(lead) + len(wides)), *range(inputs, inputs + outs)}

        def body(*refs):
            def half(step):
                cut = pl.ds(step * part, part)
                views = [ref.at[:, :, cut] if n in columns else ref for n, ref in enumerate(refs)]
                if not plain:
                    views[0] = (refs[0][0], step)
                kernel(*views)

            for step in range(steps):
                half(step)

        return pl.pallas_call(
            body,
            in_specs=[smem] * len(lead)
            + [vmem] * (len(wides) + len(slims))
            + [pl.BlockSpec(memory_space=pl.ANY)] * len(after),
            out_specs=[vmem] * (outs + len(slim_outs)),
            out_shape=[wide_shape] * outs + [slim_shape(*sizes) for sizes in slim_outs],
            scratch_shapes=[pltpu.VMEM((groups * GROUP, rows), jnp.float32) for groups in scratch],
            compiler_params=pltpu.CompilerParams(vmem_limit_bytes=20 * 1024 * 1024),
            cost_estimate=pl.CostEstimate(
                flops=flops, bytes_accessed=20 * rows * width, transcendentals=0
            ),
        )(*lead, *wides, *[value for _, _, value in slims], *after)

    query_mate = send(queries, mates)
    key_back = send(key_vectors, chain)
    grad_mate = send(out_grad, mates)
    value_back = send(value_vectors, ahead)
    grad_own, value_own, stats = call(
        functools.partial(stats_kernel, heads, power), 1,
        [queries, query_mate, key_vectors, key_back, out_grad, value_vectors], [], 2, [(2, 2)],
    )
    stats_mate = send(stats, mates)
    rows_in = [queries, grad_own, query_mate, grad_mate]
    tensors = rows_in + [key_vectors, value_own, key_back, value_back]
    constants = (heads, scaling, power)
    if ring:
        value_sent, shift = call(
            functools.partial(values_kernel, True, (1,), *constants), 1, rows_in + [key_back],
            [(2, 2, stats), (2, 2, stats_mate)], 1, [(2, 1)],
        )
        (dots,) = call(
            functools.partial(dots_kernel, False, *constants), 2, tensors, [(2, 1, shift)], 0, [(2, 1)]
        )
        dots_in = [(2, 1, shift), (2, 1, dots), (2, 1, send(dots, mates))]
        (value_part,) = call(
            functools.partial(values_kernel, False, (0,), *constants), 1, rows_in + [key_vectors],
            [(2, 1, shift)], 1, [], after=[dots],
        )
        base = []
    else:
        query_third = send(query_mate, relay)
        held, stats_mate = lax.optimization_barrier((grad_mate, stats_mate))
        grad_third = send(held, relay)
        query_third, _ = lax.optimization_barrier((query_third, value_back))
        (third_stats,) = call(
            functools.partial(third_stats_kernel, third, heads, power), 1, [query_third, key_back], [],
            0, [(1, 2)],
        )
        stats_in = [(2, 2, stats), (2, 2, stats_mate)]
        stats_in += [(1, 2, send(third_stats, to_even)), (1, 2, send(third_stats, to_odd))]
        bundle, dots, shift = call(
            functools.partial(dots_kernel, True, *constants), 2, tensors, stats_in, 0,
            [(2, 3), (2, 1), (2, 1)],
        )
        even, odd, dots_mate = send(bundle, from_even), send(bundle, relay), send(dots, mates)
        value_part, value_back_part = call(
            functools.partial(values_kernel, False, (0, 1), *constants), 2, rows_in + [key_vectors, key_back],
            [(2, 1, shift)], 2, [],
        )
        value_back_part, dots_mate = lax.optimization_barrier((value_back_part, dots_mate))
        value_sent, key_third, query_extra, third_dots = call(
            functools.partial(third_kernel, third, *constants), 2,
            [query_third, grad_third, key_back, value_back, value_back_part],
            [(1, 2, third_stats), (2, 3, even), (2, 3, odd)],
            3, [(1, 1)], scratch=[1],
        )
        dots_in = [(2, 1, shift), (2, 1, dots), (2, 1, dots_mate)]
        dots_in += [(1, 1, send(third_dots, to_even)), (1, 1, send(third_dots, to_odd))]
        base = [key_third]
    value_received = send(value_sent, behind)
    key_part, key_sent, query_part, query_sent = call(
        functools.partial(keys_kernel, third, *constants), 4, tensors + base, dots_in, 4, [], scratch=[2],
    )
    key_received = send(key_sent, behind)
    query_received = [send(query_sent, mates)] + ([] if ring else [send(query_extra, to_even)])
    value_ready = (value_part.astype(jnp.float32) + value_received.astype(jnp.float32)).astype(jnp.bfloat16)
    key_ready, query_ready = call(
        sums_kernel, 0, [key_part, key_received, query_part, *query_received], [], 2, [], plain=True
    )
    return query_ready, key_ready, value_ready


def program_kernel(shift, lengths_ref, out_ref):
    start, found = jnp.int32(0), jnp.int32(0)
    for doc in range(lengths_ref.shape[0]):
        end = start + lengths_ref[doc]
        last = (end - 1) >> shift
        spans = (last - (start >> shift) >= 3) & (last & 1 == 0)
        found = jnp.where(spans, (last >> 1) - 1, found)
        out_ref[doc + 1] = lengths_ref[doc]
        start = end
    out_ref[0] = found


def program_facts(rows, doc_lengths):
    smem = pl.BlockSpec(memory_space=pltpu.SMEM)
    return pl.pallas_call(
        functools.partial(program_kernel, rows.bit_length() - 1),
        in_specs=[smem],
        out_specs=smem,
        out_shape=jax.ShapeDtypeStruct((doc_lengths.shape[0] + 1,), jnp.int32),
    )(doc_lengths)


def halo_shards(*arguments):
    *tensors, doc_lengths = arguments
    facts = program_facts(tensors[0].shape[1], doc_lengths)
    thirds = range(3, lax.axis_size("seq") - 2, 2)
    programs = [functools.partial(halo_program, third) for third in (None, *thirds)]
    return lax.switch(facts[0], programs, *tensors, facts)


def shards(queries, key_vectors, value_vectors, out_grad, doc_lengths):
    _, rows, width = queries.shape
    seq_size = lax.axis_size("seq")
    longest = rows * seq_size * 3 // 8
    fits = longest <= 3 * rows and seq_size % 2 == 0 and seq_size > 4 and rows == LANES
    heads = width // HEAD
    plan = halo_shards if fits and heads % 4 == 0 and heads <= GROUP else spread_shards
    return plan(queries, key_vectors, value_vectors, out_grad, doc_lengths)


def solution(mesh):
    return jax.shard_map(
        shards,
        mesh=mesh,
        in_specs=(
            P("section", "seq", "dp"),
            P("section", "seq", "dp"),
            P("section", "seq", "dp"),
            P("section", "seq", "dp"),
            P(),
        ),
        out_specs=(P("section", "seq", "dp"), P("section", "seq", "dp"), P("section", "seq", "dp")),
        check_vma=False,
    )
```
